32 devices in a mesh: batch: 16 (over z, y, core), head: 2 (over x).
Axes of the slice: x: 2, y: 2, z: 4, core: 2. Of those that a mesh axis runs over, the one named last changes fastest.
Arguments:
- images: bfloat16 [32, 512, 1024], P('batch', 'head'), may hold values from -6 to 6
- timesteps: int32 [32], P('batch'), may hold values from 0 to 999
- classes: int32 [32], P('batch'), may hold values from 0 to 999
- live_count: int32 [16], P('batch'), may hold values from 1 to 2, as said below
- norm_gain: float32 [3, 512], P(None, 'head'), may hold values from 0.1 to 1.9
- norm_bias: float32 [3, 512], P(None, 'head'), may hold values from -3 to 3
- conv_weight: bfloat16 [2, 9, 512, 512], P(None, None, 'head'), may hold values from -0.09375 to 0.09375
- conv_bias: float32 [2, 512], P(None, 'head'), may hold values from -3 to 3
- emb_weight: bfloat16 [2, 512, 1024], P(None, 'head'), may hold values from -0.1875 to 0.1875
- emb_bias: float32 [2, 512], P(None, 'head'), may hold values from -2 to 2
- class_table: bfloat16 [1000, 1024], replicated, may hold values from -6 to 6
- qkv_weight: bfloat16 [3, 512, 512], P(None, 'head'), may hold values from -0.25 to 0.25
- proj_weight: bfloat16 [512, 512], P('head'), may hold values from -4 to 4
- proj_bias: float32 [512], P('head'), may hold values from -3 to 3
- cotangent: bfloat16 [32, 512, 1024], P('batch', 'head'), may hold values from -6 to 6
Outputs:
- block_out: bfloat16 [32, 512, 1024], P('batch', 'head')
- images_grad: float32 [32, 512, 1024], P('batch', 'head')
- norm_gain_grad: float32 [3, 512], P(None, 'head')
- norm_bias_grad: float32 [3, 512], P(None, 'head')
- conv_weight_grad: float32 [2, 9, 512, 512], P(None, None, 'head')
- conv_bias_grad: float32 [2, 512], P(None, 'head')
- emb_weight_grad: float32 [2, 512, 1024], P(None, 'head')
- emb_bias_grad: float32 [2, 512], P(None, 'head')
- class_table_grad: float32 [1000, 1024], replicated
- qkv_weight_grad: float32 [3, 512, 512], P(None, 'head')
- proj_weight_grad: float32 [512, 512], P('head')
- proj_bias_grad: float32 [512], P('head')
The draws below stay inside these ranges and needn't reach their ends.
Inputs may be any that keep to these rules, and one draw needn't show every extreme that they name: Slots 0 to live_count - 1 of each index of batch hold images; the others are padding. One index holds 2.
All inputs are finite; a program needn't handle non-finite values.
Results may differ from the reference program's by a relative error of at most 0.02.
Values may be sent and summed in bfloat16 or wider, within the bound.
A program may use at most 192 MiB of HBM per device.

```python
import math
import jax
import jax.numpy as jnp
import numpy as np
from jax import lax

C = 512
GROUPS = 32
HEADS = 8
E = 1024
NCLS = 1000
SIDE = 32
IMG_DEV = 2
PIX = 1024
HD = 64
IMAGES = 32
N_BATCH = 16


def draw_live_count(key, part):
    key = jax.random.fold_in(key, 17)
    first_key, second_key = jax.random.split(key)
    counts = jax.random.randint(first_key, (N_BATCH,), IMG_DEV // 2, IMG_DEV + 1)
    fullest = jax.random.randint(second_key, (), 0, N_BATCH)
    return jnp.where(jnp.arange(N_BATCH) == fullest, IMG_DEV, counts).astype(jnp.int32)


def place_ends(entries, rng, low, top_value):
    shape = entries.shape
    index_at = [jax.random.randint(jax.random.fold_in(rng, axis), (), 0, shape[axis]) for axis in range(len(shape))]
    entries = entries.at[tuple(index_at)].set(low)
    longest = shape.index(max(shape))
    index_at[longest] = (index_at[longest] + 1) % shape[longest]
    return entries.at[tuple(index_at)].set(top_value)


def levels(rng, shape, pieces, smallest, high):
    factor_of = 1.0
    for position, shards_of in pieces:
        draws = jax.random.uniform(jax.random.fold_in(jax.random.fold_in(rng, 6), position), (shards_of,), jnp.float32, smallest / len(pieces), high / len(pieces))
        factor_of = factor_of * jnp.repeat(jnp.exp(draws), shape[position] // shards_of).reshape((-1,) + (1,) * (len(shape) - 1 - position))
    return factor_of


def rank_bounds(count, skew):
    loads = [(1 << 20) // math.isqrt(grade ** skew) + 1 for grade in range(1, count + 1)]
    deviation = 1 + sum(loads) // (1 << 30)
    return np.cumsum(np.array([max(1, weight // deviation) for weight in loads]))


def ranked_ids(own_key, extent, number_of, lean):
    table = rank_bounds(number_of, lean)
    pick = jax.random.randint(jax.random.fold_in(own_key, 1), extent, 0, int(table[number_of - 1]))
    standing = jnp.searchsorted(jnp.asarray(table, jnp.int32), pick, side="right")
    return jax.random.permutation(jax.random.fold_in(own_key, 2), number_of)[standing].astype(jnp.int32)


def centred(stream_key, shape, deviation, limit, shards=(), kind=jnp.bfloat16):
    entries = deviation * jax.random.normal(stream_key, shape, jnp.float32)
    if shards:
        entries = entries * levels(stream_key, shape, shards, -0.22, 0.18)
    return jnp.clip(entries, -limit, limit).astype(kind)


def setup_inputs(seed: int = 0) -> dict:
    streams_of = jax.random.split(jax.random.key(seed), 16)
    images = centred(streams_of[0], (IMAGES, C, PIX), 1.0, 6.0, ((0, 16), (1, 2)))
    timesteps = place_ends(jax.random.randint(streams_of[1], (IMAGES,), 0, 1000), jax.random.fold_in(streams_of[1], 1), 0, 999).astype(jnp.int32)
    classes = place_ends(ranked_ids(streams_of[2], (IMAGES,), NCLS, 2), jax.random.fold_in(streams_of[2], 3), 0, NCLS - 1).astype(jnp.int32)
    live_count = draw_live_count(jax.random.fold_in(streams_of[15], 71), 0)
    norm_gain = jnp.clip(1.0 + 0.18 * jax.random.normal(streams_of[4], (3, C), jnp.float32), 0.1, 1.9)
    norm_bias = centred(streams_of[5], (3, C), 0.5, 3.0, ((1, 2),), jnp.float32)
    conv_weight = centred(streams_of[6], (2, 9, C, C), (9 * C) ** -0.5, 0.09375, ((2, 2),))
    conv_bias = centred(streams_of[7], (2, C), 0.5, 3.0, ((1, 2),), jnp.float32)
    emb_weight = centred(streams_of[8], (2, C, E), E ** -0.5, 0.1875, ((1, 2),))
    emb_bias = centred(streams_of[9], (2, C), 0.3, 2.0, ((1, 2),), jnp.float32)
    class_table = centred(streams_of[10], (NCLS, E), 1.0, 6.0)
    qkv_weight = centred(streams_of[11], (3, C, C), C ** -0.5, 0.25, ((1, 2),))
    proj_weight = centred(streams_of[12], (C, C), (max(C // 256, 1)) ** -0.5, 4.0, ((0, 2),))
    proj_bias = centred(streams_of[13], (C,), 0.5, 3.0, ((0, 2),), jnp.float32)
    cotangent = centred(streams_of[14], (IMAGES, C, PIX), 1.0, 6.0, ((0, 16), (1, 2)))
    return dict(images=images, timesteps=timesteps, classes=classes, live_count=live_count, norm_gain=norm_gain, norm_bias=norm_bias, conv_weight=conv_weight, conv_bias=conv_bias, emb_weight=emb_weight, emb_bias=emb_bias, class_table=class_table, qkv_weight=qkv_weight, proj_weight=proj_weight, proj_bias=proj_bias, cotangent=cotangent)


EPS = 1e-05
HIGH = lax.Precision.HIGHEST

@jax.custom_vjp
def low(v):
    return lax.optimization_barrier(v.astype(jnp.bfloat16)).astype(jnp.float32)

@jax.custom_vjp
def low_back(v):
    return v

def low_keep(v):
    return (low(v), None)

def low_pass(kept, grad):
    return (grad,)

def back_keep(v):
    return (v, None)

def back_low(kept, grad):
    return (low(grad),)
low.defvjp(low_keep, low_pass)
low_back.defvjp(back_keep, back_low)

def group_norm(source, gain, offset):
    grouped = source.reshape(GROUPS, -1)
    centre = grouped - lax.optimization_barrier(jnp.mean(grouped, axis=1, keepdims=True))
    scaled = centre * lax.rsqrt(lax.optimization_barrier(jnp.mean(jnp.square(centre), axis=1, keepdims=True)) + EPS)
    return scaled.reshape(source.shape) * gain[:, None] + offset[:, None]

def moved(source, row_step, col_step):
    grid = source.reshape(source.shape[0], SIDE, SIDE)
    padded = jnp.pad(grid, ((0, 0), (1, 1), (1, 1)))
    window = padded[:, 1 + row_step:1 + row_step + SIDE, 1 + col_step:1 + col_step + SIDE]
    return window.reshape(source.shape)

def convolve(source, weight, offset):
    result = jnp.dot(weight[0], moved(source, -1, -1), precision=HIGH) + offset[:, None]
    for tap_index in range(1, 9):
        result = result + jnp.dot(weight[tap_index], moved(source, tap_index // 3 - 1, tap_index % 3 - 1), precision=HIGH)
    return result

def features(timestep):
    half_width = E // 2
    freqs = jnp.exp(-math.log(10000.0) * jnp.arange(half_width, dtype=jnp.float32) / half_width)
    angles = timestep.astype(jnp.float32) * freqs
    return jnp.concatenate([jnp.cos(angles), jnp.sin(angles)])

def one_picture(params, picture, timestep, class_id, live_flag):
    norm_gain, norm_bias, conv_weight, conv_bias, emb_weight, emb_bias, class_table, qkv_weight, proj_weight, proj_bias = params
    embed = jax.nn.silu(features(timestep) + class_table[class_id])
    scale = jnp.dot(emb_weight[0], embed, precision=HIGH) + emb_bias[0]
    shift = jnp.dot(emb_weight[1], embed, precision=HIGH) + emb_bias[1]
    first = low(jax.nn.silu(group_norm(picture, norm_gain[0], norm_bias[0])))
    hidden = low_back(convolve(first, conv_weight[0], conv_bias[0]))
    inner = group_norm(hidden, norm_gain[1], norm_bias[1]) * (1.0 + scale[:, None]) + shift[:, None]
    second = low(jax.nn.silu(inner))
    branch = low_back(convolve(second, conv_weight[1], conv_bias[1]))
    resid = picture + branch
    normed = low(group_norm(resid, norm_gain[2], norm_bias[2]))
    query = low_back(low(jnp.dot(qkv_weight[0], normed, precision=HIGH))).reshape(HEADS, HD, PIX)
    keys = low_back(low(jnp.dot(qkv_weight[1], normed, precision=HIGH))).reshape(HEADS, HD, PIX)
    values = low_back(low(jnp.dot(qkv_weight[2], normed, precision=HIGH))).reshape(HEADS, HD, PIX)
    scores = low_back(jnp.einsum('hdi,hdj->hij', query, keys, precision=HIGH) * HD ** (-0.5))
    highest = lax.optimization_barrier(jnp.max(scores, axis=2, keepdims=True))
    expo = jnp.exp(scores - highest)
    probs = expo / lax.optimization_barrier(jnp.sum(expo, axis=2, keepdims=True))
    weights = low(probs)
    mixed = low_back(low(jnp.einsum('hdj,hij->hdi', values, weights, precision=HIGH))).reshape(C, PIX)
    result = resid + jnp.dot(proj_weight.T, mixed, precision=HIGH) + proj_bias[:, None]
    return live_flag * result

def reference(images, timesteps, classes, live_count, norm_gain, norm_bias, conv_weight, conv_bias, emb_weight, emb_bias, class_table, qkv_weight, proj_weight, proj_bias, cotangent):
    params = (norm_gain.astype(jnp.float32), norm_bias.astype(jnp.float32), conv_weight.astype(jnp.float32), conv_bias.astype(jnp.float32), emb_weight.astype(jnp.float32), emb_bias.astype(jnp.float32), class_table.astype(jnp.float32), qkv_weight.astype(jnp.float32), proj_weight.astype(jnp.float32), proj_bias.astype(jnp.float32))
    pictures = images.astype(jnp.float32)
    slots = jnp.arange(IMAGES, dtype=jnp.int32)
    flags = (slots % IMG_DEV < live_count[slots // IMG_DEV]).astype(jnp.float32)

    def forward(params_in, pictures_in):

        def per_picture(item):
            picture, timestep, class_id, live_flag = item
            return one_picture(params_in, picture, timestep, class_id, live_flag)
        return lax.map(jax.checkpoint(per_picture), (pictures_in, timesteps, classes, flags))
    result, pullback = jax.vjp(forward, params, pictures)
    grads, picture_grad = pullback(cotangent.astype(jnp.float32))
    return (result.astype(jnp.bfloat16), picture_grad, grads[0], grads[1], grads[2], grads[3], grads[4], grads[5], grads[6], grads[7], grads[8], grads[9])
```

```python
import functools
import math

import jax
import jax.numpy as jnp
from jax import lax
from jax.experimental import pallas as pl
from jax.experimental.pallas import tpu as pltpu
from jax.sharding import PartitionSpec as P

C = 512
GROUPS = 32
HEADS = 8
SIDE = 32


EPS = 1e-05
HIGH = lax.Precision.HIGHEST
CONTRACT_FIRST = (((0,), (0,)), ((), ()))
CONTRACT_LAST = (((1,), (1,)), ((), ()))


def silu_slope(values):
    sigma = jax.nn.sigmoid(values)
    return sigma * (1.0 + values * (1.0 - sigma))


def moved(source, grid_side, row_step, col_step):
    grid = source.reshape(source.shape[0], grid_side, grid_side)
    padded = jnp.pad(grid, ((0, 0), (1, 1), (1, 1)))
    window = padded[
        :, 1 + row_step : 1 + row_step + grid_side, 1 + col_step : 1 + col_step + grid_side
    ]
    return window.reshape(source.shape)


def group_unit(source, groups):
    grouped = source.reshape(groups, -1)
    centre = grouped - jnp.mean(grouped, axis=1, keepdims=True)
    inverse = lax.rsqrt(jnp.mean(jnp.square(centre), axis=1, keepdims=True) + EPS)
    return ((centre * inverse).reshape(source.shape), inverse)


def group_back(grad_unit, unit_rows, inverse, groups):
    flat_grad = grad_unit.reshape(groups, -1)
    flat_unit = unit_rows.reshape(groups, -1)
    result = flat_grad - jnp.mean(flat_grad, axis=1, keepdims=True)
    result = (result - flat_unit * jnp.mean(flat_grad * flat_unit, axis=1, keepdims=True)) * inverse
    return result.reshape(grad_unit.shape)


def conv_apply(weight, source, grid_side):
    result = jnp.dot(
        weight[0], moved(source, grid_side, -1, -1), preferred_element_type=jnp.float32
    )
    for tap_index in range(1, 9):
        result = result + jnp.dot(
            weight[tap_index],
            moved(source, grid_side, tap_index // 3 - 1, tap_index % 3 - 1),
            preferred_element_type=jnp.float32,
        )
    return result


def conv_transpose(weight, grads, grid_side):
    result = lax.dot_general(
        weight[0], moved(grads, grid_side, 1, 1), CONTRACT_FIRST, preferred_element_type=jnp.float32
    )
    for tap_index in range(1, 9):
        result = result + lax.dot_general(
            weight[tap_index],
            moved(grads, grid_side, 1 - tap_index // 3, 1 - tap_index % 3),
            CONTRACT_FIRST,
            preferred_element_type=jnp.float32,
        )
    return result


def conv_weight_grads(grads, source, grid_side):
    return jnp.stack(
        [
            lax.dot_general(
                grads,
                moved(source, grid_side, tap_index // 3 - 1, tap_index % 3 - 1),
                CONTRACT_LAST,
                preferred_element_type=jnp.float32,
            )
            for tap_index in range(9)
        ]
    )


def features(timestep, emb_width):
    half_width = emb_width // 2
    freqs = jnp.exp(-math.log(10000.0) * jnp.arange(half_width, dtype=jnp.float32) / half_width)
    angles = timestep.astype(jnp.float32) * freqs
    return jnp.concatenate([jnp.cos(angles), jnp.sin(angles)])


def shards(
    images,
    timesteps,
    classes,
    live_count,
    norm_gain,
    norm_bias,
    conv_weight,
    conv_bias,
    emb_weight,
    emb_bias,
    class_table,
    qkv_weight,
    proj_weight,
    proj_bias,
    cotangent,
):
    slot_count, chan_dev, pixel_count = images.shape
    grid_side = SIDE
    groups = chan_dev // (C // GROUPS)
    head_size = C // HEADS
    heads_dev = chan_dev // head_size
    att_scale = head_size ** (-0.5)
    emb_dense = emb_weight.astype(jnp.float32)
    class_total, emb_width = class_table.shape

    def gather_channels(rows_low):
        return lax.all_gather(rows_low, "head", axis=0, tiled=True)

    def input_grad(which_conv, grad_rows):
        weight_cols = conv_weight[which_conv]
        return lax.psum_scatter(
            conv_transpose(weight_cols, grad_rows, grid_side).astype(jnp.bfloat16),
            "head",
            scatter_dimension=0,
            tiled=True,
        ).astype(jnp.float32)

    def per_slot(slot_index, carry):
        (
            outputs,
            grads_in,
            gain_acc,
            bias_acc,
            convw_acc,
            convb_acc,
            embw_acc,
            embb_acc,
            table_acc,
            qkv_acc,
            projw_acc,
            projb_acc,
        ) = carry
        picture = lax.dynamic_index_in_dim(images, slot_index, 0, keepdims=False).astype(
            jnp.float32
        )
        live_flag = (slot_index < live_count[0]).astype(jnp.float32)
        class_id = classes[slot_index]
        table_row = lax.dynamic_index_in_dim(class_table, class_id, 0, keepdims=False).astype(
            jnp.float32
        )
        pre_embed = features(timesteps[slot_index], emb_width) + table_row
        embed = jax.nn.silu(pre_embed)
        scale = jnp.dot(emb_dense[0], embed, precision=HIGH) + emb_bias[0]
        shift = jnp.dot(emb_dense[1], embed, precision=HIGH) + emb_bias[1]
        unit_zero, inverse_zero = group_unit(picture, groups)
        pre_first = unit_zero * norm_gain[0][:, None] + norm_bias[0][:, None]
        first_full = gather_channels(jax.nn.silu(pre_first).astype(jnp.bfloat16))
        hidden = conv_apply(conv_weight[0], first_full, grid_side) + conv_bias[0][:, None]
        unit_one, inverse_one = group_unit(hidden, groups)
        normed_one = unit_one * norm_gain[1][:, None] + norm_bias[1][:, None]
        pre_second = normed_one * (1.0 + scale[:, None]) + shift[:, None]
        second_full = gather_channels(jax.nn.silu(pre_second).astype(jnp.bfloat16))
        resid = picture + conv_apply(conv_weight[1], second_full, grid_side) + conv_bias[1][:, None]
        unit_two, inverse_two = group_unit(resid, groups)
        normed_full = gather_channels(
            (unit_two * norm_gain[2][:, None] + norm_bias[2][:, None]).astype(jnp.bfloat16)
        )
        query = (
            jnp.dot(qkv_weight[0], normed_full, preferred_element_type=jnp.float32)
            .astype(jnp.bfloat16)
            .reshape(heads_dev, head_size, pixel_count)
        )
        keys = (
            jnp.dot(qkv_weight[1], normed_full, preferred_element_type=jnp.float32)
            .astype(jnp.bfloat16)
            .reshape(heads_dev, head_size, pixel_count)
        )
        values = (
            jnp.dot(qkv_weight[2], normed_full, preferred_element_type=jnp.float32)
            .astype(jnp.bfloat16)
            .reshape(heads_dev, head_size, pixel_count)
        )
        scores = (
            jnp.einsum("hdi,hdj->hij", query, keys, preferred_element_type=jnp.float32) * att_scale
        )
        highest = jnp.max(scores, axis=2, keepdims=True)
        expo = jnp.exp(scores - highest)
        totals = jnp.sum(expo, axis=2, keepdims=True)
        log_total = highest + jnp.log(totals)
        weights = (expo / totals).astype(jnp.bfloat16)
        mixed = (
            jnp.einsum("hdj,hij->hdi", values, weights, preferred_element_type=jnp.float32)
            .astype(jnp.bfloat16)
            .reshape(chan_dev, pixel_count)
        )
        weight_cols = proj_weight
        proj_term = lax.psum_scatter(
            lax.dot_general(
                weight_cols, mixed, CONTRACT_FIRST, preferred_element_type=jnp.float32
            ).astype(jnp.bfloat16),
            "head",
            scatter_dimension=0,
            tiled=True,
        ).astype(jnp.float32)
        result = resid + proj_term + proj_bias[:, None]
        outputs = lax.dynamic_update_index_in_dim(
            outputs, (live_flag * result).astype(jnp.bfloat16), slot_index, 0
        )
        grad_low = lax.dynamic_index_in_dim(cotangent, slot_index, 0, keepdims=False)
        grad_out = live_flag * grad_low.astype(jnp.float32)
        grad_full = lax.all_gather(grad_low, "head", axis=0, tiled=True) * live_flag.astype(
            jnp.bfloat16
        )
        grad_mixed = jnp.dot(proj_weight, grad_full, preferred_element_type=jnp.float32).astype(
            jnp.bfloat16
        )
        projw_acc = projw_acc + lax.dot_general(
            mixed, grad_full, CONTRACT_LAST, preferred_element_type=jnp.float32
        )
        projb_acc = projb_acc + jnp.sum(grad_out, axis=1)
        again = (
            jnp.einsum("hdi,hdj->hij", query, keys, preferred_element_type=jnp.float32) * att_scale
        )
        probs = jnp.exp(again - log_total)
        grad_heads = grad_mixed.reshape(heads_dev, head_size, pixel_count)
        grad_probs = jnp.einsum(
            "hdi,hdj->hij", grad_heads, values, preferred_element_type=jnp.float32
        )
        grad_scores = (
            probs * (grad_probs - jnp.sum(grad_probs * probs, axis=2, keepdims=True))
        ).astype(jnp.bfloat16)
        grad_query = (
            jnp.einsum("hij,hdj->hdi", grad_scores, keys, preferred_element_type=jnp.float32)
            * att_scale
        ).astype(jnp.bfloat16)
        grad_keys = (
            jnp.einsum("hij,hdi->hdj", grad_scores, query, preferred_element_type=jnp.float32)
            * att_scale
        ).astype(jnp.bfloat16)
        grad_values = jnp.einsum(
            "hdi,hij->hdj", grad_heads, weights, preferred_element_type=jnp.float32
        ).astype(jnp.bfloat16)
        stacked = jnp.stack([grad_query, grad_keys, grad_values]).reshape(3, chan_dev, pixel_count)
        weight_cols = qkv_weight
        grad_normed = lax.psum_scatter(
            lax.dot_general(
                weight_cols,
                stacked,
                (((0, 1), (0, 1)), ((), ())),
                preferred_element_type=jnp.float32,
            ).astype(jnp.bfloat16),
            "head",
            scatter_dimension=0,
            tiled=True,
        ).astype(jnp.float32)
        qkv_acc = qkv_acc + lax.dot_general(
            stacked, normed_full, (((2,), (1,)), ((), ())), preferred_element_type=jnp.float32
        )
        grad_resid = grad_out + group_back(
            grad_normed * norm_gain[2][:, None], unit_two, inverse_two, groups
        )
        grad_branch = grad_resid.astype(jnp.bfloat16)
        grad_second = input_grad(1, grad_branch)
        grad_pre = grad_second * silu_slope(pre_second)
        scale_grad = jnp.sum(grad_pre * normed_one, axis=1)
        shift_grad = jnp.sum(grad_pre, axis=1)
        grad_normed_one = grad_pre * (1.0 + scale[:, None])
        grad_hidden = group_back(
            grad_normed_one * norm_gain[1][:, None], unit_one, inverse_one, groups
        ).astype(jnp.bfloat16)
        grad_first = input_grad(0, grad_hidden)
        grad_pre_first = grad_first * silu_slope(pre_first)
        picture_grad = grad_resid + group_back(
            grad_pre_first * norm_gain[0][:, None], unit_zero, inverse_zero, groups
        )
        grads_in = lax.dynamic_update_index_in_dim(grads_in, picture_grad, slot_index, 0)
        gain_acc = gain_acc + jnp.stack(
            [
                jnp.sum(grad_pre_first * unit_zero, axis=1),
                jnp.sum(grad_normed_one * unit_one, axis=1),
                jnp.sum(grad_normed * unit_two, axis=1),
            ]
        )
        bias_acc = bias_acc + jnp.stack(
            [
                jnp.sum(grad_pre_first, axis=1),
                jnp.sum(grad_normed_one, axis=1),
                jnp.sum(grad_normed, axis=1),
            ]
        )
        convw_acc = convw_acc + jnp.stack(
            [
                conv_weight_grads(grad_hidden, first_full, grid_side),
                conv_weight_grads(grad_branch, second_full, grid_side),
            ]
        )
        convb_acc = convb_acc + jnp.stack(
            [
                jnp.sum(grad_hidden.astype(jnp.float32), axis=1),
                jnp.sum(grad_branch.astype(jnp.float32), axis=1),
            ]
        )
        embw_acc = embw_acc + jnp.stack(
            [scale_grad[:, None] * embed[None, :], shift_grad[:, None] * embed[None, :]]
        )
        embb_acc = embb_acc + jnp.stack([scale_grad, shift_grad])
        grad_embed = jnp.dot(scale_grad, emb_dense[0], precision=HIGH) + jnp.dot(
            shift_grad, emb_dense[1], precision=HIGH
        )
        class_row = grad_embed * silu_slope(pre_embed)
        old_row = lax.dynamic_index_in_dim(table_acc, class_id, 0, keepdims=True)
        table_acc = lax.dynamic_update_index_in_dim(
            table_acc, old_row + class_row[None, :], class_id, 0
        )
        return (
            outputs,
            grads_in,
            gain_acc,
            bias_acc,
            convw_acc,
            convb_acc,
            embw_acc,
            embb_acc,
            table_acc,
            qkv_acc,
            projw_acc,
            projb_acc,
        )

    table_start = jnp.zeros(class_table.shape, jnp.float32)
    initial = (
        jnp.zeros(images.shape, jnp.bfloat16),
        jnp.zeros(images.shape, jnp.float32),
        jnp.zeros(norm_gain.shape, jnp.float32),
        jnp.zeros(norm_bias.shape, jnp.float32),
        jnp.zeros(conv_weight.shape, jnp.float32),
        jnp.zeros(conv_bias.shape, jnp.float32),
        jnp.zeros(emb_weight.shape, jnp.float32),
        jnp.zeros(emb_bias.shape, jnp.float32),
        table_start,
        jnp.zeros(qkv_weight.shape, jnp.float32),
        jnp.zeros(proj_weight.shape, jnp.float32),
        jnp.zeros(proj_bias.shape, jnp.float32),
    )
    final = lax.fori_loop(0, slot_count, per_slot, initial)
    (
        outputs,
        grads_in,
        gain_acc,
        bias_acc,
        convw_acc,
        convb_acc,
        embw_acc,
        embb_acc,
        table_acc,
        qkv_acc,
        projw_acc,
        projb_acc,
    ) = final
    table_total = lax.psum(table_acc, ("batch", "head"))
    summed = (
        lax.psum(gain_acc.astype(jnp.bfloat16), "batch").astype(jnp.float32),
        lax.psum(bias_acc.astype(jnp.bfloat16), "batch").astype(jnp.float32),
        lax.psum(convw_acc.astype(jnp.bfloat16), "batch").astype(jnp.float32),
        lax.psum(convb_acc.astype(jnp.bfloat16), "batch").astype(jnp.float32),
        lax.psum(embw_acc.astype(jnp.bfloat16), "batch").astype(jnp.float32),
        lax.psum(embb_acc.astype(jnp.bfloat16), "batch").astype(jnp.float32),
        lax.psum(qkv_acc.astype(jnp.bfloat16), "batch").astype(jnp.float32),
        lax.psum(projw_acc.astype(jnp.bfloat16), "batch").astype(jnp.float32),
        lax.psum(projb_acc.astype(jnp.bfloat16), "batch").astype(jnp.float32),
    )
    return (
        outputs,
        grads_in,
        summed[0],
        summed[1],
        summed[2],
        summed[3],
        summed[4],
        summed[5],
        table_total,
        summed[6],
        summed[7],
        summed[8],
    )


PIX = 1024
BF = jnp.bfloat16
F32 = jnp.float32
NN = (((1,), (0,)), ((), ()))
TN = (((0,), (0,)), ((), ()))
NT = (((1,), (1,)), ((), ()))
VMEM = pl.BlockSpec(memory_space=pltpu.VMEM)
SMEM = pl.BlockSpec(memory_space=pltpu.SMEM)

GAIN, BIAS, CONVB, PROJB, SCALE, SHIFT = 0, 3, 6, 8, 9, 10


def mm(left, right, dims=NN):
    return lax.dot_general(left, right, dims, preferred_element_type=F32)


def kernel_call(kernel, outs, scratch, flops, scalars, *args):
    moved_bytes = sum(a.size * a.dtype.itemsize for a in args)
    moved_bytes += sum(math.prod(o.shape) * o.dtype.itemsize for o in outs)
    return pl.pallas_call(
        kernel,
        out_shape=outs,
        in_specs=[SMEM] + [VMEM] * len(args),
        out_specs=[VMEM] * len(outs),
        scratch_shapes=scratch,
        cost_estimate=pl.CostEstimate(flops=flops, bytes_accessed=moved_bytes, transcendentals=0),
        compiler_params=pltpu.CompilerParams(vmem_limit_bytes=56 * 2**20),
    )(scalars, *args)


def out(shape, dtype):
    return jax.ShapeDtypeStruct(shape, dtype)


def rows(start, count):
    return pl.ds(pl.multiple_of(start, count), count)


def edge_masks(sign):
    pixel = lax.broadcasted_iota(jnp.int32, (1, PIX), 1)
    col, row = pixel % SIDE, pixel // SIDE
    table = {}
    for step in (-1, 1):
        moved_step = sign * step
        table["col", step] = ((col + moved_step >= 0) & (col + moved_step < SIDE)).astype(F32)
        table["row", step] = ((row + moved_step >= 0) & (row + moved_step < SIDE)).astype(F32)
    return table


def put_taps(dest, masks, values, first_row, depth, base, sign):
    count = values.shape[0]
    for col_step in (-1, 0, 1):
        across = values
        if col_step:
            across = pltpu.roll(values, (-sign * col_step) % PIX, 1) * masks["col", col_step]
        for row_step in (-1, 0, 1):
            copy = across
            if row_step:
                copy = pltpu.roll(across, (-sign * row_step * SIDE) % PIX, 1) * masks["row", row_step]
            tap = 3 * (row_step + 1) + col_step + 1
            dest[rows(tap * depth + first_row, count), base : base + PIX] = copy.astype(BF)


def taps_of(dest, masks, source, offset, depth, base, sign):
    def step(index, carry):
        piece = source[rows(index * 16, 16), :].astype(F32)
        put_taps(dest, masks, piece, offset + index * 16, depth, base, sign)
        return carry

    lax.fori_loop(0, source.shape[0] // 16, step, 0, unroll=2)


def place_conv(full, index, own, part, peer):
    half, core = index[0], index[1]
    full[:, rows(half * 256, 256), :] = own[...]
    full[:, rows((1 - half) * 256 + core * 128, 128), :] = part[...]
    full[:, rows((1 - half) * 256 + (1 - core) * 128, 128), :] = peer[...]


def conv_dots(dest, full, col, dims, finish):
    for column in range(0, PIX, 512):
        total = None
        for tap in range(9):
            term = mm(full[tap], col[tap * 512 : (tap + 1) * 512, column : column + 512], dims)
            total = term if total is None else total + term
        dest[:, column : column + 512] = finish(total, column)


def group_stats(block):
    centre = jnp.mean(block, keepdims=True)
    moved_block = block - centre
    inverse = lax.rsqrt(jnp.mean(jnp.square(moved_block), keepdims=True) + EPS)
    return centre, inverse, moved_block * inverse


def keep_stats(stats, where, centre, inverse):
    stats[where, 0:1] = jnp.broadcast_to(centre, (16, 1))
    stats[where, 1:2] = jnp.broadcast_to(inverse, (16, 1))


def unit_of(block, stats, where):
    return (block - stats[where, 0:1]) * stats[where, 1:2]


def unit_back(grad, unit, inverse):
    mean_grad = jnp.mean(grad, keepdims=True)
    mean_both = jnp.mean(grad * unit, keepdims=True)
    return (grad - mean_grad - unit * mean_both) * inverse


def row_sum(block):
    return jnp.sum(block, axis=1, keepdims=True)


def first_conv(index, own, peer, par, w_own, w_part, w_peer, first, hidden, stats0, stats1, second, col, full):
    half = index[0]
    place_conv(full, index, w_own, w_part, w_peer)
    masks = edge_masks(1)
    for source, base in ((own, half * 256), (peer, (1 - half) * 256)):

        def norm(group, carry, source=source, base=base):
            where = rows(base + group * 16, 16)
            centre, inverse, unit = group_stats(source[rows(group * 16, 16), :].astype(F32))
            keep_stats(stats0, where, centre, inverse)
            low = jax.nn.silu(unit * par[where, GAIN : GAIN + 1] + par[where, BIAS : BIAS + 1]).astype(BF)
            first[where, :] = low
            put_taps(col, masks, low.astype(F32), base + group * 16, 512, 0, 1)
            return carry

        lax.fori_loop(0, 16, norm, 0, unroll=2)
    conv_dots(hidden, full, col, NN, lambda total, column: total + par[:, CONVB : CONVB + 1])

    def again(group, carry):
        where = rows(group * 16, 16)
        centre, inverse, unit = group_stats(hidden[where, :])
        keep_stats(stats1, where, centre, inverse)
        normed = unit * par[where, GAIN + 1 : GAIN + 2] + par[where, BIAS + 1 : BIAS + 2]
        pre = normed * (1.0 + par[where, SCALE : SCALE + 1]) + par[where, SHIFT : SHIFT + 1]
        second[where, :] = jax.nn.silu(pre).astype(BF)
        return carry

    lax.fori_loop(0, 32, again, 0, unroll=2)


def second_conv(index, source, own, peer, par, w_own, w_part, w_peer, resid, stats2, normed, col, full):
    half = index[0]
    place_conv(full, index, w_own, w_part, w_peer)
    taps_of(col, edge_masks(1), source, 0, 512, 0, 1)
    conv_dots(resid, full, col, NN, lambda total, column: total + par[:, CONVB + 1 : CONVB + 2])
    for picture, base in ((own, half * 256), (peer, (1 - half) * 256)):

        def norm(group, carry, picture=picture, base=base):
            where = rows(base + group * 16, 16)
            block = resid[where, :] + picture[rows(group * 16, 16), :].astype(F32)
            resid[where, :] = block
            centre, inverse, unit = group_stats(block)
            keep_stats(stats2, where, centre, inverse)
            normed[where, :] = (unit * par[where, GAIN + 2 : GAIN + 3] + par[where, BIAS + 2 : BIAS + 3]).astype(BF)
            return carry

        lax.fori_loop(0, 16, norm, 0, unroll=2)


def place_square(full, index, own, peer):
    half = index[0]
    count = own.shape[0]
    full[rows(half * count, count), :] = own[...]
    full[rows((1 - half) * count, count), :] = peer[...]


def attention(
    index, normed, resid, stats2, par, cot_own, cot_peer, q_own, q_peer, p_own, p_peer,
    mixed, grad_q, grad_k, grad_v, grad_out, grad_resid, grad_branch, small,
    wq, wk, wv, wp, query, keys, values, grad_mixed, weights, grad_scores, grad_normed,
):
    half = index[0]
    live = index[2] > 0
    for which, full in enumerate((wq, wk, wv)):
        place_square(full, index, q_own.at[which], q_peer.at[which])
    place_square(wp, index, p_own, p_peer)
    for cotangent, base in ((cot_own, half * 256), (cot_peer, (1 - half) * 256)):
        grad_out[rows(base, 256), :] = jnp.where(live, cotangent[...], jnp.zeros_like(cotangent[...]))
    for column in range(0, PIX, 512):
        where = slice(column, column + 512)
        query[:, where] = (mm(wq[...], normed[:, where]).astype(BF).astype(F32) * 0.125).astype(BF)
        keys[:, where] = mm(wk[...], normed[:, where]).astype(BF)
        values[:, where] = mm(wv[...], normed[:, where]).astype(BF)
        grad_mixed[:, where] = mm(wp[...], grad_out[:, where]).astype(BF)

    def head(number, carry):
        where = rows(number * 64, 64)
        q, k, v, g = query[where, :], keys[where, :], values[where, :], grad_mixed[where, :]
        scores = mm(k.T, q)
        expo = jnp.exp(scores - jnp.max(scores, axis=0, keepdims=True))
        low = (expo * (1.0 / jnp.sum(expo, axis=0, keepdims=True))).astype(BF)
        weights[...] = low
        mix = mm(v, low)
        mixed[where, :] = mix.astype(BF)
        delta = jnp.sum(mix * g.astype(F32), axis=0, keepdims=True)
        inner = (low.astype(F32) * (mm(v.T, g) - delta)).astype(BF)
        grad_scores[...] = inner
        grad_q[where, :] = (mm(k, inner) * 0.125).astype(BF)
        grad_k[where, :] = mm(grad_scores[...], q.T).T.astype(BF)
        grad_v[where, :] = mm(weights[...], g.T).T.astype(BF)
        return carry

    lax.fori_loop(0, HEADS, head, 0)
    for column in range(0, PIX, 512):
        where = slice(column, column + 512)
        grad_normed[:, where] = (
            mm(wq[...], grad_q[:, where], TN)
            + mm(wk[...], grad_k[:, where], TN)
            + mm(wv[...], grad_v[:, where], TN)
        )

    def back(group, carry):
        where = rows(group * 16, 16)
        unit = unit_of(resid[where, :], stats2, where)
        grad = grad_normed[where, :]
        outer = grad_out[where, :].astype(F32)
        total = outer + unit_back(grad * par[where, GAIN + 2 : GAIN + 3], unit, stats2[where, 1:2])
        low = total.astype(BF)
        grad_resid[where, :] = total
        grad_branch[where, :] = low
        small[where, 0:1] = row_sum(grad * unit)
        small[where, 1:2] = row_sum(grad)
        small[where, 2:3] = row_sum(low.astype(F32))
        small[where, 3:4] = row_sum(outer)
        return carry

    lax.fori_loop(0, 32, back, 0, unroll=2)


def projections(
    index, normed, resid, par, mixed, grad_q, grad_k, grad_v, grad_out, p_own, p_peer, block, grads, wp
):
    live = index[2] > 0
    place_square(wp, index, p_own, p_peer)
    for column in range(0, PIX, 512):
        where = slice(column, column + 512)
        total = resid[:, where] + mm(wp[...], mixed[:, where], TN) + par[:, PROJB : PROJB + 1]
        block[:, where] = jnp.where(live, total, jnp.zeros_like(total)).astype(BF)
    pairs = ((grad_q, normed), (grad_k, normed), (grad_v, normed), (mixed, grad_out))
    for which, (left, right) in enumerate(pairs):
        result = mm(left[...], right[...], NT).astype(BF)
        for part in range(32):
            plane, chunk = part // 16, part % 16
            grads[chunk // 8, plane, chunk % 8, which] = result[part * 16 : (part + 1) * 16]


def second_back(
    index, grad_branch, hidden, stats1, par, w_own, w_part, w_peer, grad_hidden, small, col, full, grad_second
):
    place_conv(full, index, w_own, w_part, w_peer)
    taps_of(col, edge_masks(-1), grad_branch, 0, 512, 0, -1)
    conv_dots(grad_second, full, col, TN, lambda total, column: total)

    def back(group, carry):
        where = rows(group * 16, 16)
        unit = unit_of(hidden[where, :], stats1, where)
        gain = par[where, GAIN + 1 : GAIN + 2]
        normed = unit * gain + par[where, BIAS + 1 : BIAS + 2]
        scale = 1.0 + par[where, SCALE : SCALE + 1]
        grad_pre = grad_second[where, :] * silu_slope(normed * scale + par[where, SHIFT : SHIFT + 1])
        grad = grad_pre * scale
        low = unit_back(grad * gain, unit, stats1[where, 1:2]).astype(BF)
        grad_hidden[where, :] = low
        small[where, 0:1] = row_sum(grad_pre * normed)
        small[where, 1:2] = row_sum(grad_pre)
        small[where, 2:3] = row_sum(grad * unit)
        small[where, 3:4] = row_sum(grad)
        small[where, 4:5] = row_sum(low.astype(F32))
        return carry

    lax.fori_loop(0, 32, back, 0, unroll=2)


def first_back(
    index, grad_hidden, own, peer, stats0, par, grad_resid, w_own, w_part, w_peer,
    near, far, small, col, full, grad_first,
):
    half = index[0]
    place_conv(full, index, w_own, w_part, w_peer)
    taps_of(col, edge_masks(-1), grad_hidden, 0, 512, 0, -1)
    conv_dots(grad_first, full, col, TN, lambda total, column: total)
    for picture, base, dest in ((own, half * 256, near), (peer, (1 - half) * 256, far)):

        def back(group, carry, picture=picture, base=base, dest=dest):
            here = rows(group * 16, 16)
            where = rows(base + group * 16, 16)
            unit = unit_of(picture[here, :].astype(F32), stats0, where)
            gain = par[where, GAIN : GAIN + 1]
            grad = grad_first[where, :] * silu_slope(unit * gain + par[where, BIAS : BIAS + 1])
            total = grad_resid[where, :] + unit_back(grad * gain, unit, stats0[where, 1:2])
            dest[here, :] = total.astype(dest.dtype)
            small[where, 0:1] = row_sum(grad * unit)
            small[where, 1:2] = row_sum(grad)
            return carry

        lax.fori_loop(0, 16, back, 0, unroll=2)


def weight_back(index, grad_own, grad_peer, source_own, source_peer, grads, col, turned):
    masks = edge_masks(-1)
    taps_of(col, masks, grad_own, 0, 256, 0, -1)
    taps_of(col, masks, grad_peer, 0, 256, PIX, -1)
    turned[:PIX, :] = source_own[...].T
    turned[PIX:, :] = source_peer[...].T
    for tap in range(9):
        result = mm(col[tap * 256 : (tap + 1) * 256, :], turned[...]).astype(BF)
        for part in range(16):
            grads[part, tap] = result[part * 16 : (part + 1) * 16]


def paired(
    batch_size,
    images,
    timesteps,
    classes,
    live_count,
    norm_gain,
    norm_bias,
    conv_weight,
    conv_bias,
    emb_weight,
    emb_bias,
    class_table,
    qkv_weight,
    proj_weight,
    proj_bias,
    cotangent,
):
    half = lax.axis_index("head")
    place = lax.axis_index("batch")
    core = place % 2
    bits = batch_size.bit_length() - 1

    def across(value):
        return lax.ppermute(value, "head", [(0, 1), (1, 0)])

    def over(value, bit):
        return lax.ppermute(value, "batch", [(i, i ^ (1 << bit)) for i in range(batch_size)])

    def pick(value, index):
        return lax.dynamic_index_in_dim(value, index, 0, keepdims=False)

    def by_half(near, far, axis):
        return jnp.where(
            half == 0,
            jnp.concatenate([near, far], axis),
            jnp.concatenate([far, near], axis),
        )

    def my_bit(bit):
        return (place >> bit) & 1

    def widen(value, bit):
        peer = over(value, bit)
        return jnp.where(
            my_bit(bit) == 0, jnp.concatenate([value, peer]), jnp.concatenate([peer, value])
        )

    def halve(value, bit):
        pair = value.reshape((2, value.shape[0] // 2) + value.shape[1:])
        arrived = over(pick(pair, 1 - my_bit(bit)), bit)
        return (pick(pair, my_bit(bit)).astype(F32) + arrived.astype(F32)).astype(BF)

    image_own = pick(images, half)
    image_peer = across(pick(images, 1 - half))
    cot_own = pick(cotangent, half)
    cot_peer = across(pick(cotangent, 1 - half))

    def conv_parts(which):
        own = conv_weight[which]
        part = across(lax.dynamic_slice_in_dim(own, core * 128, 128, 1))
        return own, part, over(part, 0)

    weights0 = conv_parts(0)
    weights1 = conv_parts(1)
    q_peer = across(qkv_weight)
    p_peer = across(proj_weight)

    table_rows = jnp.stack([pick(class_table, classes[slot]) for slot in range(2)]).astype(F32)
    emb_width = class_table.shape[1]
    pre_embed = jnp.stack([features(timesteps[slot], emb_width) for slot in range(2)]) + table_rows
    embed = jax.nn.silu(pre_embed)
    dense = emb_weight.astype(F32)
    mod = jnp.einsum("mce,be->bmc", dense, embed, precision=HIGH) + emb_bias[None]
    params = jnp.concatenate([norm_gain, norm_bias, conv_bias, proj_bias[None]])
    par_near = jnp.concatenate([params, pick(mod, half)])
    par_far = across(jnp.concatenate([params, pick(mod, 1 - half)]))
    par = by_half(par_near, par_far, 1).T

    live = (half < live_count[0]).astype(jnp.int32)
    scalars = jnp.stack([half, core, live]).astype(jnp.int32)
    full_bf = out((512, PIX), BF)
    full_f32 = out((512, PIX), F32)
    half_bf = out((256, PIX), BF)
    half_f32 = out((256, PIX), F32)
    stats = out((512, 2), F32)
    taps = pltpu.VMEM((9 * 512, PIX), BF)
    conv_full = pltpu.VMEM((9, 512, 512), BF)
    square = pltpu.VMEM((512, 512), BF)
    wide_bf = pltpu.VMEM((512, PIX), BF)
    wide_f32 = pltpu.VMEM((512, PIX), F32)
    pixels = pltpu.VMEM((PIX, PIX), BF)
    conv_flops = 2 * 9 * 512 * 512 * PIX

    first, hidden, stats0, stats1, second = kernel_call(
        first_conv, [full_bf, full_f32, stats, stats, full_bf], [taps, conv_full], conv_flops,
        scalars, image_own, image_peer, par, *weights0,
    )
    resid, stats2, normed = kernel_call(
        second_conv, [full_f32, stats, full_bf], [taps, conv_full], conv_flops,
        scalars, second, image_own, image_peer, par, *weights1,
    )
    mixed, grad_q, grad_k, grad_v, grad_out, grad_resid, grad_branch, small2 = kernel_call(
        attention,
        [full_bf] * 5 + [full_f32, full_bf, out((512, 4), F32)],
        [square] * 4 + [wide_bf] * 4 + [pixels] * 2 + [wide_f32],
        4 * conv_flops,
        scalars, normed, resid, stats2, par, cot_own, cot_peer, qkv_weight, q_peer, proj_weight, p_peer,
    )
    first_peer = across(first)
    second_peer = across(second)

    def halves(value):
        pair = value.reshape(2, 256, PIX)
        return pick(pair, half), across(pick(pair, 1 - half))

    branch_own, branch_peer = halves(grad_branch)
    grad_hidden, small1 = kernel_call(
        second_back, [full_bf, out((512, 5), F32)], [taps, conv_full, wide_f32], conv_flops,
        scalars, grad_branch, hidden, stats1, par, *weights1,
    )
    hidden_own, hidden_peer = halves(grad_hidden)
    block, square_grads = kernel_call(
        projections, [full_bf, out((2, 2, 8, 4, 16, 512), BF)], [square], conv_flops // 2,
        scalars, normed, resid, par, mixed, grad_q, grad_k, grad_v, grad_out, proj_weight, p_peer,
    )
    block_own, block_peer = halves(block)
    conv_grads = out((16, 9, 16, 512), BF)
    tap_pair = pltpu.VMEM((9 * 256, 2 * PIX), BF)
    turned = pltpu.VMEM((2 * PIX, 512), BF)

    def weight_grad(grad_own, grad_peer, source, source_peer):
        return kernel_call(
            weight_back, [conv_grads], [tap_pair, turned], conv_flops,
            scalars, grad_own, grad_peer, source, source_peer,
        )[0]

    conv_grad1 = weight_grad(branch_own, branch_peer, second, second_peer)
    conv_grad0 = weight_grad(hidden_own, hidden_peer, first, first_peer)
    near, far, small0 = kernel_call(
        first_back, [half_f32, half_bf, out((512, 2), F32)], [taps, conv_full, wide_f32], conv_flops,
        scalars, grad_hidden, image_own, image_peer, stats0, par, grad_resid, *weights0,
    )
    far = across(far).astype(F32)

    def reduce_conv(value):
        for bit in range(bits):
            value = halve(value, bit)
        for bit in reversed(range(bits)):
            value = widen(value, bit)
        return value.transpose(1, 0, 2, 3).reshape(9, 256, 512).astype(F32)

    conv_total1 = reduce_conv(conv_grad1)
    conv_total0 = reduce_conv(conv_grad0)

    squares = halve(square_grads, 0)[0]
    keep_part, send_part = pick(squares, half), pick(squares, 1 - half)
    squares = (keep_part.astype(F32) + across(send_part).astype(F32)).astype(BF)
    for bit in range(1, bits):
        squares = halve(squares, bit)
    for bit in reversed(range(bits)):
        squares = widen(squares, bit)
    squares = squares.transpose(1, 0, 2, 3).reshape(4, 256, 512).astype(F32)

    small = jnp.concatenate([small0, small1, small2], 1).T.reshape(11, 2, 256).transpose(1, 0, 2)
    small_own, small_peer = pick(small, half), across(pick(small, 1 - half))
    sums = small_own + small_peer
    for bit in range(bits):
        sums = sums + over(sums, bit)
    emb_own, emb_peer = small_own[2:4], small_peer[2:4]
    emb_grads = by_half(emb_own[None], emb_peer[None], 0)
    pre_all = pre_embed
    ids = classes
    for bit in range(bits):
        emb_grads = widen(emb_grads, bit)
        pre_all = widen(pre_all, bit)
        ids = widen(ids, bit)
    emb_total = jnp.einsum("bmc,be->mce", emb_grads, jax.nn.silu(pre_all), precision=HIGH)
    rows_part = jnp.einsum("bmc,mce->be", emb_grads, dense, precision=HIGH)
    class_rows = (rows_part + across(rows_part)) * silu_slope(pre_all)
    chosen = (lax.iota(jnp.int32, class_table.shape[0])[:, None] == ids[None, :]).astype(F32)
    table_total = jnp.dot(chosen, class_rows, precision=HIGH)
    return (
        by_half(block_own[None], block_peer[None], 0),
        by_half(near[None], far[None], 0),
        jnp.stack([sums[0], sums[4], sums[7]]),
        jnp.stack([sums[1], sums[5], sums[8]]),
        jnp.stack([conv_total0, conv_total1]),
        jnp.stack([sums[6], sums[9]]),
        emb_total,
        sums[2:4],
        table_total,
        squares[:3],
        squares[3],
        sums[10],
    )


def solution(mesh):
    in_specs = (
        P("batch", "head", None),
        P("batch"),
        P("batch"),
        P("batch"),
        P(None, "head"),
        P(None, "head"),
        P(None, None, "head", None),
        P(None, "head"),
        P(None, "head", None),
        P(None, "head"),
        P(),
        P(None, "head", None),
        P("head", None),
        P("head"),
        P("batch", "head", None),
    )
    out_specs = (
        P("batch", "head", None),
        P("batch", "head", None),
        P(None, "head"),
        P(None, "head"),
        P(None, None, "head", None),
        P(None, "head"),
        P(None, "head", None),
        P(None, "head"),
        P(),
        P(None, "head", None),
        P("head", None),
        P("head"),
    )
    body = shards
    batch_size = mesh.shape["batch"]
    if mesh.shape["head"] == 2 and batch_size in (8, 16):
        body = functools.partial(paired, batch_size)
    return jax.shard_map(body, mesh=mesh, in_specs=in_specs, out_specs=out_specs, check_vma=False)
```

```python
import functools
import math

import jax
import jax.numpy as jnp
from jax import lax
from jax.experimental import pallas as pl
from jax.experimental.pallas import tpu as pltpu
from jax.sharding import PartitionSpec as P

C = 512
GROUPS = 32
HEADS = 8
SIDE = 32


EPS = 1e-05
HIGH = lax.Precision.HIGHEST
CONTRACT_FIRST = (((0,), (0,)), ((), ()))
CONTRACT_LAST = (((1,), (1,)), ((), ()))


def silu_slope(values):
    sigma = jax.nn.sigmoid(values)
    return sigma * (1.0 + values * (1.0 - sigma))


def moved(source, grid_side, row_step, col_step):
    grid = source.reshape(source.shape[0], grid_side, grid_side)
    padded = jnp.pad(grid, ((0, 0), (1, 1), (1, 1)))
    window = padded[
        :, 1 + row_step : 1 + row_step + grid_side, 1 + col_step : 1 + col_step + grid_side
    ]
    return window.reshape(source.shape)


def group_unit(source, groups):
    grouped = source.reshape(groups, -1)
    centre = grouped - jnp.mean(grouped, axis=1, keepdims=True)
    inverse = lax.rsqrt(jnp.mean(jnp.square(centre), axis=1, keepdims=True) + EPS)
    return ((centre * inverse).reshape(source.shape), inverse)


def group_back(grad_unit, unit_rows, inverse, groups):
    flat_grad = grad_unit.reshape(groups, -1)
    flat_unit = unit_rows.reshape(groups, -1)
    result = flat_grad - jnp.mean(flat_grad, axis=1, keepdims=True)
    result = (result - flat_unit * jnp.mean(flat_grad * flat_unit, axis=1, keepdims=True)) * inverse
    return result.reshape(grad_unit.shape)


def conv_apply(weight, source, grid_side):
    result = jnp.dot(
        weight[0], moved(source, grid_side, -1, -1), preferred_element_type=jnp.float32
    )
    for tap_index in range(1, 9):
        result = result + jnp.dot(
            weight[tap_index],
            moved(source, grid_side, tap_index // 3 - 1, tap_index % 3 - 1),
            preferred_element_type=jnp.float32,
        )
    return result


def conv_transpose(weight, grads, grid_side):
    result = lax.dot_general(
        weight[0], moved(grads, grid_side, 1, 1), CONTRACT_FIRST, preferred_element_type=jnp.float32
    )
    for tap_index in range(1, 9):
        result = result + lax.dot_general(
            weight[tap_index],
            moved(grads, grid_side, 1 - tap_index // 3, 1 - tap_index % 3),
            CONTRACT_FIRST,
            preferred_element_type=jnp.float32,
        )
    return result


def conv_weight_grads(grads, source, grid_side):
    return jnp.stack(
        [
            lax.dot_general(
                grads,
                moved(source, grid_side, tap_index // 3 - 1, tap_index % 3 - 1),
                CONTRACT_LAST,
                preferred_element_type=jnp.float32,
            )
            for tap_index in range(9)
        ]
    )


def features(timestep, emb_width):
    half_width = emb_width // 2
    freqs = jnp.exp(-math.log(10000.0) * jnp.arange(half_width, dtype=jnp.float32) / half_width)
    angles = timestep.astype(jnp.float32) * freqs
    return jnp.concatenate([jnp.cos(angles), jnp.sin(angles)])


def shards(
    images,
    timesteps,
    classes,
    live_count,
    norm_gain,
    norm_bias,
    conv_weight,
    conv_bias,
    emb_weight,
    emb_bias,
    class_table,
    qkv_weight,
    proj_weight,
    proj_bias,
    cotangent,
):
    slot_count, chan_dev, pixel_count = images.shape
    grid_side = SIDE
    groups = chan_dev // (C // GROUPS)
    head_size = C // HEADS
    heads_dev = chan_dev // head_size
    att_scale = head_size ** (-0.5)
    emb_dense = emb_weight.astype(jnp.float32)
    class_total, emb_width = class_table.shape

    def gather_channels(rows_low):
        return lax.all_gather(rows_low, "head", axis=0, tiled=True)

    def input_grad(which_conv, grad_rows):
        weight_cols = conv_weight[which_conv]
        return lax.psum_scatter(
            conv_transpose(weight_cols, grad_rows, grid_side).astype(jnp.bfloat16),
            "head",
            scatter_dimension=0,
            tiled=True,
        ).astype(jnp.float32)

    def per_slot(slot_index, carry):
        (
            outputs,
            grads_in,
            gain_acc,
            bias_acc,
            convw_acc,
            convb_acc,
            embw_acc,
            embb_acc,
            table_acc,
            qkv_acc,
            projw_acc,
            projb_acc,
        ) = carry
        picture = lax.dynamic_index_in_dim(images, slot_index, 0, keepdims=False).astype(
            jnp.float32
        )
        live_flag = (slot_index < live_count[0]).astype(jnp.float32)
        class_id = classes[slot_index]
        table_row = lax.dynamic_index_in_dim(class_table, class_id, 0, keepdims=False).astype(
            jnp.float32
        )
        pre_embed = features(timesteps[slot_index], emb_width) + table_row
        embed = jax.nn.silu(pre_embed)
        scale = jnp.dot(emb_dense[0], embed, precision=HIGH) + emb_bias[0]
        shift = jnp.dot(emb_dense[1], embed, precision=HIGH) + emb_bias[1]
        unit_zero, inverse_zero = group_unit(picture, groups)
        pre_first = unit_zero * norm_gain[0][:, None] + norm_bias[0][:, None]
        first_full = gather_channels(jax.nn.silu(pre_first).astype(jnp.bfloat16))
        hidden = conv_apply(conv_weight[0], first_full, grid_side) + conv_bias[0][:, None]
        unit_one, inverse_one = group_unit(hidden, groups)
        normed_one = unit_one * norm_gain[1][:, None] + norm_bias[1][:, None]
        pre_second = normed_one * (1.0 + scale[:, None]) + shift[:, None]
        second_full = gather_channels(jax.nn.silu(pre_second).astype(jnp.bfloat16))
        resid = picture + conv_apply(conv_weight[1], second_full, grid_side) + conv_bias[1][:, None]
        unit_two, inverse_two = group_unit(resid, groups)
        normed_full = gather_channels(
            (unit_two * norm_gain[2][:, None] + norm_bias[2][:, None]).astype(jnp.bfloat16)
        )
        query = (
            jnp.dot(qkv_weight[0], normed_full, preferred_element_type=jnp.float32)
            .astype(jnp.bfloat16)
            .reshape(heads_dev, head_size, pixel_count)
        )
        keys = (
            jnp.dot(qkv_weight[1], normed_full, preferred_element_type=jnp.float32)
            .astype(jnp.bfloat16)
            .reshape(heads_dev, head_size, pixel_count)
        )
        values = (
            jnp.dot(qkv_weight[2], normed_full, preferred_element_type=jnp.float32)
            .astype(jnp.bfloat16)
            .reshape(heads_dev, head_size, pixel_count)
        )
        scores = (
            jnp.einsum("hdi,hdj->hij", query, keys, preferred_element_type=jnp.float32) * att_scale
        )
        highest = jnp.max(scores, axis=2, keepdims=True)
        expo = jnp.exp(scores - highest)
        totals = jnp.sum(expo, axis=2, keepdims=True)
        log_total = highest + jnp.log(totals)
        weights = (expo / totals).astype(jnp.bfloat16)
        mixed = (
            jnp.einsum("hdj,hij->hdi", values, weights, preferred_element_type=jnp.float32)
            .astype(jnp.bfloat16)
            .reshape(chan_dev, pixel_count)
        )
        weight_cols = proj_weight
        proj_term = lax.psum_scatter(
            lax.dot_general(
                weight_cols, mixed, CONTRACT_FIRST, preferred_element_type=jnp.float32
            ).astype(jnp.bfloat16),
            "head",
            scatter_dimension=0,
            tiled=True,
        ).astype(jnp.float32)
        result = resid + proj_term + proj_bias[:, None]
        outputs = lax.dynamic_update_index_in_dim(
            outputs, (live_flag * result).astype(jnp.bfloat16), slot_index, 0
        )
        grad_low = lax.dynamic_index_in_dim(cotangent, slot_index, 0, keepdims=False)
        grad_out = live_flag * grad_low.astype(jnp.float32)
        grad_full = lax.all_gather(grad_low, "head", axis=0, tiled=True) * live_flag.astype(
            jnp.bfloat16
        )
        grad_mixed = jnp.dot(proj_weight, grad_full, preferred_element_type=jnp.float32).astype(
            jnp.bfloat16
        )
        projw_acc = projw_acc + lax.dot_general(
            mixed, grad_full, CONTRACT_LAST, preferred_element_type=jnp.float32
        )
        projb_acc = projb_acc + jnp.sum(grad_out, axis=1)
        again = (
            jnp.einsum("hdi,hdj->hij", query, keys, preferred_element_type=jnp.float32) * att_scale
        )
        probs = jnp.exp(again - log_total)
        grad_heads = grad_mixed.reshape(heads_dev, head_size, pixel_count)
        grad_probs = jnp.einsum(
            "hdi,hdj->hij", grad_heads, values, preferred_element_type=jnp.float32
        )
        grad_scores = (
            probs * (grad_probs - jnp.sum(grad_probs * probs, axis=2, keepdims=True))
        ).astype(jnp.bfloat16)
        grad_query = (
            jnp.einsum("hij,hdj->hdi", grad_scores, keys, preferred_element_type=jnp.float32)
            * att_scale
        ).astype(jnp.bfloat16)
        grad_keys = (
            jnp.einsum("hij,hdi->hdj", grad_scores, query, preferred_element_type=jnp.float32)
            * att_scale
        ).astype(jnp.bfloat16)
        grad_values = jnp.einsum(
            "hdi,hij->hdj", grad_heads, weights, preferred_element_type=jnp.float32
        ).astype(jnp.bfloat16)
        stacked = jnp.stack([grad_query, grad_keys, grad_values]).reshape(3, chan_dev, pixel_count)
        weight_cols = qkv_weight
        grad_normed = lax.psum_scatter(
            lax.dot_general(
                weight_cols,
                stacked,
                (((0, 1), (0, 1)), ((), ())),
                preferred_element_type=jnp.float32,
            ).astype(jnp.bfloat16),
            "head",
            scatter_dimension=0,
            tiled=True,
        ).astype(jnp.float32)
        qkv_acc = qkv_acc + lax.dot_general(
            stacked, normed_full, (((2,), (1,)), ((), ())), preferred_element_type=jnp.float32
        )
        grad_resid = grad_out + group_back(
            grad_normed * norm_gain[2][:, None], unit_two, inverse_two, groups
        )
        grad_branch = grad_resid.astype(jnp.bfloat16)
        grad_second = input_grad(1, grad_branch)
        grad_pre = grad_second * silu_slope(pre_second)
        scale_grad = jnp.sum(grad_pre * normed_one, axis=1)
        shift_grad = jnp.sum(grad_pre, axis=1)
        grad_normed_one = grad_pre * (1.0 + scale[:, None])
        grad_hidden = group_back(
            grad_normed_one * norm_gain[1][:, None], unit_one, inverse_one, groups
        ).astype(jnp.bfloat16)
        grad_first = input_grad(0, grad_hidden)
        grad_pre_first = grad_first * silu_slope(pre_first)
        picture_grad = grad_resid + group_back(
            grad_pre_first * norm_gain[0][:, None], unit_zero, inverse_zero, groups
        )
        grads_in = lax.dynamic_update_index_in_dim(grads_in, picture_grad, slot_index, 0)
        gain_acc = gain_acc + jnp.stack(
            [
                jnp.sum(grad_pre_first * unit_zero, axis=1),
                jnp.sum(grad_normed_one * unit_one, axis=1),
                jnp.sum(grad_normed * unit_two, axis=1),
            ]
        )
        bias_acc = bias_acc + jnp.stack(
            [
                jnp.sum(grad_pre_first, axis=1),
                jnp.sum(grad_normed_one, axis=1),
                jnp.sum(grad_normed, axis=1),
            ]
        )
        convw_acc = convw_acc + jnp.stack(
            [
                conv_weight_grads(grad_hidden, first_full, grid_side),
                conv_weight_grads(grad_branch, second_full, grid_side),
            ]
        )
        convb_acc = convb_acc + jnp.stack(
            [
                jnp.sum(grad_hidden.astype(jnp.float32), axis=1),
                jnp.sum(grad_branch.astype(jnp.float32), axis=1),
            ]
        )
        embw_acc = embw_acc + jnp.stack(
            [scale_grad[:, None] * embed[None, :], shift_grad[:, None] * embed[None, :]]
        )
        embb_acc = embb_acc + jnp.stack([scale_grad, shift_grad])
        grad_embed = jnp.dot(scale_grad, emb_dense[0], precision=HIGH) + jnp.dot(
            shift_grad, emb_dense[1], precision=HIGH
        )
        class_row = grad_embed * silu_slope(pre_embed)
        old_row = lax.dynamic_index_in_dim(table_acc, class_id, 0, keepdims=True)
        table_acc = lax.dynamic_update_index_in_dim(
            table_acc, old_row + class_row[None, :], class_id, 0
        )
        return (
            outputs,
            grads_in,
            gain_acc,
            bias_acc,
            convw_acc,
            convb_acc,
            embw_acc,
            embb_acc,
            table_acc,
            qkv_acc,
            projw_acc,
            projb_acc,
        )

    table_start = jnp.zeros(class_table.shape, jnp.float32)
    initial = (
        jnp.zeros(images.shape, jnp.bfloat16),
        jnp.zeros(images.shape, jnp.float32),
        jnp.zeros(norm_gain.shape, jnp.float32),
        jnp.zeros(norm_bias.shape, jnp.float32),
        jnp.zeros(conv_weight.shape, jnp.float32),
        jnp.zeros(conv_bias.shape, jnp.float32),
        jnp.zeros(emb_weight.shape, jnp.float32),
        jnp.zeros(emb_bias.shape, jnp.float32),
        table_start,
        jnp.zeros(qkv_weight.shape, jnp.float32),
        jnp.zeros(proj_weight.shape, jnp.float32),
        jnp.zeros(proj_bias.shape, jnp.float32),
    )
    final = lax.fori_loop(0, slot_count, per_slot, initial)
    (
        outputs,
        grads_in,
        gain_acc,
        bias_acc,
        convw_acc,
        convb_acc,
        embw_acc,
        embb_acc,
        table_acc,
        qkv_acc,
        projw_acc,
        projb_acc,
    ) = final
    table_total = lax.psum(table_acc, ("batch", "head"))
    summed = (
        lax.psum(gain_acc.astype(jnp.bfloat16), "batch").astype(jnp.float32),
        lax.psum(bias_acc.astype(jnp.bfloat16), "batch").astype(jnp.float32),
        lax.psum(convw_acc.astype(jnp.bfloat16), "batch").astype(jnp.float32),
        lax.psum(convb_acc.astype(jnp.bfloat16), "batch").astype(jnp.float32),
        lax.psum(embw_acc.astype(jnp.bfloat16), "batch").astype(jnp.float32),
        lax.psum(embb_acc.astype(jnp.bfloat16), "batch").astype(jnp.float32),
        lax.psum(qkv_acc.astype(jnp.bfloat16), "batch").astype(jnp.float32),
        lax.psum(projw_acc.astype(jnp.bfloat16), "batch").astype(jnp.float32),
        lax.psum(projb_acc.astype(jnp.bfloat16), "batch").astype(jnp.float32),
    )
    return (
        outputs,
        grads_in,
        summed[0],
        summed[1],
        summed[2],
        summed[3],
        summed[4],
        summed[5],
        table_total,
        summed[6],
        summed[7],
        summed[8],
    )


PIX = 1024
BLOCK = 128
BF = jnp.bfloat16
F32 = jnp.float32
NN = (((1,), (0,)), ((), ()))
TN = (((0,), (0,)), ((), ()))
NT = (((1,), (1,)), ((), ()))
VMEM = pl.BlockSpec(memory_space=pltpu.VMEM)
SMEM = pl.BlockSpec(memory_space=pltpu.SMEM)

GAIN, BIAS, CONVB, PROJB, SCALE, SHIFT = 0, 3, 6, 8, 9, 10


def mm(left, right, dims=NN):
    return lax.dot_general(left, right, dims, preferred_element_type=F32)


def kernel_call(kernel, outs, scratch, flops, scalars, *args):
    moved_bytes = sum(a.size * a.dtype.itemsize for a in args)
    moved_bytes += sum(math.prod(o.shape) * o.dtype.itemsize for o in outs)
    return pl.pallas_call(
        kernel,
        out_shape=outs,
        in_specs=[SMEM] + [VMEM] * len(args),
        out_specs=[VMEM] * len(outs),
        scratch_shapes=scratch,
        cost_estimate=pl.CostEstimate(flops=flops, bytes_accessed=moved_bytes, transcendentals=0),
        compiler_params=pltpu.CompilerParams(vmem_limit_bytes=56 * 2**20),
    )(scalars, *args)


def out(shape, dtype):
    return jax.ShapeDtypeStruct(shape, dtype)


def rows(start, count):
    return pl.ds(pl.multiple_of(start, count), count)


def edge_masks(sign):
    pixel = lax.broadcasted_iota(jnp.int32, (1, PIX), 1)
    col, row = pixel % SIDE, pixel // SIDE
    table = {}
    for step in (-1, 1):
        moved_step = sign * step
        table["col", step] = ((col + moved_step >= 0) & (col + moved_step < SIDE)).astype(F32)
        table["row", step] = ((row + moved_step >= 0) & (row + moved_step < SIDE)).astype(F32)
    return table


def put_taps(dest, masks, values, first_row, depth, base, sign):
    count = values.shape[0]
    for col_step in (-1, 0, 1):
        across = values
        if col_step:
            across = pltpu.roll(values, (-sign * col_step) % PIX, 1) * masks["col", col_step]
        for row_step in (-1, 0, 1):
            copy = across
            if row_step:
                copy = pltpu.roll(across, (-sign * row_step * SIDE) % PIX, 1) * masks["row", row_step]
            tap = 3 * (row_step + 1) + col_step + 1
            dest[rows(tap * depth + first_row, count), base : base + PIX] = copy.astype(BF)


def taps_of(dest, masks, source, offset, depth, base, sign):
    for start in range(0, source.shape[0], 128):
        piece = source[start : start + 128, :].astype(F32)
        put_taps(dest, masks, piece, offset + start, depth, base, sign)


def place_conv(full, index, own, peer):
    half = index[0]
    full[:, rows(half * 256, 256), :] = own[...]
    full[:, rows((1 - half) * 256, 256), :] = peer[...]


def conv_dots(dest, full, col, dims, finish):
    for column in range(0, PIX, 512):
        total = None
        for tap in range(9):
            term = mm(full[tap], col[tap * 512 : (tap + 1) * 512, column : column + 512], dims)
            total = term if total is None else total + term
        dest[:, column : column + 512] = finish(total, column)


def grouped(block):
    return block.reshape((-1, 16) + block.shape[1:])


def group_mean(block):
    return jnp.sum(block, axis=(1, 2), keepdims=True) * (1.0 / (16 * PIX))


def group_stats(block, stats, where):
    parts = grouped(block)
    centre = group_mean(parts)
    parts = parts - centre
    inverse = lax.rsqrt(group_mean(jnp.square(parts)) + EPS)
    count = block.shape[0]
    stats[where, 0:1] = jnp.broadcast_to(centre, (count // 16, 16, 1)).reshape(count, 1)
    stats[where, 1:2] = jnp.broadcast_to(inverse, (count // 16, 16, 1)).reshape(count, 1)
    return (parts * inverse).reshape(block.shape)


def unit_of(block, stats, where):
    return (block - stats[where, 0:1]) * stats[where, 1:2]


def unit_back(grad, unit, inverse):
    parts, units = grouped(grad), grouped(unit)
    result = parts - group_mean(parts) - units * group_mean(parts * units)
    return result.reshape(grad.shape) * inverse


def row_sum(block):
    return jnp.sum(block, axis=1, keepdims=True)


def first_conv(index, own, peer, par, w_own, w_peer, first, hidden, stats0, stats1, second, col, full):
    half = index[0]
    place_conv(full, index, w_own, w_peer)
    masks = edge_masks(1)
    for source, base in ((own, half * 256), (peer, (1 - half) * 256)):

        def norm(group, carry, source=source, base=base):
            where = rows(base + group * BLOCK, BLOCK)
            unit = group_stats(source[rows(group * BLOCK, BLOCK), :].astype(F32), stats0, where)
            low = jax.nn.silu(unit * par[where, GAIN : GAIN + 1] + par[where, BIAS : BIAS + 1]).astype(BF)
            first[where, :] = low
            put_taps(col, masks, low.astype(F32), base + group * BLOCK, 512, 0, 1)
            return carry

        lax.fori_loop(0, 256 // BLOCK, norm, 0)
    conv_dots(hidden, full, col, NN, lambda total, column: total + par[:, CONVB : CONVB + 1])

    def again(group, carry):
        where = rows(group * BLOCK, BLOCK)
        unit = group_stats(hidden[where, :], stats1, where)
        normed = unit * par[where, GAIN + 1 : GAIN + 2] + par[where, BIAS + 1 : BIAS + 2]
        pre = normed * (1.0 + par[where, SCALE : SCALE + 1]) + par[where, SHIFT : SHIFT + 1]
        second[where, :] = jax.nn.silu(pre).astype(BF)
        return carry

    lax.fori_loop(0, 512 // BLOCK, again, 0)


def second_conv(index, source, own, peer, par, w_own, w_peer, resid, stats2, normed, col, full):
    half = index[0]
    place_conv(full, index, w_own, w_peer)
    taps_of(col, edge_masks(1), source, 0, 512, 0, 1)
    conv_dots(resid, full, col, NN, lambda total, column: total + par[:, CONVB + 1 : CONVB + 2])
    for picture, base in ((own, half * 256), (peer, (1 - half) * 256)):

        def norm(group, carry, picture=picture, base=base):
            where = rows(base + group * BLOCK, BLOCK)
            block = resid[where, :] + picture[rows(group * BLOCK, BLOCK), :].astype(F32)
            resid[where, :] = block
            unit = group_stats(block, stats2, where)
            normed[where, :] = (unit * par[where, GAIN + 2 : GAIN + 3] + par[where, BIAS + 2 : BIAS + 3]).astype(BF)
            return carry

        lax.fori_loop(0, 256 // BLOCK, norm, 0)


def place_square(full, index, own, peer):
    half = index[0]
    count = own.shape[0]
    full[rows(half * count, count), :] = own[...]
    full[rows((1 - half) * count, count), :] = peer[...]


def attention(
    index, normed, resid, stats2, par, cot_own, cot_peer, q_own, q_peer, p_own, p_peer,
    mixed, grad_q, grad_k, grad_v, grad_out, grad_resid, grad_branch, small,
    wq, wk, wv, wp, query, keys, values, grad_mixed, weights, grad_scores, grad_normed,
):
    half = index[0]
    live = index[2] > 0
    for which, full in enumerate((wq, wk, wv)):
        place_square(full, index, q_own.at[which], q_peer.at[which])
    place_square(wp, index, p_own, p_peer)
    for cotangent, base in ((cot_own, half * 256), (cot_peer, (1 - half) * 256)):
        grad_out[rows(base, 256), :] = jnp.where(live, cotangent[...], jnp.zeros_like(cotangent[...]))
    for column in range(0, PIX, 512):
        where = slice(column, column + 512)
        query[:, where] = (mm(wq[...], normed[:, where]).astype(BF).astype(F32) * 0.125).astype(BF)
        keys[:, where] = mm(wk[...], normed[:, where]).astype(BF)
        values[:, where] = mm(wv[...], normed[:, where]).astype(BF)
        grad_mixed[:, where] = mm(wp[...], grad_out[:, where]).astype(BF)

    def head(number, carry):
        where = rows(number * 64, 64)
        q, k, v, g = query[where, :], keys[where, :], values[where, :], grad_mixed[where, :]
        scores = mm(k.T, q)
        expo = jnp.exp(scores - jnp.max(scores, axis=0, keepdims=True))
        low = (expo * (1.0 / jnp.sum(expo, axis=0, keepdims=True))).astype(BF)
        weights[...] = low
        mix = mm(v, low)
        mixed[where, :] = mix.astype(BF)
        delta = jnp.sum(mix * g.astype(F32), axis=0, keepdims=True)
        inner = (low.astype(F32) * (mm(v.T, g) - delta)).astype(BF)
        grad_scores[...] = inner
        grad_q[where, :] = (mm(k, inner) * 0.125).astype(BF)
        grad_k[where, :] = mm(grad_scores[...], q.T).T.astype(BF)
        grad_v[where, :] = mm(weights[...], g.T).T.astype(BF)
        return carry

    lax.fori_loop(0, HEADS, head, 0)
    for column in range(0, PIX, 512):
        where = slice(column, column + 512)
        grad_normed[:, where] = (
            mm(wq[...], grad_q[:, where], TN)
            + mm(wk[...], grad_k[:, where], TN)
            + mm(wv[...], grad_v[:, where], TN)
        )

    def back(group, carry):
        where = rows(group * BLOCK, BLOCK)
        unit = unit_of(resid[where, :], stats2, where)
        grad = grad_normed[where, :]
        outer = grad_out[where, :].astype(F32)
        total = outer + unit_back(grad * par[where, GAIN + 2 : GAIN + 3], unit, stats2[where, 1:2])
        low = total.astype(BF)
        grad_resid[where, :] = total
        grad_branch[where, :] = low
        small[where, 0:1] = row_sum(grad * unit)
        small[where, 1:2] = row_sum(grad)
        small[where, 2:3] = row_sum(low.astype(F32))
        small[where, 3:4] = row_sum(outer)
        return carry

    lax.fori_loop(0, 512 // BLOCK, back, 0)


def projections(
    index, normed, resid, par, mixed, grad_q, grad_k, grad_v, grad_out, p_own, p_peer, block, grads, wp
):
    live = index[2] > 0
    place_square(wp, index, p_own, p_peer)
    for column in range(0, PIX, 512):
        where = slice(column, column + 512)
        total = resid[:, where] + mm(wp[...], mixed[:, where], TN) + par[:, PROJB : PROJB + 1]
        block[:, where] = jnp.where(live, total, jnp.zeros_like(total)).astype(BF)
    pairs = ((grad_q, normed), (grad_k, normed), (grad_v, normed), (mixed, grad_out))
    for which, (left, right) in enumerate(pairs):
        result = mm(left[...], right[...], NT).astype(BF)
        for part in range(32):
            plane, chunk = part // 16, part % 16
            grads[chunk // 8, plane, chunk % 8, which] = result[part * 16 : (part + 1) * 16]


def second_back(
    index, grad_branch, hidden, stats1, par, w_own, w_peer, grad_hidden, small, col, full, grad_second
):
    place_conv(full, index, w_own, w_peer)
    taps_of(col, edge_masks(-1), grad_branch, 0, 512, 0, -1)
    conv_dots(grad_second, full, col, TN, lambda total, column: total)

    def back(group, carry):
        where = rows(group * BLOCK, BLOCK)
        unit = unit_of(hidden[where, :], stats1, where)
        gain = par[where, GAIN + 1 : GAIN + 2]
        normed = unit * gain + par[where, BIAS + 1 : BIAS + 2]
        scale = 1.0 + par[where, SCALE : SCALE + 1]
        grad_pre = grad_second[where, :] * silu_slope(normed * scale + par[where, SHIFT : SHIFT + 1])
        grad = grad_pre * scale
        low = unit_back(grad * gain, unit, stats1[where, 1:2]).astype(BF)
        grad_hidden[where, :] = low
        small[where, 0:1] = row_sum(grad_pre * normed)
        small[where, 1:2] = row_sum(grad_pre)
        small[where, 2:3] = row_sum(grad * unit)
        small[where, 3:4] = row_sum(grad)
        small[where, 4:5] = row_sum(low.astype(F32))
        return carry

    lax.fori_loop(0, 512 // BLOCK, back, 0)


def first_back(
    index, grad_hidden, own, peer, stats0, par, grad_resid, w_own, w_peer,
    near, far, small, col, full, grad_first,
):
    half = index[0]
    place_conv(full, index, w_own, w_peer)
    taps_of(col, edge_masks(-1), grad_hidden, 0, 512, 0, -1)
    conv_dots(grad_first, full, col, TN, lambda total, column: total)
    for picture, base, dest in ((own, half * 256, near), (peer, (1 - half) * 256, far)):

        def back(group, carry, picture=picture, base=base, dest=dest):
            here = rows(group * BLOCK, BLOCK)
            where = rows(base + group * BLOCK, BLOCK)
            unit = unit_of(picture[here, :].astype(F32), stats0, where)
            gain = par[where, GAIN : GAIN + 1]
            grad = grad_first[where, :] * silu_slope(unit * gain + par[where, BIAS : BIAS + 1])
            total = grad_resid[where, :] + unit_back(grad * gain, unit, stats0[where, 1:2])
            dest[here, :] = total.astype(dest.dtype)
            small[where, 0:1] = row_sum(grad * unit)
            small[where, 1:2] = row_sum(grad)
            return carry

        lax.fori_loop(0, 256 // BLOCK, back, 0)


def weight_back(index, grad_own, grad_peer, source_own, source_peer, grads, col, turned):
    masks = edge_masks(-1)
    taps_of(col, masks, grad_own, 0, 256, 0, -1)
    taps_of(col, masks, grad_peer, 0, 256, PIX, -1)
    turned[:PIX, :] = source_own[...].T
    turned[PIX:, :] = source_peer[...].T
    for tap in range(9):
        result = mm(col[tap * 256 : (tap + 1) * 256, :], turned[...]).astype(BF)
        for part in range(16):
            grads[part, tap] = result[part * 16 : (part + 1) * 16]


def remote(source, dest, sends, recvs, slot, target):
    return pltpu.make_async_remote_copy(
        src_ref=source,
        dst_ref=dest,
        send_sem=sends.at[slot],
        recv_sem=recvs.at[slot],
        device_id=target,
        device_id_type=pl.DeviceIdType.MESH,
    )


def meet(targets):
    barrier = pltpu.get_barrier_semaphore()
    for target in targets:
        pl.semaphore_signal(barrier, inc=1, device_id=target, device_id_type=pl.DeviceIdType.MESH)
    pl.semaphore_wait(barrier, len(targets))


def position():
    place = lax.axis_index("batch")
    return place, place % 2, (place // 2) % 2, place // 4


PIECES = 6
KINDS = 10


def gather(
    pre_embed, params, emb_weight, emb_bias, images, conv_weight, qkv_weight, proj_weight,
    par, image_peer, conv_peer, qkv_peer, proj_peer,
    par_send, par_recv, sends, recvs, few_sends, few_recvs,
):
    half = lax.axis_index("head")
    place, core, up, deep = position()
    z_low = deep % 2
    to_x = {"head": 1 - half}
    to_y = {"batch": place + 2 * (1 - 2 * up)}
    to_z = {"batch": place + 4 * (1 - 2 * z_low)}
    to_core = {"batch": place + (1 - 2 * core)}
    meet([to_x, to_y, to_z, to_core])

    def block(flip_core=0, flip_y=0, flip_z=0):
        c = 1 - core if flip_core else core
        y = 1 - up if flip_y else up
        z = 1 - z_low if flip_z else z_low
        return (c + 2 * y + 4 * z) * 32

    def views(piece, near, start, count):
        where = rows(start, count)
        if piece < 4:
            taps = pl.ds(0, 5) if piece % 2 == 0 else pl.ds(5, 4)
            return (conv_weight if near else conv_peer).at[piece // 2, taps, where, :]
        if piece == 4:
            return (qkv_weight if near else qkv_peer).at[:, where, :]
        return (proj_weight if near else proj_peer).at[where, :]

    def copy(piece, kind, start, count, target, near=False):
        return remote(
            views(piece, near, start, count), views(piece, False, start, count),
            sends.at[piece], recvs.at[piece], kind, target,
        )

    def regions(flip_core):
        return (
            (block(flip_core), 32),
            (block(flip_core, 1), 32),
            (block(flip_core, 0, 1), 32),
            (block(flip_core, 1, 1), 16),
            (block(flip_core, 1, 1) + 16, 16),
        )

    mine, others = regions(0), regions(1)

    def arrived(piece, kind):
        start, count = mine[kind] if kind < 5 else others[kind - 5]
        copy(piece, kind, start, count, to_core).wait_recv()

    def over_x(piece):
        arrived(piece, 0)
        for kind, target in ((1, to_y), (2, to_z), (5, to_core)):
            copy(piece, kind, block(), 32, target).start()

    def over_yz(piece):
        arrived(piece, 2)
        copy(piece, 3, block(0, 0, 1), 16, to_y).start()
        copy(piece, 7, block(0, 0, 1), 32, to_core).start()
        arrived(piece, 1)
        copy(piece, 4, block(0, 1, 0) + 16, 16, to_z).start()
        copy(piece, 6, block(0, 1, 0), 32, to_core).start()

    def diagonal(piece):
        arrived(piece, 3)
        copy(piece, 8, block(0, 1, 1), 16, to_core).start()
        arrived(piece, 4)
        copy(piece, 9, block(0, 1, 1) + 16, 16, to_core).start()

    for piece in range(PIECES):
        copy(piece, 0, block(), 32, to_x, near=True).start()
    picture = remote(images.at[1 - half], image_peer, few_sends, few_recvs, 0, to_x)
    picture.start()
    embed = jax.nn.silu(pre_embed[...])
    own_row = jnp.where(half == 0, embed[0:1], embed[1:2])
    peer_row = jnp.where(half == 0, embed[1:2], embed[0:1])
    near = rows(half * 256, 256)
    par[near, 0:9] = params[...]
    par_send[:, 0:9] = params[...]
    for which in range(2):
        dense = emb_weight[which].astype(F32)
        offset = emb_bias[:, which : which + 1]
        par[near, SCALE + which : SCALE + which + 1] = row_sum(dense * own_row) + offset
        par_send[:, SCALE + which : SCALE + which + 1] = row_sum(dense * peer_row) + offset
    block_copy = remote(par_send, par_recv, few_sends, few_recvs, 1, to_x)
    block_copy.start()

    over_x(0)
    over_x(1)
    over_yz(0)
    over_x(2)
    over_yz(1)
    diagonal(0)
    over_x(3)
    over_yz(2)
    diagonal(1)
    over_x(4)
    over_x(5)
    over_yz(3)
    diagonal(2)
    over_yz(4)
    over_yz(5)
    diagonal(3)
    diagonal(4)
    diagonal(5)
    block_copy.wait_recv()
    par[rows((1 - half) * 256, 256), :] = par_recv[:, 0:11]
    picture.wait_recv()
    for piece in range(PIECES):
        for kind in range(5, 10):
            arrived(piece, kind)
    for piece in range(PIECES):
        copy(piece, 0, block(), 32, to_x).wait_send()
        for kind, start, count in (
            (1, block(), 32), (2, block(), 32), (5, block(), 32),
            (3, block(0, 0, 1), 16), (7, block(0, 0, 1), 32),
            (4, block(0, 1, 0) + 16, 16), (6, block(0, 1, 0), 32),
            (8, block(0, 1, 1), 16), (9, block(0, 1, 1) + 16, 16),
        ):
            copy(piece, kind, start, count, to_x).wait_send()
    picture.wait_send()
    block_copy.wait_send()


def gather_call(pre_embed, params, emb_weight, emb_bias, images, conv_weight, qkv_weight, proj_weight):
    anywhere = pl.BlockSpec(memory_space=pl.ANY)
    return pl.pallas_call(
        gather,
        out_shape=[
            out((512, 11), F32),
            out(images.shape[1:], BF),
            out(conv_weight.shape, BF),
            out(qkv_weight.shape, BF),
            out(proj_weight.shape, BF),
        ],
        in_specs=[VMEM] * 4 + [anywhere] * 4,
        out_specs=[VMEM] + [anywhere] * 4,
        scratch_shapes=[
            pltpu.VMEM((256, 128), F32),
            pltpu.VMEM((256, 128), F32),
            pltpu.SemaphoreType.DMA((PIECES, KINDS)),
            pltpu.SemaphoreType.DMA((PIECES, KINDS)),
            pltpu.SemaphoreType.DMA((2,)),
            pltpu.SemaphoreType.DMA((2,)),
        ],
        cost_estimate=pl.CostEstimate(flops=0, bytes_accessed=100 * 2**20, transcendentals=0),
        compiler_params=pltpu.CompilerParams(
            collective_id=1, has_side_effects=True, vmem_limit_bytes=24 * 2**20
        ),
    )(pre_embed, params, emb_weight, emb_bias, images, conv_weight, qkv_weight, proj_weight)


SENDS = 11


class Sum:
    def __init__(self, source, total, scratch, planes):
        self.source, self.total, self.planes = source, total, planes
        self.sends, self.recvs, self.core_in, self.first, self.y_in, self.second, self.z_in = scratch[:7]
        if planes:
            self.x_in, self.middle = scratch[7:]
        self.half = lax.axis_index("head")
        self.place, self.core, self.up, self.deep = position()
        self.steps = [self.start, self.core_done]
        if planes:
            self.steps.append(self.x_done)
        self.steps += [self.y_done, self.z_done, self.z_back, self.y_back, self.finish]
        self.open = []

    def to_core(self):
        return {"batch": self.place + 1 - 2 * self.core}

    def to_y(self):
        return {"batch": self.place + 2 * (1 - 2 * self.up)}

    def to_z(self, ahead):
        return {"batch": (self.deep + ahead) % 4 * 4 + self.place % 4}

    def send(self, slot, source, dest, target):
        copy = remote(source, dest, self.sends, self.recvs, slot, target)
        copy.start()
        self.open.append(copy)

    def arrived(self, slot, dest):
        remote(dest, dest, self.sends, self.recvs, slot, self.to_core()).wait_recv()

    def start(self):
        other = 1 - self.core
        part = self.source.at[other] if self.planes else self.source.at[pl.ds(other * 8, 8)]
        self.send(0, part, self.core_in, self.to_core())

    def add(self, dest, left, *right):
        total = left.astype(F32)
        for term in right:
            total = total + term.astype(F32)
        dest[...] = total.astype(BF)

    def core_done(self):
        self.arrived(0, self.core_in)
        if self.planes:
            self.add(self.middle, self.source[self.core], self.core_in[...])
            self.send(10, self.middle.at[1 - self.half], self.x_in, {"head": 1 - self.half})
        else:
            self.add(self.first, self.source[pl.ds(self.core * 8, 8)], self.core_in[...])
            self.send_y()

    def x_done(self):
        self.arrived(10, self.x_in)
        self.add(self.first, self.middle[self.half], self.x_in[...])
        self.send_y()

    def send_y(self):
        self.send(1, self.first.at[pl.ds((1 - self.up) * 4, 4)], self.y_in, self.to_y())

    def y_done(self):
        self.arrived(1, self.y_in)
        self.add(self.second, self.first[pl.ds(self.up * 4, 4)], self.y_in[...])
        for ahead in (2, 1, 3):
            chunk = self.second.at[(self.deep + ahead) % 4]
            self.send(1 + ahead, chunk, self.z_in.at[ahead - 1], self.to_z(ahead))

    def chunk(self, deep):
        return self.core * 8 + self.up * 4 + deep

    def z_done(self):
        for ahead in (1, 2, 3):
            self.arrived(1 + ahead, self.z_in.at[ahead - 1])
        mine = self.total.at[self.chunk(self.deep)]
        self.add(mine, self.second[self.deep], self.z_in[0], self.z_in[1], self.z_in[2])
        for ahead in (2, 1, 3):
            self.send(4 + ahead, mine, mine, self.to_z(ahead))

    def z_back(self):
        for ahead in (1, 2, 3):
            self.arrived(4 + ahead, self.total.at[self.chunk((self.deep + 4 - ahead) % 4)])
        part = self.total.at[pl.ds(self.chunk(0), 4)]
        self.send(8, part, part, self.to_y())

    def y_back(self):
        self.arrived(8, self.total.at[pl.ds(self.core * 8 + (1 - self.up) * 4, 4)])
        part = self.total.at[pl.ds(self.core * 8, 8)]
        self.send(9, part, part, self.to_core())

    def finish(self):
        self.arrived(9, self.total.at[pl.ds((1 - self.core) * 8, 8)])
        for copy in self.open:
            copy.wait_send()


def sum_scratch(tail, planes):
    shapes = [
        pltpu.SemaphoreType.DMA((SENDS,)),
        pltpu.SemaphoreType.DMA((SENDS,)),
        pltpu.VMEM(((2, 8) if planes else (8,)) + tail, BF),
        pltpu.VMEM((8,) + tail, BF),
        pltpu.VMEM((4,) + tail, BF),
        pltpu.VMEM((4,) + tail, BF),
        pltpu.VMEM((3,) + tail, BF),
    ]
    if planes:
        shapes += [pltpu.VMEM((8,) + tail, BF), pltpu.VMEM((2, 8) + tail, BF)]
    return shapes


def batch_sums(squares, grads1, grads0, squares_sum, sum1, sum0, *scratch):
    place, core, up, deep = position()
    half = lax.axis_index("head")
    targets = [{"head": 1 - half}, {"batch": place + 1 - 2 * core}, {"batch": place + 2 * (1 - 2 * up)}]
    targets += [{"batch": (deep + ahead) % 4 * 4 + place % 4} for ahead in (1, 2, 3)]
    meet(targets)
    chains = [Sum(squares, squares_sum, scratch[:9], True)]
    scratch = scratch[9:]
    for source, total in ((grads1, sum1), (grads0, sum0)):
        for number, taps in enumerate(TAP_PARTS):
            chains.append(
                Sum(source.at[:, taps], total.at[:, taps], scratch[:7], False)
            )
            scratch = scratch[7:]
    for tick in range(len(chains) + 8):
        for number, chain in enumerate(chains):
            if 0 <= tick - number < len(chain.steps):
                chain.steps[tick - number]()


TAP_PARTS = (slice(0, 3), slice(3, 6), slice(6, 9))


def batch_sums_call(squares, grads1, grads0):
    scratch = sum_scratch((4, 16, 512), True)
    for part in TAP_PARTS * 2:
        scratch += sum_scratch((part.stop - part.start, 16, 512), False)
    return pl.pallas_call(
        batch_sums,
        out_shape=[out((16, 4, 16, 512), BF), out(grads1.shape, BF), out(grads0.shape, BF)],
        in_specs=[VMEM] * 3,
        out_specs=[VMEM] * 3,
        scratch_shapes=scratch,
        cost_estimate=pl.CostEstimate(flops=0, bytes_accessed=200 * 2**20, transcendentals=0),
        compiler_params=pltpu.CompilerParams(
            collective_id=2, has_side_effects=True, vmem_limit_bytes=56 * 2**20
        ),
    )(squares, grads1, grads0)


def paired(
    batch_size,
    images,
    timesteps,
    classes,
    live_count,
    norm_gain,
    norm_bias,
    conv_weight,
    conv_bias,
    emb_weight,
    emb_bias,
    class_table,
    qkv_weight,
    proj_weight,
    proj_bias,
    cotangent,
):
    half = lax.axis_index("head")
    place = lax.axis_index("batch")
    bits = batch_size.bit_length() - 1

    def across(value):
        return lax.ppermute(value, "head", [(0, 1), (1, 0)])

    def over(value, bit):
        return lax.ppermute(value, "batch", [(i, i ^ (1 << bit)) for i in range(batch_size)])

    def pick(value, index):
        return lax.dynamic_index_in_dim(value, index, 0, keepdims=False)

    def by_half(near, far, axis):
        return jnp.where(
            half == 0,
            jnp.concatenate([near, far], axis),
            jnp.concatenate([far, near], axis),
        )

    def my_bit(bit):
        return (place >> bit) & 1

    def widen(value, bit):
        peer = over(value, bit)
        return jnp.where(
            my_bit(bit) == 0, jnp.concatenate([value, peer]), jnp.concatenate([peer, value])
        )

    image_own = pick(images, half)
    cot_own = pick(cotangent, half)
    cot_peer = across(pick(cotangent, 1 - half))

    table_rows = jnp.stack([pick(class_table, classes[slot]) for slot in range(2)]).astype(F32)
    emb_width = class_table.shape[1]
    pre_embed = jnp.stack([features(timesteps[slot], emb_width) for slot in range(2)]) + table_rows
    params = jnp.concatenate([norm_gain, norm_bias, conv_bias, proj_bias[None]]).T
    par, image_peer, conv_peer, q_peer, p_peer = gather_call(
        pre_embed, params, emb_weight, emb_bias.T, images, conv_weight, qkv_weight, proj_weight
    )
    weights0 = (conv_weight[0], conv_peer[0])
    weights1 = (conv_weight[1], conv_peer[1])
    dense = emb_weight.astype(F32)
    live = (half < live_count[0]).astype(jnp.int32)
    scalars = jnp.stack([half, 0 * half, live]).astype(jnp.int32)
    full_bf = out((512, PIX), BF)
    full_f32 = out((512, PIX), F32)
    half_bf = out((256, PIX), BF)
    half_f32 = out((256, PIX), F32)
    stats = out((512, 2), F32)
    taps = pltpu.VMEM((9 * 512, PIX), BF)
    conv_full = pltpu.VMEM((9, 512, 512), BF)
    square = pltpu.VMEM((512, 512), BF)
    wide_bf = pltpu.VMEM((512, PIX), BF)
    wide_f32 = pltpu.VMEM((512, PIX), F32)
    pixels = pltpu.VMEM((PIX, PIX), BF)
    conv_flops = 2 * 9 * 512 * 512 * PIX

    first, hidden, stats0, stats1, second = kernel_call(
        first_conv, [full_bf, full_f32, stats, stats, full_bf], [taps, conv_full], conv_flops,
        scalars, image_own, image_peer, par, *weights0,
    )
    resid, stats2, normed = kernel_call(
        second_conv, [full_f32, stats, full_bf], [taps, conv_full], conv_flops,
        scalars, second, image_own, image_peer, par, *weights1,
    )
    mixed, grad_q, grad_k, grad_v, grad_out, grad_resid, grad_branch, small2 = kernel_call(
        attention,
        [full_bf] * 5 + [full_f32, full_bf, out((512, 4), F32)],
        [square] * 4 + [wide_bf] * 4 + [pixels] * 2 + [wide_f32],
        4 * conv_flops,
        scalars, normed, resid, stats2, par, cot_own, cot_peer, qkv_weight, q_peer, proj_weight, p_peer,
    )
    first_peer = across(first)
    second_peer = across(second)

    def halves(value):
        pair = value.reshape(2, 256, PIX)
        return pick(pair, half), across(pick(pair, 1 - half))

    branch_own, branch_peer = halves(grad_branch)
    grad_hidden, small1 = kernel_call(
        second_back, [full_bf, out((512, 5), F32)], [taps, conv_full, wide_f32], conv_flops,
        scalars, grad_branch, hidden, stats1, par, *weights1,
    )
    hidden_own, hidden_peer = halves(grad_hidden)
    block, square_grads = kernel_call(
        projections, [full_bf, out((2, 2, 8, 4, 16, 512), BF)], [square], conv_flops // 2,
        scalars, normed, resid, par, mixed, grad_q, grad_k, grad_v, grad_out, proj_weight, p_peer,
    )
    block_own, block_peer = halves(block)
    conv_grads = out((16, 9, 16, 512), BF)
    tap_pair = pltpu.VMEM((9 * 256, 2 * PIX), BF)
    turned = pltpu.VMEM((2 * PIX, 512), BF)

    def weight_grad(grad_own, grad_peer, source, source_peer):
        return kernel_call(
            weight_back, [conv_grads], [tap_pair, turned], conv_flops,
            scalars, grad_own, grad_peer, source, source_peer,
        )[0]

    conv_grad1 = weight_grad(branch_own, branch_peer, second, second_peer)
    conv_grad0 = weight_grad(hidden_own, hidden_peer, first, first_peer)
    near, far, small0 = kernel_call(
        first_back, [half_f32, half_bf, out((512, 2), F32)], [taps, conv_full, wide_f32], conv_flops,
        scalars, grad_hidden, image_own, image_peer, stats0, par, grad_resid, *weights0,
    )
    far = across(far).astype(F32)

    square_sum, conv_sum1, conv_sum0 = batch_sums_call(
        square_grads.reshape(2, 2, 8, 4, 16, 512), conv_grad1, conv_grad0
    )

    def whole(value):
        return value.transpose(1, 0, 2, 3).reshape(value.shape[1], 256, 512).astype(F32)

    conv_total1, conv_total0, squares = whole(conv_sum1), whole(conv_sum0), whole(square_sum)
    small = jnp.concatenate([small0, small1, small2], 1).T.reshape(11, 2, 256).transpose(1, 0, 2)
    small_own, small_peer = pick(small, half), across(pick(small, 1 - half))
    sums = small_own + small_peer
    for bit in range(bits):
        sums = sums + over(sums, bit)
    emb_own, emb_peer = small_own[2:4], small_peer[2:4]
    emb_grads = by_half(emb_own[None], emb_peer[None], 0)
    pre_all = pre_embed
    ids = classes
    for bit in range(bits):
        emb_grads = widen(emb_grads, bit)
        pre_all = widen(pre_all, bit)
        ids = widen(ids, bit)
    emb_total = jnp.einsum("bmc,be->mce", emb_grads, jax.nn.silu(pre_all), precision=HIGH)
    rows_part = jnp.einsum("bmc,mce->be", emb_grads, dense, precision=HIGH)
    class_rows = (rows_part + across(rows_part)) * silu_slope(pre_all)
    chosen = (lax.iota(jnp.int32, class_table.shape[0])[:, None] == ids[None, :]).astype(F32)
    table_total = jnp.dot(chosen, class_rows, precision=HIGH)
    return (
        by_half(block_own[None], block_peer[None], 0),
        by_half(near[None], far[None], 0),
        jnp.stack([sums[0], sums[4], sums[7]]),
        jnp.stack([sums[1], sums[5], sums[8]]),
        jnp.stack([conv_total0, conv_total1]),
        jnp.stack([sums[6], sums[9]]),
        emb_total,
        sums[2:4],
        table_total,
        squares[:3],
        squares[3],
        sums[10],
    )


def solution(mesh):
    in_specs = (
        P("batch", "head", None),
        P("batch"),
        P("batch"),
        P("batch"),
        P(None, "head"),
        P(None, "head"),
        P(None, None, "head", None),
        P(None, "head"),
        P(None, "head", None),
        P(None, "head"),
        P(),
        P(None, "head", None),
        P("head", None),
        P("head"),
        P("batch", "head", None),
    )
    out_specs = (
        P("batch", "head", None),
        P("batch", "head", None),
        P(None, "head"),
        P(None, "head"),
        P(None, None, "head", None),
        P(None, "head"),
        P(None, "head", None),
        P(None, "head"),
        P(),
        P(None, "head", None),
        P("head", None),
        P("head"),
    )
    body = shards
    batch_size = mesh.shape["batch"]
    if mesh.shape["head"] == 2 and batch_size == 16:
        body = functools.partial(paired, batch_size)
    return jax.shard_map(body, mesh=mesh, in_specs=in_specs, out_specs=out_specs, check_vma=False)
```

```python
import math

import jax
import jax.numpy as jnp
from jax import lax
from jax.experimental import pallas as pl
from jax.experimental.pallas import tpu as pltpu
from jax.sharding import PartitionSpec as P

C = 512
GROUPS = 32
HEADS = 8
SIDE = 32


EPS = 1e-05
HIGH = lax.Precision.HIGHEST
CONTRACT_FIRST = (((0,), (0,)), ((), ()))
CONTRACT_LAST = (((1,), (1,)), ((), ()))


def silu_slope(values):
    sigma = jax.nn.sigmoid(values)
    return sigma * (1.0 + values * (1.0 - sigma))


def moved(source, grid_side, row_step, col_step):
    grid = source.reshape(source.shape[0], grid_side, grid_side)
    padded = jnp.pad(grid, ((0, 0), (1, 1), (1, 1)))
    window = padded[
        :, 1 + row_step : 1 + row_step + grid_side, 1 + col_step : 1 + col_step + grid_side
    ]
    return window.reshape(source.shape)


def group_unit(source, groups):
    grouped = source.reshape(groups, -1)
    centre = grouped - jnp.mean(grouped, axis=1, keepdims=True)
    inverse = lax.rsqrt(jnp.mean(jnp.square(centre), axis=1, keepdims=True) + EPS)
    return ((centre * inverse).reshape(source.shape), inverse)


def group_back(grad_unit, unit_rows, inverse, groups):
    flat_grad = grad_unit.reshape(groups, -1)
    flat_unit = unit_rows.reshape(groups, -1)
    result = flat_grad - jnp.mean(flat_grad, axis=1, keepdims=True)
    result = (result - flat_unit * jnp.mean(flat_grad * flat_unit, axis=1, keepdims=True)) * inverse
    return result.reshape(grad_unit.shape)


def conv_apply(weight, source, grid_side):
    result = jnp.dot(
        weight[0], moved(source, grid_side, -1, -1), preferred_element_type=jnp.float32
    )
    for tap_index in range(1, 9):
        result = result + jnp.dot(
            weight[tap_index],
            moved(source, grid_side, tap_index // 3 - 1, tap_index % 3 - 1),
            preferred_element_type=jnp.float32,
        )
    return result


def conv_transpose(weight, grads, grid_side):
    result = lax.dot_general(
        weight[0], moved(grads, grid_side, 1, 1), CONTRACT_FIRST, preferred_element_type=jnp.float32
    )
    for tap_index in range(1, 9):
        result = result + lax.dot_general(
            weight[tap_index],
            moved(grads, grid_side, 1 - tap_index // 3, 1 - tap_index % 3),
            CONTRACT_FIRST,
            preferred_element_type=jnp.float32,
        )
    return result


def conv_weight_grads(grads, source, grid_side):
    return jnp.stack(
        [
            lax.dot_general(
                grads,
                moved(source, grid_side, tap_index // 3 - 1, tap_index % 3 - 1),
                CONTRACT_LAST,
                preferred_element_type=jnp.float32,
            )
            for tap_index in range(9)
        ]
    )


def features(timestep, emb_width):
    half_width = emb_width // 2
    freqs = jnp.exp(-math.log(10000.0) * jnp.arange(half_width, dtype=jnp.float32) / half_width)
    angles = timestep.astype(jnp.float32) * freqs
    return jnp.concatenate([jnp.cos(angles), jnp.sin(angles)])


def shards(
    images,
    timesteps,
    classes,
    live_count,
    norm_gain,
    norm_bias,
    conv_weight,
    conv_bias,
    emb_weight,
    emb_bias,
    class_table,
    qkv_weight,
    proj_weight,
    proj_bias,
    cotangent,
):
    slot_count, chan_dev, pixel_count = images.shape
    grid_side = SIDE
    groups = chan_dev // (C // GROUPS)
    head_size = C // HEADS
    heads_dev = chan_dev // head_size
    att_scale = head_size ** (-0.5)
    emb_dense = emb_weight.astype(jnp.float32)
    class_total, emb_width = class_table.shape

    def gather_channels(rows_low):
        return lax.all_gather(rows_low, "head", axis=0, tiled=True)

    def input_grad(which_conv, grad_rows):
        weight_cols = conv_weight[which_conv]
        return lax.psum_scatter(
            conv_transpose(weight_cols, grad_rows, grid_side).astype(jnp.bfloat16),
            "head",
            scatter_dimension=0,
            tiled=True,
        ).astype(jnp.float32)

    def per_slot(slot_index, carry):
        (
            outputs,
            grads_in,
            gain_acc,
            bias_acc,
            convw_acc,
            convb_acc,
            embw_acc,
            embb_acc,
            table_acc,
            qkv_acc,
            projw_acc,
            projb_acc,
        ) = carry
        picture = lax.dynamic_index_in_dim(images, slot_index, 0, keepdims=False).astype(
            jnp.float32
        )
        live_flag = (slot_index < live_count[0]).astype(jnp.float32)
        class_id = classes[slot_index]
        table_row = lax.dynamic_index_in_dim(class_table, class_id, 0, keepdims=False).astype(
            jnp.float32
        )
        pre_embed = features(timesteps[slot_index], emb_width) + table_row
        embed = jax.nn.silu(pre_embed)
        scale = jnp.dot(emb_dense[0], embed, precision=HIGH) + emb_bias[0]
        shift = jnp.dot(emb_dense[1], embed, precision=HIGH) + emb_bias[1]
        unit_zero, inverse_zero = group_unit(picture, groups)
        pre_first = unit_zero * norm_gain[0][:, None] + norm_bias[0][:, None]
        first_full = gather_channels(jax.nn.silu(pre_first).astype(jnp.bfloat16))
        hidden = conv_apply(conv_weight[0], first_full, grid_side) + conv_bias[0][:, None]
        unit_one, inverse_one = group_unit(hidden, groups)
        normed_one = unit_one * norm_gain[1][:, None] + norm_bias[1][:, None]
        pre_second = normed_one * (1.0 + scale[:, None]) + shift[:, None]
        second_full = gather_channels(jax.nn.silu(pre_second).astype(jnp.bfloat16))
        resid = picture + conv_apply(conv_weight[1], second_full, grid_side) + conv_bias[1][:, None]
        unit_two, inverse_two = group_unit(resid, groups)
        normed_full = gather_channels(
            (unit_two * norm_gain[2][:, None] + norm_bias[2][:, None]).astype(jnp.bfloat16)
        )
        query = (
            jnp.dot(qkv_weight[0], normed_full, preferred_element_type=jnp.float32)
            .astype(jnp.bfloat16)
            .reshape(heads_dev, head_size, pixel_count)
        )
        keys = (
            jnp.dot(qkv_weight[1], normed_full, preferred_element_type=jnp.float32)
            .astype(jnp.bfloat16)
            .reshape(heads_dev, head_size, pixel_count)
        )
        values = (
            jnp.dot(qkv_weight[2], normed_full, preferred_element_type=jnp.float32)
            .astype(jnp.bfloat16)
            .reshape(heads_dev, head_size, pixel_count)
        )
        scores = (
            jnp.einsum("hdi,hdj->hij", query, keys, preferred_element_type=jnp.float32) * att_scale
        )
        highest = jnp.max(scores, axis=2, keepdims=True)
        expo = jnp.exp(scores - highest)
        totals = jnp.sum(expo, axis=2, keepdims=True)
        log_total = highest + jnp.log(totals)
        weights = (expo / totals).astype(jnp.bfloat16)
        mixed = (
            jnp.einsum("hdj,hij->hdi", values, weights, preferred_element_type=jnp.float32)
            .astype(jnp.bfloat16)
            .reshape(chan_dev, pixel_count)
        )
        weight_cols = proj_weight
        proj_term = lax.psum_scatter(
            lax.dot_general(
                weight_cols, mixed, CONTRACT_FIRST, preferred_element_type=jnp.float32
            ).astype(jnp.bfloat16),
            "head",
            scatter_dimension=0,
            tiled=True,
        ).astype(jnp.float32)
        result = resid + proj_term + proj_bias[:, None]
        outputs = lax.dynamic_update_index_in_dim(
            outputs, (live_flag * result).astype(jnp.bfloat16), slot_index, 0
        )
        grad_low = lax.dynamic_index_in_dim(cotangent, slot_index, 0, keepdims=False)
        grad_out = live_flag * grad_low.astype(jnp.float32)
        grad_full = lax.all_gather(grad_low, "head", axis=0, tiled=True) * live_flag.astype(
            jnp.bfloat16
        )
        grad_mixed = jnp.dot(proj_weight, grad_full, preferred_element_type=jnp.float32).astype(
            jnp.bfloat16
        )
        projw_acc = projw_acc + lax.dot_general(
            mixed, grad_full, CONTRACT_LAST, preferred_element_type=jnp.float32
        )
        projb_acc = projb_acc + jnp.sum(grad_out, axis=1)
        again = (
            jnp.einsum("hdi,hdj->hij", query, keys, preferred_element_type=jnp.float32) * att_scale
        )
        probs = jnp.exp(again - log_total)
        grad_heads = grad_mixed.reshape(heads_dev, head_size, pixel_count)
        grad_probs = jnp.einsum(
            "hdi,hdj->hij", grad_heads, values, preferred_element_type=jnp.float32
        )
        grad_scores = (
            probs * (grad_probs - jnp.sum(grad_probs * probs, axis=2, keepdims=True))
        ).astype(jnp.bfloat16)
        grad_query = (
            jnp.einsum("hij,hdj->hdi", grad_scores, keys, preferred_element_type=jnp.float32)
            * att_scale
        ).astype(jnp.bfloat16)
        grad_keys = (
            jnp.einsum("hij,hdi->hdj", grad_scores, query, preferred_element_type=jnp.float32)
            * att_scale
        ).astype(jnp.bfloat16)
        grad_values = jnp.einsum(
            "hdi,hij->hdj", grad_heads, weights, preferred_element_type=jnp.float32
        ).astype(jnp.bfloat16)
        stacked = jnp.stack([grad_query, grad_keys, grad_values]).reshape(3, chan_dev, pixel_count)
        weight_cols = qkv_weight
        grad_normed = lax.psum_scatter(
            lax.dot_general(
                weight_cols,
                stacked,
                (((0, 1), (0, 1)), ((), ())),
                preferred_element_type=jnp.float32,
            ).astype(jnp.bfloat16),
            "head",
            scatter_dimension=0,
            tiled=True,
        ).astype(jnp.float32)
        qkv_acc = qkv_acc + lax.dot_general(
            stacked, normed_full, (((2,), (1,)), ((), ())), preferred_element_type=jnp.float32
        )
        grad_resid = grad_out + group_back(
            grad_normed * norm_gain[2][:, None], unit_two, inverse_two, groups
        )
        grad_branch = grad_resid.astype(jnp.bfloat16)
        grad_second = input_grad(1, grad_branch)
        grad_pre = grad_second * silu_slope(pre_second)
        scale_grad = jnp.sum(grad_pre * normed_one, axis=1)
        shift_grad = jnp.sum(grad_pre, axis=1)
        grad_normed_one = grad_pre * (1.0 + scale[:, None])
        grad_hidden = group_back(
            grad_normed_one * norm_gain[1][:, None], unit_one, inverse_one, groups
        ).astype(jnp.bfloat16)
        grad_first = input_grad(0, grad_hidden)
        grad_pre_first = grad_first * silu_slope(pre_first)
        picture_grad = grad_resid + group_back(
            grad_pre_first * norm_gain[0][:, None], unit_zero, inverse_zero, groups
        )
        grads_in = lax.dynamic_update_index_in_dim(grads_in, picture_grad, slot_index, 0)
        gain_acc = gain_acc + jnp.stack(
            [
                jnp.sum(grad_pre_first * unit_zero, axis=1),
                jnp.sum(grad_normed_one * unit_one, axis=1),
                jnp.sum(grad_normed * unit_two, axis=1),
            ]
        )
        bias_acc = bias_acc + jnp.stack(
            [
                jnp.sum(grad_pre_first, axis=1),
                jnp.sum(grad_normed_one, axis=1),
                jnp.sum(grad_normed, axis=1),
            ]
        )
        convw_acc = convw_acc + jnp.stack(
            [
                conv_weight_grads(grad_hidden, first_full, grid_side),
                conv_weight_grads(grad_branch, second_full, grid_side),
            ]
        )
        convb_acc = convb_acc + jnp.stack(
            [
                jnp.sum(grad_hidden.astype(jnp.float32), axis=1),
                jnp.sum(grad_branch.astype(jnp.float32), axis=1),
            ]
        )
        embw_acc = embw_acc + jnp.stack(
            [scale_grad[:, None] * embed[None, :], shift_grad[:, None] * embed[None, :]]
        )
        embb_acc = embb_acc + jnp.stack([scale_grad, shift_grad])
        grad_embed = jnp.dot(scale_grad, emb_dense[0], precision=HIGH) + jnp.dot(
            shift_grad, emb_dense[1], precision=HIGH
        )
        class_row = grad_embed * silu_slope(pre_embed)
        old_row = lax.dynamic_index_in_dim(table_acc, class_id, 0, keepdims=True)
        table_acc = lax.dynamic_update_index_in_dim(
            table_acc, old_row + class_row[None, :], class_id, 0
        )
        return (
            outputs,
            grads_in,
            gain_acc,
            bias_acc,
            convw_acc,
            convb_acc,
            embw_acc,
            embb_acc,
            table_acc,
            qkv_acc,
            projw_acc,
            projb_acc,
        )

    table_start = jnp.zeros(class_table.shape, jnp.float32)
    initial = (
        jnp.zeros(images.shape, jnp.bfloat16),
        jnp.zeros(images.shape, jnp.float32),
        jnp.zeros(norm_gain.shape, jnp.float32),
        jnp.zeros(norm_bias.shape, jnp.float32),
        jnp.zeros(conv_weight.shape, jnp.float32),
        jnp.zeros(conv_bias.shape, jnp.float32),
        jnp.zeros(emb_weight.shape, jnp.float32),
        jnp.zeros(emb_bias.shape, jnp.float32),
        table_start,
        jnp.zeros(qkv_weight.shape, jnp.float32),
        jnp.zeros(proj_weight.shape, jnp.float32),
        jnp.zeros(proj_bias.shape, jnp.float32),
    )
    final = lax.fori_loop(0, slot_count, per_slot, initial)
    (
        outputs,
        grads_in,
        gain_acc,
        bias_acc,
        convw_acc,
        convb_acc,
        embw_acc,
        embb_acc,
        table_acc,
        qkv_acc,
        projw_acc,
        projb_acc,
    ) = final
    table_total = lax.psum(table_acc, ("batch", "head"))
    summed = (
        lax.psum(gain_acc.astype(jnp.bfloat16), "batch").astype(jnp.float32),
        lax.psum(bias_acc.astype(jnp.bfloat16), "batch").astype(jnp.float32),
        lax.psum(convw_acc.astype(jnp.bfloat16), "batch").astype(jnp.float32),
        lax.psum(convb_acc.astype(jnp.bfloat16), "batch").astype(jnp.float32),
        lax.psum(embw_acc.astype(jnp.bfloat16), "batch").astype(jnp.float32),
        lax.psum(embb_acc.astype(jnp.bfloat16), "batch").astype(jnp.float32),
        lax.psum(qkv_acc.astype(jnp.bfloat16), "batch").astype(jnp.float32),
        lax.psum(projw_acc.astype(jnp.bfloat16), "batch").astype(jnp.float32),
        lax.psum(projb_acc.astype(jnp.bfloat16), "batch").astype(jnp.float32),
    )
    return (
        outputs,
        grads_in,
        summed[0],
        summed[1],
        summed[2],
        summed[3],
        summed[4],
        summed[5],
        table_total,
        summed[6],
        summed[7],
        summed[8],
    )


PIX = 1024
BLOCK = 128
BF = jnp.bfloat16
F32 = jnp.float32
NN = (((1,), (0,)), ((), ()))
TN = (((0,), (0,)), ((), ()))
NT = (((1,), (1,)), ((), ()))
VMEM = pl.BlockSpec(memory_space=pltpu.VMEM)
SMEM = pl.BlockSpec(memory_space=pltpu.SMEM)

GAIN, BIAS, CONVB, PROJB, SCALE, SHIFT = 0, 3, 6, 8, 9, 10


def mm(left, right, dims=NN):
    return lax.dot_general(left, right, dims, preferred_element_type=F32)


class Far:
    def __init__(self, array):
        self.array = array


ANYWHERE = pl.BlockSpec(memory_space=pl.ANY)


def operands(args):
    arrays = [arg.array if isinstance(arg, Far) else arg for arg in args]
    specs = [ANYWHERE if isinstance(arg, Far) else VMEM for arg in args]
    return arrays, specs


def kernel_call(kernel, outs, scratch, flops, scalars, *args):
    arrays, specs = operands(args)
    moved_bytes = sum(a.size * a.dtype.itemsize for a in arrays)
    moved_bytes += sum(math.prod(o.shape) * o.dtype.itemsize for o in outs)
    return pl.pallas_call(
        kernel,
        out_shape=outs,
        in_specs=[SMEM] + specs,
        out_specs=[VMEM] * len(outs),
        scratch_shapes=[pltpu.SemaphoreType.DMA((8,))] + scratch,
        cost_estimate=pl.CostEstimate(flops=flops, bytes_accessed=moved_bytes, transcendentals=0),
        compiler_params=pltpu.CompilerParams(vmem_limit_bytes=56 * 2**20),
    )(scalars, *arrays)


def fetch(sems, slot, source, dest):
    copy = pltpu.make_async_copy(source, dest, sems.at[slot])
    copy.start()
    return copy


def out(shape, dtype):
    return jax.ShapeDtypeStruct(shape, dtype)


def rows(start, count):
    return pl.ds(pl.multiple_of(start, count), count)


def edge_masks(sign):
    pixel = lax.broadcasted_iota(jnp.int32, (1, PIX), 1)
    col, row = pixel % SIDE, pixel // SIDE
    table = {}
    for step in (-1, 1):
        moved_step = sign * step
        table["col", step] = ((col + moved_step >= 0) & (col + moved_step < SIDE)).astype(F32)
        table["row", step] = ((row + moved_step >= 0) & (row + moved_step < SIDE)).astype(F32)
    return table


def put_taps(dest, masks, values, first_row, depth, base, sign):
    count = values.shape[0]
    for col_step in (-1, 0, 1):
        across = values
        if col_step:
            across = pltpu.roll(values, (-sign * col_step) % PIX, 1) * masks["col", col_step]
        for row_step in (-1, 0, 1):
            copy = across
            if row_step:
                copy = pltpu.roll(across, (-sign * row_step * SIDE) % PIX, 1) * masks["row", row_step]
            tap = 3 * (row_step + 1) + col_step + 1
            dest[rows(tap * depth + first_row, count), base : base + PIX] = copy.astype(BF)


def taps_of(dest, masks, source, offset, depth, base, sign):
    for start in range(0, source.shape[0], 128):
        piece = source[start : start + 128, :].astype(F32)
        put_taps(dest, masks, piece, offset + start, depth, base, sign)


def fetch_conv(sems, full, half, which, own, peer):
    return (
        fetch(sems, 0, own.at[which], full.at[:, rows(half * 256, 256), :]),
        fetch(sems, 1, peer.at[which], full.at[:, rows((1 - half) * 256, 256), :]),
    )


def wait(copies):
    for copy in copies:
        copy.wait()


def conv_dots(dest, full, col, dims, finish):
    for column in range(0, PIX, 512):
        total = None
        for tap in range(9):
            term = mm(full[tap], col[tap * 512 : (tap + 1) * 512, column : column + 512], dims)
            total = term if total is None else total + term
        dest[:, column : column + 512] = finish(total, column)


def grouped(block):
    return block.reshape((-1, 16) + block.shape[1:])


def group_mean(block):
    return jnp.sum(block, axis=(1, 2), keepdims=True) * (1.0 / (16 * PIX))


def group_stats(block, stats, where):
    parts = grouped(block)
    centre = group_mean(parts)
    parts = parts - centre
    inverse = lax.rsqrt(group_mean(jnp.square(parts)) + EPS)
    count = block.shape[0]
    stats[where, 0:1] = jnp.broadcast_to(centre, (count // 16, 16, 1)).reshape(count, 1)
    stats[where, 1:2] = jnp.broadcast_to(inverse, (count // 16, 16, 1)).reshape(count, 1)
    return (parts * inverse).reshape(block.shape)


def unit_of(block, stats, where):
    return (block - stats[where, 0:1]) * stats[where, 1:2]


def unit_back(grad, unit, inverse):
    parts, units = grouped(grad), grouped(unit)
    result = parts - group_mean(parts) - units * group_mean(parts * units)
    return result.reshape(grad.shape) * inverse


def row_sum(block):
    return jnp.sum(block, axis=1, keepdims=True)


def first_conv(
    index, images, peer, par, w_own, w_peer, first, hidden, stats0, stats1, second, sems, own, col, full
):
    half = index[0]
    picture = fetch(sems, 2, images.at[half], own)
    arriving = fetch_conv(sems, full, half, 0, w_own, w_peer)
    picture.wait()
    masks = edge_masks(1)
    for source, base in ((own, half * 256), (peer, (1 - half) * 256)):

        def norm(group, carry, source=source, base=base):
            where = rows(base + group * BLOCK, BLOCK)
            unit = group_stats(source[rows(group * BLOCK, BLOCK), :].astype(F32), stats0, where)
            low = jax.nn.silu(unit * par[where, GAIN : GAIN + 1] + par[where, BIAS : BIAS + 1]).astype(BF)
            first[where, :] = low
            put_taps(col, masks, low.astype(F32), base + group * BLOCK, 512, 0, 1)
            return carry

        lax.fori_loop(0, 256 // BLOCK, norm, 0)
    wait(arriving)
    conv_dots(hidden, full, col, NN, lambda total, column: total + par[:, CONVB : CONVB + 1])

    def again(group, carry):
        where = rows(group * BLOCK, BLOCK)
        unit = group_stats(hidden[where, :], stats1, where)
        normed = unit * par[where, GAIN + 1 : GAIN + 2] + par[where, BIAS + 1 : BIAS + 2]
        pre = normed * (1.0 + par[where, SCALE : SCALE + 1]) + par[where, SHIFT : SHIFT + 1]
        second[where, :] = jax.nn.silu(pre).astype(BF)
        return carry

    lax.fori_loop(0, 512 // BLOCK, again, 0)


def second_conv(
    index, source, images, peer, par, w_own, w_peer, resid, stats2, normed, sems, own, col, full
):
    half = index[0]
    arriving = fetch_conv(sems, full, half, 1, w_own, w_peer)
    picture = fetch(sems, 2, images.at[half], own)
    taps_of(col, edge_masks(1), source, 0, 512, 0, 1)
    wait(arriving)
    conv_dots(resid, full, col, NN, lambda total, column: total + par[:, CONVB + 1 : CONVB + 2])
    picture.wait()
    for picture, base in ((own, half * 256), (peer, (1 - half) * 256)):

        def norm(group, carry, picture=picture, base=base):
            where = rows(base + group * BLOCK, BLOCK)
            block = resid[where, :] + picture[rows(group * BLOCK, BLOCK), :].astype(F32)
            resid[where, :] = block
            unit = group_stats(block, stats2, where)
            normed[where, :] = (unit * par[where, GAIN + 2 : GAIN + 3] + par[where, BIAS + 2 : BIAS + 3]).astype(BF)
            return carry

        lax.fori_loop(0, 256 // BLOCK, norm, 0)


def fetch_square(sems, slot, full, half, own, peer):
    count = own.shape[-2]
    near, far = rows(half * count, count), rows((1 - half) * count, count)
    if len(full.shape) == 3:
        near, far = (slice(None), near), (slice(None), far)
    return fetch(sems, slot, own, full.at[near]), fetch(sems, slot + 1, peer, full.at[far])


def attention(
    index, normed, resid, stats2, par, cotangent, cot_peer, q_own, q_peer, p_own, p_peer,
    mixed, grad_q, grad_k, grad_v, grad_out, grad_resid, grad_branch, small,
    sems, wqkv, wp, query, keys, values, grad_mixed, weights, grad_scores, grad_normed, resid_in,
):
    half = index[0]
    live = index[2].astype(BF)
    arriving = fetch_square(sems, 0, wqkv, half, q_own, q_peer)
    later = fetch_square(sems, 2, wp, half, p_own, p_peer)
    later += (
        fetch(sems, 4, cotangent.at[half], grad_out.at[rows(half * 256, 256)]),
        fetch(sems, 5, cot_peer, grad_out.at[rows((1 - half) * 256, 256)]),
    )
    last = fetch(sems, 6, resid, resid_in)
    wait(arriving)
    for column in range(0, PIX, 512):
        where = slice(column, column + 512)
        query[:, where] = (mm(wqkv[0], normed[:, where]).astype(BF).astype(F32) * 0.125).astype(BF)
        keys[:, where] = mm(wqkv[1], normed[:, where]).astype(BF)
        values[:, where] = mm(wqkv[2], normed[:, where]).astype(BF)
    wait(later)
    grad_out[...] = grad_out[...] * live
    for column in range(0, PIX, 512):
        where = slice(column, column + 512)
        grad_mixed[:, where] = mm(wp[...], grad_out[:, where]).astype(BF)

    def head(number, carry):
        where = rows(number * 64, 64)
        q, k, v, g = query[where, :], keys[where, :], values[where, :], grad_mixed[where, :]
        scores = mm(k.T, q)
        expo = jnp.exp(scores - jnp.max(scores, axis=0, keepdims=True))
        low = (expo * (1.0 / jnp.sum(expo, axis=0, keepdims=True))).astype(BF)
        weights[...] = low
        mix = mm(v, low)
        mixed[where, :] = mix.astype(BF)
        delta = jnp.sum(mix * g.astype(F32), axis=0, keepdims=True)
        inner = (low.astype(F32) * (mm(v.T, g) - delta)).astype(BF)
        grad_scores[...] = inner
        grad_q[where, :] = (mm(k, inner) * 0.125).astype(BF)
        grad_k[where, :] = mm(grad_scores[...], q.T).T.astype(BF)
        grad_v[where, :] = mm(weights[...], g.T).T.astype(BF)
        return carry

    lax.fori_loop(0, HEADS, head, 0)
    for column in range(0, PIX, 512):
        where = slice(column, column + 512)
        grad_normed[:, where] = (
            mm(wqkv[0], grad_q[:, where], TN)
            + mm(wqkv[1], grad_k[:, where], TN)
            + mm(wqkv[2], grad_v[:, where], TN)
        )
    last.wait()

    def back(group, carry):
        where = rows(group * BLOCK, BLOCK)
        unit = unit_of(resid_in[where, :], stats2, where)
        grad = grad_normed[where, :]
        outer = grad_out[where, :].astype(F32)
        total = outer + unit_back(grad * par[where, GAIN + 2 : GAIN + 3], unit, stats2[where, 1:2])
        low = total.astype(BF)
        grad_resid[where, :] = total
        grad_branch[where, :] = low
        small[where, 0:1] = row_sum(grad * unit)
        small[where, 1:2] = row_sum(grad)
        small[where, 2:3] = row_sum(low.astype(F32))
        small[where, 3:4] = row_sum(outer)
        return carry

    lax.fori_loop(0, 512 // BLOCK, back, 0)


def projections(
    index, normed, resid, par, mixed, grad_q, grad_k, grad_v, grad_out, p_own, p_peer, block, grads, sems, wp
):
    live = index[2] > 0
    wait(fetch_square(sems, 0, wp, index[0], p_own, p_peer))
    for column in range(0, PIX, 512):
        where = slice(column, column + 512)
        total = resid[:, where] + mm(wp[...], mixed[:, where], TN) + par[:, PROJB : PROJB + 1]
        block[:, where] = jnp.where(live, total, jnp.zeros_like(total)).astype(BF)
    pairs = ((grad_q, normed), (grad_k, normed), (grad_v, normed), (mixed, grad_out))
    for which, (left, right) in enumerate(pairs):
        result = mm(left[...], right[...], NT).astype(BF)
        for part in range(32):
            plane, chunk = part // 16, part % 16
            grads[chunk // 8, plane, chunk % 8, which] = result[part * 16 : (part + 1) * 16]


def second_back(
    index, grad_branch, hidden, stats1, par, w_own, w_peer,
    grad_hidden, small, sems, col, full, grad_second, hidden_in,
):
    arriving = fetch_conv(sems, full, index[0], 1, w_own, w_peer)
    last = fetch(sems, 2, hidden, hidden_in)
    taps_of(col, edge_masks(-1), grad_branch, 0, 512, 0, -1)
    wait(arriving)
    conv_dots(grad_second, full, col, TN, lambda total, column: total)
    last.wait()

    def back(group, carry):
        where = rows(group * BLOCK, BLOCK)
        unit = unit_of(hidden_in[where, :], stats1, where)
        gain = par[where, GAIN + 1 : GAIN + 2]
        normed = unit * gain + par[where, BIAS + 1 : BIAS + 2]
        scale = 1.0 + par[where, SCALE : SCALE + 1]
        grad_pre = grad_second[where, :] * silu_slope(normed * scale + par[where, SHIFT : SHIFT + 1])
        grad = grad_pre * scale
        low = unit_back(grad * gain, unit, stats1[where, 1:2]).astype(BF)
        grad_hidden[where, :] = low
        small[where, 0:1] = row_sum(grad_pre * normed)
        small[where, 1:2] = row_sum(grad_pre)
        small[where, 2:3] = row_sum(grad * unit)
        small[where, 3:4] = row_sum(grad)
        small[where, 4:5] = row_sum(low.astype(F32))
        return carry

    lax.fori_loop(0, 512 // BLOCK, back, 0)


def remote(source, dest, sends, recvs, slot, target):
    return pltpu.make_async_remote_copy(
        src_ref=source,
        dst_ref=dest,
        send_sem=sends.at[slot],
        recv_sem=recvs.at[slot],
        device_id=target,
        device_id_type=pl.DeviceIdType.MESH,
    )


def meet(targets):
    barrier = pltpu.get_barrier_semaphore()
    for target in targets:
        pl.semaphore_signal(barrier, inc=1, device_id=target, device_id_type=pl.DeviceIdType.MESH)
    pl.semaphore_wait(barrier, len(targets))


def position():
    place = lax.axis_index("batch")
    return place, place % 2, (place // 2) % 2, place // 4


PIECES = 6
KINDS = 10


def gather(
    pre_embed, params, emb_weight, emb_bias, images, conv_weight, qkv_weight, proj_weight,
    par, image_peer, conv_peer, qkv_peer, proj_peer,
    par_send, par_recv, sends, recvs, few_sends, few_recvs,
):
    half = lax.axis_index("head")
    place, core, up, deep = position()
    z_low = deep % 2
    to_x = {"head": 1 - half}
    to_y = {"batch": place + 2 * (1 - 2 * up)}
    to_z = {"batch": place + 4 * (1 - 2 * z_low)}
    to_core = {"batch": place + (1 - 2 * core)}
    meet([to_x, to_y, to_z, to_core])

    def block(flip_core=0, flip_y=0, flip_z=0):
        c = 1 - core if flip_core else core
        y = 1 - up if flip_y else up
        z = 1 - z_low if flip_z else z_low
        return (c + 2 * y + 4 * z) * 32

    def views(piece, near, start, count):
        where = rows(start, count)
        if piece < 4:
            taps = pl.ds(0, 5) if piece % 2 == 0 else pl.ds(5, 4)
            return (conv_weight if near else conv_peer).at[piece // 2, taps, where, :]
        if piece == 4:
            return (qkv_weight if near else qkv_peer).at[:, where, :]
        return (proj_weight if near else proj_peer).at[where, :]

    def copy(piece, kind, start, count, target, near=False):
        return remote(
            views(piece, near, start, count), views(piece, False, start, count),
            sends.at[piece], recvs.at[piece], kind, target,
        )

    def regions(flip_core):
        return (
            (block(flip_core), 32),
            (block(flip_core, 1), 32),
            (block(flip_core, 0, 1), 32),
            (block(flip_core, 1, 1), 16),
            (block(flip_core, 1, 1) + 16, 16),
        )

    mine, others = regions(0), regions(1)

    def arrived(piece, kind):
        start, count = mine[kind] if kind < 5 else others[kind - 5]
        copy(piece, kind, start, count, to_core).wait_recv()

    def over_x(piece):
        arrived(piece, 0)
        for kind, target in ((1, to_y), (2, to_z), (5, to_core)):
            copy(piece, kind, block(), 32, target).start()

    def over_yz(piece):
        arrived(piece, 2)
        copy(piece, 3, block(0, 0, 1), 16, to_y).start()
        copy(piece, 7, block(0, 0, 1), 32, to_core).start()
        arrived(piece, 1)
        copy(piece, 4, block(0, 1, 0) + 16, 16, to_z).start()
        copy(piece, 6, block(0, 1, 0), 32, to_core).start()

    def diagonal(piece):
        arrived(piece, 3)
        copy(piece, 8, block(0, 1, 1), 16, to_core).start()
        arrived(piece, 4)
        copy(piece, 9, block(0, 1, 1) + 16, 16, to_core).start()

    for piece in range(PIECES):
        copy(piece, 0, block(), 32, to_x, near=True).start()
    picture = remote(images.at[1 - half], image_peer, few_sends, few_recvs, 0, to_x)
    picture.start()
    embed = jax.nn.silu(pre_embed[...])
    own_row = jnp.where(half == 0, embed[0:1], embed[1:2])
    peer_row = jnp.where(half == 0, embed[1:2], embed[0:1])
    near = rows(half * 256, 256)
    par[near, 0:9] = params[...]
    par_send[:, 0:9] = params[...]
    for which in range(2):
        dense = emb_weight[which].astype(F32)
        offset = emb_bias[:, which : which + 1]
        par[near, SCALE + which : SCALE + which + 1] = row_sum(dense * own_row) + offset
        par_send[:, SCALE + which : SCALE + which + 1] = row_sum(dense * peer_row) + offset
    block_copy = remote(par_send, par_recv, few_sends, few_recvs, 1, to_x)
    block_copy.start()

    over_x(0)
    over_x(1)
    over_yz(0)
    over_x(2)
    over_yz(1)
    diagonal(0)
    over_x(3)
    over_yz(2)
    diagonal(1)
    over_x(4)
    over_x(5)
    over_yz(3)
    diagonal(2)
    over_yz(4)
    over_yz(5)
    diagonal(3)
    diagonal(4)
    diagonal(5)
    block_copy.wait_recv()
    par[rows((1 - half) * 256, 256), :] = par_recv[:, 0:11]
    picture.wait_recv()
    for piece in range(PIECES):
        for kind in range(5, 10):
            arrived(piece, kind)
    for piece in range(PIECES):
        copy(piece, 0, block(), 32, to_x).wait_send()
        for kind, start, count in (
            (1, block(), 32), (2, block(), 32), (5, block(), 32),
            (3, block(0, 0, 1), 16), (7, block(0, 0, 1), 32),
            (4, block(0, 1, 0) + 16, 16), (6, block(0, 1, 0), 32),
            (8, block(0, 1, 1), 16), (9, block(0, 1, 1) + 16, 16),
        ):
            copy(piece, kind, start, count, to_x).wait_send()
    picture.wait_send()
    block_copy.wait_send()


def gather_call(pre_embed, params, emb_weight, emb_bias, images, conv_weight, qkv_weight, proj_weight):
    return pl.pallas_call(
        gather,
        out_shape=[
            out((512, 11), F32),
            out(images.shape[1:], BF),
            out(conv_weight.shape, BF),
            out(qkv_weight.shape, BF),
            out(proj_weight.shape, BF),
        ],
        in_specs=[VMEM] * 4 + [ANYWHERE] * 4,
        out_specs=[VMEM] + [ANYWHERE] * 4,
        scratch_shapes=[
            pltpu.VMEM((256, 128), F32),
            pltpu.VMEM((256, 128), F32),
            pltpu.SemaphoreType.DMA((PIECES, KINDS)),
            pltpu.SemaphoreType.DMA((PIECES, KINDS)),
            pltpu.SemaphoreType.DMA((2,)),
            pltpu.SemaphoreType.DMA((2,)),
        ],
        cost_estimate=pl.CostEstimate(flops=0, bytes_accessed=100 * 2**20, transcendentals=0),
        compiler_params=pltpu.CompilerParams(
            collective_id=1, has_side_effects=True, vmem_limit_bytes=24 * 2**20
        ),
    )(pre_embed, params, emb_weight, emb_bias, images, conv_weight, qkv_weight, proj_weight)


SENDS = 12


class Sum:
    def __init__(self, source, total, scratch, planes):
        self.source, self.total, self.planes = source, total, planes
        self.sends, self.recvs, self.core_in, self.first, self.y_in, self.second, self.z_in, self.result = scratch[:8]
        if planes:
            self.x_in, self.middle = scratch[8:10]
        self.half = lax.axis_index("head")
        self.place, self.core, self.up, self.deep = position()
        self.steps = [self.start, self.core_done]
        if planes:
            self.steps.append(self.x_done)
        self.steps += [self.y_done, self.z_done, self.z_back, self.y_back, self.finish]
        self.open = []

    def to_core(self):
        return {"batch": self.place + 1 - 2 * self.core}

    def to_y(self):
        return {"batch": self.place + 2 * (1 - 2 * self.up)}

    def to_z(self, ahead):
        return {"batch": (self.deep + ahead) % 4 * 4 + self.place % 4}

    def send(self, slot, source, dest, target):
        copy = remote(source, dest, self.sends, self.recvs, slot, target)
        copy.start()
        self.open.append(copy)

    def arrived(self, slot, dest):
        remote(dest, dest, self.sends, self.recvs, slot, self.to_core()).wait_recv()

    def start(self):
        other = 1 - self.core
        part = self.source.at[other] if self.planes else self.source.at[pl.ds(other * 8, 8)]
        self.send(0, part, self.core_in, self.to_core())

    def add(self, dest, left, *right):
        total = left.astype(F32)
        for term in right:
            total = total + term.astype(F32)
        dest[...] = total.astype(BF)

    def core_done(self):
        self.arrived(0, self.core_in)
        if self.planes:
            self.add(self.middle, self.source[self.core], self.core_in[...])
            self.send(10, self.middle.at[1 - self.half], self.x_in, {"head": 1 - self.half})
        else:
            self.add(self.first, self.source[pl.ds(self.core * 8, 8)], self.core_in[...])
            self.send_y()

    def x_done(self):
        self.arrived(10, self.x_in)
        self.add(self.first, self.middle[self.half], self.x_in[...])
        self.send_y()

    def send_y(self):
        self.send(1, self.first.at[pl.ds((1 - self.up) * 4, 4)], self.y_in, self.to_y())

    def y_done(self):
        self.arrived(1, self.y_in)
        self.add(self.second, self.first[pl.ds(self.up * 4, 4)], self.y_in[...])
        for ahead in (2, 1, 3):
            chunk = self.second.at[(self.deep + ahead) % 4]
            self.send(1 + ahead, chunk, self.z_in.at[ahead - 1], self.to_z(ahead))

    def chunk(self, deep):
        return self.core * 8 + self.up * 4 + deep

    def z_done(self):
        for ahead in (1, 2, 3):
            self.arrived(1 + ahead, self.z_in.at[ahead - 1])
        self.add(self.result, self.second[self.deep], self.z_in[0], self.z_in[1], self.z_in[2])
        mine = self.total.at[self.chunk(self.deep)]
        for ahead in (2, 1, 3):
            self.send(4 + ahead, self.result, mine, self.to_z(ahead))
        self.kept = pltpu.make_async_copy(self.result, mine, self.sends.at[11])
        self.kept.start()

    def z_back(self):
        for ahead in (1, 2, 3):
            self.arrived(4 + ahead, self.total.at[self.chunk((self.deep + 4 - ahead) % 4)])
        self.kept.wait()
        part = self.total.at[pl.ds(self.chunk(0), 4)]
        self.send(8, part, part, self.to_y())

    def y_back(self):
        self.arrived(8, self.total.at[pl.ds(self.core * 8 + (1 - self.up) * 4, 4)])
        part = self.total.at[pl.ds(self.core * 8, 8)]
        self.send(9, part, part, self.to_core())

    def finish(self):
        self.arrived(9, self.total.at[pl.ds((1 - self.core) * 8, 8)])
        for copy in self.open:
            copy.wait_send()


def sum_scratch(tail, planes):
    shapes = [
        pltpu.SemaphoreType.DMA((SENDS,)),
        pltpu.SemaphoreType.DMA((SENDS,)),
        pltpu.VMEM(((2, 8) if planes else (8,)) + tail, BF),
        pltpu.VMEM((8,) + tail, BF),
        pltpu.VMEM((4,) + tail, BF),
        pltpu.VMEM((4,) + tail, BF),
        pltpu.VMEM((3,) + tail, BF),
        pltpu.VMEM(tail, BF),
    ]
    if planes:
        shapes += [pltpu.VMEM((8,) + tail, BF), pltpu.VMEM((2, 8) + tail, BF)]
    return shapes


def weight_back(grads, chunk_taps, col, turned):
    for tap in chunk_taps:
        result = mm(col[tap * 256 : (tap + 1) * 256, :], turned[:PIX, :])
        result = result + mm(col[(9 + tap) * 256 : (10 + tap) * 256, :], turned[PIX:, :])
        result = result.astype(BF)
        for part in range(16):
            grads[part, tap] = result[part * 16 : (part + 1) * 16]


PARTS = ((0, 2), (2, 4), (4, 6), (6, 8), (8, 9))
HALVES = ((0, 2), (2, 4))
def tail(
    squares, branch_own, branch_peer, second, second_peer, first, first_peer, grad_hidden,
    images, image_peer, stats0, par, grad_resid, w_own, w_peer, block, small1, small2, pre_embed, emb_weight,
    square_sum, sum1, sum0, images_grad, block_out, sums, emb_total, class_rows, class_ids,
    sems, sends, recvs, all_sends, all_recvs,
    grads1, grads0, col, turned, full, grad_first, resid_in, source_in, hidden_in,
    far, far_in, columns, flat, mod, mod_send, pres, rows_own, rows_in, total, total_in,
    *scratch,
):
    half = lax.axis_index("head")
    place, core, up, deep = position()
    to_x = {"head": 1 - half}
    others = [{"batch": (place + ahead) % 16} for ahead in range(1, 16)]
    meet([to_x] + others)
    near, away = rows(half * 256, 256), rows((1 - half) * 256, 256)
    exchanges = []

    def send(slot, source, dest, target):
        copy = remote(source, dest, sends, recvs, slot, target)
        copy.start()
        exchanges.append(copy)
        return copy

    chains = []
    for low, high in HALVES:
        where = pl.ds(low, high - low)
        chains.append(
            Sum(squares.at[:, :, :, where], square_sum.at[:, where], scratch[:10], True)
        )
        scratch = scratch[10:]
    for source, dest in ((grads1, sum1), (grads0, sum0)):
        for low, high in PARTS:
            where = pl.ds(low, high - low)
            chains.append(Sum(source.at[:, where], dest.at[:, where], scratch[:8], False))
            scratch = scratch[8:]
    done = [0] * len(chains)

    def advance(numbers):
        for number in numbers:
            if done[number] < len(chains[number].steps):
                chains[number].steps[done[number]]()
                done[number] += 1

    advance((0, 1))
    hidden_copy = send(0, grad_hidden.at[away], hidden_in, to_x)
    send(1, block.at[away], block_out.at[half], to_x)
    columns[...] = jnp.zeros_like(columns)
    columns[:, 2:7] = small1[...]
    columns[:, 7:11] = small2[...]
    flat[...] = columns[...].T[0:16]
    mod[place, half] = flat[2:4, near]
    mod_send[...] = flat[2:4, away]
    send(2, mod_send, mod.at[place, half], to_x)
    pres[place] = pre_embed[...]
    for ahead, target in enumerate(others):
        remote(pres.at[place], pres.at[place], all_sends, all_recvs, ahead, target).start()
    weights = fetch_conv(sems, full, half, 0, w_own, w_peer)
    inputs = (
        fetch(sems, 2, second, source_in.at[0]),
        fetch(sems, 3, second_peer, source_in.at[1]),
    )
    late = (fetch(sems, 4, grad_resid, resid_in),)
    kept = fetch(sems, 7, block.at[near], block_out.at[half])

    masks = edge_masks(-1)
    taps_of(col, masks, branch_own, 0, 256, 0, -1)
    taps_of(col.at[pl.ds(9 * 256, 9 * 256)], masks, branch_peer, 0, 256, 0, -1)
    wait(inputs)
    turned[:PIX, :] = source_in[0].T
    turned[PIX:, :] = source_in[1].T
    inputs = (
        fetch(sems, 2, first, source_in.at[0]),
        fetch(sems, 3, first_peer, source_in.at[1]),
    )
    for number, part in enumerate(PARTS):
        weight_back(grads1, range(*part), col, turned)
        advance((0, 1))
        advance(range(2, 3 + number))
    remote(mod_send, mod.at[place, 1 - half], sends, recvs, 2, to_x).wait_recv()
    for ahead, target in enumerate(others):
        remote(mod.at[place], mod.at[place], all_sends, all_recvs, 15 + ahead, target).start()
    advance(range(7))

    hidden_copy.wait_recv()
    taps_of(col, masks, grad_hidden.at[near], 0, 256, 0, -1)
    taps_of(col.at[pl.ds(9 * 256, 9 * 256)], masks, hidden_in, 0, 256, 0, -1)
    wait(inputs)
    turned[:PIX, :] = source_in[0].T
    turned[PIX:, :] = source_in[1].T
    picture = source_in.at[0]
    late += (
        fetch(sems, 5, images.at[half], picture.at[near]),
        fetch(sems, 6, image_peer, picture.at[away]),
    )
    advance(range(7))
    for number, part in enumerate(PARTS):
        weight_back(grads0, range(*part), col, turned)
        advance(range(8 + number))

    taps_of(col, masks, grad_hidden, 0, 512, 0, -1)
    wait(weights)
    advance(range(12))
    for column in range(0, PIX, 512):
        result = None
        for tap in range(9):
            term = mm(full[tap], col[tap * 512 : (tap + 1) * 512, column : column + 512], TN)
            result = term if result is None else result + term
        grad_first[:, column : column + 512] = result
        advance(range(12))
    wait(late)
    for base, mine in ((half * 256, True), ((1 - half) * 256, False)):

        def back(group, carry, base=base, mine=mine):
            here = rows(group * BLOCK, BLOCK)
            where = rows(base + group * BLOCK, BLOCK)
            unit = unit_of(picture[where, :].astype(F32), stats0, where)
            gain = par[where, GAIN : GAIN + 1]
            grad = grad_first[where, :] * silu_slope(unit * gain + par[where, BIAS : BIAS + 1])
            result = resid_in[where, :] + unit_back(grad * gain, unit, stats0[where, 1:2])
            if mine:
                images_grad[half, here, :] = result
            else:
                far[here, :] = result.astype(BF)
            columns[where, 0:1] = row_sum(grad * unit)
            columns[where, 1:2] = row_sum(grad)
            return carry

        lax.fori_loop(0, 256 // BLOCK, back, 0)
        advance(range(12))
    send(3, far, far_in, to_x)

    flat[...] = columns[...].T[0:16]
    total[0] = flat[:, away]
    send(4, total.at[0], total_in.at[0], to_x)

    for ahead in range(15):
        origin = (place + 15 - ahead) % 16
        remote(pres.at[origin], pres.at[origin], all_sends, all_recvs, ahead, to_x).wait_recv()
        remote(mod.at[origin], mod.at[origin], all_sends, all_recvs, 15 + ahead, to_x).wait_recv()
    width = emb_weight.shape[2]
    for slot in range(2):
        embed = jax.nn.silu(pres[:, slot, :width])
        result = None
        for which in range(2):
            factor = mod[:, slot, which, :]
            term = lax.dot_general(factor, embed, TN, precision=HIGH, preferred_element_type=F32)
            if slot == 0:
                emb_total[which] = term
            else:
                emb_total[which] += term
            dense = emb_weight[which].astype(F32)
            term = lax.dot_general(factor, dense, NN, precision=HIGH, preferred_element_type=F32)
            result = term if result is None else result + term
        rows_own[slot] = result
        class_ids[slot] = pres[:, slot, width:]
    send(5, rows_own, rows_in, to_x)
    advance(range(12))

    def gather_small(step, slot, target):
        remote(total.at[step], total_in.at[step], sends, recvs, slot, target).wait_recv()

    gather_small(0, 4, to_x)
    total[1] = flat[:, near] + total_in[0]
    send(6, total.at[1], total_in.at[1], {"batch": place + 1 - 2 * core})
    advance(range(12))
    gather_small(1, 6, to_x)
    total[2] = total[1] + total_in[1]
    send(7, total.at[2], total_in.at[2], {"batch": place + 2 * (1 - 2 * up)})
    advance(range(12))
    gather_small(2, 7, to_x)
    total[3] = total[2] + total_in[2]
    for ahead in (1, 2, 3):
        send(7 + ahead, total.at[3], total_in.at[3 + deep], {"batch": (deep + ahead) % 4 * 4 + place % 4})
    total_in[3 + deep] = total[3]
    advance(range(12))
    for ahead in (1, 2, 3):
        origin = (deep + 4 - ahead) % 4
        remote(total.at[3], total_in.at[3 + origin], sends, recvs, 7 + ahead, to_x).wait_recv()
    sums[...] = (total_in[3] + total_in[4]) + (total_in[5] + total_in[6])
    remote(rows_own, rows_in, sends, recvs, 5, to_x).wait_recv()
    for slot in range(2):
        class_rows[slot] = (rows_own[slot] + rows_in[slot]) * silu_slope(pres[:, slot, :width])
    remote(far, far_in, sends, recvs, 3, to_x).wait_recv()
    images_grad[1 - half] = far_in[...].astype(F32)
    for _ in range(10):
        advance(range(12))
    remote(block.at[away], block_out.at[1 - half], sends, recvs, 1, to_x).wait_recv()
    kept.wait()
    for copy in exchanges:
        copy.wait_send()
    for ahead, target in enumerate(others):
        remote(pres.at[place], pres.at[place], all_sends, all_recvs, ahead, target).wait_send()
        remote(mod.at[place], mod.at[place], all_sends, all_recvs, 15 + ahead, target).wait_send()


def tail_call(squares, *args):
    arrays, specs = operands((squares,) + args)
    scratch = [
        pltpu.SemaphoreType.DMA((8,)),
        pltpu.SemaphoreType.DMA((11,)),
        pltpu.SemaphoreType.DMA((11,)),
        pltpu.SemaphoreType.DMA((30,)),
        pltpu.SemaphoreType.DMA((30,)),
        pltpu.VMEM((16, 9, 16, 512), BF),
        pltpu.VMEM((16, 9, 16, 512), BF),
        pltpu.VMEM((9 * 512, PIX), BF),
        pltpu.VMEM((2 * PIX, 512), BF),
        pltpu.VMEM((9, 512, 512), BF),
        pltpu.VMEM((512, PIX), F32),
        pltpu.VMEM((512, PIX), F32),
        pltpu.VMEM((2, 512, PIX), BF),
        pltpu.VMEM((256, PIX), BF),
        pltpu.VMEM((256, PIX), BF),
        pltpu.VMEM((256, PIX), BF),
        pltpu.VMEM((512, 128), F32),
        pltpu.VMEM((16, 512), F32),
        pltpu.VMEM((16, 2, 2, 256), F32),
        pltpu.VMEM((2, 256), F32),
        pltpu.VMEM((16, 2, 1024 + 128), F32),
        pltpu.VMEM((2, 16, 1024), F32),
        pltpu.VMEM((2, 16, 1024), F32),
        pltpu.VMEM((4, 16, 256), F32),
        pltpu.VMEM((7, 16, 256), F32),
    ]
    for low, high in HALVES:
        scratch += sum_scratch((high - low, 16, 512), True)
    for low, high in PARTS * 2:
        scratch += sum_scratch((high - low, 16, 512), False)
    outs = [
        (out((16, 4, 16, 512), BF), ANYWHERE),
        (out((16, 9, 16, 512), BF), ANYWHERE),
        (out((16, 9, 16, 512), BF), ANYWHERE),
        (out((2, 256, PIX), F32), VMEM),
        (out((2, 256, PIX), BF), ANYWHERE),
        (out((16, 256), F32), VMEM),
        (out((2, 256, 1024), F32), VMEM),
        (out((2, 16, 1024), F32), VMEM),
        (out((2, 16, 128), F32), VMEM),
    ]
    return pl.pallas_call(
        tail,
        out_shape=[o for o, _ in outs],
        in_specs=specs,
        out_specs=[spec for _, spec in outs],
        scratch_shapes=scratch,
        cost_estimate=pl.CostEstimate(flops=2 * 10**10, bytes_accessed=200 * 2**20, transcendentals=0),
        compiler_params=pltpu.CompilerParams(
            collective_id=2, has_side_effects=True, vmem_limit_bytes=60 * 2**20
        ),
    )(*arrays)


def paired(
    images,
    timesteps,
    classes,
    live_count,
    norm_gain,
    norm_bias,
    conv_weight,
    conv_bias,
    emb_weight,
    emb_bias,
    class_table,
    qkv_weight,
    proj_weight,
    proj_bias,
    cotangent,
):
    half = lax.axis_index("head")

    def across(value):
        return lax.ppermute(value, "head", [(0, 1), (1, 0)])

    def pick(value, index):
        return lax.dynamic_index_in_dim(value, index, 0, keepdims=False)

    table_rows = jnp.stack([pick(class_table, classes[slot]) for slot in range(2)]).astype(F32)
    emb_width = class_table.shape[1]
    pre_embed = jnp.stack([features(timesteps[slot], emb_width) for slot in range(2)]) + table_rows
    params = jnp.concatenate([norm_gain, norm_bias, conv_bias, proj_bias[None]]).T
    par, image_peer, conv_peer, q_peer, p_peer = gather_call(
        pre_embed, params, emb_weight, emb_bias.T, images, conv_weight, qkv_weight, proj_weight
    )
    cot_peer = across(pick(cotangent, 1 - half))
    live = (half < live_count[0]).astype(jnp.int32)
    scalars = jnp.stack([half, 0 * half, live]).astype(jnp.int32)
    full_bf = out((512, PIX), BF)
    full_f32 = out((512, PIX), F32)
    stats = out((512, 2), F32)
    taps = pltpu.VMEM((9 * 512, PIX), BF)
    conv_full = pltpu.VMEM((9, 512, 512), BF)
    square = pltpu.VMEM((512, 512), BF)
    half_bf = pltpu.VMEM((256, PIX), BF)
    wide_bf = pltpu.VMEM((512, PIX), BF)
    wide_f32 = pltpu.VMEM((512, PIX), F32)
    pixels = pltpu.VMEM((PIX, PIX), BF)
    conv_flops = 2 * 9 * 512 * 512 * PIX
    conv_pair = (Far(conv_weight), Far(conv_peer))

    first, hidden, stats0, stats1, second = kernel_call(
        first_conv, [full_bf, full_f32, stats, stats, full_bf], [half_bf, taps, conv_full], conv_flops,
        scalars, Far(images), image_peer, par, *conv_pair,
    )
    resid, stats2, normed = kernel_call(
        second_conv, [full_f32, stats, full_bf], [half_bf, taps, conv_full], conv_flops,
        scalars, second, Far(images), image_peer, par, *conv_pair,
    )
    first_peer = across(first)
    second_peer = across(second)
    mixed, grad_q, grad_k, grad_v, grad_out, grad_resid, grad_branch, small2 = kernel_call(
        attention,
        [full_bf] * 5 + [full_f32, full_bf, out((512, 4), F32)],
        [pltpu.VMEM((3, 512, 512), BF), square] + [wide_bf] * 4 + [pixels] * 2 + [wide_f32] * 2,
        4 * conv_flops,
        scalars, normed, Far(resid), stats2, par, Far(cotangent), Far(cot_peer),
        Far(qkv_weight), Far(q_peer), Far(proj_weight), Far(p_peer),
    )
    pair = grad_branch.reshape(2, 256, PIX)
    branch_own, branch_peer = pick(pair, half), across(pick(pair, 1 - half))
    grad_hidden, small1 = kernel_call(
        second_back, [full_bf, out((512, 5), F32)], [taps, conv_full, wide_f32, wide_f32], conv_flops,
        scalars, grad_branch, Far(hidden), stats1, par, *conv_pair,
    )
    block, square_grads = kernel_call(
        projections, [full_bf, out((2, 2, 8, 4, 16, 512), BF)], [square], conv_flops // 2,
        scalars, normed, resid, par, mixed, grad_q, grad_k, grad_v, grad_out,
        Far(proj_weight), Far(p_peer),
    )
    ids = jnp.broadcast_to(classes.astype(F32)[:, None], (2, 128))
    square_sum, conv_sum1, conv_sum0, images_grad, block_out, sums, emb_total, class_rows, ids = tail_call(
        square_grads, branch_own, branch_peer, Far(second), Far(second_peer), Far(first), Far(first_peer),
        grad_hidden, Far(images), Far(image_peer), stats0, par, Far(grad_resid), *conv_pair, Far(block),
        small1, small2, jnp.concatenate([pre_embed, ids], 1), emb_weight,
    )

    def whole(value):
        return value.transpose(1, 0, 2, 3).reshape(value.shape[1], 256, 512).astype(F32)

    squares = whole(square_sum)
    ids = ids[:, :, 0].reshape(-1).astype(jnp.int32)
    chosen = (lax.iota(jnp.int32, class_table.shape[0])[:, None] == ids[None, :]).astype(F32)
    table_total = jnp.dot(chosen, class_rows.reshape(-1, emb_width), precision=HIGH)
    return (
        block_out,
        images_grad,
        jnp.stack([sums[0], sums[4], sums[7]]),
        jnp.stack([sums[1], sums[5], sums[8]]),
        jnp.stack([whole(conv_sum0), whole(conv_sum1)]),
        jnp.stack([sums[6], sums[9]]),
        emb_total,
        sums[2:4],
        table_total,
        squares[:3],
        squares[3],
        sums[10],
    )


def solution(mesh):
    in_specs = (
        P("batch", "head", None),
        P("batch"),
        P("batch"),
        P("batch"),
        P(None, "head"),
        P(None, "head"),
        P(None, None, "head", None),
        P(None, "head"),
        P(None, "head", None),
        P(None, "head"),
        P(),
        P(None, "head", None),
        P("head", None),
        P("head"),
        P("batch", "head", None),
    )
    out_specs = (
        P("batch", "head", None),
        P("batch", "head", None),
        P(None, "head"),
        P(None, "head"),
        P(None, None, "head", None),
        P(None, "head"),
        P(None, "head", None),
        P(None, "head"),
        P(),
        P(None, "head", None),
        P("head", None),
        P("head"),
    )
    body = shards
    if mesh.shape["head"] == 2 and mesh.shape["batch"] == 16:
        body = paired
    return jax.shard_map(body, mesh=mesh, in_specs=in_specs, out_specs=out_specs, check_vma=False)
```

```python
import math

import jax
import jax.numpy as jnp
from jax import lax
from jax.experimental import pallas as pl
from jax.experimental.pallas import tpu as pltpu
from jax.sharding import PartitionSpec as P

C = 512
GROUPS = 32
HEADS = 8
SIDE = 32


EPS = 1e-05
HIGH = lax.Precision.HIGHEST
CONTRACT_FIRST = (((0,), (0,)), ((), ()))
CONTRACT_LAST = (((1,), (1,)), ((), ()))


def silu_slope(values):
    sigma = jax.nn.sigmoid(values)
    return sigma * (1.0 + values * (1.0 - sigma))


def moved(source, grid_side, row_step, col_step):
    grid = source.reshape(source.shape[0], grid_side, grid_side)
    padded = jnp.pad(grid, ((0, 0), (1, 1), (1, 1)))
    window = padded[
        :, 1 + row_step : 1 + row_step + grid_side, 1 + col_step : 1 + col_step + grid_side
    ]
    return window.reshape(source.shape)


def group_unit(source, groups):
    grouped = source.reshape(groups, -1)
    centre = grouped - jnp.mean(grouped, axis=1, keepdims=True)
    inverse = lax.rsqrt(jnp.mean(jnp.square(centre), axis=1, keepdims=True) + EPS)
    return ((centre * inverse).reshape(source.shape), inverse)


def group_back(grad_unit, unit_rows, inverse, groups):
    flat_grad = grad_unit.reshape(groups, -1)
    flat_unit = unit_rows.reshape(groups, -1)
    result = flat_grad - jnp.mean(flat_grad, axis=1, keepdims=True)
    result = (result - flat_unit * jnp.mean(flat_grad * flat_unit, axis=1, keepdims=True)) * inverse
    return result.reshape(grad_unit.shape)


def conv_apply(weight, source, grid_side):
    result = jnp.dot(
        weight[0], moved(source, grid_side, -1, -1), preferred_element_type=jnp.float32
    )
    for tap_index in range(1, 9):
        result = result + jnp.dot(
            weight[tap_index],
            moved(source, grid_side, tap_index // 3 - 1, tap_index % 3 - 1),
            preferred_element_type=jnp.float32,
        )
    return result


def conv_transpose(weight, grads, grid_side):
    result = lax.dot_general(
        weight[0], moved(grads, grid_side, 1, 1), CONTRACT_FIRST, preferred_element_type=jnp.float32
    )
    for tap_index in range(1, 9):
        result = result + lax.dot_general(
            weight[tap_index],
            moved(grads, grid_side, 1 - tap_index // 3, 1 - tap_index % 3),
            CONTRACT_FIRST,
            preferred_element_type=jnp.float32,
        )
    return result


def conv_weight_grads(grads, source, grid_side):
    return jnp.stack(
        [
            lax.dot_general(
                grads,
                moved(source, grid_side, tap_index // 3 - 1, tap_index % 3 - 1),
                CONTRACT_LAST,
                preferred_element_type=jnp.float32,
            )
            for tap_index in range(9)
        ]
    )


def features(timestep, emb_width):
    half_width = emb_width // 2
    freqs = jnp.exp(-math.log(10000.0) * jnp.arange(half_width, dtype=jnp.float32) / half_width)
    angles = timestep.astype(jnp.float32) * freqs
    return jnp.concatenate([jnp.cos(angles), jnp.sin(angles)])


def shards(
    images,
    timesteps,
    classes,
    live_count,
    norm_gain,
    norm_bias,
    conv_weight,
    conv_bias,
    emb_weight,
    emb_bias,
    class_table,
    qkv_weight,
    proj_weight,
    proj_bias,
    cotangent,
):
    slot_count, chan_dev, pixel_count = images.shape
    grid_side = SIDE
    groups = chan_dev // (C // GROUPS)
    head_size = C // HEADS
    heads_dev = chan_dev // head_size
    att_scale = head_size ** (-0.5)
    emb_dense = emb_weight.astype(jnp.float32)
    class_total, emb_width = class_table.shape

    def gather_channels(rows_low):
        return lax.all_gather(rows_low, "head", axis=0, tiled=True)

    def input_grad(which_conv, grad_rows):
        weight_cols = conv_weight[which_conv]
        return lax.psum_scatter(
            conv_transpose(weight_cols, grad_rows, grid_side).astype(jnp.bfloat16),
            "head",
            scatter_dimension=0,
            tiled=True,
        ).astype(jnp.float32)

    def per_slot(slot_index, carry):
        (
            outputs,
            grads_in,
            gain_acc,
            bias_acc,
            convw_acc,
            convb_acc,
            embw_acc,
            embb_acc,
            table_acc,
            qkv_acc,
            projw_acc,
            projb_acc,
        ) = carry
        picture = lax.dynamic_index_in_dim(images, slot_index, 0, keepdims=False).astype(
            jnp.float32
        )
        live_flag = (slot_index < live_count[0]).astype(jnp.float32)
        class_id = classes[slot_index]
        table_row = lax.dynamic_index_in_dim(class_table, class_id, 0, keepdims=False).astype(
            jnp.float32
        )
        pre_embed = features(timesteps[slot_index], emb_width) + table_row
        embed = jax.nn.silu(pre_embed)
        scale = jnp.dot(emb_dense[0], embed, precision=HIGH) + emb_bias[0]
        shift = jnp.dot(emb_dense[1], embed, precision=HIGH) + emb_bias[1]
        unit_zero, inverse_zero = group_unit(picture, groups)
        pre_first = unit_zero * norm_gain[0][:, None] + norm_bias[0][:, None]
        first_full = gather_channels(jax.nn.silu(pre_first).astype(jnp.bfloat16))
        hidden = conv_apply(conv_weight[0], first_full, grid_side) + conv_bias[0][:, None]
        unit_one, inverse_one = group_unit(hidden, groups)
        normed_one = unit_one * norm_gain[1][:, None] + norm_bias[1][:, None]
        pre_second = normed_one * (1.0 + scale[:, None]) + shift[:, None]
        second_full = gather_channels(jax.nn.silu(pre_second).astype(jnp.bfloat16))
        resid = picture + conv_apply(conv_weight[1], second_full, grid_side) + conv_bias[1][:, None]
        unit_two, inverse_two = group_unit(resid, groups)
        normed_full = gather_channels(
            (unit_two * norm_gain[2][:, None] + norm_bias[2][:, None]).astype(jnp.bfloat16)
        )
        query = (
            jnp.dot(qkv_weight[0], normed_full, preferred_element_type=jnp.float32)
            .astype(jnp.bfloat16)
            .reshape(heads_dev, head_size, pixel_count)
        )
        keys = (
            jnp.dot(qkv_weight[1], normed_full, preferred_element_type=jnp.float32)
            .astype(jnp.bfloat16)
            .reshape(heads_dev, head_size, pixel_count)
        )
        values = (
            jnp.dot(qkv_weight[2], normed_full, preferred_element_type=jnp.float32)
            .astype(jnp.bfloat16)
            .reshape(heads_dev, head_size, pixel_count)
        )
        scores = (
            jnp.einsum("hdi,hdj->hij", query, keys, preferred_element_type=jnp.float32) * att_scale
        )
        highest = jnp.max(scores, axis=2, keepdims=True)
        expo = jnp.exp(scores - highest)
        totals = jnp.sum(expo, axis=2, keepdims=True)
        log_total = highest + jnp.log(totals)
        weights = (expo / totals).astype(jnp.bfloat16)
        mixed = (
            jnp.einsum("hdj,hij->hdi", values, weights, preferred_element_type=jnp.float32)
            .astype(jnp.bfloat16)
            .reshape(chan_dev, pixel_count)
        )
        weight_cols = proj_weight
        proj_term = lax.psum_scatter(
            lax.dot_general(
                weight_cols, mixed, CONTRACT_FIRST, preferred_element_type=jnp.float32
            ).astype(jnp.bfloat16),
            "head",
            scatter_dimension=0,
            tiled=True,
        ).astype(jnp.float32)
        result = resid + proj_term + proj_bias[:, None]
        outputs = lax.dynamic_update_index_in_dim(
            outputs, (live_flag * result).astype(jnp.bfloat16), slot_index, 0
        )
        grad_low = lax.dynamic_index_in_dim(cotangent, slot_index, 0, keepdims=False)
        grad_out = live_flag * grad_low.astype(jnp.float32)
        grad_full = lax.all_gather(grad_low, "head", axis=0, tiled=True) * live_flag.astype(
            jnp.bfloat16
        )
        grad_mixed = jnp.dot(proj_weight, grad_full, preferred_element_type=jnp.float32).astype(
            jnp.bfloat16
        )
        projw_acc = projw_acc + lax.dot_general(
            mixed, grad_full, CONTRACT_LAST, preferred_element_type=jnp.float32
        )
        projb_acc = projb_acc + jnp.sum(grad_out, axis=1)
        again = (
            jnp.einsum("hdi,hdj->hij", query, keys, preferred_element_type=jnp.float32) * att_scale
        )
        probs = jnp.exp(again - log_total)
        grad_heads = grad_mixed.reshape(heads_dev, head_size, pixel_count)
        grad_probs = jnp.einsum(
            "hdi,hdj->hij", grad_heads, values, preferred_element_type=jnp.float32
        )
        grad_scores = (
            probs * (grad_probs - jnp.sum(grad_probs * probs, axis=2, keepdims=True))
        ).astype(jnp.bfloat16)
        grad_query = (
            jnp.einsum("hij,hdj->hdi", grad_scores, keys, preferred_element_type=jnp.float32)
            * att_scale
        ).astype(jnp.bfloat16)
        grad_keys = (
            jnp.einsum("hij,hdi->hdj", grad_scores, query, preferred_element_type=jnp.float32)
            * att_scale
        ).astype(jnp.bfloat16)
        grad_values = jnp.einsum(
            "hdi,hij->hdj", grad_heads, weights, preferred_element_type=jnp.float32
        ).astype(jnp.bfloat16)
        stacked = jnp.stack([grad_query, grad_keys, grad_values]).reshape(3, chan_dev, pixel_count)
        weight_cols = qkv_weight
        grad_normed = lax.psum_scatter(
            lax.dot_general(
                weight_cols,
                stacked,
                (((0, 1), (0, 1)), ((), ())),
                preferred_element_type=jnp.float32,
            ).astype(jnp.bfloat16),
            "head",
            scatter_dimension=0,
            tiled=True,
        ).astype(jnp.float32)
        qkv_acc = qkv_acc + lax.dot_general(
            stacked, normed_full, (((2,), (1,)), ((), ())), preferred_element_type=jnp.float32
        )
        grad_resid = grad_out + group_back(
            grad_normed * norm_gain[2][:, None], unit_two, inverse_two, groups
        )
        grad_branch = grad_resid.astype(jnp.bfloat16)
        grad_second = input_grad(1, grad_branch)
        grad_pre = grad_second * silu_slope(pre_second)
        scale_grad = jnp.sum(grad_pre * normed_one, axis=1)
        shift_grad = jnp.sum(grad_pre, axis=1)
        grad_normed_one = grad_pre * (1.0 + scale[:, None])
        grad_hidden = group_back(
            grad_normed_one * norm_gain[1][:, None], unit_one, inverse_one, groups
        ).astype(jnp.bfloat16)
        grad_first = input_grad(0, grad_hidden)
        grad_pre_first = grad_first * silu_slope(pre_first)
        picture_grad = grad_resid + group_back(
            grad_pre_first * norm_gain[0][:, None], unit_zero, inverse_zero, groups
        )
        grads_in = lax.dynamic_update_index_in_dim(grads_in, picture_grad, slot_index, 0)
        gain_acc = gain_acc + jnp.stack(
            [
                jnp.sum(grad_pre_first * unit_zero, axis=1),
                jnp.sum(grad_normed_one * unit_one, axis=1),
                jnp.sum(grad_normed * unit_two, axis=1),
            ]
        )
        bias_acc = bias_acc + jnp.stack(
            [
                jnp.sum(grad_pre_first, axis=1),
                jnp.sum(grad_normed_one, axis=1),
                jnp.sum(grad_normed, axis=1),
            ]
        )
        convw_acc = convw_acc + jnp.stack(
            [
                conv_weight_grads(grad_hidden, first_full, grid_side),
                conv_weight_grads(grad_branch, second_full, grid_side),
            ]
        )
        convb_acc = convb_acc + jnp.stack(
            [
                jnp.sum(grad_hidden.astype(jnp.float32), axis=1),
                jnp.sum(grad_branch.astype(jnp.float32), axis=1),
            ]
        )
        embw_acc = embw_acc + jnp.stack(
            [scale_grad[:, None] * embed[None, :], shift_grad[:, None] * embed[None, :]]
        )
        embb_acc = embb_acc + jnp.stack([scale_grad, shift_grad])
        grad_embed = jnp.dot(scale_grad, emb_dense[0], precision=HIGH) + jnp.dot(
            shift_grad, emb_dense[1], precision=HIGH
        )
        class_row = grad_embed * silu_slope(pre_embed)
        old_row = lax.dynamic_index_in_dim(table_acc, class_id, 0, keepdims=True)
        table_acc = lax.dynamic_update_index_in_dim(
            table_acc, old_row + class_row[None, :], class_id, 0
        )
        return (
            outputs,
            grads_in,
            gain_acc,
            bias_acc,
            convw_acc,
            convb_acc,
            embw_acc,
            embb_acc,
            table_acc,
            qkv_acc,
            projw_acc,
            projb_acc,
        )

    table_start = jnp.zeros(class_table.shape, jnp.float32)
    initial = (
        jnp.zeros(images.shape, jnp.bfloat16),
        jnp.zeros(images.shape, jnp.float32),
        jnp.zeros(norm_gain.shape, jnp.float32),
        jnp.zeros(norm_bias.shape, jnp.float32),
        jnp.zeros(conv_weight.shape, jnp.float32),
        jnp.zeros(conv_bias.shape, jnp.float32),
        jnp.zeros(emb_weight.shape, jnp.float32),
        jnp.zeros(emb_bias.shape, jnp.float32),
        table_start,
        jnp.zeros(qkv_weight.shape, jnp.float32),
        jnp.zeros(proj_weight.shape, jnp.float32),
        jnp.zeros(proj_bias.shape, jnp.float32),
    )
    final = lax.fori_loop(0, slot_count, per_slot, initial)
    (
        outputs,
        grads_in,
        gain_acc,
        bias_acc,
        convw_acc,
        convb_acc,
        embw_acc,
        embb_acc,
        table_acc,
        qkv_acc,
        projw_acc,
        projb_acc,
    ) = final
    table_total = lax.psum(table_acc, ("batch", "head"))
    summed = (
        lax.psum(gain_acc.astype(jnp.bfloat16), "batch").astype(jnp.float32),
        lax.psum(bias_acc.astype(jnp.bfloat16), "batch").astype(jnp.float32),
        lax.psum(convw_acc.astype(jnp.bfloat16), "batch").astype(jnp.float32),
        lax.psum(convb_acc.astype(jnp.bfloat16), "batch").astype(jnp.float32),
        lax.psum(embw_acc.astype(jnp.bfloat16), "batch").astype(jnp.float32),
        lax.psum(embb_acc.astype(jnp.bfloat16), "batch").astype(jnp.float32),
        lax.psum(qkv_acc.astype(jnp.bfloat16), "batch").astype(jnp.float32),
        lax.psum(projw_acc.astype(jnp.bfloat16), "batch").astype(jnp.float32),
        lax.psum(projb_acc.astype(jnp.bfloat16), "batch").astype(jnp.float32),
    )
    return (
        outputs,
        grads_in,
        summed[0],
        summed[1],
        summed[2],
        summed[3],
        summed[4],
        summed[5],
        table_total,
        summed[6],
        summed[7],
        summed[8],
    )


PIX = 1024
BLOCK = 128
BF = jnp.bfloat16
F32 = jnp.float32
NN = (((1,), (0,)), ((), ()))
TN = (((0,), (0,)), ((), ()))
NT = (((1,), (1,)), ((), ()))
VMEM = pl.BlockSpec(memory_space=pltpu.VMEM)
SMEM = pl.BlockSpec(memory_space=pltpu.SMEM)

GAIN, BIAS, CONVB, PROJB, SCALE, SHIFT = 0, 3, 6, 8, 9, 10


def mm(left, right, dims=NN):
    return lax.dot_general(left, right, dims, preferred_element_type=F32)


class Far:
    def __init__(self, array):
        self.array = array


ANYWHERE = pl.BlockSpec(memory_space=pl.ANY)


def operands(args):
    arrays = [arg.array if isinstance(arg, Far) else arg for arg in args]
    specs = [ANYWHERE if isinstance(arg, Far) else VMEM for arg in args]
    return arrays, specs


def kernel_call(kernel, outs, scratch, flops, scalars, *args):
    arrays, specs = operands(args)
    moved_bytes = sum(a.size * a.dtype.itemsize for a in arrays)
    moved_bytes += sum(math.prod(o.shape) * o.dtype.itemsize for o in outs)
    return pl.pallas_call(
        kernel,
        out_shape=outs,
        in_specs=[SMEM] + specs,
        out_specs=[VMEM] * len(outs),
        scratch_shapes=[pltpu.SemaphoreType.DMA((8,))] + scratch,
        cost_estimate=pl.CostEstimate(flops=flops, bytes_accessed=moved_bytes, transcendentals=0),
        compiler_params=pltpu.CompilerParams(vmem_limit_bytes=56 * 2**20),
    )(scalars, *arrays)


def fetch(sems, slot, source, dest):
    copy = pltpu.make_async_copy(source, dest, sems.at[slot])
    copy.start()
    return copy


def out(shape, dtype):
    return jax.ShapeDtypeStruct(shape, dtype)


def rows(start, count):
    return pl.ds(pl.multiple_of(start, count), count)


def edge_masks(sign):
    pixel = lax.broadcasted_iota(jnp.int32, (1, PIX), 1)
    col, row = pixel % SIDE, pixel // SIDE
    table = {}
    for step in (-1, 1):
        moved_step = sign * step
        table["col", step] = ((col + moved_step >= 0) & (col + moved_step < SIDE)).astype(F32)
        table["row", step] = ((row + moved_step >= 0) & (row + moved_step < SIDE)).astype(F32)
    return table


def put_taps(dest, masks, values, first_row, depth, base, sign):
    count = values.shape[0]
    for col_step in (-1, 0, 1):
        across = values
        if col_step:
            across = pltpu.roll(values, (-sign * col_step) % PIX, 1) * masks["col", col_step]
        for row_step in (-1, 0, 1):
            copy = across
            if row_step:
                copy = pltpu.roll(across, (-sign * row_step * SIDE) % PIX, 1) * masks["row", row_step]
            tap = 3 * (row_step + 1) + col_step + 1
            dest[rows(tap * depth + first_row, count), base : base + PIX] = copy.astype(BF)


def taps_of(dest, masks, source, offset, depth, base, sign):
    for start in range(0, source.shape[0], 128):
        piece = source[start : start + 128, :].astype(F32)
        put_taps(dest, masks, piece, offset + start, depth, base, sign)


def fetch_conv(sems, full, half, which, own, peer):
    return (
        fetch(sems, 0, own.at[which], full.at[:, rows(half * 256, 256), :]),
        fetch(sems, 1, peer.at[which], full.at[:, rows((1 - half) * 256, 256), :]),
    )


def wait(copies):
    for copy in copies:
        copy.wait()


def conv_dots(dest, full, col, dims, finish):
    for column in range(0, PIX, 512):
        total = None
        for tap in range(9):
            term = mm(full[tap], col[tap * 512 : (tap + 1) * 512, column : column + 512], dims)
            total = term if total is None else total + term
        dest[:, column : column + 512] = finish(total, column)


def grouped(block):
    return block.reshape((-1, 16) + block.shape[1:])


def group_mean(block):
    return jnp.sum(block, axis=(1, 2), keepdims=True) * (1.0 / (16 * PIX))


def group_stats(block, stats, where):
    parts = grouped(block)
    centre = group_mean(parts)
    parts = parts - centre
    inverse = lax.rsqrt(group_mean(jnp.square(parts)) + EPS)
    count = block.shape[0]
    stats[where, 0:1] = jnp.broadcast_to(centre, (count // 16, 16, 1)).reshape(count, 1)
    stats[where, 1:2] = jnp.broadcast_to(inverse, (count // 16, 16, 1)).reshape(count, 1)
    return (parts * inverse).reshape(block.shape)


def unit_of(block, stats, where):
    return (block - stats[where, 0:1]) * stats[where, 1:2]


def unit_back(grad, unit, inverse):
    parts, units = grouped(grad), grouped(unit)
    result = parts - group_mean(parts) - units * group_mean(parts * units)
    return result.reshape(grad.shape) * inverse


def row_sum(block):
    return jnp.sum(block, axis=1, keepdims=True)


def first_conv(
    index, images, peer, par, w_own, w_peer, first, hidden, stats0, stats1, second, sems, own, col, full
):
    half = index[0]
    picture = fetch(sems, 2, images.at[half], own)
    arriving = fetch_conv(sems, full, half, 0, w_own, w_peer)
    picture.wait()
    masks = edge_masks(1)
    for source, base in ((own, half * 256), (peer, (1 - half) * 256)):

        def norm(group, carry, source=source, base=base):
            where = rows(base + group * BLOCK, BLOCK)
            unit = group_stats(source[rows(group * BLOCK, BLOCK), :].astype(F32), stats0, where)
            low = jax.nn.silu(unit * par[where, GAIN : GAIN + 1] + par[where, BIAS : BIAS + 1]).astype(BF)
            first[where, :] = low
            put_taps(col, masks, low.astype(F32), base + group * BLOCK, 512, 0, 1)
            return carry

        lax.fori_loop(0, 256 // BLOCK, norm, 0)
    wait(arriving)
    conv_dots(hidden, full, col, NN, lambda total, column: total + par[:, CONVB : CONVB + 1])

    def again(group, carry):
        where = rows(group * BLOCK, BLOCK)
        unit = group_stats(hidden[where, :], stats1, where)
        normed = unit * par[where, GAIN + 1 : GAIN + 2] + par[where, BIAS + 1 : BIAS + 2]
        pre = normed * (1.0 + par[where, SCALE : SCALE + 1]) + par[where, SHIFT : SHIFT + 1]
        second[where, :] = jax.nn.silu(pre).astype(BF)
        return carry

    lax.fori_loop(0, 512 // BLOCK, again, 0)


def second_conv(
    index, source, images, peer, par, w_own, w_peer, resid, stats2, normed, sems, own, col, full
):
    half = index[0]
    arriving = fetch_conv(sems, full, half, 1, w_own, w_peer)
    picture = fetch(sems, 2, images.at[half], own)
    taps_of(col, edge_masks(1), source, 0, 512, 0, 1)
    wait(arriving)
    conv_dots(resid, full, col, NN, lambda total, column: total + par[:, CONVB + 1 : CONVB + 2])
    picture.wait()
    for picture, base in ((own, half * 256), (peer, (1 - half) * 256)):

        def norm(group, carry, picture=picture, base=base):
            where = rows(base + group * BLOCK, BLOCK)
            block = resid[where, :] + picture[rows(group * BLOCK, BLOCK), :].astype(F32)
            resid[where, :] = block
            unit = group_stats(block, stats2, where)
            normed[where, :] = (unit * par[where, GAIN + 2 : GAIN + 3] + par[where, BIAS + 2 : BIAS + 3]).astype(BF)
            return carry

        lax.fori_loop(0, 256 // BLOCK, norm, 0)


def fetch_square(sems, slot, full, half, own, peer):
    count = own.shape[-2]
    near, far = rows(half * count, count), rows((1 - half) * count, count)
    if len(full.shape) == 3:
        near, far = (slice(None), near), (slice(None), far)
    return fetch(sems, slot, own, full.at[near]), fetch(sems, slot + 1, peer, full.at[far])


def attention(
    index, normed, resid, stats2, par, cotangent, cot_peer, q_own, q_peer, p_own, p_peer,
    mixed, grad_q, grad_k, grad_v, grad_out, grad_resid, grad_branch, small,
    sems, wqkv, wp, query, keys, values, grad_mixed, weights, grad_scores, grad_normed, resid_in,
):
    half = index[0]
    live = index[2].astype(BF)
    arriving = fetch_square(sems, 0, wqkv, half, q_own, q_peer)
    later = fetch_square(sems, 2, wp, half, p_own, p_peer)
    later += (
        fetch(sems, 4, cotangent.at[half], grad_out.at[rows(half * 256, 256)]),
        fetch(sems, 5, cot_peer, grad_out.at[rows((1 - half) * 256, 256)]),
    )
    last = fetch(sems, 6, resid, resid_in)
    wait(arriving)
    for column in range(0, PIX, 512):
        where = slice(column, column + 512)
        query[:, where] = (mm(wqkv[0], normed[:, where]).astype(BF).astype(F32) * 0.125).astype(BF)
        keys[:, where] = mm(wqkv[1], normed[:, where]).astype(BF)
        values[:, where] = mm(wqkv[2], normed[:, where]).astype(BF)
    wait(later)
    grad_out[...] = grad_out[...] * live
    for column in range(0, PIX, 512):
        where = slice(column, column + 512)
        grad_mixed[:, where] = mm(wp[...], grad_out[:, where]).astype(BF)

    def head(number, carry):
        where = rows(number * 64, 64)
        q, k, v, g = query[where, :], keys[where, :], values[where, :], grad_mixed[where, :]
        scores = mm(k.T, q)
        expo = jnp.exp(scores - jnp.max(scores, axis=0, keepdims=True))
        low = (expo * (1.0 / jnp.sum(expo, axis=0, keepdims=True))).astype(BF)
        weights[...] = low
        mix = mm(v, low)
        mixed[where, :] = mix.astype(BF)
        delta = jnp.sum(mix * g.astype(F32), axis=0, keepdims=True)
        inner = (low.astype(F32) * (mm(v.T, g) - delta)).astype(BF)
        grad_scores[...] = inner
        grad_q[where, :] = (mm(k, inner) * 0.125).astype(BF)
        grad_k[where, :] = mm(grad_scores[...], q.T).T.astype(BF)
        grad_v[where, :] = mm(weights[...], g.T).T.astype(BF)
        return carry

    lax.fori_loop(0, HEADS, head, 0)
    for column in range(0, PIX, 512):
        where = slice(column, column + 512)
        grad_normed[:, where] = (
            mm(wqkv[0], grad_q[:, where], TN)
            + mm(wqkv[1], grad_k[:, where], TN)
            + mm(wqkv[2], grad_v[:, where], TN)
        )
    last.wait()

    def back(group, carry):
        where = rows(group * BLOCK, BLOCK)
        unit = unit_of(resid_in[where, :], stats2, where)
        grad = grad_normed[where, :]
        outer = grad_out[where, :].astype(F32)
        total = outer + unit_back(grad * par[where, GAIN + 2 : GAIN + 3], unit, stats2[where, 1:2])
        low = total.astype(BF)
        grad_resid[where, :] = total
        grad_branch[where, :] = low
        small[where, 0:1] = row_sum(grad * unit)
        small[where, 1:2] = row_sum(grad)
        small[where, 2:3] = row_sum(low.astype(F32))
        small[where, 3:4] = row_sum(outer)
        return carry

    lax.fori_loop(0, 512 // BLOCK, back, 0)


def remote(source, dest, sends, recvs, slot, target):
    return pltpu.make_async_remote_copy(
        src_ref=source,
        dst_ref=dest,
        send_sem=sends.at[slot],
        recv_sem=recvs.at[slot],
        device_id=target,
        device_id_type=pl.DeviceIdType.MESH,
    )


def meet(targets):
    barrier = pltpu.get_barrier_semaphore()
    for target in targets:
        pl.semaphore_signal(barrier, inc=1, device_id=target, device_id_type=pl.DeviceIdType.MESH)
    pl.semaphore_wait(barrier, len(targets))


def position():
    place = lax.axis_index("batch")
    return place, place % 2, (place // 2) % 2, place // 4


PIECES = 6
KINDS = 10


def gather(
    pre_embed, params, emb_weight, emb_bias, images, conv_weight, qkv_weight, proj_weight,
    par, image_peer, conv_peer, qkv_peer, proj_peer,
    par_send, par_recv, sends, recvs, few_sends, few_recvs,
):
    half = lax.axis_index("head")
    place, core, up, deep = position()
    z_low = deep % 2
    to_x = {"head": 1 - half}
    to_y = {"batch": place + 2 * (1 - 2 * up)}
    to_z = {"batch": place + 4 * (1 - 2 * z_low)}
    to_core = {"batch": place + (1 - 2 * core)}
    meet([to_x, to_y, to_z, to_core])

    def block(flip_core=0, flip_y=0, flip_z=0):
        c = 1 - core if flip_core else core
        y = 1 - up if flip_y else up
        z = 1 - z_low if flip_z else z_low
        return (c + 2 * y + 4 * z) * 32

    def views(piece, near, start, count):
        where = rows(start, count)
        if piece < 4:
            taps = pl.ds(0, 5) if piece % 2 == 0 else pl.ds(5, 4)
            return (conv_weight if near else conv_peer).at[piece // 2, taps, where, :]
        if piece == 4:
            return (qkv_weight if near else qkv_peer).at[:, where, :]
        return (proj_weight if near else proj_peer).at[where, :]

    def copy(piece, kind, start, count, target, near=False):
        return remote(
            views(piece, near, start, count), views(piece, False, start, count),
            sends.at[piece], recvs.at[piece], kind, target,
        )

    def regions(flip_core):
        return (
            (block(flip_core), 32),
            (block(flip_core, 1), 32),
            (block(flip_core, 0, 1), 32),
            (block(flip_core, 1, 1), 16),
            (block(flip_core, 1, 1) + 16, 16),
        )

    mine, others = regions(0), regions(1)

    def arrived(piece, kind):
        start, count = mine[kind] if kind < 5 else others[kind - 5]
        copy(piece, kind, start, count, to_core).wait_recv()

    def over_x(piece):
        arrived(piece, 0)
        for kind, target in ((1, to_y), (2, to_z), (5, to_core)):
            copy(piece, kind, block(), 32, target).start()

    def over_yz(piece):
        arrived(piece, 2)
        copy(piece, 3, block(0, 0, 1), 16, to_y).start()
        copy(piece, 7, block(0, 0, 1), 32, to_core).start()
        arrived(piece, 1)
        copy(piece, 4, block(0, 1, 0) + 16, 16, to_z).start()
        copy(piece, 6, block(0, 1, 0), 32, to_core).start()

    def diagonal(piece):
        arrived(piece, 3)
        copy(piece, 8, block(0, 1, 1), 16, to_core).start()
        arrived(piece, 4)
        copy(piece, 9, block(0, 1, 1) + 16, 16, to_core).start()

    for piece in range(PIECES):
        copy(piece, 0, block(), 32, to_x, near=True).start()
    picture = remote(images.at[1 - half], image_peer, few_sends, few_recvs, 0, to_x)
    picture.start()
    embed = jax.nn.silu(pre_embed[...])
    own_row = jnp.where(half == 0, embed[0:1], embed[1:2])
    peer_row = jnp.where(half == 0, embed[1:2], embed[0:1])
    near = rows(half * 256, 256)
    par[near, 0:9] = params[...]
    par_send[:, 0:9] = params[...]
    for which in range(2):
        dense = emb_weight[which].astype(F32)
        offset = emb_bias[:, which : which + 1]
        par[near, SCALE + which : SCALE + which + 1] = row_sum(dense * own_row) + offset
        par_send[:, SCALE + which : SCALE + which + 1] = row_sum(dense * peer_row) + offset
    block_copy = remote(par_send, par_recv, few_sends, few_recvs, 1, to_x)
    block_copy.start()

    over_x(0)
    over_x(1)
    over_yz(0)
    over_x(2)
    over_yz(1)
    diagonal(0)
    over_x(3)
    over_yz(2)
    diagonal(1)
    over_x(4)
    over_x(5)
    over_yz(3)
    diagonal(2)
    over_yz(4)
    over_yz(5)
    diagonal(3)
    diagonal(4)
    diagonal(5)
    block_copy.wait_recv()
    par[rows((1 - half) * 256, 256), :] = par_recv[:, 0:11]
    picture.wait_recv()
    for piece in range(PIECES):
        for kind in range(5, 10):
            arrived(piece, kind)
    for piece in range(PIECES):
        copy(piece, 0, block(), 32, to_x).wait_send()
        for kind, start, count in (
            (1, block(), 32), (2, block(), 32), (5, block(), 32),
            (3, block(0, 0, 1), 16), (7, block(0, 0, 1), 32),
            (4, block(0, 1, 0) + 16, 16), (6, block(0, 1, 0), 32),
            (8, block(0, 1, 1), 16), (9, block(0, 1, 1) + 16, 16),
        ):
            copy(piece, kind, start, count, to_x).wait_send()
    picture.wait_send()
    block_copy.wait_send()


def gather_call(pre_embed, params, emb_weight, emb_bias, images, conv_weight, qkv_weight, proj_weight):
    return pl.pallas_call(
        gather,
        out_shape=[
            out((512, 11), F32),
            out(images.shape[1:], BF),
            out(conv_weight.shape, BF),
            out(qkv_weight.shape, BF),
            out(proj_weight.shape, BF),
        ],
        in_specs=[VMEM] * 4 + [ANYWHERE] * 4,
        out_specs=[VMEM] + [ANYWHERE] * 4,
        scratch_shapes=[
            pltpu.VMEM((256, 128), F32),
            pltpu.VMEM((256, 128), F32),
            pltpu.SemaphoreType.DMA((PIECES, KINDS)),
            pltpu.SemaphoreType.DMA((PIECES, KINDS)),
            pltpu.SemaphoreType.DMA((2,)),
            pltpu.SemaphoreType.DMA((2,)),
        ],
        cost_estimate=pl.CostEstimate(flops=0, bytes_accessed=100 * 2**20, transcendentals=0),
        compiler_params=pltpu.CompilerParams(
            collective_id=1, has_side_effects=True, vmem_limit_bytes=24 * 2**20
        ),
    )(pre_embed, params, emb_weight, emb_bias, images, conv_weight, qkv_weight, proj_weight)


SENDS = 12


class Sum:
    def __init__(self, source, total, scratch, planes):
        self.source, self.total, self.planes = source, total, planes
        self.sends, self.recvs, self.core_in, self.first, self.y_in, self.second, self.z_in, self.result = scratch[:8]
        if planes:
            self.middle, self.x_in = scratch[8:10]
        self.half = lax.axis_index("head")
        self.place, self.core, self.up, self.deep = position()
        self.steps = [self.start, self.core_done, self.y_done, self.z_done]
        if planes:
            self.steps.append(self.x_done)
        self.steps += [self.z_back, self.y_back, self.finish]
        self.open = []
        self.count = 0

    def advance(self):
        if self.count < len(self.steps):
            self.steps[self.count]()
            self.count += 1

    def part(self, array, start, count):
        where = pl.ds(start, count)
        return array.at[:, where] if self.planes else array.at[where]

    def to_core(self):
        return {"batch": self.place + 1 - 2 * self.core}

    def to_y(self):
        return {"batch": self.place + 2 * (1 - 2 * self.up)}

    def to_z(self, ahead):
        return {"batch": (self.deep + ahead) % 4 * 4 + self.place % 4}

    def send(self, slot, source, dest, target):
        copy = remote(source, dest, self.sends, self.recvs, slot, target)
        copy.start()
        self.open.append(copy)

    def arrived(self, slot, dest):
        remote(dest, dest, self.sends, self.recvs, slot, self.to_core()).wait_recv()

    def of_core(self, core):
        return self.source.at[core] if self.planes else self.source.at[pl.ds(core * 8, 8)]

    def start(self):
        self.send(0, self.of_core(1 - self.core), self.core_in, self.to_core())

    def add(self, dest, left, *right):
        total = left[...].astype(F32)
        for term in right:
            total = total + term[...].astype(F32)
        dest[...] = total.astype(BF)

    def core_done(self):
        self.arrived(0, self.core_in)
        self.add(self.first, self.of_core(self.core), self.core_in)
        self.send(1, self.part(self.first, (1 - self.up) * 4, 4), self.y_in, self.to_y())

    def y_done(self):
        self.arrived(1, self.y_in)
        self.add(self.second, self.part(self.first, self.up * 4, 4), self.y_in)
        for ahead in (2, 1, 3):
            chunk = self.part(self.second, (self.deep + ahead) % 4, 1)
            self.send(1 + ahead, chunk, self.z_in.at[ahead - 1], self.to_z(ahead))

    def z_done(self):
        for ahead in (1, 2, 3):
            self.arrived(1 + ahead, self.z_in.at[ahead - 1])
        mine = self.part(self.second, self.deep, 1)
        terms = [self.z_in.at[number] for number in range(3)]
        if self.planes:
            self.add(self.middle, mine, *terms)
            self.send(10, self.middle.at[1 - self.half], self.x_in, {"head": 1 - self.half})
        else:
            self.add(self.result, mine, *terms)
            self.give()

    def x_done(self):
        self.arrived(10, self.x_in)
        self.add(self.result, self.middle.at[self.half], self.x_in)
        self.give()

    def chunks(self, start, count):
        return self.total.at[pl.ds(start, count)]

    def chunk(self, deep):
        return self.core * 8 + self.up * 4 + deep

    def give(self):
        mine = self.chunks(self.chunk(self.deep), 1)
        for ahead in (2, 1, 3):
            self.send(4 + ahead, self.result, mine, self.to_z(ahead))
        self.kept = pltpu.make_async_copy(self.result, mine, self.sends.at[11])
        self.kept.start()

    def z_back(self):
        for ahead in (1, 2, 3):
            self.arrived(4 + ahead, self.chunks(self.chunk((self.deep + 4 - ahead) % 4), 1))
        self.kept.wait()
        part = self.chunks(self.chunk(0), 4)
        self.send(8, part, part, self.to_y())

    def y_back(self):
        self.arrived(8, self.chunks(self.core * 8 + (1 - self.up) * 4, 4))
        part = self.chunks(self.core * 8, 8)
        self.send(9, part, part, self.to_core())

    def finish(self):
        self.arrived(9, self.chunks((1 - self.core) * 8, 8))
        for copy in self.open:
            copy.wait_send()


def sum_scratch(tail, planes):
    lead = (2,) if planes else ()
    shapes = [
        pltpu.SemaphoreType.DMA((SENDS,)),
        pltpu.SemaphoreType.DMA((SENDS,)),
        pltpu.VMEM(lead + (8,) + tail, BF),
        pltpu.VMEM(lead + (8,) + tail, BF),
        pltpu.VMEM(lead + (4,) + tail, BF),
        pltpu.VMEM(lead + (4,) + tail, BF),
        pltpu.VMEM((3,) + lead + (1,) + tail, BF),
        pltpu.VMEM((1,) + tail, BF),
    ]
    if planes:
        shapes += [pltpu.VMEM((2, 1) + tail, BF), pltpu.VMEM((1,) + tail, BF)]
    return shapes


def weight_back(grads, chunk_taps, col, turned):
    for tap in chunk_taps:
        result = mm(col[tap * 256 : (tap + 1) * 256, :], turned[:PIX, :])
        result = result + mm(col[(9 + tap) * 256 : (10 + tap) * 256, :], turned[PIX:, :])
        result = result.astype(BF)
        for part in range(16):
            grads[part, tap] = result[part * 16 : (part + 1) * 16]


PARTS = ((0, 3), (3, 6), (6, 9))


def backward(
    grad_branch, normed, grad_q, grad_k, grad_v, mixed, grad_out, resid, hidden, second, second_peer,
    first, first_peer, grad_resid, images, image_peer, w_own, w_peer, p_own, p_peer,
    stats0, stats1, par, small2, pre_embed, emb_weight, keep,
    square_sum, sum1, sum0, images_grad, block_out, sums, emb_total, class_rows, class_ids,
    sems, sends, recvs, all_sends, all_recvs,
    squares, grads1, grads0, col, turned, full, slope_in, wide_in, source_in, branch_in, hidden_in, grad_hidden,
    far, far_in, columns, flat, mod, mod_send, pres, rows_own, rows_in, total, total_in,
    *scratch,
):
    half = lax.axis_index("head")
    place, core, up, deep = position()
    to_x = {"head": 1 - half}
    others = [{"batch": (place + ahead) % 16} for ahead in range(1, 16)]
    near, away = rows(half * 256, 256), rows((1 - half) * 256, 256)
    exchanges = []

    staged = [
        fetch(sems, number, source, col.at[pl.ds(number * 512, 512)])
        for number, source in enumerate((grad_q, grad_k, grad_v, mixed, normed, grad_out))
    ]
    weights = fetch_conv(sems.at[pl.ds(6, 2)], full, half, 1, w_own, w_peer)
    late = fetch(sems, 8, hidden, wide_in)
    inputs = (
        fetch(sems, 9, second, source_in.at[0]),
        fetch(sems, 10, second_peer, source_in.at[1]),
    )
    meet([to_x] + others)

    def send(slot, source, dest, target):
        copy = remote(source, dest, sends, recvs, slot, target)
        copy.start()
        exchanges.append(copy)
        return copy

    branch_copy = send(0, grad_branch.at[away], branch_in, to_x)

    chains = [Sum(squares, square_sum, scratch[:10], True)]
    scratch = scratch[10:]
    for source, dest in ((grads1, sum1), (grads0, sum0)):
        for low, high in PARTS:
            where = pl.ds(low, high - low)
            chains.append(Sum(source.at[:, where], dest.at[:, where], scratch[:8], False))
            scratch = scratch[8:]

    def advance(*numbers):
        for number in numbers:
            chains[number].advance()

    wait(staged)
    for which, right in enumerate((4, 4, 4, 5)):
        result = mm(
            col[which * 512 : (which + 1) * 512, :], col[right * 512 : (right + 1) * 512, :], NT
        ).astype(BF)
        for part in range(32):
            plane, chunk = part // 16, part % 16
            squares[chunk // 8, plane, chunk % 8, which] = result[part * 16 : (part + 1) * 16]
    advance(0)

    masks = edge_masks(-1)
    taps_of(col, masks, grad_branch, 0, 512, 0, -1)
    wait(weights)

    def conv_back(column):
        result = None
        for tap in range(9):
            term = mm(full[tap], col[tap * 512 : (tap + 1) * 512, column : column + 512], TN)
            result = term if result is None else result + term
        slope_in[:, column : column + 512] = result

    conv_back(0)
    advance(0)
    conv_back(512)
    weights = fetch_conv(sems.at[pl.ds(6, 2)], full, half, 0, w_own, w_peer)
    columns[...] = jnp.zeros_like(columns)
    columns[:, 7:11] = small2[...]
    late.wait()

    def back_one(group, carry):
        where = rows(group * BLOCK, BLOCK)
        unit = unit_of(wide_in[where, :], stats1, where)
        gain = par[where, GAIN + 1 : GAIN + 2]
        unscaled = unit * gain + par[where, BIAS + 1 : BIAS + 2]
        scale = 1.0 + par[where, SCALE : SCALE + 1]
        grad_pre = slope_in[where, :] * silu_slope(unscaled * scale + par[where, SHIFT : SHIFT + 1])
        grad = grad_pre * scale
        low = unit_back(grad * gain, unit, stats1[where, 1:2]).astype(BF)
        grad_hidden[where, :] = low
        columns[where, 2:3] = row_sum(grad_pre * unscaled)
        columns[where, 3:4] = row_sum(grad_pre)
        columns[where, 4:5] = row_sum(grad * unit)
        columns[where, 5:6] = row_sum(grad)
        columns[where, 6:7] = row_sum(low.astype(F32))
        return carry

    lax.fori_loop(0, 512 // BLOCK, back_one, 0)
    hidden_copy = send(1, grad_hidden.at[away], hidden_in, to_x)
    late = fetch(sems, 8, grad_resid, wide_in)
    flat[...] = columns[...].T[0:16]
    mod[place, half] = flat[2:4, near]
    mod_send[...] = flat[2:4, away]
    send(2, mod_send, mod.at[place, half], to_x)
    pres[place] = pre_embed[...]
    for ahead, target in enumerate(others):
        remote(pres.at[place], pres.at[place], all_sends, all_recvs, ahead, target).start()

    branch_copy.wait_recv()
    pair = col.at[pl.ds(9 * 256, 9 * 256)]
    taps_of(col, masks, grad_branch.at[near], 0, 256, 0, -1)
    taps_of(pair, masks, branch_in, 0, 256, 0, -1)
    wait(inputs)
    turned[:PIX, :] = source_in[0].T
    turned[PIX:, :] = source_in[1].T
    inputs = (
        fetch(sems, 9, first, source_in.at[0]),
        fetch(sems, 10, first_peer, source_in.at[1]),
    )
    weight_back(grads1, range(*PARTS[0]), col, turned)
    advance(1)
    weight_back(grads1, range(*PARTS[1]), col, turned)
    advance(0, 2, 1)
    weight_back(grads1, range(*PARTS[2]), col, turned)
    advance(3, 2)
    remote(mod_send, mod.at[place, 1 - half], sends, recvs, 2, to_x).wait_recv()
    for ahead, target in enumerate(others):
        remote(mod.at[place], mod.at[place], all_sends, all_recvs, 15 + ahead, target).start()

    taps_of(col, masks, grad_hidden.at[near], 0, 256, 0, -1)
    advance(3, 1)
    hidden_copy.wait_recv()
    taps_of(pair, masks, hidden_in, 0, 256, 0, -1)
    wait(inputs)
    turned[:PIX, :] = source_in[0].T
    turned[PIX:, :] = source_in[1].T
    picture = source_in.at[0]
    inputs = (
        fetch(sems, 9, images.at[half], picture.at[near]),
        fetch(sems, 10, image_peer, picture.at[away]),
        fetch(sems, 0, mixed, source_in.at[1]),
    )
    advance(2)
    weight_back(grads0, range(*PARTS[0]), col, turned)
    advance(4)
    weight_back(grads0, range(*PARTS[1]), col, turned)
    advance(5, 4, 0, 3)
    weight_back(grads0, range(*PARTS[2]), col, turned)
    advance(6, 5, 0)

    squeezed = fetch_square(sems.at[pl.ds(1, 2)], 0, turned.at[pl.ds(0, 512)], half, p_own, p_peer)
    taps_of(col, masks, grad_hidden, 0, 512, 0, -1)
    advance(6, 1)
    wait(weights)
    conv_back(0)
    advance(2, 0, 4)
    conv_back(512)
    advance(3, 1, 5)
    wait(inputs)
    late.wait()
    for base, mine in ((half * 256, True), ((1 - half) * 256, False)):

        def back_zero(group, carry, base=base, mine=mine):
            here = rows(group * BLOCK, BLOCK)
            where = rows(base + group * BLOCK, BLOCK)
            unit = unit_of(picture[where, :].astype(F32), stats0, where)
            gain = par[where, GAIN : GAIN + 1]
            grad = slope_in[where, :] * silu_slope(unit * gain + par[where, BIAS : BIAS + 1])
            result = wide_in[where, :] + unit_back(grad * gain, unit, stats0[where, 1:2])
            if mine:
                images_grad[half, here, :] = result
            else:
                far[here, :] = result.astype(BF)
            columns[where, 0:1] = row_sum(grad * unit)
            columns[where, 1:2] = row_sum(grad)
            return carry

        lax.fori_loop(0, 256 // BLOCK, back_zero, 0)
        if mine:
            advance(0, 2, 6)
        else:
            advance(3, 1, 4)
    send(3, far, far_in, to_x)
    late = fetch(sems, 8, resid, wide_in)

    flat[...] = columns[...].T[0:16]
    total[0] = flat[:, away]
    send(4, total.at[0], total_in.at[0], to_x)

    wait(squeezed)
    late.wait()
    for column in range(0, PIX, 512):
        where = slice(column, column + 512)
        result = wide_in[:, where] + mm(turned[:512, :], source_in[1, :, where], TN) + par[:, PROJB : PROJB + 1]
        col[0:512, where] = (result * keep[0:1, 0:1]).astype(BF)
    block = col.at[pl.ds(0, 512)]
    send(6, block.at[away], block_out.at[half], to_x)
    kept = fetch(sems, 3, block.at[near], block_out.at[half])
    advance(0, 2, 5)

    def landed(slot, step):
        remote(total.at[0], total_in.at[step], sends, recvs, slot, to_x).wait_recv()

    landed(4, 0)
    total[1] = flat[:, near] + total_in[0]
    send(7, total.at[1], total_in.at[1], {"batch": place + 1 - 2 * core})
    advance(3, 6)

    for ahead in range(15):
        origin = (place + 15 - ahead) % 16
        remote(pres.at[origin], pres.at[origin], all_sends, all_recvs, ahead, to_x).wait_recv()
        remote(mod.at[origin], mod.at[origin], all_sends, all_recvs, 15 + ahead, to_x).wait_recv()
    width = emb_weight.shape[2]
    for slot in range(2):
        embed = jax.nn.silu(pres[:, slot, :width])
        result = None
        for which in range(2):
            factor = mod[:, slot, which, :]
            term = lax.dot_general(factor, embed, TN, precision=HIGH, preferred_element_type=F32)
            if slot == 0:
                emb_total[which] = term
            else:
                emb_total[which] += term
            dense = emb_weight[which].astype(F32)
            term = lax.dot_general(factor, dense, NN, precision=HIGH, preferred_element_type=F32)
            result = term if result is None else result + term
        rows_own[slot] = result
        class_ids[slot] = pres[:, slot, width:]
    send(5, rows_own, rows_in, to_x)
    landed(7, 1)
    total[2] = total[1] + total_in[1]
    send(8, total.at[2], total_in.at[2], {"batch": place + 2 * (1 - 2 * up)})
    advance(4, 1, 5)
    landed(8, 2)
    total[3] = total[2] + total_in[2]
    for ahead in (1, 2, 3):
        send(8 + ahead, total.at[3], total_in.at[3 + deep], {"batch": (deep + ahead) % 4 * 4 + place % 4})
    total_in[3 + deep] = total[3]
    advance(2, 6, 3)
    for ahead in (1, 2, 3):
        landed(8 + ahead, 3 + (deep + 4 - ahead) % 4)
    sums[...] = (total_in[3] + total_in[4]) + (total_in[5] + total_in[6])
    remote(rows_own, rows_in, sends, recvs, 5, to_x).wait_recv()
    for slot in range(2):
        class_rows[slot] = (rows_own[slot] + rows_in[slot]) * silu_slope(pres[:, slot, :width])
    remote(far, far_in, sends, recvs, 3, to_x).wait_recv()
    images_grad[1 - half] = far_in[...].astype(F32)
    for _ in range(8):
        advance(0, 1, 2, 3, 4, 5, 6)
    remote(block.at[away], block_out.at[1 - half], sends, recvs, 6, to_x).wait_recv()
    kept.wait()
    for copy in exchanges:
        copy.wait_send()
    for ahead, target in enumerate(others):
        remote(pres.at[place], pres.at[place], all_sends, all_recvs, ahead, target).wait_send()
        remote(mod.at[place], mod.at[place], all_sends, all_recvs, 15 + ahead, target).wait_send()


def backward_call(*args):
    arrays, specs = operands(args)
    dma = pltpu.SemaphoreType.DMA
    scratch = [
        dma((11,)), dma((12,)), dma((12,)), dma((30,)), dma((30,)),
        pltpu.VMEM((2, 2, 8, 4, 16, 512), BF),
        pltpu.VMEM((16, 9, 16, 512), BF),
        pltpu.VMEM((16, 9, 16, 512), BF),
        pltpu.VMEM((9 * 512, PIX), BF),
        pltpu.VMEM((2 * PIX, 512), BF),
        pltpu.VMEM((9, 512, 512), BF),
        pltpu.VMEM((512, PIX), F32),
        pltpu.VMEM((512, PIX), F32),
        pltpu.VMEM((2, 512, PIX), BF),
        pltpu.VMEM((256, PIX), BF),
        pltpu.VMEM((256, PIX), BF),
        pltpu.VMEM((512, PIX), BF),
        pltpu.VMEM((256, PIX), BF),
        pltpu.VMEM((256, PIX), BF),
        pltpu.VMEM((512, 128), F32),
        pltpu.VMEM((16, 512), F32),
        pltpu.VMEM((16, 2, 2, 256), F32),
        pltpu.VMEM((2, 256), F32),
        pltpu.VMEM((16, 2, 1024 + 128), F32),
        pltpu.VMEM((2, 16, 1024), F32),
        pltpu.VMEM((2, 16, 1024), F32),
        pltpu.VMEM((4, 16, 256), F32),
        pltpu.VMEM((7, 16, 256), F32),
    ]
    scratch += sum_scratch((4, 16, 512), True)
    for low, high in PARTS * 2:
        scratch += sum_scratch((high - low, 16, 512), False)
    outs = [
        (out((16, 4, 16, 512), BF), ANYWHERE),
        (out((16, 9, 16, 512), BF), ANYWHERE),
        (out((16, 9, 16, 512), BF), ANYWHERE),
        (out((2, 256, PIX), F32), VMEM),
        (out((2, 256, PIX), BF), ANYWHERE),
        (out((16, 256), F32), VMEM),
        (out((2, 256, 1024), F32), VMEM),
        (out((2, 16, 1024), F32), VMEM),
        (out((2, 16, 128), F32), VMEM),
    ]
    return pl.pallas_call(
        backward,
        out_shape=[o for o, _ in outs],
        in_specs=specs,
        out_specs=[spec for _, spec in outs],
        scratch_shapes=scratch,
        cost_estimate=pl.CostEstimate(flops=4 * 10**10, bytes_accessed=200 * 2**20, transcendentals=0),
        compiler_params=pltpu.CompilerParams(
            collective_id=2, has_side_effects=True, vmem_limit_bytes=60 * 2**20
        ),
    )(*arrays)


def paired(
    images,
    timesteps,
    classes,
    live_count,
    norm_gain,
    norm_bias,
    conv_weight,
    conv_bias,
    emb_weight,
    emb_bias,
    class_table,
    qkv_weight,
    proj_weight,
    proj_bias,
    cotangent,
):
    half = lax.axis_index("head")

    def across(value):
        return lax.ppermute(value, "head", [(0, 1), (1, 0)])

    def pick(value, index):
        return lax.dynamic_index_in_dim(value, index, 0, keepdims=False)

    table_rows = jnp.stack([pick(class_table, classes[slot]) for slot in range(2)]).astype(F32)
    emb_width = class_table.shape[1]
    pre_embed = jnp.stack([features(timesteps[slot], emb_width) for slot in range(2)]) + table_rows
    params = jnp.concatenate([norm_gain, norm_bias, conv_bias, proj_bias[None]]).T
    par, image_peer, conv_peer, q_peer, p_peer = gather_call(
        pre_embed, params, emb_weight, emb_bias.T, images, conv_weight, qkv_weight, proj_weight
    )
    cot_peer = across(pick(cotangent, 1 - half))
    live = (half < live_count[0]).astype(jnp.int32)
    scalars = jnp.stack([half, 0 * half, live]).astype(jnp.int32)
    full_bf = out((512, PIX), BF)
    full_f32 = out((512, PIX), F32)
    stats = out((512, 2), F32)
    taps = pltpu.VMEM((9 * 512, PIX), BF)
    conv_full = pltpu.VMEM((9, 512, 512), BF)
    square = pltpu.VMEM((512, 512), BF)
    half_bf = pltpu.VMEM((256, PIX), BF)
    wide_bf = pltpu.VMEM((512, PIX), BF)
    wide_f32 = pltpu.VMEM((512, PIX), F32)
    pixels = pltpu.VMEM((PIX, PIX), BF)
    conv_flops = 2 * 9 * 512 * 512 * PIX
    conv_pair = (Far(conv_weight), Far(conv_peer))

    first, hidden, stats0, stats1, second = kernel_call(
        first_conv, [full_bf, full_f32, stats, stats, full_bf], [half_bf, taps, conv_full], conv_flops,
        scalars, Far(images), image_peer, par, *conv_pair,
    )
    resid, stats2, normed = kernel_call(
        second_conv, [full_f32, stats, full_bf], [half_bf, taps, conv_full], conv_flops,
        scalars, second, Far(images), image_peer, par, *conv_pair,
    )
    first_peer = across(first)
    second_peer = across(second)
    mixed, grad_q, grad_k, grad_v, grad_out, grad_resid, grad_branch, small2 = kernel_call(
        attention,
        [full_bf] * 5 + [full_f32, full_bf, out((512, 4), F32)],
        [pltpu.VMEM((3, 512, 512), BF), square] + [wide_bf] * 4 + [pixels] * 2 + [wide_f32] * 2,
        4 * conv_flops,
        scalars, normed, Far(resid), stats2, par, Far(cotangent), Far(cot_peer),
        Far(qkv_weight), Far(q_peer), Far(proj_weight), Far(p_peer),
    )
    ids = jnp.broadcast_to(classes.astype(F32)[:, None], (2, 128))
    keep = jnp.broadcast_to(live.astype(F32), (8, 128))
    square_sum, conv_sum1, conv_sum0, images_grad, block_out, sums, emb_total, class_rows, ids = backward_call(
        grad_branch, *map(Far, (normed, grad_q, grad_k, grad_v, mixed, grad_out, resid, hidden)),
        *map(Far, (second, second_peer, first, first_peer, grad_resid, images, image_peer)),
        *conv_pair, Far(proj_weight), Far(p_peer), stats0, stats1, par, small2,
        jnp.concatenate([pre_embed, ids], 1), emb_weight, keep,
    )

    def whole(value):
        return value.transpose(1, 0, 2, 3).reshape(value.shape[1], 256, 512).astype(F32)

    squares = whole(square_sum)
    ids = ids[:, :, 0].reshape(-1).astype(jnp.int32)
    chosen = (lax.iota(jnp.int32, class_table.shape[0])[:, None] == ids[None, :]).astype(F32)
    table_total = jnp.dot(chosen, class_rows.reshape(-1, emb_width), precision=HIGH)
    return (
        block_out,
        images_grad,
        jnp.stack([sums[0], sums[4], sums[7]]),
        jnp.stack([sums[1], sums[5], sums[8]]),
        jnp.stack([whole(conv_sum0), whole(conv_sum1)]),
        jnp.stack([sums[6], sums[9]]),
        emb_total,
        sums[2:4],
        table_total,
        squares[:3],
        squares[3],
        sums[10],
    )


def solution(mesh):
    in_specs = (
        P("batch", "head", None),
        P("batch"),
        P("batch"),
        P("batch"),
        P(None, "head"),
        P(None, "head"),
        P(None, None, "head", None),
        P(None, "head"),
        P(None, "head", None),
        P(None, "head"),
        P(),
        P(None, "head", None),
        P("head", None),
        P("head"),
        P("batch", "head", None),
    )
    out_specs = (
        P("batch", "head", None),
        P("batch", "head", None),
        P(None, "head"),
        P(None, "head"),
        P(None, None, "head", None),
        P(None, "head"),
        P(None, "head", None),
        P(None, "head"),
        P(),
        P(None, "head", None),
        P("head", None),
        P("head"),
    )
    body = shards
    if mesh.shape["head"] == 2 and mesh.shape["batch"] == 16:
        body = paired
    return jax.shard_map(body, mesh=mesh, in_specs=in_specs, out_specs=out_specs, check_vma=False)
```

```python
import math

import jax
import jax.numpy as jnp
from jax import lax
from jax.experimental import pallas as pl
from jax.experimental.pallas import tpu as pltpu
from jax.sharding import PartitionSpec as P

C = 512
GROUPS = 32
HEADS = 8
SIDE = 32


EPS = 1e-05
HIGH = lax.Precision.HIGHEST
CONTRACT_FIRST = (((0,), (0,)), ((), ()))
CONTRACT_LAST = (((1,), (1,)), ((), ()))


def silu_slope(values):
    sigma = jax.nn.sigmoid(values)
    return sigma * (1.0 + values * (1.0 - sigma))


def moved(source, grid_side, row_step, col_step):
    grid = source.reshape(source.shape[0], grid_side, grid_side)
    padded = jnp.pad(grid, ((0, 0), (1, 1), (1, 1)))
    window = padded[
        :, 1 + row_step : 1 + row_step + grid_side, 1 + col_step : 1 + col_step + grid_side
    ]
    return window.reshape(source.shape)


def group_unit(source, groups):
    grouped = source.reshape(groups, -1)
    centre = grouped - jnp.mean(grouped, axis=1, keepdims=True)
    inverse = lax.rsqrt(jnp.mean(jnp.square(centre), axis=1, keepdims=True) + EPS)
    return ((centre * inverse).reshape(source.shape), inverse)


def group_back(grad_unit, unit_rows, inverse, groups):
    flat_grad = grad_unit.reshape(groups, -1)
    flat_unit = unit_rows.reshape(groups, -1)
    result = flat_grad - jnp.mean(flat_grad, axis=1, keepdims=True)
    result = (result - flat_unit * jnp.mean(flat_grad * flat_unit, axis=1, keepdims=True)) * inverse
    return result.reshape(grad_unit.shape)


def conv_apply(weight, source, grid_side):
    result = jnp.dot(
        weight[0], moved(source, grid_side, -1, -1), preferred_element_type=jnp.float32
    )
    for tap_index in range(1, 9):
        result = result + jnp.dot(
            weight[tap_index],
            moved(source, grid_side, tap_index // 3 - 1, tap_index % 3 - 1),
            preferred_element_type=jnp.float32,
        )
    return result


def conv_transpose(weight, grads, grid_side):
    result = lax.dot_general(
        weight[0], moved(grads, grid_side, 1, 1), CONTRACT_FIRST, preferred_element_type=jnp.float32
    )
    for tap_index in range(1, 9):
        result = result + lax.dot_general(
            weight[tap_index],
            moved(grads, grid_side, 1 - tap_index // 3, 1 - tap_index % 3),
            CONTRACT_FIRST,
            preferred_element_type=jnp.float32,
        )
    return result


def conv_weight_grads(grads, source, grid_side):
    return jnp.stack(
        [
            lax.dot_general(
                grads,
                moved(source, grid_side, tap_index // 3 - 1, tap_index % 3 - 1),
                CONTRACT_LAST,
                preferred_element_type=jnp.float32,
            )
            for tap_index in range(9)
        ]
    )


def features(timestep, emb_width):
    half_width = emb_width // 2
    freqs = jnp.exp(-math.log(10000.0) * jnp.arange(half_width, dtype=jnp.float32) / half_width)
    angles = timestep.astype(jnp.float32) * freqs
    return jnp.concatenate([jnp.cos(angles), jnp.sin(angles)])


def shards(
    images,
    timesteps,
    classes,
    live_count,
    norm_gain,
    norm_bias,
    conv_weight,
    conv_bias,
    emb_weight,
    emb_bias,
    class_table,
    qkv_weight,
    proj_weight,
    proj_bias,
    cotangent,
):
    slot_count, chan_dev, pixel_count = images.shape
    grid_side = SIDE
    groups = chan_dev // (C // GROUPS)
    head_size = C // HEADS
    heads_dev = chan_dev // head_size
    att_scale = head_size ** (-0.5)
    emb_dense = emb_weight.astype(jnp.float32)
    class_total, emb_width = class_table.shape

    def gather_channels(rows_low):
        return lax.all_gather(rows_low, "head", axis=0, tiled=True)

    def input_grad(which_conv, grad_rows):
        weight_cols = conv_weight[which_conv]
        return lax.psum_scatter(
            conv_transpose(weight_cols, grad_rows, grid_side).astype(jnp.bfloat16),
            "head",
            scatter_dimension=0,
            tiled=True,
        ).astype(jnp.float32)

    def per_slot(slot_index, carry):
        (
            outputs,
            grads_in,
            gain_acc,
            bias_acc,
            convw_acc,
            convb_acc,
            embw_acc,
            embb_acc,
            table_acc,
            qkv_acc,
            projw_acc,
            projb_acc,
        ) = carry
        picture = lax.dynamic_index_in_dim(images, slot_index, 0, keepdims=False).astype(
            jnp.float32
        )
        live_flag = (slot_index < live_count[0]).astype(jnp.float32)
        class_id = classes[slot_index]
        table_row = lax.dynamic_index_in_dim(class_table, class_id, 0, keepdims=False).astype(
            jnp.float32
        )
        pre_embed = features(timesteps[slot_index], emb_width) + table_row
        embed = jax.nn.silu(pre_embed)
        scale = jnp.dot(emb_dense[0], embed, precision=HIGH) + emb_bias[0]
        shift = jnp.dot(emb_dense[1], embed, precision=HIGH) + emb_bias[1]
        unit_zero, inverse_zero = group_unit(picture, groups)
        pre_first = unit_zero * norm_gain[0][:, None] + norm_bias[0][:, None]
        first_full = gather_channels(jax.nn.silu(pre_first).astype(jnp.bfloat16))
        hidden = conv_apply(conv_weight[0], first_full, grid_side) + conv_bias[0][:, None]
        unit_one, inverse_one = group_unit(hidden, groups)
        normed_one = unit_one * norm_gain[1][:, None] + norm_bias[1][:, None]
        pre_second = normed_one * (1.0 + scale[:, None]) + shift[:, None]
        second_full = gather_channels(jax.nn.silu(pre_second).astype(jnp.bfloat16))
        resid = picture + conv_apply(conv_weight[1], second_full, grid_side) + conv_bias[1][:, None]
        unit_two, inverse_two = group_unit(resid, groups)
        normed_full = gather_channels(
            (unit_two * norm_gain[2][:, None] + norm_bias[2][:, None]).astype(jnp.bfloat16)
        )
        query = (
            jnp.dot(qkv_weight[0], normed_full, preferred_element_type=jnp.float32)
            .astype(jnp.bfloat16)
            .reshape(heads_dev, head_size, pixel_count)
        )
        keys = (
            jnp.dot(qkv_weight[1], normed_full, preferred_element_type=jnp.float32)
            .astype(jnp.bfloat16)
            .reshape(heads_dev, head_size, pixel_count)
        )
        values = (
            jnp.dot(qkv_weight[2], normed_full, preferred_element_type=jnp.float32)
            .astype(jnp.bfloat16)
            .reshape(heads_dev, head_size, pixel_count)
        )
        scores = (
            jnp.einsum("hdi,hdj->hij", query, keys, preferred_element_type=jnp.float32) * att_scale
        )
        highest = jnp.max(scores, axis=2, keepdims=True)
        expo = jnp.exp(scores - highest)
        totals = jnp.sum(expo, axis=2, keepdims=True)
        log_total = highest + jnp.log(totals)
        weights = (expo / totals).astype(jnp.bfloat16)
        mixed = (
            jnp.einsum("hdj,hij->hdi", values, weights, preferred_element_type=jnp.float32)
            .astype(jnp.bfloat16)
            .reshape(chan_dev, pixel_count)
        )
        weight_cols = proj_weight
        proj_term = lax.psum_scatter(
            lax.dot_general(
                weight_cols, mixed, CONTRACT_FIRST, preferred_element_type=jnp.float32
            ).astype(jnp.bfloat16),
            "head",
            scatter_dimension=0,
            tiled=True,
        ).astype(jnp.float32)
        result = resid + proj_term + proj_bias[:, None]
        outputs = lax.dynamic_update_index_in_dim(
            outputs, (live_flag * result).astype(jnp.bfloat16), slot_index, 0
        )
        grad_low = lax.dynamic_index_in_dim(cotangent, slot_index, 0, keepdims=False)
        grad_out = live_flag * grad_low.astype(jnp.float32)
        grad_full = lax.all_gather(grad_low, "head", axis=0, tiled=True) * live_flag.astype(
            jnp.bfloat16
        )
        grad_mixed = jnp.dot(proj_weight, grad_full, preferred_element_type=jnp.float32).astype(
            jnp.bfloat16
        )
        projw_acc = projw_acc + lax.dot_general(
            mixed, grad_full, CONTRACT_LAST, preferred_element_type=jnp.float32
        )
        projb_acc = projb_acc + jnp.sum(grad_out, axis=1)
        again = (
            jnp.einsum("hdi,hdj->hij", query, keys, preferred_element_type=jnp.float32) * att_scale
        )
        probs = jnp.exp(again - log_total)
        grad_heads = grad_mixed.reshape(heads_dev, head_size, pixel_count)
        grad_probs = jnp.einsum(
            "hdi,hdj->hij", grad_heads, values, preferred_element_type=jnp.float32
        )
        grad_scores = (
            probs * (grad_probs - jnp.sum(grad_probs * probs, axis=2, keepdims=True))
        ).astype(jnp.bfloat16)
        grad_query = (
            jnp.einsum("hij,hdj->hdi", grad_scores, keys, preferred_element_type=jnp.float32)
            * att_scale
        ).astype(jnp.bfloat16)
        grad_keys = (
            jnp.einsum("hij,hdi->hdj", grad_scores, query, preferred_element_type=jnp.float32)
            * att_scale
        ).astype(jnp.bfloat16)
        grad_values = jnp.einsum(
            "hdi,hij->hdj", grad_heads, weights, preferred_element_type=jnp.float32
        ).astype(jnp.bfloat16)
        stacked = jnp.stack([grad_query, grad_keys, grad_values]).reshape(3, chan_dev, pixel_count)
        weight_cols = qkv_weight
        grad_normed = lax.psum_scatter(
            lax.dot_general(
                weight_cols,
                stacked,
                (((0, 1), (0, 1)), ((), ())),
                preferred_element_type=jnp.float32,
            ).astype(jnp.bfloat16),
            "head",
            scatter_dimension=0,
            tiled=True,
        ).astype(jnp.float32)
        qkv_acc = qkv_acc + lax.dot_general(
            stacked, normed_full, (((2,), (1,)), ((), ())), preferred_element_type=jnp.float32
        )
        grad_resid = grad_out + group_back(
            grad_normed * norm_gain[2][:, None], unit_two, inverse_two, groups
        )
        grad_branch = grad_resid.astype(jnp.bfloat16)
        grad_second = input_grad(1, grad_branch)
        grad_pre = grad_second * silu_slope(pre_second)
        scale_grad = jnp.sum(grad_pre * normed_one, axis=1)
        shift_grad = jnp.sum(grad_pre, axis=1)
        grad_normed_one = grad_pre * (1.0 + scale[:, None])
        grad_hidden = group_back(
            grad_normed_one * norm_gain[1][:, None], unit_one, inverse_one, groups
        ).astype(jnp.bfloat16)
        grad_first = input_grad(0, grad_hidden)
        grad_pre_first = grad_first * silu_slope(pre_first)
        picture_grad = grad_resid + group_back(
            grad_pre_first * norm_gain[0][:, None], unit_zero, inverse_zero, groups
        )
        grads_in = lax.dynamic_update_index_in_dim(grads_in, picture_grad, slot_index, 0)
        gain_acc = gain_acc + jnp.stack(
            [
                jnp.sum(grad_pre_first * unit_zero, axis=1),
                jnp.sum(grad_normed_one * unit_one, axis=1),
                jnp.sum(grad_normed * unit_two, axis=1),
            ]
        )
        bias_acc = bias_acc + jnp.stack(
            [
                jnp.sum(grad_pre_first, axis=1),
                jnp.sum(grad_normed_one, axis=1),
                jnp.sum(grad_normed, axis=1),
            ]
        )
        convw_acc = convw_acc + jnp.stack(
            [
                conv_weight_grads(grad_hidden, first_full, grid_side),
                conv_weight_grads(grad_branch, second_full, grid_side),
            ]
        )
        convb_acc = convb_acc + jnp.stack(
            [
                jnp.sum(grad_hidden.astype(jnp.float32), axis=1),
                jnp.sum(grad_branch.astype(jnp.float32), axis=1),
            ]
        )
        embw_acc = embw_acc + jnp.stack(
            [scale_grad[:, None] * embed[None, :], shift_grad[:, None] * embed[None, :]]
        )
        embb_acc = embb_acc + jnp.stack([scale_grad, shift_grad])
        grad_embed = jnp.dot(scale_grad, emb_dense[0], precision=HIGH) + jnp.dot(
            shift_grad, emb_dense[1], precision=HIGH
        )
        class_row = grad_embed * silu_slope(pre_embed)
        old_row = lax.dynamic_index_in_dim(table_acc, class_id, 0, keepdims=True)
        table_acc = lax.dynamic_update_index_in_dim(
            table_acc, old_row + class_row[None, :], class_id, 0
        )
        return (
            outputs,
            grads_in,
            gain_acc,
            bias_acc,
            convw_acc,
            convb_acc,
            embw_acc,
            embb_acc,
            table_acc,
            qkv_acc,
            projw_acc,
            projb_acc,
        )

    table_start = jnp.zeros(class_table.shape, jnp.float32)
    initial = (
        jnp.zeros(images.shape, jnp.bfloat16),
        jnp.zeros(images.shape, jnp.float32),
        jnp.zeros(norm_gain.shape, jnp.float32),
        jnp.zeros(norm_bias.shape, jnp.float32),
        jnp.zeros(conv_weight.shape, jnp.float32),
        jnp.zeros(conv_bias.shape, jnp.float32),
        jnp.zeros(emb_weight.shape, jnp.float32),
        jnp.zeros(emb_bias.shape, jnp.float32),
        table_start,
        jnp.zeros(qkv_weight.shape, jnp.float32),
        jnp.zeros(proj_weight.shape, jnp.float32),
        jnp.zeros(proj_bias.shape, jnp.float32),
    )
    final = lax.fori_loop(0, slot_count, per_slot, initial)
    (
        outputs,
        grads_in,
        gain_acc,
        bias_acc,
        convw_acc,
        convb_acc,
        embw_acc,
        embb_acc,
        table_acc,
        qkv_acc,
        projw_acc,
        projb_acc,
    ) = final
    table_total = lax.psum(table_acc, ("batch", "head"))
    summed = (
        lax.psum(gain_acc.astype(jnp.bfloat16), "batch").astype(jnp.float32),
        lax.psum(bias_acc.astype(jnp.bfloat16), "batch").astype(jnp.float32),
        lax.psum(convw_acc.astype(jnp.bfloat16), "batch").astype(jnp.float32),
        lax.psum(convb_acc.astype(jnp.bfloat16), "batch").astype(jnp.float32),
        lax.psum(embw_acc.astype(jnp.bfloat16), "batch").astype(jnp.float32),
        lax.psum(embb_acc.astype(jnp.bfloat16), "batch").astype(jnp.float32),
        lax.psum(qkv_acc.astype(jnp.bfloat16), "batch").astype(jnp.float32),
        lax.psum(projw_acc.astype(jnp.bfloat16), "batch").astype(jnp.float32),
        lax.psum(projb_acc.astype(jnp.bfloat16), "batch").astype(jnp.float32),
    )
    return (
        outputs,
        grads_in,
        summed[0],
        summed[1],
        summed[2],
        summed[3],
        summed[4],
        summed[5],
        table_total,
        summed[6],
        summed[7],
        summed[8],
    )


PIX = 1024
BLOCK = 128
BF = jnp.bfloat16
F32 = jnp.float32
NN = (((1,), (0,)), ((), ()))
TN = (((0,), (0,)), ((), ()))
NT = (((1,), (1,)), ((), ()))
VMEM = pl.BlockSpec(memory_space=pltpu.VMEM)
SMEM = pl.BlockSpec(memory_space=pltpu.SMEM)

GAIN, BIAS, CONVB, PROJB, SCALE, SHIFT = 0, 3, 6, 8, 9, 10


def mm(left, right, dims=NN):
    return lax.dot_general(left, right, dims, preferred_element_type=F32)


class Far:
    def __init__(self, array):
        self.array = array


ANYWHERE = pl.BlockSpec(memory_space=pl.ANY)


class Scalars(Far):
    pass


def operands(args):
    arrays = [arg.array if isinstance(arg, Far) else arg for arg in args]
    specs = []
    for arg in args:
        if isinstance(arg, Scalars):
            specs.append(SMEM)
        else:
            specs.append(ANYWHERE if isinstance(arg, Far) else VMEM)
    return arrays, specs


def kernel_call(kernel, outs, scratch, flops, *args):
    arrays, specs = operands(args)
    moved_bytes = sum(a.size * a.dtype.itemsize for a in arrays)
    moved_bytes += sum(math.prod(o.shape) * o.dtype.itemsize for o in outs)
    return pl.pallas_call(
        kernel,
        out_shape=outs,
        in_specs=specs,
        out_specs=[VMEM] * len(outs),
        scratch_shapes=[pltpu.SemaphoreType.DMA((8,))] + scratch,
        cost_estimate=pl.CostEstimate(flops=flops, bytes_accessed=moved_bytes, transcendentals=0),
        compiler_params=pltpu.CompilerParams(vmem_limit_bytes=56 * 2**20),
    )(*arrays)


def split(value, axis):
    parts = []
    for _ in range(3):
        part = value.astype(BF)
        parts.append(part)
        value = value - part.astype(F32)
    return jnp.concatenate(parts, axis)


def fetch(sems, slot, source, dest):
    copy = pltpu.make_async_copy(source, dest, sems.at[slot])
    copy.start()
    return copy


def out(shape, dtype):
    return jax.ShapeDtypeStruct(shape, dtype)


def rows(start, count):
    return pl.ds(pl.multiple_of(start, count), count)


def edge_masks(sign):
    pixel = lax.broadcasted_iota(jnp.int32, (1, PIX), 1)
    col, row = pixel % SIDE, pixel // SIDE
    table = {}
    for step in (-1, 1):
        moved_step = sign * step
        table["col", step] = ((col + moved_step >= 0) & (col + moved_step < SIDE)).astype(F32)
        table["row", step] = ((row + moved_step >= 0) & (row + moved_step < SIDE)).astype(F32)
    return table


def put_taps(dest, masks, values, first_row, depth, base, sign):
    count = values.shape[0]
    for col_step in (-1, 0, 1):
        across = values
        if col_step:
            across = pltpu.roll(values, (-sign * col_step) % PIX, 1) * masks["col", col_step]
        for row_step in (-1, 0, 1):
            copy = across
            if row_step:
                copy = pltpu.roll(across, (-sign * row_step * SIDE) % PIX, 1) * masks["row", row_step]
            tap = 3 * (row_step + 1) + col_step + 1
            dest[rows(tap * depth + first_row, count), base : base + PIX] = copy.astype(BF)


def taps_of(dest, masks, source, offset, depth, base, sign):
    for start in range(0, source.shape[0], 128):
        piece = source[start : start + 128, :].astype(F32)
        put_taps(dest, masks, piece, offset + start, depth, base, sign)


def fetch_conv(sems, full, half, which, own, peer):
    return (
        fetch(sems, 0, own.at[which], full.at[:, rows(half * 256, 256), :]),
        fetch(sems, 1, peer.at[which], full.at[:, rows((1 - half) * 256, 256), :]),
    )


def wait(copies):
    for copy in copies:
        copy.wait()


def conv_dots(dest, full, col, dims, finish):
    for column in range(0, PIX, 512):
        total = None
        for tap in range(9):
            term = mm(full[tap], col[tap * 512 : (tap + 1) * 512, column : column + 512], dims)
            total = term if total is None else total + term
        dest[:, column : column + 512] = finish(total, column)


def grouped(block):
    return block.reshape((-1, 16) + block.shape[1:])


def group_mean(block):
    return jnp.sum(block, axis=(1, 2), keepdims=True) * (1.0 / (16 * PIX))


def group_stats(block, stats, where):
    parts = grouped(block)
    centre = group_mean(parts)
    parts = parts - centre
    inverse = lax.rsqrt(group_mean(jnp.square(parts)) + EPS)
    count = block.shape[0]
    for column, value in enumerate((centre, inverse)):
        stats[where, column : column + 1] = jnp.broadcast_to(value, (count // 16, 16, 1)).reshape(count, 1)
    return (parts * inverse).reshape(block.shape)


def unit_of(block, stats, where):
    return (block - stats[where, 0:1]) * stats[where, 1:2]


def unit_back(grad, unit, inverse):
    parts, units = grouped(grad), grouped(unit)
    result = parts - group_mean(parts) - units * group_mean(parts * units)
    return result.reshape(grad.shape) * inverse


def row_sum(block):
    return jnp.sum(block, axis=1, keepdims=True)


def fetch_square(sems, slot, full, half, own, peer):
    count = own.shape[-2]
    near, far = rows(half * count, count), rows((1 - half) * count, count)
    if len(full.shape) == 3:
        near, far = (slice(None), near), (slice(None), far)
    return fetch(sems, slot, own, full.at[near]), fetch(sems, slot + 1, peer, full.at[far])


def attention(
    live_count, normed, resid, stats2, par, cotangent, cot_peer, q_own, q_peer, p_own, p_peer,
    mixed, grad_q, grad_k, grad_v, grad_out, grad_resid, grad_branch, small,
    sems, wqkv, wp, query, keys, values, grad_mixed, weights, grad_scores, grad_normed, resid_in,
):
    half = lax.axis_index("head")
    live = (half < live_count[0]).astype(BF)
    arriving = fetch_square(sems, 0, wqkv, half, q_own, q_peer)
    later = fetch_square(sems, 2, wp, half, p_own, p_peer)
    later += (
        fetch(sems, 4, cotangent.at[half], grad_out.at[rows(half * 256, 256)]),
        fetch(sems, 5, cot_peer, grad_out.at[rows((1 - half) * 256, 256)]),
    )
    last = fetch(sems, 6, resid, resid_in)
    wait(arriving)
    for column in range(0, PIX, 512):
        where = slice(column, column + 512)
        query[:, where] = (mm(wqkv[0], normed[:, where]).astype(BF).astype(F32) * 0.125).astype(BF)
        keys[:, where] = mm(wqkv[1], normed[:, where]).astype(BF)
        values[:, where] = mm(wqkv[2], normed[:, where]).astype(BF)
    wait(later)
    grad_out[...] = grad_out[...] * live
    for column in range(0, PIX, 512):
        where = slice(column, column + 512)
        grad_mixed[:, where] = mm(wp[...], grad_out[:, where]).astype(BF)

    def head(number, carry):
        where = rows(number * 64, 64)
        q, k, v, g = query[where, :], keys[where, :], values[where, :], grad_mixed[where, :]
        scores = mm(k.T, q)
        expo = jnp.exp(scores - jnp.max(scores, axis=0, keepdims=True))
        low = (expo * (1.0 / jnp.sum(expo, axis=0, keepdims=True))).astype(BF)
        weights[...] = low
        mix = mm(v, low)
        mixed[where, :] = mix.astype(BF)
        delta = jnp.sum(mix * g.astype(F32), axis=0, keepdims=True)
        inner = (low.astype(F32) * (mm(v.T, g) - delta)).astype(BF)
        grad_scores[...] = inner
        grad_q[where, :] = (mm(k, inner) * 0.125).astype(BF)
        grad_k[where, :] = mm(grad_scores[...], q.T).T.astype(BF)
        grad_v[where, :] = mm(weights[...], g.T).T.astype(BF)
        return carry

    lax.fori_loop(0, HEADS, head, 0)
    for column in range(0, PIX, 512):
        where = slice(column, column + 512)
        grad_normed[:, where] = (
            mm(wqkv[0], grad_q[:, where], TN)
            + mm(wqkv[1], grad_k[:, where], TN)
            + mm(wqkv[2], grad_v[:, where], TN)
        )
    last.wait()

    def back(group, carry):
        where = rows(group * BLOCK, BLOCK)
        unit = unit_of(resid_in[where, :], stats2, where)
        grad = grad_normed[where, :]
        outer = grad_out[where, :].astype(F32)
        total = outer + unit_back(grad * par[where, GAIN + 2 : GAIN + 3], unit, stats2[where, 1:2])
        low = total.astype(BF)
        grad_resid[where, :] = total
        grad_branch[where, :] = low
        small[where, 0:1] = row_sum(grad * unit)
        small[where, 1:2] = row_sum(grad)
        small[where, 2:3] = row_sum(low.astype(F32))
        small[where, 3:4] = row_sum(outer)
        return carry

    lax.fori_loop(0, 512 // BLOCK, back, 0)


def remote(source, dest, sends, recvs, slot, target):
    return pltpu.make_async_remote_copy(
        src_ref=source,
        dst_ref=dest,
        send_sem=sends.at[slot],
        recv_sem=recvs.at[slot],
        device_id=target,
        device_id_type=pl.DeviceIdType.MESH,
    )


def meet(targets):
    barrier = pltpu.get_barrier_semaphore()
    for target in targets:
        pl.semaphore_signal(barrier, inc=1, device_id=target, device_id_type=pl.DeviceIdType.MESH)
    pl.semaphore_wait(barrier, len(targets))


def position():
    place = lax.axis_index("batch")
    return place, place % 2, (place // 2) % 2, place // 4


PIECES = 6
KINDS = 10


def forward(
    timesteps, classes, norm_gain, norm_bias, conv_bias, proj_bias, emb_bias, emb_weight, class_table,
    images, cotangent, conv_weight, qkv_weight, proj_weight,
    par, pre_embed, image_peer, cot_peer, conv_peer, qkv_peer, proj_peer,
    first, first_near, first_other, hidden, stats0, stats1, second, resid, stats2, normed,
    sends, recvs, few_sends, few_recvs, sems, par_send, par_recv, lines, table, own, peer, other, spare, col, full,
):
    half = lax.axis_index("head")
    place, core, up, deep = position()
    z_low = deep % 2
    to_x = {"head": 1 - half}
    to_y = {"batch": place + 2 * (1 - 2 * up)}
    to_z = {"batch": place + 4 * (1 - 2 * z_low)}
    to_core = {"batch": place + (1 - 2 * core)}
    near, away = rows(half * 256, 256), rows((1 - half) * 256, 256)
    pictures = (
        fetch(sems, 0, images.at[half], own),
        fetch(sems, 1, images.at[1 - half], other),
    )
    table_copy = fetch(sems, 2, class_table, table)
    own_weights = fetch(sems, 3, conv_weight.at[0], full.at[:, near, :])
    meet([to_x, to_y, to_z, to_core])

    def block(flip_core=0, flip_y=0, flip_z=0):
        c = 1 - core if flip_core else core
        y = 1 - up if flip_y else up
        z = 1 - z_low if flip_z else z_low
        return (c + 2 * y + 4 * z) * 32

    def views(piece, local, start, count):
        where = rows(start, count)
        if piece < 4:
            taps = pl.ds(0, 5) if piece % 2 == 0 else pl.ds(5, 4)
            return (conv_weight if local else conv_peer).at[piece // 2, taps, where, :]
        if piece == 4:
            return (qkv_weight if local else qkv_peer).at[:, where, :]
        return (proj_weight if local else proj_peer).at[where, :]

    def copy(piece, kind, start, count, target, local=False):
        return remote(
            views(piece, local, start, count), views(piece, False, start, count),
            sends.at[piece], recvs.at[piece], kind, target,
        )

    def regions(flip_core):
        return (
            (block(flip_core), 32),
            (block(flip_core, 1), 32),
            (block(flip_core, 0, 1), 32),
            (block(flip_core, 1, 1), 16),
            (block(flip_core, 1, 1) + 16, 16),
        )

    mine, others = regions(0), regions(1)

    def arrived(piece, kind):
        start, count = mine[kind] if kind < 5 else others[kind - 5]
        copy(piece, kind, start, count, to_core).wait_recv()

    def over_x(piece):
        arrived(piece, 0)
        for kind, target in ((1, to_y), (2, to_z), (5, to_core)):
            copy(piece, kind, block(), 32, target).start()

    def over_yz(piece):
        arrived(piece, 2)
        copy(piece, 3, block(0, 0, 1), 16, to_y).start()
        copy(piece, 7, block(0, 0, 1), 32, to_core).start()
        arrived(piece, 1)
        copy(piece, 4, block(0, 1, 0) + 16, 16, to_z).start()
        copy(piece, 6, block(0, 1, 0), 32, to_core).start()

    def diagonal(piece):
        arrived(piece, 3)
        copy(piece, 8, block(0, 1, 1), 16, to_core).start()
        arrived(piece, 4)
        copy(piece, 9, block(0, 1, 1) + 16, 16, to_core).start()

    def complete(piece):
        for kind in range(5, 10):
            arrived(piece, kind)

    def fetch_x(*pieces):
        for piece in pieces:
            copy(piece, 0, block(), 32, to_x, local=True).start()

    fetch_x(0, 1)

    table_copy.wait()
    width = class_table.shape[1]
    numbers = lax.broadcasted_iota(jnp.int32, (1, table.shape[0]), 1)
    freqs = jnp.exp(
        lax.broadcasted_iota(jnp.int32, (1, width // 2), 1).astype(F32) * (-math.log(10000.0) / (width // 2))
    )
    for slot in range(2):
        chosen = (numbers == classes[slot]).astype(BF)
        angles = timesteps[slot].astype(F32) * freqs
        pre_embed[slot : slot + 1, : width // 2] = jnp.cos(angles)
        pre_embed[slot : slot + 1, width // 2 : width] = jnp.sin(angles)
        line = mm(jnp.broadcast_to(chosen, (8, table.shape[0])), table[...])
        pre_embed[slot : slot + 1, :width] += line[0:1]
        pre_embed[slot : slot + 1, width:] = jnp.broadcast_to(classes[slot].astype(F32), (1, 128))
    embed = jax.nn.silu(pre_embed[:, :width])
    own_row = jnp.where(half == 0, embed[0:1], embed[1:2])
    peer_row = jnp.where(half == 0, embed[1:2], embed[0:1])
    lines[...] = jnp.zeros_like(lines)
    lines[0:3] = norm_gain[...]
    lines[3:6] = norm_bias[...]
    lines[6:8] = conv_bias[...]
    lines[8:9] = proj_bias[...]
    lines[9:11] = emb_bias[...]
    turned = lines[...].T
    par_send[:, 0:11] = turned[:, 0:11]
    par[near, :] = turned[:, 0:11]
    for which in range(2):
        dense = emb_weight[which].astype(F32)
        par[near, SCALE + which : SCALE + which + 1] += row_sum(dense * own_row)
        par_send[:, SCALE + which : SCALE + which + 1] += row_sum(dense * peer_row)
    block_copy = remote(par_send, par_recv, few_sends, few_recvs, 1, to_x)
    block_copy.start()

    masks = edge_masks(1)
    wait(pictures)

    def norm_zero(source, dest, base, stats, offset, group):
        here = rows(group * BLOCK, BLOCK)
        where = rows(base + group * BLOCK, BLOCK)
        unit = group_stats(source[here, :].astype(F32), stats, rows(offset + group * BLOCK, BLOCK))
        low = jax.nn.silu(unit * par[where, GAIN : GAIN + 1] + par[where, BIAS : BIAS + 1]).astype(BF)
        dest[rows(offset + group * BLOCK, BLOCK), :] = low
        return low.astype(F32)

    def norm_near(group, carry):
        low = norm_zero(own, first, half * 256, stats0, half * 256, group)
        first_near[rows(group * BLOCK, BLOCK), :] = low.astype(BF)
        put_taps(col, masks, low, half * 256 + group * BLOCK, 512, 0, 1)
        return carry

    def norm_other(group, carry):
        norm_zero(other, first_other, half * 256, spare, 0, group)
        return carry

    lax.fori_loop(0, 256 // BLOCK, norm_near, 0)
    over_x(0)
    over_x(1)
    picture = remote(images.at[1 - half], image_peer, few_sends, few_recvs, 0, to_x)
    picture.start()
    lax.fori_loop(0, 256 // BLOCK, norm_other, 0)
    over_yz(0)
    over_yz(1)
    block_copy.wait_recv()
    par[away, :] = par_recv[:, 0:11]
    diagonal(0)
    fetch_x(2, 3)
    diagonal(1)
    picture.wait_recv()
    loaded = fetch(sems, 0, image_peer, peer)
    fetch_x(4, 5)
    cot_copy = remote(cotangent.at[1 - half], cot_peer, few_sends, few_recvs, 2, to_x)
    cot_copy.start()
    complete(0)
    complete(1)
    peer_weights = fetch(sems, 4, conv_peer.at[0], full.at[:, away, :])
    loaded.wait()

    def norm_far(group, carry):
        low = norm_zero(peer, first, (1 - half) * 256, stats0, (1 - half) * 256, group)
        put_taps(col, masks, low, (1 - half) * 256 + group * BLOCK, 512, 0, 1)
        return carry

    lax.fori_loop(0, 256 // BLOCK, norm_far, 0)
    own_weights.wait()

    def conv_part(dest, mine, column, bias):
        where = near if mine else away
        result = None
        for tap in range(9):
            term = mm(full[tap, where, :], col[tap * 512 : (tap + 1) * 512, column : column + 512])
            result = term if result is None else result + term
        dest[where, column : column + 512] = result + par[where, bias : bias + 1]

    conv_part(hidden, True, 0, CONVB)
    over_x(2)
    conv_part(hidden, True, 512, CONVB)
    over_x(3)
    peer_weights.wait()
    conv_part(hidden, False, 0, CONVB)
    over_yz(2)
    over_x(4)
    over_x(5)
    conv_part(hidden, False, 512, CONVB)
    over_yz(3)
    diagonal(2)
    own_weights = fetch(sems, 3, conv_weight.at[1], full.at[:, near, :])

    def norm_one(group, carry):
        where = rows(group * BLOCK, BLOCK)
        unit = group_stats(hidden[where, :], stats1, where)
        unscaled = unit * par[where, GAIN + 1 : GAIN + 2] + par[where, BIAS + 1 : BIAS + 2]
        pre = unscaled * (1.0 + par[where, SCALE : SCALE + 1]) + par[where, SHIFT : SHIFT + 1]
        low = jax.nn.silu(pre).astype(BF)
        second[where, :] = low
        put_taps(col, masks, low.astype(F32), group * BLOCK, 512, 0, 1)
        return carry

    lax.fori_loop(0, 512 // BLOCK, norm_one, 0)
    over_yz(4)
    over_yz(5)
    diagonal(3)
    own_weights.wait()
    conv_part(resid, True, 0, CONVB + 1)
    complete(2)
    complete(3)
    peer_weights = fetch(sems, 4, conv_peer.at[1], full.at[:, away, :])
    diagonal(4)
    diagonal(5)
    conv_part(resid, True, 512, CONVB + 1)
    peer_weights.wait()
    conv_part(resid, False, 0, CONVB + 1)
    conv_part(resid, False, 512, CONVB + 1)
    for image, base in ((own, half * 256), (peer, (1 - half) * 256)):

        def norm_two(group, carry, image=image, base=base):
            where = rows(base + group * BLOCK, BLOCK)
            total = resid[where, :] + image[rows(group * BLOCK, BLOCK), :].astype(F32)
            resid[where, :] = total
            unit = group_stats(total, stats2, where)
            normed[where, :] = (unit * par[where, GAIN + 2 : GAIN + 3] + par[where, BIAS + 2 : BIAS + 3]).astype(BF)
            return carry

        lax.fori_loop(0, 256 // BLOCK, norm_two, 0)
    complete(4)
    complete(5)
    cot_copy.wait_recv()
    for piece in range(PIECES):
        copy(piece, 0, block(), 32, to_x).wait_send()
        for kind, start, count in (
            (1, block(), 32), (2, block(), 32), (5, block(), 32),
            (3, block(0, 0, 1), 16), (7, block(0, 0, 1), 32),
            (4, block(0, 1, 0) + 16, 16), (6, block(0, 1, 0), 32),
            (8, block(0, 1, 1), 16), (9, block(0, 1, 1) + 16, 16),
        ):
            copy(piece, kind, start, count, to_x).wait_send()
    picture.wait_send()
    block_copy.wait_send()
    cot_copy.wait_send()


def forward_call(timesteps, classes, *args):
    arrays, specs = operands((Scalars(timesteps), Scalars(classes)) + args)
    images, cotangent, conv_weight, qkv_weight, proj_weight = arrays[-5:]
    width = arrays[-6].shape[1]
    half_bf = out((256, PIX), BF)
    full_bf = out((512, PIX), BF)
    full_f32 = out((512, PIX), F32)
    stats = out((512, 2), F32)
    dma = pltpu.SemaphoreType.DMA
    half_scratch = pltpu.VMEM((256, PIX), BF)
    return pl.pallas_call(
        forward,
        out_shape=[
            out((512, 11), F32),
            out((2, width + 128), F32),
            half_bf,
            half_bf,
            out(conv_weight.shape, BF),
            out(qkv_weight.shape, BF),
            out(proj_weight.shape, BF),
            full_bf, half_bf, half_bf, full_f32, stats, stats, full_bf, full_f32, stats, full_bf,
        ],
        in_specs=specs,
        out_specs=[VMEM] * 2 + [ANYWHERE] * 5 + [VMEM] * 10,
        scratch_shapes=[
            dma((PIECES, KINDS)), dma((PIECES, KINDS)), dma((3,)), dma((3,)), dma((5,)),
            pltpu.VMEM((256, 128), F32),
            pltpu.VMEM((256, 128), F32),
            pltpu.VMEM((16, 256), F32),
            pltpu.VMEM(arrays[-6].shape, BF),
            half_scratch, half_scratch, half_scratch,
            pltpu.VMEM((256, 2), F32),
            pltpu.VMEM((9 * 512, PIX), BF),
            pltpu.VMEM((9, 512, 512), BF),
        ],
        cost_estimate=pl.CostEstimate(flops=2 * 10**10, bytes_accessed=100 * 2**20, transcendentals=0),
        compiler_params=pltpu.CompilerParams(
            collective_id=1, has_side_effects=True, vmem_limit_bytes=58 * 2**20
        ),
    )(*arrays)


SENDS = 12


class Sum:
    def __init__(self, source, total, scratch, planes):
        self.source, self.total, self.planes = source, total, planes
        self.sends, self.recvs, self.core_in, self.first, self.y_in, self.second, self.z_in, self.result = scratch[:8]
        if planes:
            self.middle, self.x_in = scratch[8:10]
        self.half = lax.axis_index("head")
        self.place, self.core, self.up, self.deep = position()
        self.steps = [self.start, self.core_done, self.y_done, self.z_done]
        if planes:
            self.steps.append(self.x_done)
        self.steps += [self.z_back, self.y_back, self.finish]
        self.open = []
        self.count = 0

    def advance(self):
        if self.count < len(self.steps):
            self.steps[self.count]()
            self.count += 1

    def part(self, array, start, count):
        where = pl.ds(start, count)
        return array.at[:, where] if self.planes else array.at[where]

    def to_core(self):
        return {"batch": self.place + 1 - 2 * self.core}

    def to_y(self):
        return {"batch": self.place + 2 * (1 - 2 * self.up)}

    def to_z(self, ahead):
        return {"batch": (self.deep + ahead) % 4 * 4 + self.place % 4}

    def send(self, slot, source, dest, target):
        copy = remote(source, dest, self.sends, self.recvs, slot, target)
        copy.start()
        self.open.append(copy)

    def arrived(self, slot, dest):
        remote(dest, dest, self.sends, self.recvs, slot, self.to_core()).wait_recv()

    def of_core(self, core):
        return self.source.at[core] if self.planes else self.source.at[pl.ds(core * 8, 8)]

    def start(self):
        self.send(0, self.of_core(1 - self.core), self.core_in, self.to_core())

    def add(self, dest, left, *right):
        total = left[...].astype(F32)
        for term in right:
            total = total + term[...].astype(F32)
        dest[...] = total.astype(BF)

    def core_done(self):
        self.arrived(0, self.core_in)
        self.add(self.first, self.of_core(self.core), self.core_in)
        self.send(1, self.part(self.first, (1 - self.up) * 4, 4), self.y_in, self.to_y())

    def y_done(self):
        self.arrived(1, self.y_in)
        self.add(self.second, self.part(self.first, self.up * 4, 4), self.y_in)
        for ahead in (2, 1, 3):
            chunk = self.part(self.second, (self.deep + ahead) % 4, 1)
            self.send(1 + ahead, chunk, self.z_in.at[ahead - 1], self.to_z(ahead))

    def z_done(self):
        for ahead in (1, 2, 3):
            self.arrived(1 + ahead, self.z_in.at[ahead - 1])
        mine = self.part(self.second, self.deep, 1)
        terms = [self.z_in.at[number] for number in range(3)]
        if self.planes:
            self.add(self.middle, mine, *terms)
            self.send(10, self.middle.at[1 - self.half], self.x_in, {"head": 1 - self.half})
        else:
            self.add(self.result, mine, *terms)
            self.give()

    def x_done(self):
        self.arrived(10, self.x_in)
        self.add(self.result, self.middle.at[self.half], self.x_in)
        self.give()

    def chunks(self, start, count):
        return self.total.at[pl.ds(start, count)]

    def chunk(self, deep):
        return self.core * 8 + self.up * 4 + deep

    def give(self):
        mine = self.chunks(self.chunk(self.deep), 1)
        for ahead in (2, 1, 3):
            self.send(4 + ahead, self.result, mine, self.to_z(ahead))
        self.kept = pltpu.make_async_copy(self.result, mine, self.sends.at[11])
        self.kept.start()

    def z_back(self):
        for ahead in (1, 2, 3):
            self.arrived(4 + ahead, self.chunks(self.chunk((self.deep + 4 - ahead) % 4), 1))
        self.kept.wait()
        part = self.chunks(self.chunk(0), 4)
        self.send(8, part, part, self.to_y())

    def y_back(self):
        self.arrived(8, self.chunks(self.core * 8 + (1 - self.up) * 4, 4))
        part = self.chunks(self.core * 8, 8)
        self.send(9, part, part, self.to_core())

    def finish(self):
        self.arrived(9, self.chunks((1 - self.core) * 8, 8))
        for copy in self.open:
            copy.wait_send()


def sum_scratch(tail, planes):
    lead = (2,) if planes else ()
    shapes = [
        pltpu.SemaphoreType.DMA((SENDS,)),
        pltpu.SemaphoreType.DMA((SENDS,)),
        pltpu.VMEM(lead + (8,) + tail, BF),
        pltpu.VMEM(lead + (8,) + tail, BF),
        pltpu.VMEM(lead + (4,) + tail, BF),
        pltpu.VMEM(lead + (4,) + tail, BF),
        pltpu.VMEM((3,) + lead + (1,) + tail, BF),
        pltpu.VMEM((1,) + tail, BF),
    ]
    if planes:
        shapes += [pltpu.VMEM((2, 1) + tail, BF), pltpu.VMEM((1,) + tail, BF)]
    return shapes


def weight_back(grads, chunk_taps, col, turned):
    for tap in chunk_taps:
        result = mm(col[tap * 256 : (tap + 1) * 256, :], turned[:PIX, :])
        result = result + mm(col[(9 + tap) * 256 : (10 + tap) * 256, :], turned[PIX:, :])
        result = result.astype(BF)
        for part in range(16):
            grads[part, tap] = result[part * 16 : (part + 1) * 16]


PARTS = ((0, 3), (3, 6), (6, 9))


def backward(
    live_count, grad_branch, normed, grad_q, grad_k, grad_v, mixed, grad_out, resid, hidden, second, second_peer,
    first, first_other, first_peer, grad_resid, images, image_peer, w_own, w_peer, p_own, p_peer,
    stats0, stats1, par, small2, pre_embed, emb_weight,
    square_sum, sum1, sum0, images_grad, far_in, block_out, sums, class_rows, mod_out, pre_out,
    sems, sends, recvs, all_sends, all_recvs,
    squares, grads1, grads0, col, turned, full, slope_in, wide_in, source_in, branch_in, hidden_in, grad_hidden,
    far, columns, flat, mod, mod_send, pres, rows_own, rows_in, total, total_in,
    *scratch,
):
    half = lax.axis_index("head")
    place, core, up, deep = position()
    to_x = {"head": 1 - half}
    others = [{"batch": (place + ahead) % 16} for ahead in range(1, 16)]
    near, away = rows(half * 256, 256), rows((1 - half) * 256, 256)
    keep = (half < live_count[0]).astype(F32)
    exchanges = []

    staged = [
        fetch(sems, number, source, col.at[pl.ds(number * 512, 512)])
        for number, source in enumerate((grad_q, grad_k, grad_v, mixed, normed, grad_out))
    ]
    weights = fetch_conv(sems.at[pl.ds(6, 2)], full, half, 1, w_own, w_peer)
    late = fetch(sems, 8, hidden, wide_in)
    inputs = (
        fetch(sems, 9, second, source_in.at[0]),
        fetch(sems, 10, second_peer, source_in.at[1]),
    )
    meet([to_x] + others)

    def send(slot, source, dest, target):
        copy = remote(source, dest, sends, recvs, slot, target)
        copy.start()
        exchanges.append(copy)
        return copy

    branch_copy = send(0, grad_branch.at[away], branch_in, to_x)

    chains = [Sum(squares, square_sum, scratch[:10], True)]
    scratch = scratch[10:]
    for source, dest in ((grads1, sum1), (grads0, sum0)):
        for low, high in PARTS:
            where = pl.ds(low, high - low)
            chains.append(Sum(source.at[:, where], dest.at[:, where], scratch[:8], False))
            scratch = scratch[8:]

    def advance(*numbers):
        for number in numbers:
            chains[number].advance()

    wait(staged)
    for which, right in enumerate((4, 4, 4, 5)):
        result = mm(
            col[which * 512 : (which + 1) * 512, :], col[right * 512 : (right + 1) * 512, :], NT
        ).astype(BF)
        for part in range(32):
            plane, chunk = part // 16, part % 16
            squares[chunk // 8, plane, chunk % 8, which] = result[part * 16 : (part + 1) * 16]
    advance(0)

    masks = edge_masks(-1)
    taps_of(col, masks, grad_branch, 0, 512, 0, -1)
    wait(weights)

    def conv_back(column):
        result = None
        for tap in range(9):
            term = mm(full[tap], col[tap * 512 : (tap + 1) * 512, column : column + 512], TN)
            result = term if result is None else result + term
        slope_in[:, column : column + 512] = result

    conv_back(0)
    advance(0)
    conv_back(512)
    weights = fetch_conv(sems.at[pl.ds(6, 2)], full, half, 0, w_own, w_peer)
    columns[...] = jnp.zeros_like(columns)
    columns[:, 7:11] = small2[...]
    late.wait()

    def back_one(group, carry):
        where = rows(group * BLOCK, BLOCK)
        unit = unit_of(wide_in[where, :], stats1, where)
        gain = par[where, GAIN + 1 : GAIN + 2]
        unscaled = unit * gain + par[where, BIAS + 1 : BIAS + 2]
        scale = 1.0 + par[where, SCALE : SCALE + 1]
        grad_pre = slope_in[where, :] * silu_slope(unscaled * scale + par[where, SHIFT : SHIFT + 1])
        grad = grad_pre * scale
        low = unit_back(grad * gain, unit, stats1[where, 1:2]).astype(BF)
        grad_hidden[where, :] = low
        columns[where, 2:3] = row_sum(grad_pre * unscaled)
        columns[where, 3:4] = row_sum(grad_pre)
        columns[where, 4:5] = row_sum(grad * unit)
        columns[where, 5:6] = row_sum(grad)
        columns[where, 6:7] = row_sum(low.astype(F32))
        return carry

    lax.fori_loop(0, 512 // BLOCK, back_one, 0)
    hidden_copy = send(1, grad_hidden.at[away], hidden_in, to_x)
    late = fetch(sems, 8, grad_resid, wide_in)
    flat[...] = columns[...].T[0:16]
    mod[place, half] = flat[2:4, near]
    mod_send[...] = flat[2:4, away]
    send(2, mod_send, mod.at[place, half], to_x)
    pres[place] = pre_embed[...]
    for ahead, target in enumerate(others):
        remote(pres.at[place], pres.at[place], all_sends, all_recvs, ahead, target).start()

    branch_copy.wait_recv()
    pair = col.at[pl.ds(9 * 256, 9 * 256)]
    taps_of(col, masks, grad_branch.at[near], 0, 256, 0, -1)
    taps_of(pair, masks, branch_in, 0, 256, 0, -1)
    wait(inputs)
    turned[:PIX, :] = source_in[0].T
    turned[PIX:, :] = source_in[1].T
    inputs = (
        fetch(sems, 9, first, source_in.at[0]),
        fetch(sems, 10, first_other, source_in.at[1, near]),
        fetch(sems, 11, first_peer, source_in.at[1, away]),
    )
    weight_back(grads1, range(*PARTS[0]), col, turned)
    advance(1)
    weight_back(grads1, range(*PARTS[1]), col, turned)
    advance(0, 2, 1)
    weight_back(grads1, range(*PARTS[2]), col, turned)
    advance(3, 2)
    remote(mod_send, mod.at[place, 1 - half], sends, recvs, 2, to_x).wait_recv()
    for ahead, target in enumerate(others):
        remote(mod.at[place], mod.at[place], all_sends, all_recvs, 15 + ahead, target).start()

    taps_of(col, masks, grad_hidden.at[near], 0, 256, 0, -1)
    advance(3, 1)
    hidden_copy.wait_recv()
    taps_of(pair, masks, hidden_in, 0, 256, 0, -1)
    wait(inputs)
    turned[:PIX, :] = source_in[0].T
    turned[PIX:, :] = source_in[1].T
    picture = source_in.at[0]
    inputs = (
        fetch(sems, 9, images.at[half], picture.at[near]),
        fetch(sems, 10, image_peer, picture.at[away]),
        fetch(sems, 0, mixed, source_in.at[1]),
    )
    advance(2)
    weight_back(grads0, range(*PARTS[0]), col, turned)
    advance(4)
    weight_back(grads0, range(*PARTS[1]), col, turned)
    advance(5, 4, 0, 3)
    weight_back(grads0, range(*PARTS[2]), col, turned)
    advance(6, 5, 0)

    squeezed = fetch_square(sems.at[pl.ds(1, 2)], 0, turned.at[pl.ds(0, 512)], half, p_own, p_peer)
    taps_of(col, masks, grad_hidden, 0, 512, 0, -1)
    advance(6, 1)
    wait(weights)
    conv_back(0)
    advance(2, 0, 4)
    conv_back(512)
    advance(3, 1, 5)
    wait(inputs)
    late.wait()
    for base, mine in ((half * 256, True), ((1 - half) * 256, False)):

        def back_zero(group, carry, base=base, mine=mine):
            here = rows(group * BLOCK, BLOCK)
            where = rows(base + group * BLOCK, BLOCK)
            unit = unit_of(picture[where, :].astype(F32), stats0, where)
            gain = par[where, GAIN : GAIN + 1]
            grad = slope_in[where, :] * silu_slope(unit * gain + par[where, BIAS : BIAS + 1])
            result = wide_in[where, :] + unit_back(grad * gain, unit, stats0[where, 1:2])
            if mine:
                images_grad[here, :] = result
            else:
                far[here, :] = result.astype(BF)
            columns[where, 0:1] = row_sum(grad * unit)
            columns[where, 1:2] = row_sum(grad)
            return carry

        lax.fori_loop(0, 256 // BLOCK, back_zero, 0)
        if mine:
            advance(0, 2, 6)
        else:
            advance(3, 1, 4)
    send(3, far, far_in, to_x)
    late = fetch(sems, 8, resid, wide_in)

    flat[...] = columns[...].T[0:16]
    total[0] = flat[:, away]
    send(4, total.at[0], total_in.at[0], to_x)

    wait(squeezed)
    late.wait()
    for column in range(0, PIX, 512):
        where = slice(column, column + 512)
        result = wide_in[:, where] + mm(turned[:512, :], source_in[1, :, where], TN) + par[:, PROJB : PROJB + 1]
        col[0:512, where] = (result * keep).astype(BF)
    block = col.at[pl.ds(0, 512)]
    send(6, block.at[away], block_out.at[half], to_x)
    kept = fetch(sems, 3, block.at[near], block_out.at[half])
    advance(0, 2, 5)

    def landed(slot, step):
        remote(total.at[0], total_in.at[step], sends, recvs, slot, to_x).wait_recv()

    landed(4, 0)
    total[1] = flat[:, near] + total_in[0]
    send(7, total.at[1], total_in.at[1], {"batch": place + 1 - 2 * core})
    advance(3, 6)

    for ahead in range(15):
        origin = (place + 15 - ahead) % 16
        remote(pres.at[origin], pres.at[origin], all_sends, all_recvs, ahead, to_x).wait_recv()
        remote(mod.at[origin], mod.at[origin], all_sends, all_recvs, 15 + ahead, to_x).wait_recv()
    width = emb_weight.shape[2]
    result = None
    for which in range(2):
        factor = jnp.concatenate([mod[:, 0, which, :], mod[:, 1, which, :]], 0)
        term = mm(split(factor, 0), emb_weight[which])
        result = term if result is None else result + term
    result = result[0:32] + result[32:64] + result[64:96]
    rows_own[0] = result[0:16]
    rows_own[1] = result[16:32]
    send(5, rows_own, rows_in, to_x)
    landed(7, 1)
    total[2] = total[1] + total_in[1]
    send(8, total.at[2], total_in.at[2], {"batch": place + 2 * (1 - 2 * up)})
    advance(4, 1, 5)
    landed(8, 2)
    total[3] = total[2] + total_in[2]
    for ahead in (1, 2, 3):
        send(8 + ahead, total.at[3], total_in.at[3 + deep], {"batch": (deep + ahead) % 4 * 4 + place % 4})
    total_in[3 + deep] = total[3]
    advance(2, 6, 3)
    for ahead in (1, 2, 3):
        landed(8 + ahead, 3 + (deep + 4 - ahead) % 4)
    sums[...] = (total_in[3] + total_in[4]) + (total_in[5] + total_in[6])
    remote(rows_own, rows_in, sends, recvs, 5, to_x).wait_recv()
    for slot in range(2):
        class_rows[slot] = (rows_own[slot] + rows_in[slot]) * silu_slope(pres[:, slot, :width])
    remote(far, far_in, sends, recvs, 3, to_x).wait_recv()
    mod_out[...] = mod[...]
    pre_out[...] = pres[...]
    for _ in range(8):
        advance(0, 1, 2, 3, 4, 5, 6)
    remote(block.at[away], block_out.at[1 - half], sends, recvs, 6, to_x).wait_recv()
    kept.wait()
    for copy in exchanges:
        copy.wait_send()
    for ahead, target in enumerate(others):
        remote(pres.at[place], pres.at[place], all_sends, all_recvs, ahead, target).wait_send()
        remote(mod.at[place], mod.at[place], all_sends, all_recvs, 15 + ahead, target).wait_send()


def backward_call(*args):
    arrays, specs = operands(args)
    dma = pltpu.SemaphoreType.DMA
    scratch = [
        dma((12,)), dma((12,)), dma((12,)), dma((30,)), dma((30,)),
        pltpu.VMEM((2, 2, 8, 4, 16, 512), BF),
        pltpu.VMEM((16, 9, 16, 512), BF),
        pltpu.VMEM((16, 9, 16, 512), BF),
        pltpu.VMEM((9 * 512, PIX), BF),
        pltpu.VMEM((2 * PIX, 512), BF),
        pltpu.VMEM((9, 512, 512), BF),
        pltpu.VMEM((512, PIX), F32),
        pltpu.VMEM((512, PIX), F32),
        pltpu.VMEM((2, 512, PIX), BF),
        pltpu.VMEM((256, PIX), BF),
        pltpu.VMEM((256, PIX), BF),
        pltpu.VMEM((512, PIX), BF),
        pltpu.VMEM((256, PIX), BF),
        pltpu.VMEM((512, 128), F32),
        pltpu.VMEM((16, 512), F32),
        pltpu.VMEM((16, 2, 2, 256), F32),
        pltpu.VMEM((2, 256), F32),
        pltpu.VMEM((16, 2, 1024 + 128), F32),
        pltpu.VMEM((2, 16, 1024), F32),
        pltpu.VMEM((2, 16, 1024), F32),
        pltpu.VMEM((4, 16, 256), F32),
        pltpu.VMEM((7, 16, 256), F32),
    ]
    scratch += sum_scratch((4, 16, 512), True)
    for low, high in PARTS * 2:
        scratch += sum_scratch((high - low, 16, 512), False)
    outs = [
        (out((16, 4, 16, 512), BF), ANYWHERE),
        (out((16, 9, 16, 512), BF), ANYWHERE),
        (out((16, 9, 16, 512), BF), ANYWHERE),
        (out((256, PIX), F32), VMEM),
        (out((256, PIX), BF), ANYWHERE),
        (out((2, 256, PIX), BF), ANYWHERE),
        (out((16, 256), F32), VMEM),
        (out((2, 16, 1024), F32), VMEM),
        (out((16, 2, 2, 256), F32), VMEM),
        (out((16, 2, 1024 + 128), F32), VMEM),
    ]
    return pl.pallas_call(
        backward,
        out_shape=[o for o, _ in outs],
        in_specs=specs,
        out_specs=[spec for _, spec in outs],
        scratch_shapes=scratch,
        cost_estimate=pl.CostEstimate(flops=4 * 10**10, bytes_accessed=200 * 2**20, transcendentals=0),
        compiler_params=pltpu.CompilerParams(
            collective_id=2, has_side_effects=True, vmem_limit_bytes=60 * 2**20
        ),
    )(*arrays)


TRIPLES = ((0, 3), (3, 6), (6, 9))


def finish(
    sum0, sum1, squares, near, far, mod, pres, rows_in,
    conv, qkv, proj, images_grad, emb, table,
    ins, outs, low, low_square, wide, square, mine, other, grads, emb_out, table_out,
):
    half = lax.axis_index("head")
    width = rows_in.shape[2]
    reads = []
    for layer, source in enumerate((sum0, sum1)):
        for number, (start, stop) in enumerate(TRIPLES):
            taps = pl.ds(start, stop - start)
            reads.append(fetch(ins, layer * 3 + number, source.at[:, taps], low.at[layer, :, taps]))
    reads.append(fetch(ins, 6, squares, low_square))
    reads.append(fetch(ins, 7, near, mine))
    reads.append(fetch(ins, 8, far, other))
    writes = []

    def write(source, dest):
        writes.append(fetch(outs, len(writes), source, dest))

    numbers = lax.broadcasted_iota(jnp.int32, (32, table.shape[0]), 1)
    ids = jnp.concatenate([pres[:, slot, width : width + 1] for slot in range(2)], 0).astype(jnp.int32)
    chosen = (numbers == ids).astype(F32).astype(BF)
    class_rows = jnp.concatenate([rows_in[0], rows_in[1]], 0)
    table_out[...] = mm(jnp.concatenate([chosen] * 3, 0), split(class_rows, 0), TN)
    write(table_out, table)
    embed = jnp.concatenate([jax.nn.silu(pres[:, slot, :width]) for slot in range(2)], 0)
    parts = split(embed, 0)
    high, middle = parts[0:32], parts[32:64]
    for which in range(2):
        factor = split(jnp.concatenate([mod[:, slot, which, :] for slot in range(2)], 0), 0)
        left = jnp.concatenate([factor[0:32], factor[0:32], factor[32:64]], 0)
        emb_out[which] = mm(left, jnp.concatenate([high, middle, high], 0), TN)
    write(emb_out, emb)
    for layer in range(2):
        for number, (start, stop) in enumerate(TRIPLES):
            reads[layer * 3 + number].wait()
            for tap in range(start, stop):
                wide[layer, tap] = low[layer, :, tap].reshape(256, 512).astype(F32)
            taps = pl.ds(start, stop - start)
            write(wide.at[layer, taps], conv.at[layer, taps])
    reads[6].wait()
    for which in range(4):
        square[which] = low_square[:, which].reshape(256, 512).astype(F32)
    write(square.at[pl.ds(0, 3)], qkv)
    write(square.at[3], proj)
    reads[7].wait()
    reads[8].wait()
    grads[half] = mine[...]
    grads[1 - half] = other[...].astype(F32)
    write(grads, images_grad)
    wait(writes)


def finish_call(sum0, sum1, squares, near, far, mod, pres, rows_in, table_shape):
    width = table_shape[1]
    shapes = [
        (2, 9, 256, 512),
        (3, 256, 512),
        (256, 512),
        (2, 256, PIX),
        (2, 256, width),
        table_shape,
    ]
    dma = pltpu.SemaphoreType.DMA
    return pl.pallas_call(
        finish,
        out_shape=[out(shape, F32) for shape in shapes],
        in_specs=[ANYWHERE] * 5 + [VMEM] * 3,
        out_specs=[ANYWHERE] * len(shapes),
        scratch_shapes=[
            dma((9,)), dma((11,)),
            pltpu.VMEM((2,) + sum0.shape, BF),
            pltpu.VMEM(squares.shape, BF),
            pltpu.VMEM(shapes[0], F32),
            pltpu.VMEM((4, 256, 512), F32),
            pltpu.VMEM((256, PIX), F32),
            pltpu.VMEM((256, PIX), BF),
            pltpu.VMEM(shapes[3], F32),
            pltpu.VMEM(shapes[4], F32),
            pltpu.VMEM(shapes[5], F32),
        ],
        compiler_params=pltpu.CompilerParams(vmem_limit_bytes=58 * 2**20),
    )(sum0, sum1, squares, near, far, mod, pres, rows_in)


def paired(
    images,
    timesteps,
    classes,
    live_count,
    norm_gain,
    norm_bias,
    conv_weight,
    conv_bias,
    emb_weight,
    emb_bias,
    class_table,
    qkv_weight,
    proj_weight,
    proj_bias,
    cotangent,
):
    half = lax.axis_index("head")

    def across(value):
        return lax.ppermute(value, "head", [(0, 1), (1, 0)])

    (
        par, pre_embed, image_peer, cot_peer, conv_peer, q_peer, p_peer,
        first, first_near, first_other, hidden, stats0, stats1, second, resid, stats2, normed,
    ) = forward_call(
        timesteps, classes, norm_gain, norm_bias, conv_bias, proj_bias[None], emb_bias, emb_weight,
        *map(Far, (class_table, images, cotangent, conv_weight, qkv_weight, proj_weight)),
    )
    first_peer = across(first_near)
    second_peer = across(second)
    full_bf = out((512, PIX), BF)
    full_f32 = out((512, PIX), F32)
    square = pltpu.VMEM((512, 512), BF)
    wide_bf = pltpu.VMEM((512, PIX), BF)
    wide_f32 = pltpu.VMEM((512, PIX), F32)
    pixels = pltpu.VMEM((PIX, PIX), BF)
    mixed, grad_q, grad_k, grad_v, grad_out, grad_resid, grad_branch, small2 = kernel_call(
        attention,
        [full_bf] * 5 + [full_f32, full_bf, out((512, 4), F32)],
        [pltpu.VMEM((3, 512, 512), BF), square] + [wide_bf] * 4 + [pixels] * 2 + [wide_f32] * 2,
        3 * 10**10,
        Scalars(live_count), normed, Far(resid), stats2, par, Far(cotangent), Far(cot_peer),
        Far(qkv_weight), Far(q_peer), Far(proj_weight), Far(p_peer),
    )
    square_sum, conv_sum1, conv_sum0, near, far, block_out, sums, class_rows, mod, pre_all = backward_call(
        Scalars(live_count), grad_branch,
        *map(Far, (normed, grad_q, grad_k, grad_v, mixed, grad_out, resid, hidden, second, second_peer)),
        *map(Far, (first, first_other, first_peer, grad_resid, images, image_peer, conv_weight, conv_peer)),
        Far(proj_weight), Far(p_peer), stats0, stats1, par, small2, pre_embed, emb_weight,
    )
    conv_total, qkv_total, proj_total, images_grad, emb_total, table_total = finish_call(
        conv_sum0, conv_sum1, square_sum, near, far, mod, pre_all, class_rows, class_table.shape
    )
    return (
        block_out,
        images_grad,
        jnp.stack([sums[0], sums[4], sums[7]]),
        jnp.stack([sums[1], sums[5], sums[8]]),
        conv_total,
        jnp.stack([sums[6], sums[9]]),
        emb_total,
        sums[2:4],
        table_total,
        qkv_total,
        proj_total,
        sums[10],
    )


def solution(mesh):
    in_specs = (
        P("batch", "head", None),
        P("batch"),
        P("batch"),
        P("batch"),
        P(None, "head"),
        P(None, "head"),
        P(None, None, "head", None),
        P(None, "head"),
        P(None, "head", None),
        P(None, "head"),
        P(),
        P(None, "head", None),
        P("head", None),
        P("head"),
        P("batch", "head", None),
    )
    out_specs = (
        P("batch", "head", None),
        P("batch", "head", None),
        P(None, "head"),
        P(None, "head"),
        P(None, None, "head", None),
        P(None, "head"),
        P(None, "head", None),
        P(None, "head"),
        P(),
        P(None, "head", None),
        P("head", None),
        P("head"),
    )
    body = shards
    if mesh.shape["head"] == 2 and mesh.shape["batch"] == 16:
        body = paired
    return jax.shard_map(body, mesh=mesh, in_specs=in_specs, out_specs=out_specs, check_vma=False)
```

```python
import math

import jax
import jax.numpy as jnp
from jax import lax
from jax.experimental import pallas as pl
from jax.experimental.pallas import tpu as pltpu
from jax.sharding import PartitionSpec as P

C = 512
GROUPS = 32
HEADS = 8
SIDE = 32


EPS = 1e-05
HIGH = lax.Precision.HIGHEST
CONTRACT_FIRST = (((0,), (0,)), ((), ()))
CONTRACT_LAST = (((1,), (1,)), ((), ()))


def silu_slope(values):
    sigma = jax.nn.sigmoid(values)
    return sigma * (1.0 + values * (1.0 - sigma))


def moved(source, grid_side, row_step, col_step):
    grid = source.reshape(source.shape[0], grid_side, grid_side)
    padded = jnp.pad(grid, ((0, 0), (1, 1), (1, 1)))
    window = padded[
        :, 1 + row_step : 1 + row_step + grid_side, 1 + col_step : 1 + col_step + grid_side
    ]
    return window.reshape(source.shape)


def group_unit(source, groups):
    grouped = source.reshape(groups, -1)
    centre = grouped - jnp.mean(grouped, axis=1, keepdims=True)
    inverse = lax.rsqrt(jnp.mean(jnp.square(centre), axis=1, keepdims=True) + EPS)
    return ((centre * inverse).reshape(source.shape), inverse)


def group_back(grad_unit, unit_rows, inverse, groups):
    flat_grad = grad_unit.reshape(groups, -1)
    flat_unit = unit_rows.reshape(groups, -1)
    result = flat_grad - jnp.mean(flat_grad, axis=1, keepdims=True)
    result = (result - flat_unit * jnp.mean(flat_grad * flat_unit, axis=1, keepdims=True)) * inverse
    return result.reshape(grad_unit.shape)


def conv_apply(weight, source, grid_side):
    result = jnp.dot(
        weight[0], moved(source, grid_side, -1, -1), preferred_element_type=jnp.float32
    )
    for tap_index in range(1, 9):
        result = result + jnp.dot(
            weight[tap_index],
            moved(source, grid_side, tap_index // 3 - 1, tap_index % 3 - 1),
            preferred_element_type=jnp.float32,
        )
    return result


def conv_transpose(weight, grads, grid_side):
    result = lax.dot_general(
        weight[0], moved(grads, grid_side, 1, 1), CONTRACT_FIRST, preferred_element_type=jnp.float32
    )
    for tap_index in range(1, 9):
        result = result + lax.dot_general(
            weight[tap_index],
            moved(grads, grid_side, 1 - tap_index // 3, 1 - tap_index % 3),
            CONTRACT_FIRST,
            preferred_element_type=jnp.float32,
        )
    return result


def conv_weight_grads(grads, source, grid_side):
    return jnp.stack(
        [
            lax.dot_general(
                grads,
                moved(source, grid_side, tap_index // 3 - 1, tap_index % 3 - 1),
                CONTRACT_LAST,
                preferred_element_type=jnp.float32,
            )
            for tap_index in range(9)
        ]
    )


def features(timestep, emb_width):
    half_width = emb_width // 2
    freqs = jnp.exp(-math.log(10000.0) * jnp.arange(half_width, dtype=jnp.float32) / half_width)
    angles = timestep.astype(jnp.float32) * freqs
    return jnp.concatenate([jnp.cos(angles), jnp.sin(angles)])


def shards(
    images,
    timesteps,
    classes,
    live_count,
    norm_gain,
    norm_bias,
    conv_weight,
    conv_bias,
    emb_weight,
    emb_bias,
    class_table,
    qkv_weight,
    proj_weight,
    proj_bias,
    cotangent,
):
    slot_count, chan_dev, pixel_count = images.shape
    grid_side = SIDE
    groups = chan_dev // (C // GROUPS)
    head_size = C // HEADS
    heads_dev = chan_dev // head_size
    att_scale = head_size ** (-0.5)
    emb_dense = emb_weight.astype(jnp.float32)
    class_total, emb_width = class_table.shape

    def gather_channels(rows_low):
        return lax.all_gather(rows_low, "head", axis=0, tiled=True)

    def input_grad(which_conv, grad_rows):
        weight_cols = conv_weight[which_conv]
        return lax.psum_scatter(
            conv_transpose(weight_cols, grad_rows, grid_side).astype(jnp.bfloat16),
            "head",
            scatter_dimension=0,
            tiled=True,
        ).astype(jnp.float32)

    def per_slot(slot_index, carry):
        (
            outputs,
            grads_in,
            gain_acc,
            bias_acc,
            convw_acc,
            convb_acc,
            embw_acc,
            embb_acc,
            table_acc,
            qkv_acc,
            projw_acc,
            projb_acc,
        ) = carry
        picture = lax.dynamic_index_in_dim(images, slot_index, 0, keepdims=False).astype(
            jnp.float32
        )
        live_flag = (slot_index < live_count[0]).astype(jnp.float32)
        class_id = classes[slot_index]
        table_row = lax.dynamic_index_in_dim(class_table, class_id, 0, keepdims=False).astype(
            jnp.float32
        )
        pre_embed = features(timesteps[slot_index], emb_width) + table_row
        embed = jax.nn.silu(pre_embed)
        scale = jnp.dot(emb_dense[0], embed, precision=HIGH) + emb_bias[0]
        shift = jnp.dot(emb_dense[1], embed, precision=HIGH) + emb_bias[1]
        unit_zero, inverse_zero = group_unit(picture, groups)
        pre_first = unit_zero * norm_gain[0][:, None] + norm_bias[0][:, None]
        first_full = gather_channels(jax.nn.silu(pre_first).astype(jnp.bfloat16))
        hidden = conv_apply(conv_weight[0], first_full, grid_side) + conv_bias[0][:, None]
        unit_one, inverse_one = group_unit(hidden, groups)
        normed_one = unit_one * norm_gain[1][:, None] + norm_bias[1][:, None]
        pre_second = normed_one * (1.0 + scale[:, None]) + shift[:, None]
        second_full = gather_channels(jax.nn.silu(pre_second).astype(jnp.bfloat16))
        resid = picture + conv_apply(conv_weight[1], second_full, grid_side) + conv_bias[1][:, None]
        unit_two, inverse_two = group_unit(resid, groups)
        normed_full = gather_channels(
            (unit_two * norm_gain[2][:, None] + norm_bias[2][:, None]).astype(jnp.bfloat16)
        )
        query = (
            jnp.dot(qkv_weight[0], normed_full, preferred_element_type=jnp.float32)
            .astype(jnp.bfloat16)
            .reshape(heads_dev, head_size, pixel_count)
        )
        keys = (
            jnp.dot(qkv_weight[1], normed_full, preferred_element_type=jnp.float32)
            .astype(jnp.bfloat16)
            .reshape(heads_dev, head_size, pixel_count)
        )
        values = (
            jnp.dot(qkv_weight[2], normed_full, preferred_element_type=jnp.float32)
            .astype(jnp.bfloat16)
            .reshape(heads_dev, head_size, pixel_count)
        )
        scores = (
            jnp.einsum("hdi,hdj->hij", query, keys, preferred_element_type=jnp.float32) * att_scale
        )
        highest = jnp.max(scores, axis=2, keepdims=True)
        expo = jnp.exp(scores - highest)
        totals = jnp.sum(expo, axis=2, keepdims=True)
        log_total = highest + jnp.log(totals)
        weights = (expo / totals).astype(jnp.bfloat16)
        mixed = (
            jnp.einsum("hdj,hij->hdi", values, weights, preferred_element_type=jnp.float32)
            .astype(jnp.bfloat16)
            .reshape(chan_dev, pixel_count)
        )
        weight_cols = proj_weight
        proj_term = lax.psum_scatter(
            lax.dot_general(
                weight_cols, mixed, CONTRACT_FIRST, preferred_element_type=jnp.float32
            ).astype(jnp.bfloat16),
            "head",
            scatter_dimension=0,
            tiled=True,
        ).astype(jnp.float32)
        result = resid + proj_term + proj_bias[:, None]
        outputs = lax.dynamic_update_index_in_dim(
            outputs, (live_flag * result).astype(jnp.bfloat16), slot_index, 0
        )
        grad_low = lax.dynamic_index_in_dim(cotangent, slot_index, 0, keepdims=False)
        grad_out = live_flag * grad_low.astype(jnp.float32)
        grad_full = lax.all_gather(grad_low, "head", axis=0, tiled=True) * live_flag.astype(
            jnp.bfloat16
        )
        grad_mixed = jnp.dot(proj_weight, grad_full, preferred_element_type=jnp.float32).astype(
            jnp.bfloat16
        )
        projw_acc = projw_acc + lax.dot_general(
            mixed, grad_full, CONTRACT_LAST, preferred_element_type=jnp.float32
        )
        projb_acc = projb_acc + jnp.sum(grad_out, axis=1)
        again = (
            jnp.einsum("hdi,hdj->hij", query, keys, preferred_element_type=jnp.float32) * att_scale
        )
        probs = jnp.exp(again - log_total)
        grad_heads = grad_mixed.reshape(heads_dev, head_size, pixel_count)
        grad_probs = jnp.einsum(
            "hdi,hdj->hij", grad_heads, values, preferred_element_type=jnp.float32
        )
        grad_scores = (
            probs * (grad_probs - jnp.sum(grad_probs * probs, axis=2, keepdims=True))
        ).astype(jnp.bfloat16)
        grad_query = (
            jnp.einsum("hij,hdj->hdi", grad_scores, keys, preferred_element_type=jnp.float32)
            * att_scale
        ).astype(jnp.bfloat16)
        grad_keys = (
            jnp.einsum("hij,hdi->hdj", grad_scores, query, preferred_element_type=jnp.float32)
            * att_scale
        ).astype(jnp.bfloat16)
        grad_values = jnp.einsum(
            "hdi,hij->hdj", grad_heads, weights, preferred_element_type=jnp.float32
        ).astype(jnp.bfloat16)
        stacked = jnp.stack([grad_query, grad_keys, grad_values]).reshape(3, chan_dev, pixel_count)
        weight_cols = qkv_weight
        grad_normed = lax.psum_scatter(
            lax.dot_general(
                weight_cols,
                stacked,
                (((0, 1), (0, 1)), ((), ())),
                preferred_element_type=jnp.float32,
            ).astype(jnp.bfloat16),
            "head",
            scatter_dimension=0,
            tiled=True,
        ).astype(jnp.float32)
        qkv_acc = qkv_acc + lax.dot_general(
            stacked, normed_full, (((2,), (1,)), ((), ())), preferred_element_type=jnp.float32
        )
        grad_resid = grad_out + group_back(
            grad_normed * norm_gain[2][:, None], unit_two, inverse_two, groups
        )
        grad_branch = grad_resid.astype(jnp.bfloat16)
        grad_second = input_grad(1, grad_branch)
        grad_pre = grad_second * silu_slope(pre_second)
        scale_grad = jnp.sum(grad_pre * normed_one, axis=1)
        shift_grad = jnp.sum(grad_pre, axis=1)
        grad_normed_one = grad_pre * (1.0 + scale[:, None])
        grad_hidden = group_back(
            grad_normed_one * norm_gain[1][:, None], unit_one, inverse_one, groups
        ).astype(jnp.bfloat16)
        grad_first = input_grad(0, grad_hidden)
        grad_pre_first = grad_first * silu_slope(pre_first)
        picture_grad = grad_resid + group_back(
            grad_pre_first * norm_gain[0][:, None], unit_zero, inverse_zero, groups
        )
        grads_in = lax.dynamic_update_index_in_dim(grads_in, picture_grad, slot_index, 0)
        gain_acc = gain_acc + jnp.stack(
            [
                jnp.sum(grad_pre_first * unit_zero, axis=1),
                jnp.sum(grad_normed_one * unit_one, axis=1),
                jnp.sum(grad_normed * unit_two, axis=1),
            ]
        )
        bias_acc = bias_acc + jnp.stack(
            [
                jnp.sum(grad_pre_first, axis=1),
                jnp.sum(grad_normed_one, axis=1),
                jnp.sum(grad_normed, axis=1),
            ]
        )
        convw_acc = convw_acc + jnp.stack(
            [
                conv_weight_grads(grad_hidden, first_full, grid_side),
                conv_weight_grads(grad_branch, second_full, grid_side),
            ]
        )
        convb_acc = convb_acc + jnp.stack(
            [
                jnp.sum(grad_hidden.astype(jnp.float32), axis=1),
                jnp.sum(grad_branch.astype(jnp.float32), axis=1),
            ]
        )
        embw_acc = embw_acc + jnp.stack(
            [scale_grad[:, None] * embed[None, :], shift_grad[:, None] * embed[None, :]]
        )
        embb_acc = embb_acc + jnp.stack([scale_grad, shift_grad])
        grad_embed = jnp.dot(scale_grad, emb_dense[0], precision=HIGH) + jnp.dot(
            shift_grad, emb_dense[1], precision=HIGH
        )
        class_row = grad_embed * silu_slope(pre_embed)
        old_row = lax.dynamic_index_in_dim(table_acc, class_id, 0, keepdims=True)
        table_acc = lax.dynamic_update_index_in_dim(
            table_acc, old_row + class_row[None, :], class_id, 0
        )
        return (
            outputs,
            grads_in,
            gain_acc,
            bias_acc,
            convw_acc,
            convb_acc,
            embw_acc,
            embb_acc,
            table_acc,
            qkv_acc,
            projw_acc,
            projb_acc,
        )

    table_start = jnp.zeros(class_table.shape, jnp.float32)
    initial = (
        jnp.zeros(images.shape, jnp.bfloat16),
        jnp.zeros(images.shape, jnp.float32),
        jnp.zeros(norm_gain.shape, jnp.float32),
        jnp.zeros(norm_bias.shape, jnp.float32),
        jnp.zeros(conv_weight.shape, jnp.float32),
        jnp.zeros(conv_bias.shape, jnp.float32),
        jnp.zeros(emb_weight.shape, jnp.float32),
        jnp.zeros(emb_bias.shape, jnp.float32),
        table_start,
        jnp.zeros(qkv_weight.shape, jnp.float32),
        jnp.zeros(proj_weight.shape, jnp.float32),
        jnp.zeros(proj_bias.shape, jnp.float32),
    )
    final = lax.fori_loop(0, slot_count, per_slot, initial)
    (
        outputs,
        grads_in,
        gain_acc,
        bias_acc,
        convw_acc,
        convb_acc,
        embw_acc,
        embb_acc,
        table_acc,
        qkv_acc,
        projw_acc,
        projb_acc,
    ) = final
    table_total = lax.psum(table_acc, ("batch", "head"))
    summed = (
        lax.psum(gain_acc.astype(jnp.bfloat16), "batch").astype(jnp.float32),
        lax.psum(bias_acc.astype(jnp.bfloat16), "batch").astype(jnp.float32),
        lax.psum(convw_acc.astype(jnp.bfloat16), "batch").astype(jnp.float32),
        lax.psum(convb_acc.astype(jnp.bfloat16), "batch").astype(jnp.float32),
        lax.psum(embw_acc.astype(jnp.bfloat16), "batch").astype(jnp.float32),
        lax.psum(embb_acc.astype(jnp.bfloat16), "batch").astype(jnp.float32),
        lax.psum(qkv_acc.astype(jnp.bfloat16), "batch").astype(jnp.float32),
        lax.psum(projw_acc.astype(jnp.bfloat16), "batch").astype(jnp.float32),
        lax.psum(projb_acc.astype(jnp.bfloat16), "batch").astype(jnp.float32),
    )
    return (
        outputs,
        grads_in,
        summed[0],
        summed[1],
        summed[2],
        summed[3],
        summed[4],
        summed[5],
        table_total,
        summed[6],
        summed[7],
        summed[8],
    )


PIX = 1024
BLOCK = 128
BF = jnp.bfloat16
F32 = jnp.float32
NN = (((1,), (0,)), ((), ()))
TN = (((0,), (0,)), ((), ()))
NT = (((1,), (1,)), ((), ()))
VMEM = pl.BlockSpec(memory_space=pltpu.VMEM)
SMEM = pl.BlockSpec(memory_space=pltpu.SMEM)

GAIN, BIAS, CONVB, PROJB, SCALE, SHIFT = 0, 3, 6, 8, 9, 10


def mm(left, right, dims=NN):
    return lax.dot_general(left, right, dims, preferred_element_type=F32)


class Far:
    def __init__(self, array):
        self.array = array


ANYWHERE = pl.BlockSpec(memory_space=pl.ANY)


class Scalars(Far):
    pass


def operands(args):
    arrays = [arg.array if isinstance(arg, Far) else arg for arg in args]
    specs = []
    for arg in args:
        if isinstance(arg, Scalars):
            specs.append(SMEM)
        else:
            specs.append(ANYWHERE if isinstance(arg, Far) else VMEM)
    return arrays, specs


def kernel_call(kernel, outs, scratch, flops, *args):
    arrays, specs = operands(args)
    moved_bytes = sum(a.size * a.dtype.itemsize for a in arrays)
    moved_bytes += sum(math.prod(o.shape) * o.dtype.itemsize for o in outs)
    return pl.pallas_call(
        kernel,
        out_shape=outs,
        in_specs=specs,
        out_specs=[VMEM] * len(outs),
        scratch_shapes=[pltpu.SemaphoreType.DMA((8,))] + scratch,
        cost_estimate=pl.CostEstimate(flops=flops, bytes_accessed=moved_bytes, transcendentals=0),
        compiler_params=pltpu.CompilerParams(vmem_limit_bytes=56 * 2**20),
    )(*arrays)


def split(value, axis):
    parts = []
    for _ in range(3):
        part = value.astype(BF)
        parts.append(part)
        value = value - part.astype(F32)
    return jnp.concatenate(parts, axis)


def fetch(sems, slot, source, dest):
    copy = pltpu.make_async_copy(source, dest, sems.at[slot])
    copy.start()
    return copy


def out(shape, dtype):
    return jax.ShapeDtypeStruct(shape, dtype)


def rows(start, count):
    return pl.ds(pl.multiple_of(start, count), count)


def edge_masks(sign):
    pixel = lax.broadcasted_iota(jnp.int32, (1, PIX), 1)
    col, row = pixel % SIDE, pixel // SIDE
    table = {}
    for step in (-1, 1):
        moved_step = sign * step
        table["col", step] = ((col + moved_step >= 0) & (col + moved_step < SIDE)).astype(F32)
        table["row", step] = ((row + moved_step >= 0) & (row + moved_step < SIDE)).astype(F32)
    return table


def put_taps(dest, masks, values, first_row, depth, base, sign):
    count = values.shape[0]
    for col_step in (-1, 0, 1):
        across = values
        if col_step:
            across = pltpu.roll(values, (-sign * col_step) % PIX, 1) * masks["col", col_step]
        for row_step in (-1, 0, 1):
            copy = across
            if row_step:
                copy = pltpu.roll(across, (-sign * row_step * SIDE) % PIX, 1) * masks["row", row_step]
            tap = 3 * (row_step + 1) + col_step + 1
            dest[rows(tap * depth + first_row, count), base : base + PIX] = copy.astype(BF)


def taps_of(dest, masks, source, offset, depth, base, sign):
    for start in range(0, source.shape[0], 128):
        piece = source[start : start + 128, :].astype(F32)
        put_taps(dest, masks, piece, offset + start, depth, base, sign)


def fetch_conv(sems, full, half, which, own, peer):
    return (
        fetch(sems, 0, own.at[which], full.at[:, rows(half * 256, 256), :]),
        fetch(sems, 1, peer.at[which], full.at[:, rows((1 - half) * 256, 256), :]),
    )


def wait(copies):
    for copy in copies:
        copy.wait()


def conv_dots(dest, full, col, dims, finish):
    for column in range(0, PIX, 512):
        total = None
        for tap in range(9):
            term = mm(full[tap], col[tap * 512 : (tap + 1) * 512, column : column + 512], dims)
            total = term if total is None else total + term
        dest[:, column : column + 512] = finish(total, column)


def grouped(block):
    return block.reshape((-1, 16) + block.shape[1:])


def group_mean(block):
    return jnp.sum(block, axis=(1, 2), keepdims=True) * (1.0 / (16 * PIX))


def group_stats(block, stats, where):
    parts = grouped(block)
    centre = group_mean(parts)
    parts = parts - centre
    inverse = lax.rsqrt(group_mean(jnp.square(parts)) + EPS)
    count = block.shape[0]
    for column, value in enumerate((centre, inverse)):
        stats[where, column : column + 1] = jnp.broadcast_to(value, (count // 16, 16, 1)).reshape(count, 1)
    return (parts * inverse).reshape(block.shape)


def unit_of(block, stats, where):
    return (block - stats[where, 0:1]) * stats[where, 1:2]


def unit_back(grad, unit, inverse):
    parts, units = grouped(grad), grouped(unit)
    result = parts - group_mean(parts) - units * group_mean(parts * units)
    return result.reshape(grad.shape) * inverse


def row_sum(block):
    return jnp.sum(block, axis=1, keepdims=True)


def fetch_square(sems, slot, full, half, own, peer):
    count = own.shape[-2]
    near, far = rows(half * count, count), rows((1 - half) * count, count)
    if len(full.shape) == 3:
        near, far = (slice(None), near), (slice(None), far)
    return fetch(sems, slot, own, full.at[near]), fetch(sems, slot + 1, peer, full.at[far])


def attention(
    live_count, normed, resid, stats2, par, cotangent, cot_peer, q_own, q_peer, p_own, p_peer,
    squares, block, grad_resid, grad_branch, small,
    sems, wqkv, wp, query, keys, values, grad_mixed, mixed, grad_q, grad_k, grad_v, grad_out,
    grad_normed, resid_in, *pixel_scratch,
):
    half = lax.axis_index("head")
    live = (half < live_count[0]).astype(BF)
    arriving = fetch_square(sems, 0, wqkv, half, q_own, q_peer)
    later = fetch_square(sems, 2, wp, half, p_own, p_peer)
    later += (
        fetch(sems, 4, cotangent.at[half], grad_out.at[rows(half * 256, 256)]),
        fetch(sems, 5, cot_peer, grad_out.at[rows((1 - half) * 256, 256)]),
    )
    last = fetch(sems, 6, resid, resid_in)
    wait(arriving)
    for column in range(0, PIX, 512):
        where = slice(column, column + 512)
        query[:, where] = (mm(wqkv[0], normed[:, where]).astype(BF).astype(F32) * 0.125).astype(BF)
        keys[:, where] = mm(wqkv[1], normed[:, where]).astype(BF)
        values[:, where] = mm(wqkv[2], normed[:, where]).astype(BF)
    wait(later)
    grad_out[...] = grad_out[...] * live
    for column in range(0, PIX, 512):
        where = slice(column, column + 512)
        grad_mixed[:, where] = mm(wp[...], grad_out[:, where]).astype(BF)

    def head(number, weights, grad_scores):
        where = rows(number * 64, 64)
        q, k, v, g = query[where, :], keys[where, :], values[where, :], grad_mixed[where, :]
        scores = mm(k.T, q)
        low = jnp.exp(scores - jnp.max(scores, axis=0, keepdims=True)).astype(BF)
        weights[...] = low
        mix = mm(jnp.concatenate([v, jnp.ones((16, PIX), BF)], 0), low)
        inverse = 1.0 / mix[64:65]
        mix = mix[0:64] * inverse
        mixed[where, :] = mix.astype(BF)
        g = (g.astype(F32) * inverse).astype(BF)
        delta = jnp.sum(mix * g.astype(F32), axis=0, keepdims=True)
        inner = low * (mm(v.T, g) - delta).astype(BF)
        grad_scores[...] = inner
        grad_q[where, :] = (mm(k, inner) * 0.125).astype(BF)
        grad_k[where, :] = mm(grad_scores[...], q.T).T.astype(BF)
        grad_v[where, :] = mm(weights[...], g.T).T.astype(BF)

    def heads(index, carry):
        for number in range(4):
            head(index * 4 + number, pixel_scratch[2 * number], pixel_scratch[2 * number + 1])
        return carry

    lax.fori_loop(0, HEADS // 4, heads, 0)
    pairs = ((grad_q, normed), (grad_k, normed), (grad_v, normed), (mixed, grad_out))
    for which, (left, right) in enumerate(pairs):
        result = mm(left[...], right[...], NT).astype(BF)
        for part in range(32):
            plane, chunk = part // 16, part % 16
            squares[chunk // 8, plane, chunk % 8, which] = result[part * 16 : (part + 1) * 16]
    for column in range(0, PIX, 512):
        where = slice(column, column + 512)
        grad_normed[:, where] = (
            mm(wqkv[0], grad_q[:, where], TN)
            + mm(wqkv[1], grad_k[:, where], TN)
            + mm(wqkv[2], grad_v[:, where], TN)
        )
    last.wait()
    for column in range(0, PIX, 512):
        where = slice(column, column + 512)
        total = resid_in[:, where] + mm(wp[...], mixed[:, where], TN) + par[:, PROJB : PROJB + 1]
        block[:, where] = (total * live.astype(F32)).astype(BF)

    def back(group, carry):
        where = rows(group * BLOCK, BLOCK)
        unit = unit_of(resid_in[where, :], stats2, where)
        grad = grad_normed[where, :]
        outer = grad_out[where, :].astype(F32)
        total = outer + unit_back(grad * par[where, GAIN + 2 : GAIN + 3], unit, stats2[where, 1:2])
        low = total.astype(BF)
        grad_resid[where, :] = total
        grad_branch[where, :] = low
        small[where, 0:1] = row_sum(grad * unit)
        small[where, 1:2] = row_sum(grad)
        small[where, 2:3] = row_sum(low.astype(F32))
        small[where, 3:4] = row_sum(outer)
        return carry

    lax.fori_loop(0, 512 // BLOCK, back, 0)


def remote(source, dest, sends, recvs, slot, target):
    return pltpu.make_async_remote_copy(
        src_ref=source,
        dst_ref=dest,
        send_sem=sends.at[slot],
        recv_sem=recvs.at[slot],
        device_id=target,
        device_id_type=pl.DeviceIdType.MESH,
    )


def meet(targets):
    barrier = pltpu.get_barrier_semaphore()
    for target in targets:
        pl.semaphore_signal(barrier, inc=1, device_id=target, device_id_type=pl.DeviceIdType.MESH)
    pl.semaphore_wait(barrier, len(targets))


def position():
    place = lax.axis_index("batch")
    return place, place % 2, (place // 2) % 2, place // 4


PIECES = 6
KINDS = 10


def forward(
    timesteps, classes, norm_gain, norm_bias, conv_bias, proj_bias, emb_bias, emb_weight, class_table,
    images, cotangent, conv_weight, qkv_weight, proj_weight,
    par, pre_embed, image_peer, cot_peer, conv_peer, qkv_peer, proj_peer,
    first, first_near, first_other, hidden, stats0, stats1, second, resid, stats2, normed,
    sends, recvs, few_sends, few_recvs, sems, par_send, par_recv, lines, table, own, peer, other, spare, col, full,
):
    half = lax.axis_index("head")
    place, core, up, deep = position()
    z_low = deep % 2
    to_x = {"head": 1 - half}
    to_y = {"batch": place + 2 * (1 - 2 * up)}
    to_z = {"batch": place + 4 * (1 - 2 * z_low)}
    to_core = {"batch": place + (1 - 2 * core)}
    near, away = rows(half * 256, 256), rows((1 - half) * 256, 256)
    pictures = (
        fetch(sems, 0, images.at[half], own),
        fetch(sems, 1, images.at[1 - half], other),
    )
    table_copy = fetch(sems, 2, class_table, table)
    own_weights = fetch(sems, 3, conv_weight.at[0], full.at[:, near, :])
    meet([to_x, to_y, to_z, to_core])

    def block(flip_core=0, flip_y=0, flip_z=0):
        c = 1 - core if flip_core else core
        y = 1 - up if flip_y else up
        z = 1 - z_low if flip_z else z_low
        return (c + 2 * y + 4 * z) * 32

    def views(piece, local, start, count):
        where = rows(start, count)
        if piece < 4:
            taps = pl.ds(0, 5) if piece % 2 == 0 else pl.ds(5, 4)
            return (conv_weight if local else conv_peer).at[piece // 2, taps, where, :]
        if piece == 4:
            return (qkv_weight if local else qkv_peer).at[:, where, :]
        return (proj_weight if local else proj_peer).at[where, :]

    def copy(piece, kind, start, count, target, local=False):
        return remote(
            views(piece, local, start, count), views(piece, False, start, count),
            sends.at[piece], recvs.at[piece], kind, target,
        )

    def regions(flip_core):
        return (
            (block(flip_core), 32),
            (block(flip_core, 1), 32),
            (block(flip_core, 0, 1), 32),
            (block(flip_core, 1, 1), 16),
            (block(flip_core, 1, 1) + 16, 16),
        )

    mine, others = regions(0), regions(1)

    def arrived(piece, kind):
        start, count = mine[kind] if kind < 5 else others[kind - 5]
        copy(piece, kind, start, count, to_core).wait_recv()

    def over_x(piece):
        arrived(piece, 0)
        for kind, target in ((1, to_y), (2, to_z), (5, to_core)):
            copy(piece, kind, block(), 32, target).start()

    def over_yz(piece):
        arrived(piece, 2)
        copy(piece, 3, block(0, 0, 1), 16, to_y).start()
        copy(piece, 7, block(0, 0, 1), 32, to_core).start()
        arrived(piece, 1)
        copy(piece, 4, block(0, 1, 0) + 16, 16, to_z).start()
        copy(piece, 6, block(0, 1, 0), 32, to_core).start()

    def diagonal(piece):
        arrived(piece, 3)
        copy(piece, 8, block(0, 1, 1), 16, to_core).start()
        arrived(piece, 4)
        copy(piece, 9, block(0, 1, 1) + 16, 16, to_core).start()

    def complete(piece):
        for kind in range(5, 10):
            arrived(piece, kind)

    def fetch_x(*pieces):
        for piece in pieces:
            copy(piece, 0, block(), 32, to_x, local=True).start()

    fetch_x(0, 1)

    table_copy.wait()
    width = class_table.shape[1]
    numbers = lax.broadcasted_iota(jnp.int32, (1, table.shape[0]), 1)
    freqs = jnp.exp(
        lax.broadcasted_iota(jnp.int32, (1, width // 2), 1).astype(F32) * (-math.log(10000.0) / (width // 2))
    )
    for slot in range(2):
        chosen = (numbers == classes[slot]).astype(BF)
        angles = timesteps[slot].astype(F32) * freqs
        pre_embed[slot : slot + 1, : width // 2] = jnp.cos(angles)
        pre_embed[slot : slot + 1, width // 2 : width] = jnp.sin(angles)
        line = mm(jnp.broadcast_to(chosen, (8, table.shape[0])), table[...])
        pre_embed[slot : slot + 1, :width] += line[0:1]
        pre_embed[slot : slot + 1, width:] = jnp.broadcast_to(classes[slot].astype(F32), (1, 128))
    embed = jax.nn.silu(pre_embed[:, :width])
    own_row = jnp.where(half == 0, embed[0:1], embed[1:2])
    peer_row = jnp.where(half == 0, embed[1:2], embed[0:1])
    lines[...] = jnp.zeros_like(lines)
    lines[0:3] = norm_gain[...]
    lines[3:6] = norm_bias[...]
    lines[6:8] = conv_bias[...]
    lines[8:9] = proj_bias[...]
    lines[9:11] = emb_bias[...]
    turned = lines[...].T
    par_send[:, 0:11] = turned[:, 0:11]
    par[near, :] = turned[:, 0:11]
    for which in range(2):
        dense = emb_weight[which].astype(F32)
        par[near, SCALE + which : SCALE + which + 1] += row_sum(dense * own_row)
        par_send[:, SCALE + which : SCALE + which + 1] += row_sum(dense * peer_row)
    block_copy = remote(par_send, par_recv, few_sends, few_recvs, 1, to_x)
    block_copy.start()

    masks = edge_masks(1)
    wait(pictures)

    def norm_zero(source, dest, base, stats, offset, group):
        here = rows(group * BLOCK, BLOCK)
        where = rows(base + group * BLOCK, BLOCK)
        unit = group_stats(source[here, :].astype(F32), stats, rows(offset + group * BLOCK, BLOCK))
        low = jax.nn.silu(unit * par[where, GAIN : GAIN + 1] + par[where, BIAS : BIAS + 1]).astype(BF)
        dest[rows(offset + group * BLOCK, BLOCK), :] = low
        return low.astype(F32)

    def norm_near(group, carry):
        low = norm_zero(own, first, half * 256, stats0, half * 256, group)
        first_near[rows(group * BLOCK, BLOCK), :] = low.astype(BF)
        put_taps(col, masks, low, half * 256 + group * BLOCK, 512, 0, 1)
        return carry

    def norm_other(group, carry):
        norm_zero(other, first_other, half * 256, spare, 0, group)
        return carry

    lax.fori_loop(0, 256 // BLOCK, norm_near, 0)
    over_x(0)
    over_x(1)
    picture = remote(images.at[1 - half], image_peer, few_sends, few_recvs, 0, to_x)
    picture.start()
    lax.fori_loop(0, 256 // BLOCK, norm_other, 0)
    over_yz(0)
    over_yz(1)
    block_copy.wait_recv()
    par[away, :] = par_recv[:, 0:11]
    diagonal(0)
    fetch_x(2, 3)
    diagonal(1)
    picture.wait_recv()
    loaded = fetch(sems, 0, image_peer, peer)
    fetch_x(4, 5)
    cot_copy = remote(cotangent.at[1 - half], cot_peer, few_sends, few_recvs, 2, to_x)
    cot_copy.start()
    complete(0)
    complete(1)
    peer_weights = fetch(sems, 4, conv_peer.at[0], full.at[:, away, :])
    loaded.wait()

    def norm_far(group, carry):
        low = norm_zero(peer, first, (1 - half) * 256, stats0, (1 - half) * 256, group)
        put_taps(col, masks, low, (1 - half) * 256 + group * BLOCK, 512, 0, 1)
        return carry

    lax.fori_loop(0, 256 // BLOCK, norm_far, 0)
    own_weights.wait()

    def conv_part(dest, mine, column, bias):
        where = near if mine else away
        result = None
        for tap in range(9):
            term = mm(full[tap, where, :], col[tap * 512 : (tap + 1) * 512, column : column + 512])
            result = term if result is None else result + term
        dest[where, column : column + 512] = result + par[where, bias : bias + 1]

    conv_part(hidden, True, 0, CONVB)
    over_x(2)
    conv_part(hidden, True, 512, CONVB)
    over_x(3)
    peer_weights.wait()
    conv_part(hidden, False, 0, CONVB)
    over_yz(2)
    over_x(4)
    over_x(5)
    conv_part(hidden, False, 512, CONVB)
    over_yz(3)
    diagonal(2)
    own_weights = fetch(sems, 3, conv_weight.at[1], full.at[:, near, :])

    def norm_one(group, carry):
        where = rows(group * BLOCK, BLOCK)
        unit = group_stats(hidden[where, :], stats1, where)
        unscaled = unit * par[where, GAIN + 1 : GAIN + 2] + par[where, BIAS + 1 : BIAS + 2]
        pre = unscaled * (1.0 + par[where, SCALE : SCALE + 1]) + par[where, SHIFT : SHIFT + 1]
        low = jax.nn.silu(pre).astype(BF)
        second[where, :] = low
        put_taps(col, masks, low.astype(F32), group * BLOCK, 512, 0, 1)
        return carry

    lax.fori_loop(0, 512 // BLOCK, norm_one, 0)
    over_yz(4)
    over_yz(5)
    diagonal(3)
    own_weights.wait()
    conv_part(resid, True, 0, CONVB + 1)
    complete(2)
    complete(3)
    peer_weights = fetch(sems, 4, conv_peer.at[1], full.at[:, away, :])
    diagonal(4)
    diagonal(5)
    conv_part(resid, True, 512, CONVB + 1)
    peer_weights.wait()
    conv_part(resid, False, 0, CONVB + 1)
    conv_part(resid, False, 512, CONVB + 1)
    for image, base in ((own, half * 256), (peer, (1 - half) * 256)):

        def norm_two(group, carry, image=image, base=base):
            where = rows(base + group * BLOCK, BLOCK)
            total = resid[where, :] + image[rows(group * BLOCK, BLOCK), :].astype(F32)
            resid[where, :] = total
            unit = group_stats(total, stats2, where)
            normed[where, :] = (unit * par[where, GAIN + 2 : GAIN + 3] + par[where, BIAS + 2 : BIAS + 3]).astype(BF)
            return carry

        lax.fori_loop(0, 256 // BLOCK, norm_two, 0)
    complete(4)
    complete(5)
    cot_copy.wait_recv()
    for piece in range(PIECES):
        copy(piece, 0, block(), 32, to_x).wait_send()
        for kind, start, count in (
            (1, block(), 32), (2, block(), 32), (5, block(), 32),
            (3, block(0, 0, 1), 16), (7, block(0, 0, 1), 32),
            (4, block(0, 1, 0) + 16, 16), (6, block(0, 1, 0), 32),
            (8, block(0, 1, 1), 16), (9, block(0, 1, 1) + 16, 16),
        ):
            copy(piece, kind, start, count, to_x).wait_send()
    picture.wait_send()
    block_copy.wait_send()
    cot_copy.wait_send()


def forward_call(timesteps, classes, *args):
    arrays, specs = operands((Scalars(timesteps), Scalars(classes)) + args)
    images, cotangent, conv_weight, qkv_weight, proj_weight = arrays[-5:]
    width = arrays[-6].shape[1]
    half_bf = out((256, PIX), BF)
    full_bf = out((512, PIX), BF)
    full_f32 = out((512, PIX), F32)
    stats = out((512, 2), F32)
    dma = pltpu.SemaphoreType.DMA
    half_scratch = pltpu.VMEM((256, PIX), BF)
    return pl.pallas_call(
        forward,
        out_shape=[
            out((512, 11), F32),
            out((2, width + 128), F32),
            half_bf,
            half_bf,
            out(conv_weight.shape, BF),
            out(qkv_weight.shape, BF),
            out(proj_weight.shape, BF),
            full_bf, half_bf, half_bf, full_f32, stats, stats, full_bf, full_f32, stats, full_bf,
        ],
        in_specs=specs,
        out_specs=[VMEM] * 2 + [ANYWHERE] * 5 + [VMEM] * 10,
        scratch_shapes=[
            dma((PIECES, KINDS)), dma((PIECES, KINDS)), dma((3,)), dma((3,)), dma((5,)),
            pltpu.VMEM((256, 128), F32),
            pltpu.VMEM((256, 128), F32),
            pltpu.VMEM((16, 256), F32),
            pltpu.VMEM(arrays[-6].shape, BF),
            half_scratch, half_scratch, half_scratch,
            pltpu.VMEM((256, 2), F32),
            pltpu.VMEM((9 * 512, PIX), BF),
            pltpu.VMEM((9, 512, 512), BF),
        ],
        cost_estimate=pl.CostEstimate(flops=2 * 10**10, bytes_accessed=100 * 2**20, transcendentals=0),
        compiler_params=pltpu.CompilerParams(
            collective_id=1, has_side_effects=True, vmem_limit_bytes=58 * 2**20
        ),
    )(*arrays)


SENDS = 12


class Sum:
    def __init__(self, source, total, scratch, planes):
        self.source, self.total, self.planes = source, total, planes
        self.sends, self.recvs, self.core_in, self.first, self.y_in, self.second, self.z_in, self.result = scratch[:8]
        if planes:
            self.middle, self.x_in = scratch[8:10]
        self.half = lax.axis_index("head")
        self.place, self.core, self.up, self.deep = position()
        self.steps = [self.start, self.core_done, self.y_done, self.z_done]
        if planes:
            self.steps.append(self.x_done)
        self.steps += [self.z_back, self.y_back, self.finish]
        self.open = []
        self.count = 0

    def advance(self):
        if self.count < len(self.steps):
            self.steps[self.count]()
            self.count += 1

    def part(self, array, start, count):
        where = pl.ds(start, count)
        return array.at[:, where] if self.planes else array.at[where]

    def to_core(self):
        return {"batch": self.place + 1 - 2 * self.core}

    def to_y(self):
        return {"batch": self.place + 2 * (1 - 2 * self.up)}

    def to_z(self, ahead):
        return {"batch": (self.deep + ahead) % 4 * 4 + self.place % 4}

    def send(self, slot, source, dest, target):
        copy = remote(source, dest, self.sends, self.recvs, slot, target)
        copy.start()
        self.open.append(copy)

    def arrived(self, slot, dest):
        remote(dest, dest, self.sends, self.recvs, slot, self.to_core()).wait_recv()

    def of_core(self, core):
        return self.source.at[core] if self.planes else self.source.at[pl.ds(core * 8, 8)]

    def start(self):
        self.send(0, self.of_core(1 - self.core), self.core_in, self.to_core())

    def add(self, dest, left, *right):
        total = left[...].astype(F32)
        for term in right:
            total = total + term[...].astype(F32)
        dest[...] = total.astype(BF)

    def core_done(self):
        self.arrived(0, self.core_in)
        self.add(self.first, self.of_core(self.core), self.core_in)
        self.send(1, self.part(self.first, (1 - self.up) * 4, 4), self.y_in, self.to_y())

    def y_done(self):
        self.arrived(1, self.y_in)
        self.add(self.second, self.part(self.first, self.up * 4, 4), self.y_in)
        for ahead in (2, 1, 3):
            chunk = self.part(self.second, (self.deep + ahead) % 4, 1)
            self.send(1 + ahead, chunk, self.z_in.at[ahead - 1], self.to_z(ahead))

    def z_done(self):
        for ahead in (1, 2, 3):
            self.arrived(1 + ahead, self.z_in.at[ahead - 1])
        mine = self.part(self.second, self.deep, 1)
        terms = [self.z_in.at[number] for number in range(3)]
        if self.planes:
            self.add(self.middle, mine, *terms)
            self.send(10, self.middle.at[1 - self.half], self.x_in, {"head": 1 - self.half})
        else:
            self.add(self.result, mine, *terms)
            self.give()

    def x_done(self):
        self.arrived(10, self.x_in)
        self.add(self.result, self.middle.at[self.half], self.x_in)
        self.give()

    def chunks(self, start, count):
        return self.total.at[pl.ds(start, count)]

    def chunk(self, deep):
        return self.core * 8 + self.up * 4 + deep

    def give(self):
        mine = self.chunks(self.chunk(self.deep), 1)
        for ahead in (2, 1, 3):
            self.send(4 + ahead, self.result, mine, self.to_z(ahead))
        self.kept = pltpu.make_async_copy(self.result, mine, self.sends.at[11])
        self.kept.start()

    def z_back(self):
        for ahead in (1, 2, 3):
            self.arrived(4 + ahead, self.chunks(self.chunk((self.deep + 4 - ahead) % 4), 1))
        self.kept.wait()
        part = self.chunks(self.chunk(0), 4)
        self.send(8, part, part, self.to_y())

    def y_back(self):
        self.arrived(8, self.chunks(self.core * 8 + (1 - self.up) * 4, 4))
        part = self.chunks(self.core * 8, 8)
        self.send(9, part, part, self.to_core())

    def finish(self):
        self.arrived(9, self.chunks((1 - self.core) * 8, 8))
        for copy in self.open:
            copy.wait_send()


def sum_scratch(tail, planes):
    lead = (2,) if planes else ()
    shapes = [
        pltpu.SemaphoreType.DMA((SENDS,)),
        pltpu.SemaphoreType.DMA((SENDS,)),
        pltpu.VMEM(lead + (8,) + tail, BF),
        pltpu.VMEM(lead + (8,) + tail, BF),
        pltpu.VMEM(lead + (4,) + tail, BF),
        pltpu.VMEM(lead + (4,) + tail, BF),
        pltpu.VMEM((3,) + lead + (1,) + tail, BF),
        pltpu.VMEM((1,) + tail, BF),
    ]
    if planes:
        shapes += [pltpu.VMEM((2, 1) + tail, BF), pltpu.VMEM((1,) + tail, BF)]
    return shapes


def weight_back(grads, chunk_taps, col, turned):
    for tap in chunk_taps:
        result = mm(col[tap * 256 : (tap + 1) * 256, :], turned[:PIX, :])
        result = result + mm(col[(9 + tap) * 256 : (10 + tap) * 256, :], turned[PIX:, :])
        result = result.astype(BF)
        for part in range(16):
            grads[part, tap] = result[part * 16 : (part + 1) * 16]


PARTS = ((0, 2), (2, 4), (4, 6), (6, 8), (8, 9))
HALVES = ((0, 2), (2, 4))

(TAPS_ONE, CONV_ONE, AWAY_ONE, NEAR_ONE, PAIR_ONE, GRAD_ONE, SHARE, PAIR_ZERO,
 GRAD_ZERO, TAPS_ZERO, CONV_ZERO, AWAY_ZERO, NEAR_ZERO, ROWS, SMALL) = range(100, 115)
ORDER = (
    TAPS_ONE, 0, 1, CONV_ONE, 0, 1, CONV_ONE, AWAY_ONE, NEAR_ONE, 0, PAIR_ONE, GRAD_ONE, 2, 1,
    GRAD_ONE, 2, 3, GRAD_ONE, 0, 4, 3, GRAD_ONE, 4, 5, 2, GRAD_ONE, 6, SHARE, PAIR_ZERO, 5, 1, 3, 6,
    2, 4, GRAD_ZERO, 7, GRAD_ZERO, 5, 8, 3, 7, 6, 0, GRAD_ZERO, 1, 8, 2, 9, GRAD_ZERO, 7, 10, 4, 9,
    GRAD_ZERO, 11, TAPS_ZERO, 10, 8, 5, 11, CONV_ZERO, 2, 3, 6, 9, CONV_ZERO, 0, 2, 10, 11, 1,
    AWAY_ZERO, 3, 7, NEAR_ZERO, 3, 0, 4, ROWS, 0, 1, 8, 1, 4, 5, 6, 4, SMALL, 9, 5, 6, SMALL, 5, 10,
    6, SMALL, 11, 7, 8, 7, 9, 7, 8, 10, 8, SMALL, 9, 11, 9, 10, 11, 10, 11,
)


def backward(
    live_count, squares, grad_branch, block, hidden, second, second_peer,
    first, first_other, first_peer, grad_resid, images, image_peer, w_own, w_peer,
    stats0, stats1, par, small2, pre_embed, emb_weight,
    square_sum, sum1, sum0, images_grad, far_in, block_out, sums, class_rows, mod_out, pre_out,
    sems, sends, recvs, all_sends, all_recvs,
    grads1, grads0, col, turned, full, slope_in, wide_in, source_in, branch_in, hidden_in, grad_hidden,
    far, columns, flat, mod, mod_send, pres, rows_own, rows_in, total, total_in,
    *scratch,
):
    half = lax.axis_index("head")
    place, core, up, deep = position()
    to_x = {"head": 1 - half}
    others = [{"batch": (place + ahead) % 16} for ahead in range(1, 16)]
    near, away = rows(half * 256, 256), rows((1 - half) * 256, 256)
    exchanges = {}
    local = {}

    local["weights"] = fetch_conv(sems.at[pl.ds(6, 2)], full, half, 1, w_own, w_peer)
    local["wide"] = (fetch(sems, 8, hidden, wide_in),)
    local["inputs"] = (
        fetch(sems, 9, second, source_in.at[0]),
        fetch(sems, 10, second_peer, source_in.at[1]),
    )
    meet([to_x] + others)

    def send(slot, source, dest, target):
        exchanges[slot] = remote(source, dest, sends, recvs, slot, target)
        exchanges[slot].start()

    send(0, grad_branch.at[away], branch_in, to_x)

    chains = []
    for low, high in HALVES:
        where = pl.ds(low, high - low)
        chains.append(Sum(squares.at[:, :, :, where], square_sum.at[:, where], scratch[:10], True))
        scratch = scratch[10:]
    for source, dest in ((grads1, sum1), (grads0, sum0)):
        for low, high in PARTS:
            where = pl.ds(low, high - low)
            chains.append(Sum(source.at[:, where], dest.at[:, where], scratch[:8], False))
            scratch = scratch[8:]

    masks = edge_masks(-1)
    pair = col.at[pl.ds(9 * 256, 9 * 256)]
    picture = source_in.at[0]
    width = emb_weight.shape[2]

    def taps_one(_):
        taps_of(col, masks, grad_branch, 0, 512, 0, -1)
        wait(local["weights"])

    def conv_back(count):
        column = 512 * count
        result = None
        for tap in range(9):
            term = mm(full[tap], col[tap * 512 : (tap + 1) * 512, column : column + 512], TN)
            result = term if result is None else result + term
        slope_in[:, column : column + 512] = result

    def back_one(base):
        def step(group, carry):
            where = rows(base + group * BLOCK, BLOCK)
            unit = unit_of(wide_in[where, :], stats1, where)
            gain = par[where, GAIN + 1 : GAIN + 2]
            unscaled = unit * gain + par[where, BIAS + 1 : BIAS + 2]
            scale = 1.0 + par[where, SCALE : SCALE + 1]
            grad_pre = slope_in[where, :] * silu_slope(unscaled * scale + par[where, SHIFT : SHIFT + 1])
            grad = grad_pre * scale
            low = unit_back(grad * gain, unit, stats1[where, 1:2]).astype(BF)
            grad_hidden[where, :] = low
            columns[where, 2:3] = row_sum(grad_pre * unscaled)
            columns[where, 3:4] = row_sum(grad_pre)
            columns[where, 4:5] = row_sum(grad * unit)
            columns[where, 5:6] = row_sum(grad)
            columns[where, 6:7] = row_sum(low.astype(F32))
            return carry

        lax.fori_loop(0, 256 // BLOCK, step, 0)

    def away_one(_):
        local["weights"] = fetch_conv(sems.at[pl.ds(6, 2)], full, half, 0, w_own, w_peer)
        columns[...] = jnp.zeros_like(columns)
        columns[:, 7:11] = small2[...]
        wait(local["wide"])
        back_one((1 - half) * 256)
        send(1, grad_hidden.at[away], hidden_in, to_x)

    def near_one(_):
        back_one(half * 256)
        local["wide"] = (fetch(sems, 8, grad_resid, wide_in),)
        flat[...] = columns[...].T[0:16]
        mod[place, half] = flat[2:4, near]
        mod_send[...] = flat[2:4, away]
        send(2, mod_send, mod.at[place, half], to_x)
        pres[place] = pre_embed[...]
        for ahead, target in enumerate(others):
            remote(pres.at[place], pres.at[place], all_sends, all_recvs, ahead, target).start()

    def pair_one(_):
        exchanges[0].wait_recv()
        taps_of(col, masks, grad_branch.at[near], 0, 256, 0, -1)
        taps_of(pair, masks, branch_in, 0, 256, 0, -1)
        wait(local["inputs"])
        turned[:PIX, :] = source_in[0].T
        turned[PIX:, :] = source_in[1].T
        local["inputs"] = (
            fetch(sems, 9, first, source_in.at[0]),
            fetch(sems, 10, first_other, source_in.at[1, near]),
            fetch(sems, 11, first_peer, source_in.at[1, away]),
        )

    def grad_one(count):
        weight_back(grads1, range(*PARTS[count]), col, turned)
        if count == 0:
            send(6, block.at[away], block_out.at[half], to_x)
            local["block"] = fetch(sems, 3, block.at[near], block_out.at[half])

    def share(_):
        remote(mod_send, mod.at[place, 1 - half], sends, recvs, 2, to_x).wait_recv()
        for ahead, target in enumerate(others):
            remote(mod.at[place], mod.at[place], all_sends, all_recvs, 15 + ahead, target).start()

    def pair_zero(_):
        exchanges[1].wait_recv()
        taps_of(col, masks, grad_hidden.at[near], 0, 256, 0, -1)
        taps_of(pair, masks, hidden_in, 0, 256, 0, -1)
        wait(local["inputs"])
        turned[:PIX, :] = source_in[0].T
        turned[PIX:, :] = source_in[1].T
        local["inputs"] = (
            fetch(sems, 9, images.at[half], picture.at[near]),
            fetch(sems, 10, image_peer, picture.at[away]),
        )

    def grad_zero(count):
        weight_back(grads0, range(*PARTS[count]), col, turned)

    def taps_zero(_):
        taps_of(col, masks, grad_hidden, 0, 512, 0, -1)
        wait(local["weights"])

    def back_zero(base, dest):
        def step(group, carry):
            here = rows(group * BLOCK, BLOCK)
            where = rows(base + group * BLOCK, BLOCK)
            unit = unit_of(picture[where, :].astype(F32), stats0, where)
            gain = par[where, GAIN : GAIN + 1]
            grad = slope_in[where, :] * silu_slope(unit * gain + par[where, BIAS : BIAS + 1])
            result = wide_in[where, :] + unit_back(grad * gain, unit, stats0[where, 1:2])
            dest[here, :] = result.astype(dest.dtype)
            columns[where, 0:1] = row_sum(grad * unit)
            columns[where, 1:2] = row_sum(grad)
            return carry

        lax.fori_loop(0, 256 // BLOCK, step, 0)

    def away_zero(_):
        wait(local["inputs"])
        wait(local["wide"])
        back_zero((1 - half) * 256, far)
        send(3, far, far_in, to_x)

    def near_zero(_):
        back_zero(half * 256, images_grad)
        flat[...] = columns[...].T[0:16]
        total[0] = flat[:, away]
        send(4, total.at[0], total_in.at[0], to_x)

    def class_part(_):
        for ahead in range(15):
            origin = (place + 15 - ahead) % 16
            remote(pres.at[origin], pres.at[origin], all_sends, all_recvs, ahead, to_x).wait_recv()
            remote(mod.at[origin], mod.at[origin], all_sends, all_recvs, 15 + ahead, to_x).wait_recv()
        result = None
        for which in range(2):
            factor = jnp.concatenate([mod[:, 0, which, :], mod[:, 1, which, :]], 0)
            term = mm(split(factor, 0), emb_weight[which])
            result = term if result is None else result + term
        result = result[0:32] + result[32:64] + result[64:96]
        rows_own[0] = result[0:16]
        rows_own[1] = result[16:32]
        send(5, rows_own, rows_in, to_x)

    def landed(slot, step):
        remote(total.at[0], total_in.at[step], sends, recvs, slot, to_x).wait_recv()

    def small_sums(count):
        if count == 0:
            landed(4, 0)
            total[1] = flat[:, near] + total_in[0]
            send(7, total.at[1], total_in.at[1], {"batch": place + 1 - 2 * core})
        elif count == 1:
            landed(7, 1)
            total[2] = total[1] + total_in[1]
            send(8, total.at[2], total_in.at[2], {"batch": place + 2 * (1 - 2 * up)})
        elif count == 2:
            landed(8, 2)
            total[3] = total[2] + total_in[2]
            for ahead in (1, 2, 3):
                target = {"batch": (deep + ahead) % 4 * 4 + place % 4}
                send(8 + ahead, total.at[3], total_in.at[3 + deep], target)
            total_in[3 + deep] = total[3]
        else:
            for ahead in (1, 2, 3):
                landed(8 + ahead, 3 + (deep + 4 - ahead) % 4)
            sums[...] = (total_in[3] + total_in[4]) + (total_in[5] + total_in[6])
            remote(rows_own, rows_in, sends, recvs, 5, to_x).wait_recv()
            for slot in range(2):
                class_rows[slot] = (rows_own[slot] + rows_in[slot]) * silu_slope(pres[:, slot, :width])
            mod_out[...] = mod[...]
            pre_out[...] = pres[...]

    pieces = {
        TAPS_ONE: taps_one, CONV_ONE: conv_back, AWAY_ONE: away_one, NEAR_ONE: near_one,
        PAIR_ONE: pair_one, GRAD_ONE: grad_one, SHARE: share, PAIR_ZERO: pair_zero,
        GRAD_ZERO: grad_zero, TAPS_ZERO: taps_zero, CONV_ZERO: conv_back, AWAY_ZERO: away_zero,
        NEAR_ZERO: near_zero, ROWS: class_part, SMALL: small_sums,
    }
    counts = dict.fromkeys(pieces, 0)
    for entry in ORDER:
        if entry < 100:
            chains[entry].advance()
        else:
            pieces[entry](counts[entry])
            counts[entry] += 1
    remote(far, far_in, sends, recvs, 3, to_x).wait_recv()
    remote(block.at[away], block_out.at[1 - half], sends, recvs, 6, to_x).wait_recv()
    local["block"].wait()
    for copy in exchanges.values():
        copy.wait_send()
    for ahead, target in enumerate(others):
        remote(pres.at[place], pres.at[place], all_sends, all_recvs, ahead, target).wait_send()
        remote(mod.at[place], mod.at[place], all_sends, all_recvs, 15 + ahead, target).wait_send()


def backward_call(*args):
    arrays, specs = operands(args)
    dma = pltpu.SemaphoreType.DMA
    scratch = [
        dma((12,)), dma((12,)), dma((12,)), dma((30,)), dma((30,)),
        pltpu.VMEM((16, 9, 16, 512), BF),
        pltpu.VMEM((16, 9, 16, 512), BF),
        pltpu.VMEM((9 * 512, PIX), BF),
        pltpu.VMEM((2 * PIX, 512), BF),
        pltpu.VMEM((9, 512, 512), BF),
        pltpu.VMEM((512, PIX), F32),
        pltpu.VMEM((512, PIX), F32),
        pltpu.VMEM((2, 512, PIX), BF),
        pltpu.VMEM((256, PIX), BF),
        pltpu.VMEM((256, PIX), BF),
        pltpu.VMEM((512, PIX), BF),
        pltpu.VMEM((256, PIX), BF),
        pltpu.VMEM((512, 128), F32),
        pltpu.VMEM((16, 512), F32),
        pltpu.VMEM((16, 2, 2, 256), F32),
        pltpu.VMEM((2, 256), F32),
        pltpu.VMEM((16, 2, 1024 + 128), F32),
        pltpu.VMEM((2, 16, 1024), F32),
        pltpu.VMEM((2, 16, 1024), F32),
        pltpu.VMEM((4, 16, 256), F32),
        pltpu.VMEM((7, 16, 256), F32),
    ]
    for low, high in HALVES:
        scratch += sum_scratch((high - low, 16, 512), True)
    for low, high in PARTS * 2:
        scratch += sum_scratch((high - low, 16, 512), False)
    outs = [
        (out((16, 4, 16, 512), BF), ANYWHERE),
        (out((16, 9, 16, 512), BF), ANYWHERE),
        (out((16, 9, 16, 512), BF), ANYWHERE),
        (out((256, PIX), F32), VMEM),
        (out((256, PIX), BF), ANYWHERE),
        (out((2, 256, PIX), BF), ANYWHERE),
        (out((16, 256), F32), VMEM),
        (out((2, 16, 1024), F32), VMEM),
        (out((16, 2, 2, 256), F32), VMEM),
        (out((16, 2, 1024 + 128), F32), VMEM),
    ]
    return pl.pallas_call(
        backward,
        out_shape=[o for o, _ in outs],
        in_specs=specs,
        out_specs=[spec for _, spec in outs],
        scratch_shapes=scratch,
        cost_estimate=pl.CostEstimate(flops=4 * 10**10, bytes_accessed=200 * 2**20, transcendentals=0),
        compiler_params=pltpu.CompilerParams(
            collective_id=2, has_side_effects=True, vmem_limit_bytes=60 * 2**20
        ),
    )(*arrays)


TRIPLES = ((0, 3), (3, 6), (6, 9))


def finish(
    sum0, sum1, squares, near, far, mod, pres, rows_in, sums,
    conv, qkv, proj, images_grad, emb, table, gains, biases, conv_biases, emb_biases, proj_bias,
    ins, outs, low, low_square, wide, square, mine, other, grads, emb_out, table_out,
):
    half = lax.axis_index("head")
    width = rows_in.shape[2]
    reads = []
    for layer, source in enumerate((sum0, sum1)):
        for number, (start, stop) in enumerate(TRIPLES):
            taps = pl.ds(start, stop - start)
            reads.append(fetch(ins, layer * 3 + number, source.at[:, taps], low.at[layer, :, taps]))
    reads.append(fetch(ins, 6, squares, low_square))
    reads.append(fetch(ins, 7, near, mine))
    reads.append(fetch(ins, 8, far, other))
    writes = []

    def write(source, dest):
        writes.append(fetch(outs, len(writes), source, dest))

    for number, row in enumerate((0, 4, 7)):
        gains[number : number + 1] = sums[row : row + 1]
        biases[number : number + 1] = sums[row + 1 : row + 2]
    conv_biases[0:1] = sums[6:7]
    conv_biases[1:2] = sums[9:10]
    emb_biases[...] = sums[2:4]
    proj_bias[...] = sums[10:11]

    numbers = lax.broadcasted_iota(jnp.int32, (32, table.shape[0]), 1)
    ids = jnp.concatenate([pres[:, slot, width : width + 1] for slot in range(2)], 0).astype(jnp.int32)
    chosen = (numbers == ids).astype(F32).astype(BF)
    class_rows = jnp.concatenate([rows_in[0], rows_in[1]], 0)
    table_out[...] = mm(jnp.concatenate([chosen] * 3, 0), split(class_rows, 0), TN)
    write(table_out, table)
    embed = jnp.concatenate([jax.nn.silu(pres[:, slot, :width]) for slot in range(2)], 0)
    parts = split(embed, 0)
    high, middle = parts[0:32], parts[32:64]
    for which in range(2):
        factor = split(jnp.concatenate([mod[:, slot, which, :] for slot in range(2)], 0), 0)
        left = jnp.concatenate([factor[0:32], factor[0:32], factor[32:64]], 0)
        emb_out[which] = mm(left, jnp.concatenate([high, middle, high], 0), TN)
    write(emb_out, emb)
    for layer in range(2):
        for number, (start, stop) in enumerate(TRIPLES):
            reads[layer * 3 + number].wait()
            for tap in range(start, stop):
                wide[layer, tap] = low[layer, :, tap].reshape(256, 512).astype(F32)
            taps = pl.ds(start, stop - start)
            write(wide.at[layer, taps], conv.at[layer, taps])
    reads[6].wait()
    for which in range(4):
        square[which] = low_square[:, which].reshape(256, 512).astype(F32)
    write(square.at[pl.ds(0, 3)], qkv)
    write(square.at[3], proj)
    reads[7].wait()
    reads[8].wait()
    grads[half] = mine[...]
    grads[1 - half] = other[...].astype(F32)
    write(grads, images_grad)
    wait(writes)


def finish_call(sum0, sum1, squares, near, far, mod, pres, rows_in, sums, table_shape):
    width = table_shape[1]
    shapes = [
        (2, 9, 256, 512),
        (3, 256, 512),
        (256, 512),
        (2, 256, PIX),
        (2, 256, width),
        table_shape,
        (3, 256),
        (3, 256),
        (2, 256),
        (2, 256),
        (1, 256),
    ]
    dma = pltpu.SemaphoreType.DMA
    return pl.pallas_call(
        finish,
        out_shape=[out(shape, F32) for shape in shapes],
        in_specs=[ANYWHERE] * 5 + [VMEM] * 4,
        out_specs=[ANYWHERE] * 6 + [VMEM] * 5,
        scratch_shapes=[
            dma((9,)), dma((11,)),
            pltpu.VMEM((2,) + sum0.shape, BF),
            pltpu.VMEM(squares.shape, BF),
            pltpu.VMEM(shapes[0], F32),
            pltpu.VMEM((4, 256, 512), F32),
            pltpu.VMEM((256, PIX), F32),
            pltpu.VMEM((256, PIX), BF),
            pltpu.VMEM(shapes[3], F32),
            pltpu.VMEM(shapes[4], F32),
            pltpu.VMEM(shapes[5], F32),
        ],
        compiler_params=pltpu.CompilerParams(vmem_limit_bytes=58 * 2**20),
    )(sum0, sum1, squares, near, far, mod, pres, rows_in, sums)


def paired(
    images,
    timesteps,
    classes,
    live_count,
    norm_gain,
    norm_bias,
    conv_weight,
    conv_bias,
    emb_weight,
    emb_bias,
    class_table,
    qkv_weight,
    proj_weight,
    proj_bias,
    cotangent,
):
    half = lax.axis_index("head")

    def across(value):
        return lax.ppermute(value, "head", [(0, 1), (1, 0)])

    (
        par, pre_embed, image_peer, cot_peer, conv_peer, q_peer, p_peer,
        first, first_near, first_other, hidden, stats0, stats1, second, resid, stats2, normed,
    ) = forward_call(
        timesteps, classes, norm_gain, norm_bias, conv_bias, proj_bias[None], emb_bias, emb_weight,
        *map(Far, (class_table, images, cotangent, conv_weight, qkv_weight, proj_weight)),
    )
    first_peer = across(first_near)
    second_peer = across(second)
    full_bf = out((512, PIX), BF)
    full_f32 = out((512, PIX), F32)
    square = pltpu.VMEM((512, 512), BF)
    wide_bf = pltpu.VMEM((512, PIX), BF)
    wide_f32 = pltpu.VMEM((512, PIX), F32)
    pixels = pltpu.VMEM((PIX, PIX), BF)
    square_grads, block, grad_resid, grad_branch, small2 = kernel_call(
        attention,
        [out((2, 2, 8, 4, 16, 512), BF), full_bf, full_f32, full_bf, out((512, 4), F32)],
        [pltpu.VMEM((3, 512, 512), BF), square] + [wide_bf] * 9 + [wide_f32] * 2 + [pixels] * 8,
        3 * 10**10,
        Scalars(live_count), normed, Far(resid), stats2, par, Far(cotangent), Far(cot_peer),
        Far(qkv_weight), Far(q_peer), Far(proj_weight), Far(p_peer),
    )
    square_sum, conv_sum1, conv_sum0, near, far, block_out, sums, class_rows, mod, pre_all = backward_call(
        Scalars(live_count), square_grads, grad_branch, *map(Far, (block, hidden, second, second_peer)),
        *map(Far, (first, first_other, first_peer, grad_resid, images, image_peer, conv_weight, conv_peer)),
        stats0, stats1, par, small2, pre_embed, emb_weight,
    )
    (
        conv_total, qkv_total, proj_total, images_grad, emb_total, table_total,
        gains, biases, conv_biases, emb_biases, proj_biases,
    ) = finish_call(
        conv_sum0, conv_sum1, square_sum, near, far, mod, pre_all, class_rows, sums, class_table.shape
    )
    return (
        block_out,
        images_grad,
        gains,
        biases,
        conv_total,
        conv_biases,
        emb_total,
        emb_biases,
        table_total,
        qkv_total,
        proj_total,
        proj_biases[0],
    )


def solution(mesh):
    in_specs = (
        P("batch", "head", None),
        P("batch"),
        P("batch"),
        P("batch"),
        P(None, "head"),
        P(None, "head"),
        P(None, None, "head", None),
        P(None, "head"),
        P(None, "head", None),
        P(None, "head"),
        P(),
        P(None, "head", None),
        P("head", None),
        P("head"),
        P("batch", "head", None),
    )
    out_specs = (
        P("batch", "head", None),
        P("batch", "head", None),
        P(None, "head"),
        P(None, "head"),
        P(None, None, "head", None),
        P(None, "head"),
        P(None, "head", None),
        P(None, "head"),
        P(),
        P(None, "head", None),
        P("head", None),
        P("head"),
    )
    body = shards
    if mesh.shape["head"] == 2 and mesh.shape["batch"] == 16:
        body = paired
    return jax.shard_map(body, mesh=mesh, in_specs=in_specs, out_specs=out_specs, check_vma=False)
```

```python
import math

import jax
import jax.numpy as jnp
from jax import lax
from jax.experimental import pallas as pl
from jax.experimental.pallas import tpu as pltpu
from jax.sharding import PartitionSpec as P

C = 512
GROUPS = 32
HEADS = 8
SIDE = 32


EPS = 1e-05
HIGH = lax.Precision.HIGHEST
CONTRACT_FIRST = (((0,), (0,)), ((), ()))
CONTRACT_LAST = (((1,), (1,)), ((), ()))


def silu_slope(values):
    sigma = jax.nn.sigmoid(values)
    return sigma * (1.0 + values * (1.0 - sigma))


def moved(source, grid_side, row_step, col_step):
    grid = source.reshape(source.shape[0], grid_side, grid_side)
    padded = jnp.pad(grid, ((0, 0), (1, 1), (1, 1)))
    window = padded[
        :, 1 + row_step : 1 + row_step + grid_side, 1 + col_step : 1 + col_step + grid_side
    ]
    return window.reshape(source.shape)


def group_unit(source, groups):
    grouped = source.reshape(groups, -1)
    centre = grouped - jnp.mean(grouped, axis=1, keepdims=True)
    inverse = lax.rsqrt(jnp.mean(jnp.square(centre), axis=1, keepdims=True) + EPS)
    return ((centre * inverse).reshape(source.shape), inverse)


def group_back(grad_unit, unit_rows, inverse, groups):
    flat_grad = grad_unit.reshape(groups, -1)
    flat_unit = unit_rows.reshape(groups, -1)
    result = flat_grad - jnp.mean(flat_grad, axis=1, keepdims=True)
    result = (result - flat_unit * jnp.mean(flat_grad * flat_unit, axis=1, keepdims=True)) * inverse
    return result.reshape(grad_unit.shape)


def conv_apply(weight, source, grid_side):
    result = jnp.dot(
        weight[0], moved(source, grid_side, -1, -1), preferred_element_type=jnp.float32
    )
    for tap_index in range(1, 9):
        result = result + jnp.dot(
            weight[tap_index],
            moved(source, grid_side, tap_index // 3 - 1, tap_index % 3 - 1),
            preferred_element_type=jnp.float32,
        )
    return result


def conv_transpose(weight, grads, grid_side):
    result = lax.dot_general(
        weight[0], moved(grads, grid_side, 1, 1), CONTRACT_FIRST, preferred_element_type=jnp.float32
    )
    for tap_index in range(1, 9):
        result = result + lax.dot_general(
            weight[tap_index],
            moved(grads, grid_side, 1 - tap_index // 3, 1 - tap_index % 3),
            CONTRACT_FIRST,
            preferred_element_type=jnp.float32,
        )
    return result


def conv_weight_grads(grads, source, grid_side):
    return jnp.stack(
        [
            lax.dot_general(
                grads,
                moved(source, grid_side, tap_index // 3 - 1, tap_index % 3 - 1),
                CONTRACT_LAST,
                preferred_element_type=jnp.float32,
            )
            for tap_index in range(9)
        ]
    )


def features(timestep, emb_width):
    half_width = emb_width // 2
    freqs = jnp.exp(-math.log(10000.0) * jnp.arange(half_width, dtype=jnp.float32) / half_width)
    angles = timestep.astype(jnp.float32) * freqs
    return jnp.concatenate([jnp.cos(angles), jnp.sin(angles)])


def shards(
    images,
    timesteps,
    classes,
    live_count,
    norm_gain,
    norm_bias,
    conv_weight,
    conv_bias,
    emb_weight,
    emb_bias,
    class_table,
    qkv_weight,
    proj_weight,
    proj_bias,
    cotangent,
):
    slot_count, chan_dev, pixel_count = images.shape
    grid_side = SIDE
    groups = chan_dev // (C // GROUPS)
    head_size = C // HEADS
    heads_dev = chan_dev // head_size
    att_scale = head_size ** (-0.5)
    emb_dense = emb_weight.astype(jnp.float32)
    class_total, emb_width = class_table.shape

    def gather_channels(rows_low):
        return lax.all_gather(rows_low, "head", axis=0, tiled=True)

    def input_grad(which_conv, grad_rows):
        weight_cols = conv_weight[which_conv]
        return lax.psum_scatter(
            conv_transpose(weight_cols, grad_rows, grid_side).astype(jnp.bfloat16),
            "head",
            scatter_dimension=0,
            tiled=True,
        ).astype(jnp.float32)

    def per_slot(slot_index, carry):
        (
            outputs,
            grads_in,
            gain_acc,
            bias_acc,
            convw_acc,
            convb_acc,
            embw_acc,
            embb_acc,
            table_acc,
            qkv_acc,
            projw_acc,
            projb_acc,
        ) = carry
        picture = lax.dynamic_index_in_dim(images, slot_index, 0, keepdims=False).astype(
            jnp.float32
        )
        live_flag = (slot_index < live_count[0]).astype(jnp.float32)
        class_id = classes[slot_index]
        table_row = lax.dynamic_index_in_dim(class_table, class_id, 0, keepdims=False).astype(
            jnp.float32
        )
        pre_embed = features(timesteps[slot_index], emb_width) + table_row
        embed = jax.nn.silu(pre_embed)
        scale = jnp.dot(emb_dense[0], embed, precision=HIGH) + emb_bias[0]
        shift = jnp.dot(emb_dense[1], embed, precision=HIGH) + emb_bias[1]
        unit_zero, inverse_zero = group_unit(picture, groups)
        pre_first = unit_zero * norm_gain[0][:, None] + norm_bias[0][:, None]
        first_full = gather_channels(jax.nn.silu(pre_first).astype(jnp.bfloat16))
        hidden = conv_apply(conv_weight[0], first_full, grid_side) + conv_bias[0][:, None]
        unit_one, inverse_one = group_unit(hidden, groups)
        normed_one = unit_one * norm_gain[1][:, None] + norm_bias[1][:, None]
        pre_second = normed_one * (1.0 + scale[:, None]) + shift[:, None]
        second_full = gather_channels(jax.nn.silu(pre_second).astype(jnp.bfloat16))
        resid = picture + conv_apply(conv_weight[1], second_full, grid_side) + conv_bias[1][:, None]
        unit_two, inverse_two = group_unit(resid, groups)
        normed_full = gather_channels(
            (unit_two * norm_gain[2][:, None] + norm_bias[2][:, None]).astype(jnp.bfloat16)
        )
        query = (
            jnp.dot(qkv_weight[0], normed_full, preferred_element_type=jnp.float32)
            .astype(jnp.bfloat16)
            .reshape(heads_dev, head_size, pixel_count)
        )
        keys = (
            jnp.dot(qkv_weight[1], normed_full, preferred_element_type=jnp.float32)
            .astype(jnp.bfloat16)
            .reshape(heads_dev, head_size, pixel_count)
        )
        values = (
            jnp.dot(qkv_weight[2], normed_full, preferred_element_type=jnp.float32)
            .astype(jnp.bfloat16)
            .reshape(heads_dev, head_size, pixel_count)
        )
        scores = (
            jnp.einsum("hdi,hdj->hij", query, keys, preferred_element_type=jnp.float32) * att_scale
        )
        highest = jnp.max(scores, axis=2, keepdims=True)
        expo = jnp.exp(scores - highest)
        totals = jnp.sum(expo, axis=2, keepdims=True)
        log_total = highest + jnp.log(totals)
        weights = (expo / totals).astype(jnp.bfloat16)
        mixed = (
            jnp.einsum("hdj,hij->hdi", values, weights, preferred_element_type=jnp.float32)
            .astype(jnp.bfloat16)
            .reshape(chan_dev, pixel_count)
        )
        weight_cols = proj_weight
        proj_term = lax.psum_scatter(
            lax.dot_general(
                weight_cols, mixed, CONTRACT_FIRST, preferred_element_type=jnp.float32
            ).astype(jnp.bfloat16),
            "head",
            scatter_dimension=0,
            tiled=True,
        ).astype(jnp.float32)
        result = resid + proj_term + proj_bias[:, None]
        outputs = lax.dynamic_update_index_in_dim(
            outputs, (live_flag * result).astype(jnp.bfloat16), slot_index, 0
        )
        grad_low = lax.dynamic_index_in_dim(cotangent, slot_index, 0, keepdims=False)
        grad_out = live_flag * grad_low.astype(jnp.float32)
        grad_full = lax.all_gather(grad_low, "head", axis=0, tiled=True) * live_flag.astype(
            jnp.bfloat16
        )
        grad_mixed = jnp.dot(proj_weight, grad_full, preferred_element_type=jnp.float32).astype(
            jnp.bfloat16
        )
        projw_acc = projw_acc + lax.dot_general(
            mixed, grad_full, CONTRACT_LAST, preferred_element_type=jnp.float32
        )
        projb_acc = projb_acc + jnp.sum(grad_out, axis=1)
        again = (
            jnp.einsum("hdi,hdj->hij", query, keys, preferred_element_type=jnp.float32) * att_scale
        )
        probs = jnp.exp(again - log_total)
        grad_heads = grad_mixed.reshape(heads_dev, head_size, pixel_count)
        grad_probs = jnp.einsum(
            "hdi,hdj->hij", grad_heads, values, preferred_element_type=jnp.float32
        )
        grad_scores = (
            probs * (grad_probs - jnp.sum(grad_probs * probs, axis=2, keepdims=True))
        ).astype(jnp.bfloat16)
        grad_query = (
            jnp.einsum("hij,hdj->hdi", grad_scores, keys, preferred_element_type=jnp.float32)
            * att_scale
        ).astype(jnp.bfloat16)
        grad_keys = (
            jnp.einsum("hij,hdi->hdj", grad_scores, query, preferred_element_type=jnp.float32)
            * att_scale
        ).astype(jnp.bfloat16)
        grad_values = jnp.einsum(
            "hdi,hij->hdj", grad_heads, weights, preferred_element_type=jnp.float32
        ).astype(jnp.bfloat16)
        stacked = jnp.stack([grad_query, grad_keys, grad_values]).reshape(3, chan_dev, pixel_count)
        weight_cols = qkv_weight
        grad_normed = lax.psum_scatter(
            lax.dot_general(
                weight_cols,
                stacked,
                (((0, 1), (0, 1)), ((), ())),
                preferred_element_type=jnp.float32,
            ).astype(jnp.bfloat16),
            "head",
            scatter_dimension=0,
            tiled=True,
        ).astype(jnp.float32)
        qkv_acc = qkv_acc + lax.dot_general(
            stacked, normed_full, (((2,), (1,)), ((), ())), preferred_element_type=jnp.float32
        )
        grad_resid = grad_out + group_back(
            grad_normed * norm_gain[2][:, None], unit_two, inverse_two, groups
        )
        grad_branch = grad_resid.astype(jnp.bfloat16)
        grad_second = input_grad(1, grad_branch)
        grad_pre = grad_second * silu_slope(pre_second)
        scale_grad = jnp.sum(grad_pre * normed_one, axis=1)
        shift_grad = jnp.sum(grad_pre, axis=1)
        grad_normed_one = grad_pre * (1.0 + scale[:, None])
        grad_hidden = group_back(
            grad_normed_one * norm_gain[1][:, None], unit_one, inverse_one, groups
        ).astype(jnp.bfloat16)
        grad_first = input_grad(0, grad_hidden)
        grad_pre_first = grad_first * silu_slope(pre_first)
        picture_grad = grad_resid + group_back(
            grad_pre_first * norm_gain[0][:, None], unit_zero, inverse_zero, groups
        )
        grads_in = lax.dynamic_update_index_in_dim(grads_in, picture_grad, slot_index, 0)
        gain_acc = gain_acc + jnp.stack(
            [
                jnp.sum(grad_pre_first * unit_zero, axis=1),
                jnp.sum(grad_normed_one * unit_one, axis=1),
                jnp.sum(grad_normed * unit_two, axis=1),
            ]
        )
        bias_acc = bias_acc + jnp.stack(
            [
                jnp.sum(grad_pre_first, axis=1),
                jnp.sum(grad_normed_one, axis=1),
                jnp.sum(grad_normed, axis=1),
            ]
        )
        convw_acc = convw_acc + jnp.stack(
            [
                conv_weight_grads(grad_hidden, first_full, grid_side),
                conv_weight_grads(grad_branch, second_full, grid_side),
            ]
        )
        convb_acc = convb_acc + jnp.stack(
            [
                jnp.sum(grad_hidden.astype(jnp.float32), axis=1),
                jnp.sum(grad_branch.astype(jnp.float32), axis=1),
            ]
        )
        embw_acc = embw_acc + jnp.stack(
            [scale_grad[:, None] * embed[None, :], shift_grad[:, None] * embed[None, :]]
        )
        embb_acc = embb_acc + jnp.stack([scale_grad, shift_grad])
        grad_embed = jnp.dot(scale_grad, emb_dense[0], precision=HIGH) + jnp.dot(
            shift_grad, emb_dense[1], precision=HIGH
        )
        class_row = grad_embed * silu_slope(pre_embed)
        old_row = lax.dynamic_index_in_dim(table_acc, class_id, 0, keepdims=True)
        table_acc = lax.dynamic_update_index_in_dim(
            table_acc, old_row + class_row[None, :], class_id, 0
        )
        return (
            outputs,
            grads_in,
            gain_acc,
            bias_acc,
            convw_acc,
            convb_acc,
            embw_acc,
            embb_acc,
            table_acc,
            qkv_acc,
            projw_acc,
            projb_acc,
        )

    table_start = jnp.zeros(class_table.shape, jnp.float32)
    initial = (
        jnp.zeros(images.shape, jnp.bfloat16),
        jnp.zeros(images.shape, jnp.float32),
        jnp.zeros(norm_gain.shape, jnp.float32),
        jnp.zeros(norm_bias.shape, jnp.float32),
        jnp.zeros(conv_weight.shape, jnp.float32),
        jnp.zeros(conv_bias.shape, jnp.float32),
        jnp.zeros(emb_weight.shape, jnp.float32),
        jnp.zeros(emb_bias.shape, jnp.float32),
        table_start,
        jnp.zeros(qkv_weight.shape, jnp.float32),
        jnp.zeros(proj_weight.shape, jnp.float32),
        jnp.zeros(proj_bias.shape, jnp.float32),
    )
    final = lax.fori_loop(0, slot_count, per_slot, initial)
    (
        outputs,
        grads_in,
        gain_acc,
        bias_acc,
        convw_acc,
        convb_acc,
        embw_acc,
        embb_acc,
        table_acc,
        qkv_acc,
        projw_acc,
        projb_acc,
    ) = final
    table_total = lax.psum(table_acc, ("batch", "head"))
    summed = (
        lax.psum(gain_acc.astype(jnp.bfloat16), "batch").astype(jnp.float32),
        lax.psum(bias_acc.astype(jnp.bfloat16), "batch").astype(jnp.float32),
        lax.psum(convw_acc.astype(jnp.bfloat16), "batch").astype(jnp.float32),
        lax.psum(convb_acc.astype(jnp.bfloat16), "batch").astype(jnp.float32),
        lax.psum(embw_acc.astype(jnp.bfloat16), "batch").astype(jnp.float32),
        lax.psum(embb_acc.astype(jnp.bfloat16), "batch").astype(jnp.float32),
        lax.psum(qkv_acc.astype(jnp.bfloat16), "batch").astype(jnp.float32),
        lax.psum(projw_acc.astype(jnp.bfloat16), "batch").astype(jnp.float32),
        lax.psum(projb_acc.astype(jnp.bfloat16), "batch").astype(jnp.float32),
    )
    return (
        outputs,
        grads_in,
        summed[0],
        summed[1],
        summed[2],
        summed[3],
        summed[4],
        summed[5],
        table_total,
        summed[6],
        summed[7],
        summed[8],
    )


PIX = 1024
BLOCK = 128
BF = jnp.bfloat16
F32 = jnp.float32
NN = (((1,), (0,)), ((), ()))
TN = (((0,), (0,)), ((), ()))
NT = (((1,), (1,)), ((), ()))
VMEM = pl.BlockSpec(memory_space=pltpu.VMEM)
SMEM = pl.BlockSpec(memory_space=pltpu.SMEM)

GAIN, BIAS, CONVB, PROJB, SCALE, SHIFT = 0, 3, 6, 8, 9, 10


def mm(left, right, dims=NN):
    return lax.dot_general(left, right, dims, preferred_element_type=F32)


class Far:
    def __init__(self, array):
        self.array = array


ANYWHERE = pl.BlockSpec(memory_space=pl.ANY)


class Scalars(Far):
    pass


def operands(args):
    arrays = [arg.array if isinstance(arg, Far) else arg for arg in args]
    specs = []
    for arg in args:
        if isinstance(arg, Scalars):
            specs.append(SMEM)
        else:
            specs.append(ANYWHERE if isinstance(arg, Far) else VMEM)
    return arrays, specs


def split(value, axis):
    parts = []
    for _ in range(3):
        part = value.astype(BF)
        parts.append(part)
        value = value - part.astype(F32)
    return jnp.concatenate(parts, axis)


def fetch(sems, slot, source, dest):
    copy = pltpu.make_async_copy(source, dest, sems.at[slot])
    copy.start()
    return copy


def out(shape, dtype):
    return jax.ShapeDtypeStruct(shape, dtype)


def rows(start, count):
    return pl.ds(pl.multiple_of(start, count), count)


def edge_masks(sign):
    pixel = lax.broadcasted_iota(jnp.int32, (1, PIX), 1)
    col, row = pixel % SIDE, pixel // SIDE
    table = {}
    for step in (-1, 1):
        moved_step = sign * step
        table["col", step] = ((col + moved_step >= 0) & (col + moved_step < SIDE)).astype(F32)
        table["row", step] = ((row + moved_step >= 0) & (row + moved_step < SIDE)).astype(F32)
    return table


def put_taps(dest, masks, values, first_row, depth, base, sign):
    count = values.shape[0]
    for col_step in (-1, 0, 1):
        across = values
        if col_step:
            across = pltpu.roll(values, (-sign * col_step) % PIX, 1) * masks["col", col_step]
        for row_step in (-1, 0, 1):
            copy = across
            if row_step:
                copy = pltpu.roll(across, (-sign * row_step * SIDE) % PIX, 1) * masks["row", row_step]
            tap = 3 * (row_step + 1) + col_step + 1
            dest[rows(tap * depth + first_row, count), base : base + PIX] = copy.astype(BF)


def taps_of(dest, masks, source, offset, depth, base, sign):
    for start in range(0, source.shape[0], 128):
        piece = source[start : start + 128, :].astype(F32)
        put_taps(dest, masks, piece, offset + start, depth, base, sign)


def fetch_conv(sems, full, half, which, own, peer):
    return (
        fetch(sems, 0, own.at[which], full.at[:, rows(half * 256, 256), :]),
        fetch(sems, 1, peer.at[which], full.at[:, rows((1 - half) * 256, 256), :]),
    )


def wait(copies):
    for copy in copies:
        copy.wait()


def conv_dots(dest, full, col, dims, finish):
    for column in range(0, PIX, 512):
        total = None
        for tap in range(9):
            term = mm(full[tap], col[tap * 512 : (tap + 1) * 512, column : column + 512], dims)
            total = term if total is None else total + term
        dest[:, column : column + 512] = finish(total, column)


def grouped(block):
    return block.reshape((-1, 16) + block.shape[1:])


def group_mean(block):
    return jnp.sum(block, axis=(1, 2), keepdims=True) * (1.0 / (16 * PIX))


def group_stats(block, stats, where):
    parts = grouped(block)
    centre = group_mean(parts)
    parts = parts - centre
    inverse = lax.rsqrt(group_mean(jnp.square(parts)) + EPS)
    count = block.shape[0]
    for column, value in enumerate((centre, inverse)):
        stats[where, column : column + 1] = jnp.broadcast_to(value, (count // 16, 16, 1)).reshape(count, 1)
    return (parts * inverse).reshape(block.shape)


def unit_of(block, stats, where):
    return (block - stats[where, 0:1]) * stats[where, 1:2]


def unit_back(grad, unit, inverse):
    parts, units = grouped(grad), grouped(unit)
    result = parts - group_mean(parts) - units * group_mean(parts * units)
    return result.reshape(grad.shape) * inverse


def row_sum(block):
    return jnp.sum(block, axis=1, keepdims=True)


def fetch_square(sems, slot, full, half, own, peer):
    count = own.shape[-2]
    near, far = rows(half * count, count), rows((1 - half) * count, count)
    if len(full.shape) == 3:
        near, far = (slice(None), near), (slice(None), far)
    return fetch(sems, slot, own, full.at[near]), fetch(sems, slot + 1, peer, full.at[far])


def attention(
    live_count, normed, resid, stats2, par, cotangent, cot_peer, q_own, q_peer, p_own, p_peer,
    second, first_near, squares_out, block_out, grad_resid, grad_branch, small, second_peer, first_peer,
    sems, sends, recvs, wqkv, wp, query, keys, values, grad_mixed, mixed, grad_q, grad_k, grad_v, grad_out,
    grad_normed, resid_in, squares, block, *pixel_scratch,
):
    half = lax.axis_index("head")
    live = (half < live_count[0]).astype(BF)
    arriving = fetch_square(sems, 0, wqkv, half, q_own, q_peer)
    later = fetch_square(sems, 2, wp, half, p_own, p_peer)
    later += (
        fetch(sems, 4, cotangent.at[half], grad_out.at[rows(half * 256, 256)]),
        fetch(sems, 5, cot_peer, grad_out.at[rows((1 - half) * 256, 256)]),
    )
    last = fetch(sems, 6, resid, resid_in)
    to_x = {"head": 1 - half}
    meet([to_x])
    exchanges = (
        remote(second, second_peer, sends, recvs, 0, to_x),
        remote(first_near, first_peer, sends, recvs, 1, to_x),
    )
    exchanges[0].start()
    wait(arriving)
    for column in range(0, PIX, 512):
        where = slice(column, column + 512)
        query[:, where] = (mm(wqkv[0], normed[:, where]).astype(BF).astype(F32) * 0.125).astype(BF)
        keys[:, where] = mm(wqkv[1], normed[:, where]).astype(BF)
        values[:, where] = mm(wqkv[2], normed[:, where]).astype(BF)
    wait(later)
    grad_out[...] = grad_out[...] * live
    for column in range(0, PIX, 512):
        where = slice(column, column + 512)
        grad_mixed[:, where] = mm(wp[...], grad_out[:, where]).astype(BF)

    def head(number, weights, grad_scores):
        where = rows(number * 64, 64)
        q, k, v, g = query[where, :], keys[where, :], values[where, :], grad_mixed[where, :]
        scores = mm(k.T, q)
        low = jnp.exp(scores - jnp.max(scores, axis=0, keepdims=True)).astype(BF)
        weights[...] = low
        mix = mm(jnp.concatenate([v, jnp.ones((16, PIX), BF)], 0), low)
        inverse = 1.0 / mix[64:65]
        mix = mix[0:64] * inverse
        mixed[where, :] = mix.astype(BF)
        g = (g.astype(F32) * inverse).astype(BF)
        delta = jnp.sum(mix * g.astype(F32), axis=0, keepdims=True)
        inner = low * (mm(v.T, g) - delta).astype(BF)
        grad_scores[...] = inner
        grad_q[where, :] = (mm(k, inner) * 0.125).astype(BF)
        grad_k[where, :] = mm(grad_scores[...], q.T).T.astype(BF)
        grad_v[where, :] = mm(weights[...], g.T).T.astype(BF)

    def heads(index, carry):
        for number in range(4):
            head(index * 4 + number, pixel_scratch[2 * number], pixel_scratch[2 * number + 1])
        return carry

    exchanges[1].start()
    lax.fori_loop(0, HEADS // 4, heads, 0)
    pairs = ((grad_q, normed), (grad_k, normed), (grad_v, normed), (mixed, grad_out))
    for which, (left, right) in enumerate(pairs):
        result = mm(left[...], right[...], NT).astype(BF)
        for part in range(32):
            plane, chunk = part // 16, part % 16
            squares[chunk // 8, plane, chunk % 8, which] = result[part * 16 : (part + 1) * 16]
    outgoing = (fetch(sems, 0, squares, squares_out),)
    for column in range(0, PIX, 512):
        where = slice(column, column + 512)
        grad_normed[:, where] = (
            mm(wqkv[0], grad_q[:, where], TN)
            + mm(wqkv[1], grad_k[:, where], TN)
            + mm(wqkv[2], grad_v[:, where], TN)
        )
    last.wait()
    for column in range(0, PIX, 512):
        where = slice(column, column + 512)
        total = resid_in[:, where] + mm(wp[...], mixed[:, where], TN) + par[:, PROJB : PROJB + 1]
        block[:, where] = (total * live.astype(F32)).astype(BF)
    outgoing += (fetch(sems, 1, block, block_out),)

    def back(group, carry):
        where = rows(group * BLOCK, BLOCK)
        unit = unit_of(resid_in[where, :], stats2, where)
        grad = grad_normed[where, :]
        outer = grad_out[where, :].astype(F32)
        total = outer + unit_back(grad * par[where, GAIN + 2 : GAIN + 3], unit, stats2[where, 1:2])
        low = total.astype(BF)
        grad_resid[where, :] = total
        grad_branch[where, :] = low
        small[where, 0:1] = row_sum(grad * unit)
        small[where, 1:2] = row_sum(grad)
        small[where, 2:3] = row_sum(low.astype(F32))
        small[where, 3:4] = row_sum(outer)
        return carry

    lax.fori_loop(0, 512 // BLOCK, back, 0)
    wait(outgoing)
    wait(exchanges)


def attention_call(*args):
    arrays, specs = operands(args)
    dma = pltpu.SemaphoreType.DMA
    full_bf = out((512, PIX), BF)
    squares = out((2, 2, 8, 4, 16, 512), BF)
    wide_bf = pltpu.VMEM((512, PIX), BF)
    wide_f32 = pltpu.VMEM((512, PIX), F32)
    return pl.pallas_call(
        attention,
        out_shape=[
            squares, full_bf, out((512, PIX), F32), full_bf, out((512, 4), F32), full_bf, out((256, PIX), BF),
        ],
        in_specs=specs,
        out_specs=[ANYWHERE] * 2 + [VMEM] * 3 + [ANYWHERE] * 2,
        scratch_shapes=[
            dma((8,)), dma((2,)), dma((2,)),
            pltpu.VMEM((3, 512, 512), BF),
            pltpu.VMEM((512, 512), BF),
        ]
        + [wide_bf] * 9
        + [wide_f32] * 2
        + [pltpu.VMEM(squares.shape, BF), wide_bf]
        + [pltpu.VMEM((PIX, PIX), BF)] * 8,
        cost_estimate=pl.CostEstimate(flops=3 * 10**10, bytes_accessed=20 * 2**20, transcendentals=0),
        compiler_params=pltpu.CompilerParams(
            collective_id=3, has_side_effects=True, vmem_limit_bytes=58 * 2**20
        ),
    )(*arrays)


def remote(source, dest, sends, recvs, slot, target):
    return pltpu.make_async_remote_copy(
        src_ref=source,
        dst_ref=dest,
        send_sem=sends.at[slot],
        recv_sem=recvs.at[slot],
        device_id=target,
        device_id_type=pl.DeviceIdType.MESH,
    )


def meet(targets):
    barrier = pltpu.get_barrier_semaphore()
    for target in targets:
        pl.semaphore_signal(barrier, inc=1, device_id=target, device_id_type=pl.DeviceIdType.MESH)
    pl.semaphore_wait(barrier, len(targets))


def position():
    place = lax.axis_index("batch")
    return place, place % 2, (place // 2) % 2, place // 4


PIECES = 6
KINDS = 10


def forward(
    timesteps, classes, norm_gain, norm_bias, conv_bias, proj_bias, emb_bias, emb_weight, class_table,
    images, cotangent, conv_weight, qkv_weight, proj_weight,
    par, pre_embed, image_peer, cot_peer, conv_peer, qkv_peer, proj_peer,
    first_out, near_out, other_out, hidden_out, stats0, stats1, second_out, resid, stats2, normed,
    sends, recvs, few_sends, few_recvs, sems, put_sems, columns, par_send, par_recv, lines, table, own, peer, other, spare, col, full, full_one, *kept,
):
    half = lax.axis_index("head")
    place, core, up, deep = position()
    z_low = deep % 2
    to_x = {"head": 1 - half}
    to_y = {"batch": place + 2 * (1 - 2 * up)}
    to_z = {"batch": place + 4 * (1 - 2 * z_low)}
    to_core = {"batch": place + (1 - 2 * core)}
    near, away = rows(half * 256, 256), rows((1 - half) * 256, 256)
    pictures = (
        fetch(sems, 0, images.at[half], own),
        fetch(sems, 1, images.at[1 - half], other),
    )
    table_copy = fetch(sems, 2, class_table, table)
    fulls = (full, full_one)
    first, first_near, first_other, hidden, second = kept
    own_weights = fetch(sems, 3, conv_weight.at[0], full.at[:, near, :])
    own_later = fetch(sems, 4, conv_weight.at[1], full_one.at[:, near, :])
    outgoing = []

    def put(source, dest):
        outgoing.append(fetch(put_sems, len(outgoing), source, dest))

    meet([to_x, to_y, to_z, to_core])

    def block(flip_core=0, flip_y=0, flip_z=0):
        c = 1 - core if flip_core else core
        y = 1 - up if flip_y else up
        z = 1 - z_low if flip_z else z_low
        return (c + 2 * y + 4 * z) * 32

    def views(piece, plane, start, count):
        where = rows(start, count)
        if piece < 4:
            taps = pl.ds(0, 5) if piece % 2 == 0 else pl.ds(5, 4)
            return fulls[piece // 2].at[taps, rows(plane * 256 + start, count), :]
        if piece == 4:
            return qkv_peer.at[:, where, :]
        return proj_peer.at[where, :]

    def source(piece, start, count):
        where = rows(start, count)
        if piece < 4:
            taps = pl.ds(0, 5) if piece % 2 == 0 else pl.ds(5, 4)
            return conv_weight.at[piece // 2, taps, where, :]
        if piece == 4:
            return qkv_weight.at[:, where, :]
        return proj_weight.at[where, :]

    def copy(piece, kind, start, count, target, local=False):
        dest = views(piece, half if local else 1 - half, start, count)
        return remote(
            source(piece, start, count) if local else dest, dest,
            sends.at[piece], recvs.at[piece], kind, target,
        )

    def regions(flip_core):
        return (
            (block(flip_core), 32),
            (block(flip_core, 1), 32),
            (block(flip_core, 0, 1), 32),
            (block(flip_core, 1, 1), 16),
            (block(flip_core, 1, 1) + 16, 16),
        )

    mine, others = regions(0), regions(1)

    def arrived(piece, kind):
        start, count = mine[kind] if kind < 5 else others[kind - 5]
        copy(piece, kind, start, count, to_core).wait_recv()

    def over_x(piece):
        arrived(piece, 0)
        for kind, target in ((1, to_y), (2, to_z), (5, to_core)):
            copy(piece, kind, block(), 32, target).start()

    def over_yz(piece):
        arrived(piece, 2)
        copy(piece, 3, block(0, 0, 1), 16, to_y).start()
        copy(piece, 7, block(0, 0, 1), 32, to_core).start()
        arrived(piece, 1)
        copy(piece, 4, block(0, 1, 0) + 16, 16, to_z).start()
        copy(piece, 6, block(0, 1, 0), 32, to_core).start()

    def diagonal(piece):
        arrived(piece, 3)
        copy(piece, 8, block(0, 1, 1), 16, to_core).start()
        arrived(piece, 4)
        copy(piece, 9, block(0, 1, 1) + 16, 16, to_core).start()

    def complete(piece):
        for kind in range(5, 10):
            arrived(piece, kind)

    def fetch_x(*pieces):
        for piece in pieces:
            copy(piece, 0, block(), 32, to_x, local=True).start()

    fetch_x(0, 1)

    table_copy.wait()
    width = class_table.shape[1]
    numbers = lax.broadcasted_iota(jnp.int32, (1, table.shape[0]), 1)
    freqs = jnp.exp(
        lax.broadcasted_iota(jnp.int32, (1, width // 2), 1).astype(F32) * (-math.log(10000.0) / (width // 2))
    )
    for slot in range(2):
        chosen = (numbers == classes[slot]).astype(BF)
        angles = timesteps[slot].astype(F32) * freqs
        pre_embed[slot : slot + 1, : width // 2] = jnp.cos(angles)
        pre_embed[slot : slot + 1, width // 2 : width] = jnp.sin(angles)
        line = mm(jnp.broadcast_to(chosen, (8, table.shape[0])), table[...])
        pre_embed[slot : slot + 1, :width] += line[0:1]
        pre_embed[slot : slot + 1, width:] = jnp.broadcast_to(classes[slot].astype(F32), (1, 128))
    embed = jax.nn.silu(pre_embed[:, :width])
    own_row = jnp.where(half == 0, embed[0:1], embed[1:2])
    peer_row = jnp.where(half == 0, embed[1:2], embed[0:1])
    lines[...] = jnp.zeros_like(lines)
    lines[0:3] = norm_gain[...]
    lines[3:6] = norm_bias[...]
    lines[6:8] = conv_bias[...]
    lines[8:9] = proj_bias[...]
    lines[9:11] = emb_bias[...]
    turned = lines[...].T
    columns[:, 0:11] = turned[:, 0:11]
    par[near, :] = turned[:, 0:11]
    for which in range(2):
        dense = emb_weight[which].astype(F32)
        par[near, SCALE + which : SCALE + which + 1] += row_sum(dense * own_row)
        columns[:, SCALE + which : SCALE + which + 1] += row_sum(dense * peer_row)
    par_send[...] = columns[...].T[0:16]
    block_copy = remote(par_send, par_recv, few_sends, few_recvs, 1, to_x)
    block_copy.start()

    masks = edge_masks(1)
    wait(pictures)

    def norm_zero(source, dest, base, stats, offset, group):
        here = rows(group * BLOCK, BLOCK)
        where = rows(base + group * BLOCK, BLOCK)
        unit = group_stats(source[here, :].astype(F32), stats, rows(offset + group * BLOCK, BLOCK))
        low = jax.nn.silu(unit * par[where, GAIN : GAIN + 1] + par[where, BIAS : BIAS + 1]).astype(BF)
        dest[rows(offset + group * BLOCK, BLOCK), :] = low
        return low.astype(F32)

    def norm_near(group, carry):
        low = norm_zero(own, first, half * 256, stats0, half * 256, group)
        first_near[rows(group * BLOCK, BLOCK), :] = low.astype(BF)
        put_taps(col, masks, low, half * 256 + group * BLOCK, 512, 0, 1)
        return carry

    def norm_other(group, carry):
        norm_zero(other, first_other, half * 256, spare, 0, group)
        return carry

    def conv_part(full, dest, mine, column, bias, inputs=None):
        where = near if mine else away
        result = None
        for tap in range(9):
            depth = slice(None)
            part = pl.ds(tap * 512, 512)
            if inputs is not None:
                depth = near if inputs else away
                part = rows(tap * 512 + (half if inputs else 1 - half) * 256, 256)
            term = mm(full[tap, where, depth], col[part, column : column + 512])
            result = term if result is None else result + term
        if inputs is None or inputs:
            dest[where, column : column + 512] = result + par[where, bias : bias + 1]
        else:
            dest[where, column : column + 512] += result

    over_x(0)
    fetch_x(2, 3)
    over_x(1)
    lax.fori_loop(0, 256 // BLOCK, norm_near, 0)
    over_x(2)
    picture = remote(images.at[1 - half], image_peer, few_sends, few_recvs, 0, to_x)
    picture.start()
    over_yz(0)
    over_yz(1)
    own_weights.wait()
    conv_part(full, hidden, True, 0, CONVB, True)
    diagonal(0)
    diagonal(1)
    over_yz(2)
    conv_part(full, hidden, True, 512, CONVB, True)
    complete(0)
    complete(1)
    put(full.at[:, away, :], conv_peer.at[0])
    diagonal(2)
    block_copy.wait_recv()
    par[away, :] = par_recv[...].T[:, 0:11]
    conv_part(full, hidden, False, 0, CONVB, True)
    conv_part(full, hidden, False, 512, CONVB, True)
    lax.fori_loop(0, 256 // BLOCK, norm_other, 0)
    put(first_other, other_out)
    picture.wait_recv()
    loaded = fetch(sems, 0, image_peer, peer)
    fetch_x(4, 5)
    loaded.wait()

    def norm_far(group, carry):
        low = norm_zero(peer, first, (1 - half) * 256, stats0, (1 - half) * 256, group)
        put_taps(col, masks, low, (1 - half) * 256 + group * BLOCK, 512, 0, 1)
        return carry

    lax.fori_loop(0, 256 // BLOCK, norm_far, 0)
    over_x(3)
    cot_copy = remote(cotangent.at[1 - half], cot_peer, few_sends, few_recvs, 2, to_x)
    cot_copy.start()
    conv_part(full, hidden, True, 0, CONVB, False)
    conv_part(full, hidden, True, 512, CONVB, False)
    over_yz(3)
    over_x(4)
    over_x(5)
    conv_part(full, hidden, False, 0, CONVB, False)
    diagonal(3)
    conv_part(full, hidden, False, 512, CONVB, False)
    over_yz(4)
    over_yz(5)
    put(hidden, hidden_out)
    put(first, first_out)
    put(first_near, near_out)

    def norm_one(group, carry):
        where = rows(group * BLOCK, BLOCK)
        unit = group_stats(hidden[where, :], stats1, where)
        unscaled = unit * par[where, GAIN + 1 : GAIN + 2] + par[where, BIAS + 1 : BIAS + 2]
        pre = unscaled * (1.0 + par[where, SCALE : SCALE + 1]) + par[where, SHIFT : SHIFT + 1]
        low = jax.nn.silu(pre).astype(BF)
        second[where, :] = low
        put_taps(col, masks, low.astype(F32), group * BLOCK, 512, 0, 1)
        return carry

    lax.fori_loop(0, 512 // BLOCK, norm_one, 0)
    complete(2)
    complete(3)
    put(full_one.at[:, away, :], conv_peer.at[1])
    put(second, second_out)
    diagonal(4)
    diagonal(5)
    own_later.wait()
    conv_part(full_one, resid, True, 0, CONVB + 1)
    conv_part(full_one, resid, True, 512, CONVB + 1)
    conv_part(full_one, resid, False, 0, CONVB + 1)
    conv_part(full_one, resid, False, 512, CONVB + 1)
    for image, base in ((own, half * 256), (peer, (1 - half) * 256)):

        def norm_two(group, carry, image=image, base=base):
            where = rows(base + group * BLOCK, BLOCK)
            total = resid[where, :] + image[rows(group * BLOCK, BLOCK), :].astype(F32)
            resid[where, :] = total
            unit = group_stats(total, stats2, where)
            normed[where, :] = (unit * par[where, GAIN + 2 : GAIN + 3] + par[where, BIAS + 2 : BIAS + 3]).astype(BF)
            return carry

        lax.fori_loop(0, 256 // BLOCK, norm_two, 0)
    complete(4)
    complete(5)
    cot_copy.wait_recv()
    for piece in range(PIECES):
        copy(piece, 0, block(), 32, to_x).wait_send()
        for kind, start, count in (
            (1, block(), 32), (2, block(), 32), (5, block(), 32),
            (3, block(0, 0, 1), 16), (7, block(0, 0, 1), 32),
            (4, block(0, 1, 0) + 16, 16), (6, block(0, 1, 0), 32),
            (8, block(0, 1, 1), 16), (9, block(0, 1, 1) + 16, 16),
        ):
            copy(piece, kind, start, count, to_x).wait_send()
    wait(outgoing)
    picture.wait_send()
    block_copy.wait_send()
    cot_copy.wait_send()


def forward_call(timesteps, classes, *args):
    arrays, specs = operands((Scalars(timesteps), Scalars(classes)) + args)
    images, cotangent, conv_weight, qkv_weight, proj_weight = arrays[-5:]
    width = arrays[-6].shape[1]
    half_bf = out((256, PIX), BF)
    full_bf = out((512, PIX), BF)
    full_f32 = out((512, PIX), F32)
    stats = out((512, 2), F32)
    dma = pltpu.SemaphoreType.DMA
    half_scratch = pltpu.VMEM((256, PIX), BF)
    return pl.pallas_call(
        forward,
        out_shape=[
            out((512, 11), F32),
            out((2, width + 128), F32),
            half_bf,
            half_bf,
            out(conv_weight.shape, BF),
            out(qkv_weight.shape, BF),
            out(proj_weight.shape, BF),
            full_bf, half_bf, half_bf, full_f32, stats, stats, full_bf, full_f32, stats, full_bf,
        ],
        in_specs=specs,
        out_specs=[VMEM] * 2 + [ANYWHERE] * 9 + [VMEM] * 2 + [ANYWHERE] + [VMEM] * 3,
        scratch_shapes=[
            dma((PIECES, KINDS)), dma((PIECES, KINDS)), dma((3,)), dma((3,)), dma((5,)), dma((7,)),
            pltpu.VMEM((256, 128), F32),
            pltpu.VMEM((16, 256), F32),
            pltpu.VMEM((16, 256), F32),
            pltpu.VMEM((16, 256), F32),
            pltpu.VMEM(arrays[-6].shape, BF),
            half_scratch, half_scratch, half_scratch,
            pltpu.VMEM((256, 2), F32),
            pltpu.VMEM((9 * 512, PIX), BF),
            pltpu.VMEM((9, 512, 512), BF),
            pltpu.VMEM((9, 512, 512), BF),
            pltpu.VMEM((512, PIX), BF),
            half_scratch,
            half_scratch,
            pltpu.VMEM((512, PIX), F32),
            pltpu.VMEM((512, PIX), BF),
        ],
        cost_estimate=pl.CostEstimate(flops=2 * 10**10, bytes_accessed=100 * 2**20, transcendentals=0),
        compiler_params=pltpu.CompilerParams(
            collective_id=1, has_side_effects=True, vmem_limit_bytes=58 * 2**20
        ),
    )(*arrays)


SENDS = 12


class Sum:
    def __init__(self, source, total, scratch, planes):
        self.source, self.total, self.planes = source, total, planes
        self.sends, self.recvs, self.core_in, self.first, self.y_in, self.second, self.z_in, self.result = scratch[:8]
        if planes:
            self.middle, self.x_in = scratch[8:10]
        self.half = lax.axis_index("head")
        self.place, self.core, self.up, self.deep = position()
        self.steps = [self.start, self.core_done, self.y_done, self.z_done]
        if planes:
            self.steps.append(self.x_done)
        self.steps += [self.z_back, self.y_back, self.finish]
        self.open = []
        self.count = 0

    def advance(self):
        if self.count < len(self.steps):
            self.steps[self.count]()
            self.count += 1

    def part(self, array, start, count):
        where = pl.ds(start, count)
        return array.at[:, where] if self.planes else array.at[where]

    def to_core(self):
        return {"batch": self.place + 1 - 2 * self.core}

    def to_y(self):
        return {"batch": self.place + 2 * (1 - 2 * self.up)}

    def to_z(self, ahead):
        return {"batch": (self.deep + ahead) % 4 * 4 + self.place % 4}

    def send(self, slot, source, dest, target):
        copy = remote(source, dest, self.sends, self.recvs, slot, target)
        copy.start()
        self.open.append(copy)

    def arrived(self, slot, dest):
        remote(dest, dest, self.sends, self.recvs, slot, self.to_core()).wait_recv()

    def of_core(self, core):
        return self.source.at[core] if self.planes else self.source.at[pl.ds(core * 8, 8)]

    def start(self):
        self.send(0, self.of_core(1 - self.core), self.core_in, self.to_core())

    def add(self, dest, left, *right):
        total = left[...].astype(F32)
        for term in right:
            total = total + term[...].astype(F32)
        dest[...] = total.astype(BF)

    def core_done(self):
        self.arrived(0, self.core_in)
        self.add(self.first, self.of_core(self.core), self.core_in)
        self.send(1, self.part(self.first, (1 - self.up) * 4, 4), self.y_in, self.to_y())

    def y_done(self):
        self.arrived(1, self.y_in)
        self.add(self.second, self.part(self.first, self.up * 4, 4), self.y_in)
        for ahead in (2, 1, 3):
            chunk = self.part(self.second, (self.deep + ahead) % 4, 1)
            self.send(1 + ahead, chunk, self.z_in.at[ahead - 1], self.to_z(ahead))

    def z_done(self):
        for ahead in (1, 2, 3):
            self.arrived(1 + ahead, self.z_in.at[ahead - 1])
        mine = self.part(self.second, self.deep, 1)
        terms = [self.z_in.at[number] for number in range(3)]
        if self.planes:
            self.add(self.middle, mine, *terms)
            self.send(10, self.middle.at[1 - self.half], self.x_in, {"head": 1 - self.half})
        else:
            self.add(self.result, mine, *terms)
            self.give()

    def x_done(self):
        self.arrived(10, self.x_in)
        self.add(self.result, self.middle.at[self.half], self.x_in)
        self.give()

    def chunks(self, start, count):
        return self.total.at[pl.ds(start, count)]

    def chunk(self, deep):
        return self.core * 8 + self.up * 4 + deep

    def give(self):
        mine = self.chunks(self.chunk(self.deep), 1)
        for ahead in (2, 1, 3):
            self.send(4 + ahead, self.result, mine, self.to_z(ahead))
        self.kept = pltpu.make_async_copy(self.result, mine, self.sends.at[11])
        self.kept.start()

    def z_back(self):
        for ahead in (1, 2, 3):
            self.arrived(4 + ahead, self.chunks(self.chunk((self.deep + 4 - ahead) % 4), 1))
        self.kept.wait()
        part = self.chunks(self.chunk(0), 4)
        self.send(8, part, part, self.to_y())

    def y_back(self):
        self.arrived(8, self.chunks(self.core * 8 + (1 - self.up) * 4, 4))
        part = self.chunks(self.core * 8, 8)
        self.send(9, part, part, self.to_core())

    def finish(self):
        self.arrived(9, self.chunks((1 - self.core) * 8, 8))
        for copy in self.open:
            copy.wait_send()


def sum_scratch(tail, planes):
    lead = (2,) if planes else ()
    shapes = [
        pltpu.SemaphoreType.DMA((SENDS,)),
        pltpu.SemaphoreType.DMA((SENDS,)),
        pltpu.VMEM(lead + (8,) + tail, BF),
        pltpu.VMEM(lead + (8,) + tail, BF),
        pltpu.VMEM(lead + (4,) + tail, BF),
        pltpu.VMEM(lead + (4,) + tail, BF),
        pltpu.VMEM((3,) + lead + (1,) + tail, BF),
        pltpu.VMEM((1,) + tail, BF),
    ]
    if planes:
        shapes += [pltpu.VMEM((2, 1) + tail, BF), pltpu.VMEM((1,) + tail, BF)]
    return shapes


def weight_back(grads, chunk_taps, col, turned):
    for tap in chunk_taps:
        result = mm(col[tap * 256 : (tap + 1) * 256, :], turned[:PIX, :])
        result = result + mm(col[(9 + tap) * 256 : (10 + tap) * 256, :], turned[PIX:, :])
        result = result.astype(BF)
        for part in range(16):
            grads[part, tap] = result[part * 16 : (part + 1) * 16]


PARTS = ((0, 2), (2, 4), (4, 6), (6, 8), (8, 9))
HALVES = ((0, 2), (2, 4))

(TAPS_ONE, CONV_ONE, AWAY_ONE, NEAR_ONE, PAIR_ONE, GRAD_ONE, SHARE, PAIR_ZERO,
 GRAD_ZERO, TAPS_ZERO, CONV_ZERO, AWAY_ZERO, NEAR_ZERO, ROWS, SMALL) = range(100, 115)
ORDER = (
    TAPS_ONE, 0, 1, CONV_ONE, 0, 1, CONV_ONE, AWAY_ONE, NEAR_ONE, 0, PAIR_ONE, GRAD_ONE, 2, 1,
    GRAD_ONE, 2, 3, GRAD_ONE, 0, 4, 3, GRAD_ONE, 4, 5, 2, GRAD_ONE, 6, SHARE, PAIR_ZERO, 5, 1, 3, 6,
    2, 4, GRAD_ZERO, 7, GRAD_ZERO, 5, 8, 3, 7, 6, 0, GRAD_ZERO, 1, 8, 2, 9, GRAD_ZERO, 7, 10, 4, 9,
    GRAD_ZERO, 11, TAPS_ZERO, 10, 8, 5, 11, CONV_ZERO, 2, 3, 6, 9, CONV_ZERO, 0, 2, 10, 11, 1,
    AWAY_ZERO, 3, 7, NEAR_ZERO, 3, 0, 4, ROWS, 0, 1, 8, 1, 4, 5, 6, 4, SMALL, 9, 5, 6, SMALL, 5, 10,
    6, SMALL, 11, 7, 8, 7, 9, 7, 8, 10, 8, SMALL, 9, 11, 9, 10, 11, 10, 11,
)


def backward(
    live_count, squares, grad_branch, block, hidden, second, second_peer,
    first, first_other, first_peer, grad_resid, images, image_peer, w_own, w_peer,
    stats0, stats1, par, small2, pre_embed, emb_weight,
    square_sum, sum1, sum0, images_grad, far_in, block_out, sums, class_rows, mod_out, pre_out,
    sems, sends, recvs, all_sends, all_recvs,
    grads1, grads0, col, turned, full, slope_in, wide_in, source_in, branch_in, hidden_in, grad_hidden,
    far, columns, flat, mod, mod_send, pres, rows_own, rows_in, total, total_in,
    *scratch,
):
    half = lax.axis_index("head")
    place, core, up, deep = position()
    to_x = {"head": 1 - half}
    others = [{"batch": (place + ahead) % 16} for ahead in range(1, 16)]
    near, away = rows(half * 256, 256), rows((1 - half) * 256, 256)
    exchanges = {}
    local = {}

    local["weights"] = fetch_conv(sems.at[pl.ds(6, 2)], full, half, 1, w_own, w_peer)
    local["wide"] = (fetch(sems, 8, hidden, wide_in),)
    local["inputs"] = (
        fetch(sems, 9, second, source_in.at[0]),
        fetch(sems, 10, second_peer, source_in.at[1]),
    )
    meet([to_x] + others)

    def send(slot, source, dest, target):
        exchanges[slot] = remote(source, dest, sends, recvs, slot, target)
        exchanges[slot].start()

    send(0, grad_branch.at[away], branch_in, to_x)

    chains = []
    for low, high in HALVES:
        where = pl.ds(low, high - low)
        chains.append(Sum(squares.at[:, :, :, where], square_sum.at[:, where], scratch[:10], True))
        scratch = scratch[10:]
    for source, dest in ((grads1, sum1), (grads0, sum0)):
        for low, high in PARTS:
            where = pl.ds(low, high - low)
            chains.append(Sum(source.at[:, where], dest.at[:, where], scratch[:8], False))
            scratch = scratch[8:]

    masks = edge_masks(-1)
    pair = col.at[pl.ds(9 * 256, 9 * 256)]
    picture = source_in.at[0]
    width = emb_weight.shape[2]

    def taps_one(_):
        taps_of(col, masks, grad_branch, 0, 512, 0, -1)
        wait(local["weights"])

    def conv_back(count):
        column = 512 * count
        result = None
        for tap in range(9):
            term = mm(full[tap], col[tap * 512 : (tap + 1) * 512, column : column + 512], TN)
            result = term if result is None else result + term
        slope_in[:, column : column + 512] = result

    def back_one(base):
        def step(group, carry):
            where = rows(base + group * BLOCK, BLOCK)
            unit = unit_of(wide_in[where, :], stats1, where)
            gain = par[where, GAIN + 1 : GAIN + 2]
            unscaled = unit * gain + par[where, BIAS + 1 : BIAS + 2]
            scale = 1.0 + par[where, SCALE : SCALE + 1]
            grad_pre = slope_in[where, :] * silu_slope(unscaled * scale + par[where, SHIFT : SHIFT + 1])
            grad = grad_pre * scale
            low = unit_back(grad * gain, unit, stats1[where, 1:2]).astype(BF)
            grad_hidden[where, :] = low
            columns[where, 2:3] = row_sum(grad_pre * unscaled)
            columns[where, 3:4] = row_sum(grad_pre)
            columns[where, 4:5] = row_sum(grad * unit)
            columns[where, 5:6] = row_sum(grad)
            columns[where, 6:7] = row_sum(low.astype(F32))
            return carry

        lax.fori_loop(0, 256 // BLOCK, step, 0)

    def away_one(_):
        local["weights"] = fetch_conv(sems.at[pl.ds(6, 2)], full, half, 0, w_own, w_peer)
        columns[...] = jnp.zeros_like(columns)
        columns[:, 7:11] = small2[...]
        wait(local["wide"])
        back_one((1 - half) * 256)
        send(1, grad_hidden.at[away], hidden_in, to_x)

    def near_one(_):
        back_one(half * 256)
        local["wide"] = (fetch(sems, 8, grad_resid, wide_in),)
        flat[...] = columns[...].T[0:16]
        mod[place, half] = flat[2:4, near]
        mod_send[...] = flat[2:4, away]
        send(2, mod_send, mod.at[place, half], to_x)
        pres[place] = pre_embed[...]
        for ahead, target in enumerate(others):
            remote(pres.at[place], pres.at[place], all_sends, all_recvs, ahead, target).start()

    def pair_one(_):
        exchanges[0].wait_recv()
        taps_of(col, masks, grad_branch.at[near], 0, 256, 0, -1)
        taps_of(pair, masks, branch_in, 0, 256, 0, -1)
        wait(local["inputs"])
        turned[:PIX, :] = source_in[0].T
        turned[PIX:, :] = source_in[1].T
        local["inputs"] = (
            fetch(sems, 9, first, source_in.at[0]),
            fetch(sems, 10, first_other, source_in.at[1, near]),
            fetch(sems, 11, first_peer, source_in.at[1, away]),
        )

    def grad_one(count):
        weight_back(grads1, range(*PARTS[count]), col, turned)
        if count == 0:
            send(6, block.at[away], block_out.at[half], to_x)
            local["block"] = fetch(sems, 3, block.at[near], block_out.at[half])

    def share(_):
        remote(mod_send, mod.at[place, 1 - half], sends, recvs, 2, to_x).wait_recv()
        for ahead, target in enumerate(others):
            remote(mod.at[place], mod.at[place], all_sends, all_recvs, 15 + ahead, target).start()

    def pair_zero(_):
        exchanges[1].wait_recv()
        taps_of(col, masks, grad_hidden.at[near], 0, 256, 0, -1)
        taps_of(pair, masks, hidden_in, 0, 256, 0, -1)
        wait(local["inputs"])
        turned[:PIX, :] = source_in[0].T
        turned[PIX:, :] = source_in[1].T
        local["inputs"] = (
            fetch(sems, 9, images.at[half], picture.at[near]),
            fetch(sems, 10, image_peer, picture.at[away]),
        )

    def grad_zero(count):
        weight_back(grads0, range(*PARTS[count]), col, turned)

    def taps_zero(_):
        taps_of(col, masks, grad_hidden, 0, 512, 0, -1)
        wait(local["weights"])

    def back_zero(base, dest):
        def step(group, carry):
            here = rows(group * BLOCK, BLOCK)
            where = rows(base + group * BLOCK, BLOCK)
            unit = unit_of(picture[where, :].astype(F32), stats0, where)
            gain = par[where, GAIN : GAIN + 1]
            grad = slope_in[where, :] * silu_slope(unit * gain + par[where, BIAS : BIAS + 1])
            result = wide_in[where, :] + unit_back(grad * gain, unit, stats0[where, 1:2])
            dest[here, :] = result.astype(dest.dtype)
            columns[where, 0:1] = row_sum(grad * unit)
            columns[where, 1:2] = row_sum(grad)
            return carry

        lax.fori_loop(0, 256 // BLOCK, step, 0)

    def away_zero(_):
        wait(local["inputs"])
        wait(local["wide"])
        back_zero((1 - half) * 256, far)
        send(3, far, far_in, to_x)

    def near_zero(_):
        back_zero(half * 256, images_grad)
        flat[...] = columns[...].T[0:16]
        total[0] = flat[:, away]
        send(4, total.at[0], total_in.at[0], to_x)

    def class_part(_):
        for ahead in range(15):
            origin = (place + 15 - ahead) % 16
            remote(pres.at[origin], pres.at[origin], all_sends, all_recvs, ahead, to_x).wait_recv()
            remote(mod.at[origin], mod.at[origin], all_sends, all_recvs, 15 + ahead, to_x).wait_recv()
        result = None
        for which in range(2):
            factor = jnp.concatenate([mod[:, 0, which, :], mod[:, 1, which, :]], 0)
            term = mm(split(factor, 0), emb_weight[which])
            result = term if result is None else result + term
        result = result[0:32] + result[32:64] + result[64:96]
        rows_own[0] = result[0:16]
        rows_own[1] = result[16:32]
        send(5, rows_own, rows_in, to_x)

    def landed(slot, step):
        remote(total.at[0], total_in.at[step], sends, recvs, slot, to_x).wait_recv()

    def small_sums(count):
        if count == 0:
            landed(4, 0)
            total[1] = flat[:, near] + total_in[0]
            send(7, total.at[1], total_in.at[1], {"batch": place + 1 - 2 * core})
        elif count == 1:
            landed(7, 1)
            total[2] = total[1] + total_in[1]
            send(8, total.at[2], total_in.at[2], {"batch": place + 2 * (1 - 2 * up)})
        elif count == 2:
            landed(8, 2)
            total[3] = total[2] + total_in[2]
            for ahead in (1, 2, 3):
                target = {"batch": (deep + ahead) % 4 * 4 + place % 4}
                send(8 + ahead, total.at[3], total_in.at[3 + deep], target)
            total_in[3 + deep] = total[3]
        else:
            for ahead in (1, 2, 3):
                landed(8 + ahead, 3 + (deep + 4 - ahead) % 4)
            sums[...] = (total_in[3] + total_in[4]) + (total_in[5] + total_in[6])
            remote(rows_own, rows_in, sends, recvs, 5, to_x).wait_recv()
            for slot in range(2):
                class_rows[slot] = (rows_own[slot] + rows_in[slot]) * silu_slope(pres[:, slot, :width])
            mod_out[...] = mod[...]
            pre_out[...] = pres[...]

    pieces = {
        TAPS_ONE: taps_one, CONV_ONE: conv_back, AWAY_ONE: away_one, NEAR_ONE: near_one,
        PAIR_ONE: pair_one, GRAD_ONE: grad_one, SHARE: share, PAIR_ZERO: pair_zero,
        GRAD_ZERO: grad_zero, TAPS_ZERO: taps_zero, CONV_ZERO: conv_back, AWAY_ZERO: away_zero,
        NEAR_ZERO: near_zero, ROWS: class_part, SMALL: small_sums,
    }
    counts = dict.fromkeys(pieces, 0)
    for entry in ORDER:
        if entry < 100:
            chains[entry].advance()
        else:
            pieces[entry](counts[entry])
            counts[entry] += 1
    remote(far, far_in, sends, recvs, 3, to_x).wait_recv()
    remote(block.at[away], block_out.at[1 - half], sends, recvs, 6, to_x).wait_recv()
    local["block"].wait()
    for copy in exchanges.values():
        copy.wait_send()
    for ahead, target in enumerate(others):
        remote(pres.at[place], pres.at[place], all_sends, all_recvs, ahead, target).wait_send()
        remote(mod.at[place], mod.at[place], all_sends, all_recvs, 15 + ahead, target).wait_send()


def backward_call(*args):
    arrays, specs = operands(args)
    dma = pltpu.SemaphoreType.DMA
    scratch = [
        dma((12,)), dma((12,)), dma((12,)), dma((30,)), dma((30,)),
        pltpu.VMEM((16, 9, 16, 512), BF),
        pltpu.VMEM((16, 9, 16, 512), BF),
        pltpu.VMEM((9 * 512, PIX), BF),
        pltpu.VMEM((2 * PIX, 512), BF),
        pltpu.VMEM((9, 512, 512), BF),
        pltpu.VMEM((512, PIX), F32),
        pltpu.VMEM((512, PIX), F32),
        pltpu.VMEM((2, 512, PIX), BF),
        pltpu.VMEM((256, PIX), BF),
        pltpu.VMEM((256, PIX), BF),
        pltpu.VMEM((512, PIX), BF),
        pltpu.VMEM((256, PIX), BF),
        pltpu.VMEM((512, 128), F32),
        pltpu.VMEM((16, 512), F32),
        pltpu.VMEM((16, 2, 2, 256), F32),
        pltpu.VMEM((2, 256), F32),
        pltpu.VMEM((16, 2, 1024 + 128), F32),
        pltpu.VMEM((2, 16, 1024), F32),
        pltpu.VMEM((2, 16, 1024), F32),
        pltpu.VMEM((4, 16, 256), F32),
        pltpu.VMEM((7, 16, 256), F32),
    ]
    for low, high in HALVES:
        scratch += sum_scratch((high - low, 16, 512), True)
    for low, high in PARTS * 2:
        scratch += sum_scratch((high - low, 16, 512), False)
    outs = [
        (out((16, 4, 16, 512), BF), ANYWHERE),
        (out((16, 9, 16, 512), BF), ANYWHERE),
        (out((16, 9, 16, 512), BF), ANYWHERE),
        (out((256, PIX), F32), VMEM),
        (out((256, PIX), BF), ANYWHERE),
        (out((2, 256, PIX), BF), ANYWHERE),
        (out((16, 256), F32), VMEM),
        (out((2, 16, 1024), F32), VMEM),
        (out((16, 2, 2, 256), F32), VMEM),
        (out((16, 2, 1024 + 128), F32), VMEM),
    ]
    return pl.pallas_call(
        backward,
        out_shape=[o for o, _ in outs],
        in_specs=specs,
        out_specs=[spec for _, spec in outs],
        scratch_shapes=scratch,
        cost_estimate=pl.CostEstimate(flops=4 * 10**10, bytes_accessed=200 * 2**20, transcendentals=0),
        compiler_params=pltpu.CompilerParams(
            collective_id=2, has_side_effects=True, vmem_limit_bytes=60 * 2**20
        ),
    )(*arrays)


TRIPLES = ((0, 3), (3, 6), (6, 9))


def finish(
    sum0, sum1, squares, near, far, mod, pres, rows_in, sums,
    conv, qkv, proj, images_grad, emb, table, gains, biases, conv_biases, emb_biases, proj_bias,
    ins, outs, low, low_square, wide, square, mine, other, grads, emb_out, table_out,
):
    half = lax.axis_index("head")
    width = rows_in.shape[2]
    reads = []
    for layer, source in enumerate((sum0, sum1)):
        for number, (start, stop) in enumerate(TRIPLES):
            taps = pl.ds(start, stop - start)
            reads.append(fetch(ins, layer * 3 + number, source.at[:, taps], low.at[layer, :, taps]))
    reads.append(fetch(ins, 6, squares, low_square))
    reads.append(fetch(ins, 7, near, mine))
    reads.append(fetch(ins, 8, far, other))
    writes = []

    def write(source, dest):
        writes.append(fetch(outs, len(writes), source, dest))

    for number, row in enumerate((0, 4, 7)):
        gains[number : number + 1] = sums[row : row + 1]
        biases[number : number + 1] = sums[row + 1 : row + 2]
    conv_biases[0:1] = sums[6:7]
    conv_biases[1:2] = sums[9:10]
    emb_biases[...] = sums[2:4]
    proj_bias[...] = sums[10:11]

    numbers = lax.broadcasted_iota(jnp.int32, (32, table.shape[0]), 1)
    ids = jnp.concatenate([pres[:, slot, width : width + 1] for slot in range(2)], 0).astype(jnp.int32)
    chosen = (numbers == ids).astype(F32).astype(BF)
    class_rows = jnp.concatenate([rows_in[0], rows_in[1]], 0)
    table_out[...] = mm(jnp.concatenate([chosen] * 3, 0), split(class_rows, 0), TN)
    write(table_out, table)
    embed = jnp.concatenate([jax.nn.silu(pres[:, slot, :width]) for slot in range(2)], 0)
    parts = split(embed, 0)
    high, middle = parts[0:32], parts[32:64]
    for which in range(2):
        factor = split(jnp.concatenate([mod[:, slot, which, :] for slot in range(2)], 0), 0)
        left = jnp.concatenate([factor[0:32], factor[0:32], factor[32:64]], 0)
        emb_out[which] = mm(left, jnp.concatenate([high, middle, high], 0), TN)
    write(emb_out, emb)
    for layer in range(2):
        for number, (start, stop) in enumerate(TRIPLES):
            reads[layer * 3 + number].wait()
            for tap in range(start, stop):
                wide[layer, tap] = low[layer, :, tap].reshape(256, 512).astype(F32)
            taps = pl.ds(start, stop - start)
            write(wide.at[layer, taps], conv.at[layer, taps])
    reads[6].wait()
    for which in range(4):
        square[which] = low_square[:, which].reshape(256, 512).astype(F32)
    write(square.at[pl.ds(0, 3)], qkv)
    write(square.at[3], proj)
    reads[7].wait()
    reads[8].wait()
    grads[half] = mine[...]
    grads[1 - half] = other[...].astype(F32)
    write(grads, images_grad)
    wait(writes)


def finish_call(sum0, sum1, squares, near, far, mod, pres, rows_in, sums, table_shape):
    width = table_shape[1]
    shapes = [
        (2, 9, 256, 512),
        (3, 256, 512),
        (256, 512),
        (2, 256, PIX),
        (2, 256, width),
        table_shape,
        (3, 256),
        (3, 256),
        (2, 256),
        (2, 256),
        (1, 256),
    ]
    dma = pltpu.SemaphoreType.DMA
    return pl.pallas_call(
        finish,
        out_shape=[out(shape, F32) for shape in shapes],
        in_specs=[ANYWHERE] * 5 + [VMEM] * 4,
        out_specs=[ANYWHERE] * 6 + [VMEM] * 5,
        scratch_shapes=[
            dma((9,)), dma((11,)),
            pltpu.VMEM((2,) + sum0.shape, BF),
            pltpu.VMEM(squares.shape, BF),
            pltpu.VMEM(shapes[0], F32),
            pltpu.VMEM((4, 256, 512), F32),
            pltpu.VMEM((256, PIX), F32),
            pltpu.VMEM((256, PIX), BF),
            pltpu.VMEM(shapes[3], F32),
            pltpu.VMEM(shapes[4], F32),
            pltpu.VMEM(shapes[5], F32),
        ],
        compiler_params=pltpu.CompilerParams(vmem_limit_bytes=58 * 2**20),
    )(sum0, sum1, squares, near, far, mod, pres, rows_in, sums)


def paired(
    images,
    timesteps,
    classes,
    live_count,
    norm_gain,
    norm_bias,
    conv_weight,
    conv_bias,
    emb_weight,
    emb_bias,
    class_table,
    qkv_weight,
    proj_weight,
    proj_bias,
    cotangent,
):
    (
        par, pre_embed, image_peer, cot_peer, conv_peer, q_peer, p_peer,
        first, first_near, first_other, hidden, stats0, stats1, second, resid, stats2, normed,
    ) = forward_call(
        timesteps, classes, norm_gain, norm_bias, conv_bias, proj_bias[None], emb_bias, emb_weight,
        *map(Far, (class_table, images, cotangent, conv_weight, qkv_weight, proj_weight)),
    )
    square_grads, block, grad_resid, grad_branch, small2, second_peer, first_peer = attention_call(
        Scalars(live_count), normed, Far(resid), stats2, par, Far(cotangent), Far(cot_peer),
        Far(qkv_weight), Far(q_peer), Far(proj_weight), Far(p_peer), Far(second), Far(first_near),
    )
    square_sum, conv_sum1, conv_sum0, near, far, block_out, sums, class_rows, mod, pre_all = backward_call(
        Scalars(live_count), square_grads, grad_branch, *map(Far, (block, hidden, second, second_peer)),
        *map(Far, (first, first_other, first_peer, grad_resid, images, image_peer, conv_weight, conv_peer)),
        stats0, stats1, par, small2, pre_embed, emb_weight,
    )
    (
        conv_total, qkv_total, proj_total, images_grad, emb_total, table_total,
        gains, biases, conv_biases, emb_biases, proj_biases,
    ) = finish_call(
        conv_sum0, conv_sum1, square_sum, near, far, mod, pre_all, class_rows, sums, class_table.shape
    )
    return (
        block_out,
        images_grad,
        gains,
        biases,
        conv_total,
        conv_biases,
        emb_total,
        emb_biases,
        table_total,
        qkv_total,
        proj_total,
        proj_biases[0],
    )


def solution(mesh):
    in_specs = (
        P("batch", "head", None),
        P("batch"),
        P("batch"),
        P("batch"),
        P(None, "head"),
        P(None, "head"),
        P(None, None, "head", None),
        P(None, "head"),
        P(None, "head", None),
        P(None, "head"),
        P(),
        P(None, "head", None),
        P("head", None),
        P("head"),
        P("batch", "head", None),
    )
    out_specs = (
        P("batch", "head", None),
        P("batch", "head", None),
        P(None, "head"),
        P(None, "head"),
        P(None, None, "head", None),
        P(None, "head"),
        P(None, "head", None),
        P(None, "head"),
        P(),
        P(None, "head", None),
        P("head", None),
        P("head"),
    )
    body = shards
    if mesh.shape["head"] == 2 and mesh.shape["batch"] == 16:
        body = paired
    return jax.shard_map(body, mesh=mesh, in_specs=in_specs, out_specs=out_specs, check_vma=False)
```

```python
import math

import jax
import jax.numpy as jnp
from jax import lax
from jax.experimental import pallas as pl
from jax.experimental.pallas import tpu as pltpu
from jax.sharding import PartitionSpec as P

C = 512
GROUPS = 32
HEADS = 8
SIDE = 32


EPS = 1e-05
HIGH = lax.Precision.HIGHEST
CONTRACT_FIRST = (((0,), (0,)), ((), ()))
CONTRACT_LAST = (((1,), (1,)), ((), ()))


def silu_slope(values):
    sigma = jax.nn.sigmoid(values)
    return sigma * (1.0 + values * (1.0 - sigma))


def moved(source, grid_side, row_step, col_step):
    grid = source.reshape(source.shape[0], grid_side, grid_side)
    padded = jnp.pad(grid, ((0, 0), (1, 1), (1, 1)))
    window = padded[
        :, 1 + row_step : 1 + row_step + grid_side, 1 + col_step : 1 + col_step + grid_side
    ]
    return window.reshape(source.shape)


def group_unit(source, groups):
    grouped = source.reshape(groups, -1)
    centre = grouped - jnp.mean(grouped, axis=1, keepdims=True)
    inverse = lax.rsqrt(jnp.mean(jnp.square(centre), axis=1, keepdims=True) + EPS)
    return ((centre * inverse).reshape(source.shape), inverse)


def group_back(grad_unit, unit_rows, inverse, groups):
    flat_grad = grad_unit.reshape(groups, -1)
    flat_unit = unit_rows.reshape(groups, -1)
    result = flat_grad - jnp.mean(flat_grad, axis=1, keepdims=True)
    result = (result - flat_unit * jnp.mean(flat_grad * flat_unit, axis=1, keepdims=True)) * inverse
    return result.reshape(grad_unit.shape)


def conv_apply(weight, source, grid_side):
    result = jnp.dot(
        weight[0], moved(source, grid_side, -1, -1), preferred_element_type=jnp.float32
    )
    for tap_index in range(1, 9):
        result = result + jnp.dot(
            weight[tap_index],
            moved(source, grid_side, tap_index // 3 - 1, tap_index % 3 - 1),
            preferred_element_type=jnp.float32,
        )
    return result


def conv_transpose(weight, grads, grid_side):
    result = lax.dot_general(
        weight[0], moved(grads, grid_side, 1, 1), CONTRACT_FIRST, preferred_element_type=jnp.float32
    )
    for tap_index in range(1, 9):
        result = result + lax.dot_general(
            weight[tap_index],
            moved(grads, grid_side, 1 - tap_index // 3, 1 - tap_index % 3),
            CONTRACT_FIRST,
            preferred_element_type=jnp.float32,
        )
    return result


def conv_weight_grads(grads, source, grid_side):
    return jnp.stack(
        [
            lax.dot_general(
                grads,
                moved(source, grid_side, tap_index // 3 - 1, tap_index % 3 - 1),
                CONTRACT_LAST,
                preferred_element_type=jnp.float32,
            )
            for tap_index in range(9)
        ]
    )


def features(timestep, emb_width):
    half_width = emb_width // 2
    freqs = jnp.exp(-math.log(10000.0) * jnp.arange(half_width, dtype=jnp.float32) / half_width)
    angles = timestep.astype(jnp.float32) * freqs
    return jnp.concatenate([jnp.cos(angles), jnp.sin(angles)])


def shards(
    images,
    timesteps,
    classes,
    live_count,
    norm_gain,
    norm_bias,
    conv_weight,
    conv_bias,
    emb_weight,
    emb_bias,
    class_table,
    qkv_weight,
    proj_weight,
    proj_bias,
    cotangent,
):
    slot_count, chan_dev, pixel_count = images.shape
    grid_side = SIDE
    groups = chan_dev // (C // GROUPS)
    head_size = C // HEADS
    heads_dev = chan_dev // head_size
    att_scale = head_size ** (-0.5)
    emb_dense = emb_weight.astype(jnp.float32)
    class_total, emb_width = class_table.shape

    def gather_channels(rows_low):
        return lax.all_gather(rows_low, "head", axis=0, tiled=True)

    def input_grad(which_conv, grad_rows):
        weight_cols = conv_weight[which_conv]
        return lax.psum_scatter(
            conv_transpose(weight_cols, grad_rows, grid_side).astype(jnp.bfloat16),
            "head",
            scatter_dimension=0,
            tiled=True,
        ).astype(jnp.float32)

    def per_slot(slot_index, carry):
        (
            outputs,
            grads_in,
            gain_acc,
            bias_acc,
            convw_acc,
            convb_acc,
            embw_acc,
            embb_acc,
            table_acc,
            qkv_acc,
            projw_acc,
            projb_acc,
        ) = carry
        picture = lax.dynamic_index_in_dim(images, slot_index, 0, keepdims=False).astype(
            jnp.float32
        )
        live_flag = (slot_index < live_count[0]).astype(jnp.float32)
        class_id = classes[slot_index]
        table_row = lax.dynamic_index_in_dim(class_table, class_id, 0, keepdims=False).astype(
            jnp.float32
        )
        pre_embed = features(timesteps[slot_index], emb_width) + table_row
        embed = jax.nn.silu(pre_embed)
        scale = jnp.dot(emb_dense[0], embed, precision=HIGH) + emb_bias[0]
        shift = jnp.dot(emb_dense[1], embed, precision=HIGH) + emb_bias[1]
        unit_zero, inverse_zero = group_unit(picture, groups)
        pre_first = unit_zero * norm_gain[0][:, None] + norm_bias[0][:, None]
        first_full = gather_channels(jax.nn.silu(pre_first).astype(jnp.bfloat16))
        hidden = conv_apply(conv_weight[0], first_full, grid_side) + conv_bias[0][:, None]
        unit_one, inverse_one = group_unit(hidden, groups)
        normed_one = unit_one * norm_gain[1][:, None] + norm_bias[1][:, None]
        pre_second = normed_one * (1.0 + scale[:, None]) + shift[:, None]
        second_full = gather_channels(jax.nn.silu(pre_second).astype(jnp.bfloat16))
        resid = picture + conv_apply(conv_weight[1], second_full, grid_side) + conv_bias[1][:, None]
        unit_two, inverse_two = group_unit(resid, groups)
        normed_full = gather_channels(
            (unit_two * norm_gain[2][:, None] + norm_bias[2][:, None]).astype(jnp.bfloat16)
        )
        query = (
            jnp.dot(qkv_weight[0], normed_full, preferred_element_type=jnp.float32)
            .astype(jnp.bfloat16)
            .reshape(heads_dev, head_size, pixel_count)
        )
        keys = (
            jnp.dot(qkv_weight[1], normed_full, preferred_element_type=jnp.float32)
            .astype(jnp.bfloat16)
            .reshape(heads_dev, head_size, pixel_count)
        )
        values = (
            jnp.dot(qkv_weight[2], normed_full, preferred_element_type=jnp.float32)
            .astype(jnp.bfloat16)
            .reshape(heads_dev, head_size, pixel_count)
        )
        scores = (
            jnp.einsum("hdi,hdj->hij", query, keys, preferred_element_type=jnp.float32) * att_scale
        )
        highest = jnp.max(scores, axis=2, keepdims=True)
        expo = jnp.exp(scores - highest)
        totals = jnp.sum(expo, axis=2, keepdims=True)
        log_total = highest + jnp.log(totals)
        weights = (expo / totals).astype(jnp.bfloat16)
        mixed = (
            jnp.einsum("hdj,hij->hdi", values, weights, preferred_element_type=jnp.float32)
            .astype(jnp.bfloat16)
            .reshape(chan_dev, pixel_count)
        )
        weight_cols = proj_weight
        proj_term = lax.psum_scatter(
            lax.dot_general(
                weight_cols, mixed, CONTRACT_FIRST, preferred_element_type=jnp.float32
            ).astype(jnp.bfloat16),
            "head",
            scatter_dimension=0,
            tiled=True,
        ).astype(jnp.float32)
        result = resid + proj_term + proj_bias[:, None]
        outputs = lax.dynamic_update_index_in_dim(
            outputs, (live_flag * result).astype(jnp.bfloat16), slot_index, 0
        )
        grad_low = lax.dynamic_index_in_dim(cotangent, slot_index, 0, keepdims=False)
        grad_out = live_flag * grad_low.astype(jnp.float32)
        grad_full = lax.all_gather(grad_low, "head", axis=0, tiled=True) * live_flag.astype(
            jnp.bfloat16
        )
        grad_mixed = jnp.dot(proj_weight, grad_full, preferred_element_type=jnp.float32).astype(
            jnp.bfloat16
        )
        projw_acc = projw_acc + lax.dot_general(
            mixed, grad_full, CONTRACT_LAST, preferred_element_type=jnp.float32
        )
        projb_acc = projb_acc + jnp.sum(grad_out, axis=1)
        again = (
            jnp.einsum("hdi,hdj->hij", query, keys, preferred_element_type=jnp.float32) * att_scale
        )
        probs = jnp.exp(again - log_total)
        grad_heads = grad_mixed.reshape(heads_dev, head_size, pixel_count)
        grad_probs = jnp.einsum(
            "hdi,hdj->hij", grad_heads, values, preferred_element_type=jnp.float32
        )
        grad_scores = (
            probs * (grad_probs - jnp.sum(grad_probs * probs, axis=2, keepdims=True))
        ).astype(jnp.bfloat16)
        grad_query = (
            jnp.einsum("hij,hdj->hdi", grad_scores, keys, preferred_element_type=jnp.float32)
            * att_scale
        ).astype(jnp.bfloat16)
        grad_keys = (
            jnp.einsum("hij,hdi->hdj", grad_scores, query, preferred_element_type=jnp.float32)
            * att_scale
        ).astype(jnp.bfloat16)
        grad_values = jnp.einsum(
            "hdi,hij->hdj", grad_heads, weights, preferred_element_type=jnp.float32
        ).astype(jnp.bfloat16)
        stacked = jnp.stack([grad_query, grad_keys, grad_values]).reshape(3, chan_dev, pixel_count)
        weight_cols = qkv_weight
        grad_normed = lax.psum_scatter(
            lax.dot_general(
                weight_cols,
                stacked,
                (((0, 1), (0, 1)), ((), ())),
                preferred_element_type=jnp.float32,
            ).astype(jnp.bfloat16),
            "head",
            scatter_dimension=0,
            tiled=True,
        ).astype(jnp.float32)
        qkv_acc = qkv_acc + lax.dot_general(
            stacked, normed_full, (((2,), (1,)), ((), ())), preferred_element_type=jnp.float32
        )
        grad_resid = grad_out + group_back(
            grad_normed * norm_gain[2][:, None], unit_two, inverse_two, groups
        )
        grad_branch = grad_resid.astype(jnp.bfloat16)
        grad_second = input_grad(1, grad_branch)
        grad_pre = grad_second * silu_slope(pre_second)
        scale_grad = jnp.sum(grad_pre * normed_one, axis=1)
        shift_grad = jnp.sum(grad_pre, axis=1)
        grad_normed_one = grad_pre * (1.0 + scale[:, None])
        grad_hidden = group_back(
            grad_normed_one * norm_gain[1][:, None], unit_one, inverse_one, groups
        ).astype(jnp.bfloat16)
        grad_first = input_grad(0, grad_hidden)
        grad_pre_first = grad_first * silu_slope(pre_first)
        picture_grad = grad_resid + group_back(
            grad_pre_first * norm_gain[0][:, None], unit_zero, inverse_zero, groups
        )
        grads_in = lax.dynamic_update_index_in_dim(grads_in, picture_grad, slot_index, 0)
        gain_acc = gain_acc + jnp.stack(
            [
                jnp.sum(grad_pre_first * unit_zero, axis=1),
                jnp.sum(grad_normed_one * unit_one, axis=1),
                jnp.sum(grad_normed * unit_two, axis=1),
            ]
        )
        bias_acc = bias_acc + jnp.stack(
            [
                jnp.sum(grad_pre_first, axis=1),
                jnp.sum(grad_normed_one, axis=1),
                jnp.sum(grad_normed, axis=1),
            ]
        )
        convw_acc = convw_acc + jnp.stack(
            [
                conv_weight_grads(grad_hidden, first_full, grid_side),
                conv_weight_grads(grad_branch, second_full, grid_side),
            ]
        )
        convb_acc = convb_acc + jnp.stack(
            [
                jnp.sum(grad_hidden.astype(jnp.float32), axis=1),
                jnp.sum(grad_branch.astype(jnp.float32), axis=1),
            ]
        )
        embw_acc = embw_acc + jnp.stack(
            [scale_grad[:, None] * embed[None, :], shift_grad[:, None] * embed[None, :]]
        )
        embb_acc = embb_acc + jnp.stack([scale_grad, shift_grad])
        grad_embed = jnp.dot(scale_grad, emb_dense[0], precision=HIGH) + jnp.dot(
            shift_grad, emb_dense[1], precision=HIGH
        )
        class_row = grad_embed * silu_slope(pre_embed)
        old_row = lax.dynamic_index_in_dim(table_acc, class_id, 0, keepdims=True)
        table_acc = lax.dynamic_update_index_in_dim(
            table_acc, old_row + class_row[None, :], class_id, 0
        )
        return (
            outputs,
            grads_in,
            gain_acc,
            bias_acc,
            convw_acc,
            convb_acc,
            embw_acc,
            embb_acc,
            table_acc,
            qkv_acc,
            projw_acc,
            projb_acc,
        )

    table_start = jnp.zeros(class_table.shape, jnp.float32)
    initial = (
        jnp.zeros(images.shape, jnp.bfloat16),
        jnp.zeros(images.shape, jnp.float32),
        jnp.zeros(norm_gain.shape, jnp.float32),
        jnp.zeros(norm_bias.shape, jnp.float32),
        jnp.zeros(conv_weight.shape, jnp.float32),
        jnp.zeros(conv_bias.shape, jnp.float32),
        jnp.zeros(emb_weight.shape, jnp.float32),
        jnp.zeros(emb_bias.shape, jnp.float32),
        table_start,
        jnp.zeros(qkv_weight.shape, jnp.float32),
        jnp.zeros(proj_weight.shape, jnp.float32),
        jnp.zeros(proj_bias.shape, jnp.float32),
    )
    final = lax.fori_loop(0, slot_count, per_slot, initial)
    (
        outputs,
        grads_in,
        gain_acc,
        bias_acc,
        convw_acc,
        convb_acc,
        embw_acc,
        embb_acc,
        table_acc,
        qkv_acc,
        projw_acc,
        projb_acc,
    ) = final
    table_total = lax.psum(table_acc, ("batch", "head"))
    summed = (
        lax.psum(gain_acc.astype(jnp.bfloat16), "batch").astype(jnp.float32),
        lax.psum(bias_acc.astype(jnp.bfloat16), "batch").astype(jnp.float32),
        lax.psum(convw_acc.astype(jnp.bfloat16), "batch").astype(jnp.float32),
        lax.psum(convb_acc.astype(jnp.bfloat16), "batch").astype(jnp.float32),
        lax.psum(embw_acc.astype(jnp.bfloat16), "batch").astype(jnp.float32),
        lax.psum(embb_acc.astype(jnp.bfloat16), "batch").astype(jnp.float32),
        lax.psum(qkv_acc.astype(jnp.bfloat16), "batch").astype(jnp.float32),
        lax.psum(projw_acc.astype(jnp.bfloat16), "batch").astype(jnp.float32),
        lax.psum(projb_acc.astype(jnp.bfloat16), "batch").astype(jnp.float32),
    )
    return (
        outputs,
        grads_in,
        summed[0],
        summed[1],
        summed[2],
        summed[3],
        summed[4],
        summed[5],
        table_total,
        summed[6],
        summed[7],
        summed[8],
    )


PIX = 1024
BLOCK = 256
BF = jnp.bfloat16
F32 = jnp.float32
NN = (((1,), (0,)), ((), ()))
TN = (((0,), (0,)), ((), ()))
NT = (((1,), (1,)), ((), ()))
VMEM = pl.BlockSpec(memory_space=pltpu.VMEM)
SMEM = pl.BlockSpec(memory_space=pltpu.SMEM)

GAIN, BIAS, CONVB, PROJB, SCALE, SHIFT = 0, 3, 6, 8, 9, 10


def mm(left, right, dims=NN):
    return lax.dot_general(left, right, dims, preferred_element_type=F32)


class Far:
    def __init__(self, array):
        self.array = array


ANYWHERE = pl.BlockSpec(memory_space=pl.ANY)


class Scalars(Far):
    pass


def operands(args):
    arrays = [arg.array if isinstance(arg, Far) else arg for arg in args]
    specs = []
    for arg in args:
        if isinstance(arg, Scalars):
            specs.append(SMEM)
        else:
            specs.append(ANYWHERE if isinstance(arg, Far) else VMEM)
    return arrays, specs


def split(value, axis):
    parts = []
    for _ in range(3):
        part = value.astype(BF)
        parts.append(part)
        value = value - part.astype(F32)
    return jnp.concatenate(parts, axis)


def fetch(sems, slot, source, dest):
    copy = pltpu.make_async_copy(source, dest, sems.at[slot])
    copy.start()
    return copy


def out(shape, dtype):
    return jax.ShapeDtypeStruct(shape, dtype)


def rows(start, count):
    return pl.ds(pl.multiple_of(start, count), count)


def edge_masks(sign):
    pixel = lax.broadcasted_iota(jnp.int32, (1, PIX), 1)
    col, row = pixel % SIDE, pixel // SIDE
    table = {}
    for step in (-1, 1):
        moved_step = sign * step
        table["col", step] = ((col + moved_step >= 0) & (col + moved_step < SIDE)).astype(F32)
        table["row", step] = ((row + moved_step >= 0) & (row + moved_step < SIDE)).astype(F32)
    return table


def put_taps(dest, masks, values, first_row, depth, base, sign):
    count = values.shape[0]
    for col_step in (-1, 0, 1):
        across = values
        if col_step:
            across = pltpu.roll(values, (-sign * col_step) % PIX, 1) * masks["col", col_step]
        for row_step in (-1, 0, 1):
            copy = across
            if row_step:
                copy = pltpu.roll(across, (-sign * row_step * SIDE) % PIX, 1) * masks["row", row_step]
            tap = 3 * (row_step + 1) + col_step + 1
            dest[rows(tap * depth + first_row, count), base : base + PIX] = copy.astype(BF)


def taps_of(dest, masks, source, offset, depth, base, sign):
    for start in range(0, source.shape[0], 128):
        piece = source[start : start + 128, :].astype(F32)
        put_taps(dest, masks, piece, offset + start, depth, base, sign)


def fetch_conv(sems, full, half, which, own, peer):
    return (
        fetch(sems, 0, own.at[which], full.at[:, rows(half * 256, 256), :]),
        fetch(sems, 1, peer.at[which], full.at[:, rows((1 - half) * 256, 256), :]),
    )


def wait(copies):
    for copy in copies:
        copy.wait()


def conv_dots(dest, full, col, dims, finish):
    for column in range(0, PIX, 512):
        total = None
        for tap in range(9):
            term = mm(full[tap], col[tap * 512 : (tap + 1) * 512, column : column + 512], dims)
            total = term if total is None else total + term
        dest[:, column : column + 512] = finish(total, column)


def grouped(block):
    return block.reshape((-1, 16) + block.shape[1:])


def group_mean(block):
    return jnp.sum(block, axis=(1, 2), keepdims=True) * (1.0 / (16 * PIX))


def group_stats(block, stats, where):
    parts = grouped(block)
    centre = group_mean(parts)
    parts = parts - centre
    inverse = lax.rsqrt(group_mean(jnp.square(parts)) + EPS)
    count = block.shape[0]
    for column, value in enumerate((centre, inverse)):
        stats[where, column : column + 1] = jnp.broadcast_to(value, (count // 16, 16, 1)).reshape(count, 1)
    return (parts * inverse).reshape(block.shape)


def unit_of(block, stats, where):
    return (block - stats[where, 0:1]) * stats[where, 1:2]


def unit_back(grad, unit, inverse):
    parts, units = grouped(grad), grouped(unit)
    result = parts - group_mean(parts) - units * group_mean(parts * units)
    return result.reshape(grad.shape) * inverse


def row_sum(block):
    return jnp.sum(block, axis=1, keepdims=True)


def fetch_square(sems, slot, full, half, own, peer):
    count = own.shape[-2]
    near, far = rows(half * count, count), rows((1 - half) * count, count)
    if len(full.shape) == 3:
        near, far = (slice(None), near), (slice(None), far)
    return fetch(sems, slot, own, full.at[near]), fetch(sems, slot + 1, peer, full.at[far])


def attention(
    live_count, normed, resid, stats2, par, cotangent, cot_peer, q_own, q_peer, p_own, p_peer,
    second, first_near, squares_out, block_out, grad_resid, grad_branch, small, second_peer, first_peer,
    sems, sends, recvs, wqkv, wp, query, keys, values, grad_mixed, mixed, grad_q, grad_k, grad_v, grad_out,
    grad_normed, resid_in, squares, block, *pixel_scratch,
):
    half = lax.axis_index("head")
    live = (half < live_count[0]).astype(BF)
    arriving = fetch_square(sems, 0, wqkv, half, q_own, q_peer)
    later = fetch_square(sems, 2, wp, half, p_own, p_peer)
    later += (
        fetch(sems, 4, cotangent.at[half], grad_out.at[rows(half * 256, 256)]),
        fetch(sems, 5, cot_peer, grad_out.at[rows((1 - half) * 256, 256)]),
    )
    last = fetch(sems, 6, resid, resid_in)
    to_x = {"head": 1 - half}
    meet([to_x])
    exchanges = (
        remote(second, second_peer, sends, recvs, 0, to_x),
        remote(first_near, first_peer, sends, recvs, 1, to_x),
    )
    exchanges[0].start()
    wait(arriving)
    for column in range(0, PIX, 512):
        where = slice(column, column + 512)
        query[:, where] = (mm(wqkv[0], normed[:, where]).astype(BF).astype(F32) * 0.125).astype(BF)
        keys[:, where] = mm(wqkv[1], normed[:, where]).astype(BF)
        values[:, where] = mm(wqkv[2], normed[:, where]).astype(BF)
    wait(later)
    grad_out[...] = grad_out[...] * live
    for column in range(0, PIX, 512):
        where = slice(column, column + 512)
        grad_mixed[:, where] = mm(wp[...], grad_out[:, where]).astype(BF)

    def head(number, weights, grad_scores):
        where = rows(number * 64, 64)
        q, k, v, g = query[where, :], keys[where, :], values[where, :], grad_mixed[where, :]
        scores = mm(k.T, q)
        low = jnp.exp(scores - jnp.max(scores, axis=0, keepdims=True)).astype(BF)
        weights[...] = low
        mix = mm(jnp.concatenate([v, jnp.ones((16, PIX), BF)], 0), low)
        inverse = 1.0 / mix[64:65]
        mix = mix[0:64] * inverse
        mixed[where, :] = mix.astype(BF)
        g = (g.astype(F32) * inverse).astype(BF)
        delta = jnp.sum(mix * g.astype(F32), axis=0, keepdims=True)
        inner = low * (mm(v.T, g) - delta).astype(BF)
        grad_scores[...] = inner
        grad_q[where, :] = (mm(k, inner) * 0.125).astype(BF)
        grad_k[where, :] = mm(grad_scores[...], q.T).T.astype(BF)
        grad_v[where, :] = mm(weights[...], g.T).T.astype(BF)

    def heads(index, carry):
        for number in range(4):
            head(index * 4 + number, pixel_scratch[2 * number], pixel_scratch[2 * number + 1])
        return carry

    exchanges[1].start()
    lax.fori_loop(0, HEADS // 4, heads, 0)
    pairs = ((grad_q, normed), (grad_k, normed), (grad_v, normed), (mixed, grad_out))
    for which, (left, right) in enumerate(pairs):
        result = mm(left[...], right[...], NT).astype(BF)
        for part in range(32):
            plane, chunk = part // 16, part % 16
            squares[chunk // 8, plane, chunk % 8, which] = result[part * 16 : (part + 1) * 16]
    outgoing = (fetch(sems, 0, squares, squares_out),)
    for column in range(0, PIX, 512):
        where = slice(column, column + 512)
        grad_normed[:, where] = (
            mm(wqkv[0], grad_q[:, where], TN)
            + mm(wqkv[1], grad_k[:, where], TN)
            + mm(wqkv[2], grad_v[:, where], TN)
        )
    last.wait()
    for column in range(0, PIX, 512):
        where = slice(column, column + 512)
        total = resid_in[:, where] + mm(wp[...], mixed[:, where], TN) + par[:, PROJB : PROJB + 1]
        block[:, where] = (total * live.astype(F32)).astype(BF)
    outgoing += (fetch(sems, 1, block, block_out),)

    def back(group, carry):
        where = rows(group * BLOCK, BLOCK)
        unit = unit_of(resid_in[where, :], stats2, where)
        grad = grad_normed[where, :]
        outer = grad_out[where, :].astype(F32)
        total = outer + unit_back(grad * par[where, GAIN + 2 : GAIN + 3], unit, stats2[where, 1:2])
        low = total.astype(BF)
        grad_resid[where, :] = total
        grad_branch[where, :] = low
        small[where, 0:1] = row_sum(grad * unit)
        small[where, 1:2] = row_sum(grad)
        small[where, 2:3] = row_sum(low.astype(F32))
        small[where, 3:4] = row_sum(outer)
        return carry

    lax.fori_loop(0, 512 // BLOCK, back, 0)
    wait(outgoing)
    wait(exchanges)


def attention_call(*args):
    arrays, specs = operands(args)
    dma = pltpu.SemaphoreType.DMA
    full_bf = out((512, PIX), BF)
    squares = out((2, 2, 8, 4, 16, 512), BF)
    wide_bf = pltpu.VMEM((512, PIX), BF)
    wide_f32 = pltpu.VMEM((512, PIX), F32)
    return pl.pallas_call(
        attention,
        out_shape=[
            squares, full_bf, out((512, PIX), F32), full_bf, out((512, 4), F32), full_bf, out((256, PIX), BF),
        ],
        in_specs=specs,
        out_specs=[ANYWHERE] * 2 + [VMEM] * 3 + [ANYWHERE] * 2,
        scratch_shapes=[
            dma((8,)), dma((2,)), dma((2,)),
            pltpu.VMEM((3, 512, 512), BF),
            pltpu.VMEM((512, 512), BF),
        ]
        + [wide_bf] * 9
        + [wide_f32] * 2
        + [pltpu.VMEM(squares.shape, BF), wide_bf]
        + [pltpu.VMEM((PIX, PIX), BF)] * 8,
        cost_estimate=pl.CostEstimate(flops=3 * 10**10, bytes_accessed=20 * 2**20, transcendentals=0),
        compiler_params=pltpu.CompilerParams(
            collective_id=3, has_side_effects=True, vmem_limit_bytes=58 * 2**20
        ),
    )(*arrays)


def remote(source, dest, sends, recvs, slot, target):
    return pltpu.make_async_remote_copy(
        src_ref=source,
        dst_ref=dest,
        send_sem=sends.at[slot],
        recv_sem=recvs.at[slot],
        device_id=target,
        device_id_type=pl.DeviceIdType.MESH,
    )


def meet(targets):
    barrier = pltpu.get_barrier_semaphore()
    for target in targets:
        pl.semaphore_signal(barrier, inc=1, device_id=target, device_id_type=pl.DeviceIdType.MESH)
    pl.semaphore_wait(barrier, len(targets))


def position():
    place = lax.axis_index("batch")
    return place, place % 2, (place // 2) % 2, place // 4


PIECES = 6
KINDS = 10


def forward(
    timesteps, classes, norm_gain, norm_bias, conv_bias, proj_bias, emb_bias, emb_weight, class_table,
    images, cotangent, conv_weight, qkv_weight, proj_weight,
    par, pre_embed, image_peer, cot_peer, conv_peer, qkv_peer, proj_peer,
    first_out, near_out, other_out, hidden_out, stats0, stats1, second_out, resid, stats2, normed,
    sends, recvs, few_sends, few_recvs, sems, put_sems, columns, par_send, par_recv, lines, table, own, peer, other, spare, col, full, full_one, *kept,
):
    half = lax.axis_index("head")
    place, core, up, deep = position()
    z_low = deep % 2
    to_x = {"head": 1 - half}
    to_y = {"batch": place + 2 * (1 - 2 * up)}
    to_z = {"batch": place + 4 * (1 - 2 * z_low)}
    to_core = {"batch": place + (1 - 2 * core)}
    near, away = rows(half * 256, 256), rows((1 - half) * 256, 256)
    pictures = (
        fetch(sems, 0, images.at[half], own),
        fetch(sems, 1, images.at[1 - half], other),
    )
    table_copy = fetch(sems, 2, class_table, table)
    fulls = (full, full_one)
    first, first_near, first_other, hidden, second = kept
    own_weights = fetch(sems, 3, conv_weight.at[0], full.at[:, near, :])
    own_later = fetch(sems, 4, conv_weight.at[1], full_one.at[:, near, :])
    outgoing = []

    def put(source, dest):
        outgoing.append(fetch(put_sems, len(outgoing), source, dest))

    meet([to_x, to_y, to_z, to_core])

    def block(flip_core=0, flip_y=0, flip_z=0):
        c = 1 - core if flip_core else core
        y = 1 - up if flip_y else up
        z = 1 - z_low if flip_z else z_low
        return (c + 2 * y + 4 * z) * 32

    def views(piece, plane, start, count):
        where = rows(start, count)
        if piece < 4:
            taps = pl.ds(0, 5) if piece % 2 == 0 else pl.ds(5, 4)
            return fulls[piece // 2].at[taps, rows(plane * 256 + start, count), :]
        if piece == 4:
            return qkv_peer.at[:, where, :]
        return proj_peer.at[where, :]

    def source(piece, start, count):
        where = rows(start, count)
        if piece < 4:
            taps = pl.ds(0, 5) if piece % 2 == 0 else pl.ds(5, 4)
            return conv_weight.at[piece // 2, taps, where, :]
        if piece == 4:
            return qkv_weight.at[:, where, :]
        return proj_weight.at[where, :]

    def copy(piece, kind, start, count, target, local=False):
        dest = views(piece, half if local else 1 - half, start, count)
        return remote(
            source(piece, start, count) if local else dest, dest,
            sends.at[piece], recvs.at[piece], kind, target,
        )

    def regions(flip_core):
        return (
            (block(flip_core), 32),
            (block(flip_core, 1), 32),
            (block(flip_core, 0, 1), 32),
            (block(flip_core, 1, 1), 16),
            (block(flip_core, 1, 1) + 16, 16),
        )

    mine, others = regions(0), regions(1)

    def arrived(piece, kind):
        start, count = mine[kind] if kind < 5 else others[kind - 5]
        copy(piece, kind, start, count, to_core).wait_recv()

    def over_x(piece):
        arrived(piece, 0)
        for kind, target in ((1, to_y), (2, to_z), (5, to_core)):
            copy(piece, kind, block(), 32, target).start()

    def over_yz(piece):
        arrived(piece, 2)
        copy(piece, 3, block(0, 0, 1), 16, to_y).start()
        copy(piece, 7, block(0, 0, 1), 32, to_core).start()
        arrived(piece, 1)
        copy(piece, 4, block(0, 1, 0) + 16, 16, to_z).start()
        copy(piece, 6, block(0, 1, 0), 32, to_core).start()

    def diagonal(piece):
        arrived(piece, 3)
        copy(piece, 8, block(0, 1, 1), 16, to_core).start()
        arrived(piece, 4)
        copy(piece, 9, block(0, 1, 1) + 16, 16, to_core).start()

    def complete(piece):
        for kind in range(5, 10):
            arrived(piece, kind)

    def fetch_x(*pieces):
        for piece in pieces:
            copy(piece, 0, block(), 32, to_x, local=True).start()

    fetch_x(0, 1)

    table_copy.wait()
    width = class_table.shape[1]
    numbers = lax.broadcasted_iota(jnp.int32, (1, table.shape[0]), 1)
    freqs = jnp.exp(
        lax.broadcasted_iota(jnp.int32, (1, width // 2), 1).astype(F32) * (-math.log(10000.0) / (width // 2))
    )
    for slot in range(2):
        chosen = (numbers == classes[slot]).astype(BF)
        angles = timesteps[slot].astype(F32) * freqs
        pre_embed[slot : slot + 1, : width // 2] = jnp.cos(angles)
        pre_embed[slot : slot + 1, width // 2 : width] = jnp.sin(angles)
        line = mm(jnp.broadcast_to(chosen, (8, table.shape[0])), table[...])
        pre_embed[slot : slot + 1, :width] += line[0:1]
        pre_embed[slot : slot + 1, width:] = jnp.broadcast_to(classes[slot].astype(F32), (1, 128))
    embed = jax.nn.silu(pre_embed[:, :width])
    own_row = jnp.where(half == 0, embed[0:1], embed[1:2])
    peer_row = jnp.where(half == 0, embed[1:2], embed[0:1])
    lines[...] = jnp.zeros_like(lines)
    lines[0:3] = norm_gain[...]
    lines[3:6] = norm_bias[...]
    lines[6:8] = conv_bias[...]
    lines[8:9] = proj_bias[...]
    lines[9:11] = emb_bias[...]
    turned = lines[...].T
    columns[:, 0:11] = turned[:, 0:11]
    par[near, :] = turned[:, 0:11]
    for which in range(2):
        dense = emb_weight[which].astype(F32)
        par[near, SCALE + which : SCALE + which + 1] += row_sum(dense * own_row)
        columns[:, SCALE + which : SCALE + which + 1] += row_sum(dense * peer_row)
    par_send[...] = columns[...].T[0:16]
    block_copy = remote(par_send, par_recv, few_sends, few_recvs, 1, to_x)
    block_copy.start()

    masks = edge_masks(1)
    wait(pictures)

    def norm_zero(source, dest, base, stats, offset, group):
        here = rows(group * BLOCK, BLOCK)
        where = rows(base + group * BLOCK, BLOCK)
        unit = group_stats(source[here, :].astype(F32), stats, rows(offset + group * BLOCK, BLOCK))
        low = jax.nn.silu(unit * par[where, GAIN : GAIN + 1] + par[where, BIAS : BIAS + 1]).astype(BF)
        dest[rows(offset + group * BLOCK, BLOCK), :] = low
        return low.astype(F32)

    def norm_near(group, carry):
        low = norm_zero(own, first, half * 256, stats0, half * 256, group)
        first_near[rows(group * BLOCK, BLOCK), :] = low.astype(BF)
        put_taps(col, masks, low, half * 256 + group * BLOCK, 512, 0, 1)
        return carry

    def norm_other(group, carry):
        norm_zero(other, first_other, half * 256, spare, 0, group)
        return carry

    def conv_part(full, dest, mine, column, bias, inputs=None):
        where = near if mine else away
        result = None
        for tap in range(9):
            depth = slice(None)
            part = pl.ds(tap * 512, 512)
            if inputs is not None:
                depth = near if inputs else away
                part = rows(tap * 512 + (half if inputs else 1 - half) * 256, 256)
            term = mm(full[tap, where, depth], col[part, column : column + 512])
            result = term if result is None else result + term
        if inputs is None or inputs:
            dest[where, column : column + 512] = result + par[where, bias : bias + 1]
        else:
            dest[where, column : column + 512] += result

    over_x(0)
    fetch_x(2, 3)
    over_x(1)
    lax.fori_loop(0, 256 // BLOCK, norm_near, 0)
    over_x(2)
    picture = remote(images.at[1 - half], image_peer, few_sends, few_recvs, 0, to_x)
    picture.start()
    over_yz(0)
    over_yz(1)
    own_weights.wait()
    conv_part(full, hidden, True, 0, CONVB, True)
    diagonal(0)
    diagonal(1)
    over_yz(2)
    conv_part(full, hidden, True, 512, CONVB, True)
    complete(0)
    complete(1)
    put(full.at[:, away, :], conv_peer.at[0])
    diagonal(2)
    block_copy.wait_recv()
    par[away, :] = par_recv[...].T[:, 0:11]
    conv_part(full, hidden, False, 0, CONVB, True)
    conv_part(full, hidden, False, 512, CONVB, True)
    lax.fori_loop(0, 256 // BLOCK, norm_other, 0)
    put(first_other, other_out)
    picture.wait_recv()
    loaded = fetch(sems, 0, image_peer, peer)
    fetch_x(4, 5)
    loaded.wait()

    def norm_far(group, carry):
        low = norm_zero(peer, first, (1 - half) * 256, stats0, (1 - half) * 256, group)
        put_taps(col, masks, low, (1 - half) * 256 + group * BLOCK, 512, 0, 1)
        return carry

    lax.fori_loop(0, 256 // BLOCK, norm_far, 0)
    over_x(3)
    cot_copy = remote(cotangent.at[1 - half], cot_peer, few_sends, few_recvs, 2, to_x)
    cot_copy.start()
    conv_part(full, hidden, True, 0, CONVB, False)
    conv_part(full, hidden, True, 512, CONVB, False)
    over_yz(3)
    over_x(4)
    over_x(5)
    conv_part(full, hidden, False, 0, CONVB, False)
    diagonal(3)
    conv_part(full, hidden, False, 512, CONVB, False)
    over_yz(4)
    over_yz(5)
    put(hidden, hidden_out)
    put(first, first_out)
    put(first_near, near_out)

    def norm_one(group, carry):
        where = rows(group * BLOCK, BLOCK)
        unit = group_stats(hidden[where, :], stats1, where)
        unscaled = unit * par[where, GAIN + 1 : GAIN + 2] + par[where, BIAS + 1 : BIAS + 2]
        pre = unscaled * (1.0 + par[where, SCALE : SCALE + 1]) + par[where, SHIFT : SHIFT + 1]
        low = jax.nn.silu(pre).astype(BF)
        second[where, :] = low
        put_taps(col, masks, low.astype(F32), group * BLOCK, 512, 0, 1)
        return carry

    lax.fori_loop(0, 512 // BLOCK, norm_one, 0)
    complete(2)
    complete(3)
    put(full_one.at[:, away, :], conv_peer.at[1])
    put(second, second_out)
    diagonal(4)
    diagonal(5)
    own_later.wait()
    conv_part(full_one, resid, True, 0, CONVB + 1)
    conv_part(full_one, resid, True, 512, CONVB + 1)
    conv_part(full_one, resid, False, 0, CONVB + 1)
    conv_part(full_one, resid, False, 512, CONVB + 1)
    for image, base in ((own, half * 256), (peer, (1 - half) * 256)):

        def norm_two(group, carry, image=image, base=base):
            where = rows(base + group * BLOCK, BLOCK)
            total = resid[where, :] + image[rows(group * BLOCK, BLOCK), :].astype(F32)
            resid[where, :] = total
            unit = group_stats(total, stats2, where)
            normed[where, :] = (unit * par[where, GAIN + 2 : GAIN + 3] + par[where, BIAS + 2 : BIAS + 3]).astype(BF)
            return carry

        lax.fori_loop(0, 256 // BLOCK, norm_two, 0)
    complete(4)
    complete(5)
    cot_copy.wait_recv()
    for piece in range(PIECES):
        copy(piece, 0, block(), 32, to_x).wait_send()
        for kind, start, count in (
            (1, block(), 32), (2, block(), 32), (5, block(), 32),
            (3, block(0, 0, 1), 16), (7, block(0, 0, 1), 32),
            (4, block(0, 1, 0) + 16, 16), (6, block(0, 1, 0), 32),
            (8, block(0, 1, 1), 16), (9, block(0, 1, 1) + 16, 16),
        ):
            copy(piece, kind, start, count, to_x).wait_send()
    wait(outgoing)
    picture.wait_send()
    block_copy.wait_send()
    cot_copy.wait_send()


def forward_call(timesteps, classes, *args):
    arrays, specs = operands((Scalars(timesteps), Scalars(classes)) + args)
    images, cotangent, conv_weight, qkv_weight, proj_weight = arrays[-5:]
    width = arrays[-6].shape[1]
    half_bf = out((256, PIX), BF)
    full_bf = out((512, PIX), BF)
    full_f32 = out((512, PIX), F32)
    stats = out((512, 2), F32)
    dma = pltpu.SemaphoreType.DMA
    half_scratch = pltpu.VMEM((256, PIX), BF)
    return pl.pallas_call(
        forward,
        out_shape=[
            out((512, 11), F32),
            out((2, width + 128), F32),
            half_bf,
            half_bf,
            out(conv_weight.shape, BF),
            out(qkv_weight.shape, BF),
            out(proj_weight.shape, BF),
            full_bf, half_bf, half_bf, full_f32, stats, stats, full_bf, full_f32, stats, full_bf,
        ],
        in_specs=specs,
        out_specs=[VMEM] * 2 + [ANYWHERE] * 9 + [VMEM] * 2 + [ANYWHERE] + [VMEM] * 3,
        scratch_shapes=[
            dma((PIECES, KINDS)), dma((PIECES, KINDS)), dma((3,)), dma((3,)), dma((5,)), dma((7,)),
            pltpu.VMEM((256, 128), F32),
            pltpu.VMEM((16, 256), F32),
            pltpu.VMEM((16, 256), F32),
            pltpu.VMEM((16, 256), F32),
            pltpu.VMEM(arrays[-6].shape, BF),
            half_scratch, half_scratch, half_scratch,
            pltpu.VMEM((256, 2), F32),
            pltpu.VMEM((9 * 512, PIX), BF),
            pltpu.VMEM((9, 512, 512), BF),
            pltpu.VMEM((9, 512, 512), BF),
            pltpu.VMEM((512, PIX), BF),
            half_scratch,
            half_scratch,
            pltpu.VMEM((512, PIX), F32),
            pltpu.VMEM((512, PIX), BF),
        ],
        cost_estimate=pl.CostEstimate(flops=2 * 10**10, bytes_accessed=100 * 2**20, transcendentals=0),
        compiler_params=pltpu.CompilerParams(
            collective_id=1, has_side_effects=True, vmem_limit_bytes=58 * 2**20
        ),
    )(*arrays)


SENDS = 12


class Sum:
    def __init__(self, source, total, scratch, planes):
        self.source, self.total, self.planes = source, total, planes
        self.sends, self.recvs, self.core_in, self.first, self.y_in, self.second, self.z_in, self.result = scratch[:8]
        if planes:
            self.middle, self.x_in = scratch[8:10]
        self.half = lax.axis_index("head")
        self.place, self.core, self.up, self.deep = position()
        self.steps = [self.start, self.core_done, self.y_done, self.z_done]
        if planes:
            self.steps.append(self.x_done)
        self.steps += [self.z_back, self.y_back, self.finish]
        self.open = []
        self.count = 0

    def advance(self):
        if self.count < len(self.steps):
            self.steps[self.count]()
            self.count += 1

    def part(self, array, start, count):
        where = pl.ds(start, count)
        return array.at[:, where] if self.planes else array.at[where]

    def to_core(self):
        return {"batch": self.place + 1 - 2 * self.core}

    def to_y(self):
        return {"batch": self.place + 2 * (1 - 2 * self.up)}

    def to_z(self, ahead):
        return {"batch": (self.deep + ahead) % 4 * 4 + self.place % 4}

    def send(self, slot, source, dest, target):
        copy = remote(source, dest, self.sends, self.recvs, slot, target)
        copy.start()
        self.open.append(copy)

    def arrived(self, slot, dest):
        remote(dest, dest, self.sends, self.recvs, slot, self.to_core()).wait_recv()

    def of_core(self, core):
        return self.source.at[core] if self.planes else self.source.at[pl.ds(core * 8, 8)]

    def start(self):
        self.send(0, self.of_core(1 - self.core), self.core_in, self.to_core())

    def add(self, dest, left, *right):
        total = left[...].astype(F32)
        for term in right:
            total = total + term[...].astype(F32)
        dest[...] = total.astype(BF)

    def core_done(self):
        self.arrived(0, self.core_in)
        self.add(self.first, self.of_core(self.core), self.core_in)
        self.send(1, self.part(self.first, (1 - self.up) * 4, 4), self.y_in, self.to_y())

    def y_done(self):
        self.arrived(1, self.y_in)
        self.add(self.second, self.part(self.first, self.up * 4, 4), self.y_in)
        for ahead in (2, 1, 3):
            chunk = self.part(self.second, (self.deep + ahead) % 4, 1)
            self.send(1 + ahead, chunk, self.z_in.at[ahead - 1], self.to_z(ahead))

    def z_done(self):
        for ahead in (1, 2, 3):
            self.arrived(1 + ahead, self.z_in.at[ahead - 1])
        mine = self.part(self.second, self.deep, 1)
        terms = [self.z_in.at[number] for number in range(3)]
        if self.planes:
            self.add(self.middle, mine, *terms)
            self.send(10, self.middle.at[1 - self.half], self.x_in, {"head": 1 - self.half})
        else:
            self.add(self.result, mine, *terms)
            self.give()

    def x_done(self):
        self.arrived(10, self.x_in)
        self.add(self.result, self.middle.at[self.half], self.x_in)
        self.give()

    def chunks(self, start, count):
        return self.total.at[pl.ds(start, count)]

    def chunk(self, deep):
        return self.core * 8 + self.up * 4 + deep

    def give(self):
        mine = self.chunks(self.chunk(self.deep), 1)
        for ahead in (2, 1, 3):
            self.send(4 + ahead, self.result, mine, self.to_z(ahead))
        self.kept = pltpu.make_async_copy(self.result, mine, self.sends.at[11])
        self.kept.start()

    def z_back(self):
        for ahead in (1, 2, 3):
            self.arrived(4 + ahead, self.chunks(self.chunk((self.deep + 4 - ahead) % 4), 1))
        self.kept.wait()
        part = self.chunks(self.chunk(0), 4)
        self.send(8, part, part, self.to_y())

    def y_back(self):
        self.arrived(8, self.chunks(self.core * 8 + (1 - self.up) * 4, 4))
        part = self.chunks(self.core * 8, 8)
        self.send(9, part, part, self.to_core())

    def finish(self):
        self.arrived(9, self.chunks((1 - self.core) * 8, 8))
        for copy in self.open:
            copy.wait_send()


def sum_scratch(tail, planes):
    lead = (2,) if planes else ()
    shapes = [
        pltpu.SemaphoreType.DMA((SENDS,)),
        pltpu.SemaphoreType.DMA((SENDS,)),
        pltpu.VMEM(lead + (8,) + tail, BF),
        pltpu.VMEM(lead + (8,) + tail, BF),
        pltpu.VMEM(lead + (4,) + tail, BF),
        pltpu.VMEM(lead + (4,) + tail, BF),
        pltpu.VMEM((3,) + lead + (1,) + tail, BF),
        pltpu.VMEM((1,) + tail, BF),
    ]
    if planes:
        shapes += [pltpu.VMEM((2, 1) + tail, BF), pltpu.VMEM((1,) + tail, BF)]
    return shapes


def weight_back(grads, chunk_taps, col, turned):
    for tap in chunk_taps:
        result = mm(col[tap * 256 : (tap + 1) * 256, :], turned[:PIX, :])
        result = result + mm(col[(9 + tap) * 256 : (10 + tap) * 256, :], turned[PIX:, :])
        result = result.astype(BF)
        for part in range(16):
            grads[part, tap] = result[part * 16 : (part + 1) * 16]


PARTS = ((0, 2), (2, 4), (4, 6), (6, 8), (8, 9))
PARTS_ZERO = ((0, 3), (3, 6), (6, 8), (8, 9))
HALVES = ((0, 2), (2, 4))

(TAPS_ONE, CONV_ONE, AWAY_ONE, NEAR_ONE, PAIR_ONE, GRAD_ONE, SHARE, PAIR_ZERO,
 GRAD_ZERO, TAPS_ZERO, CONV_ZERO, AWAY_ZERO, NEAR_ZERO, ROWS, SMALL) = range(100, 115)
ORDER = (
    TAPS_ONE, 0, 1, CONV_ONE, 0, 1, CONV_ONE, AWAY_ONE, NEAR_ONE, 0, PAIR_ONE, GRAD_ONE, 2, 1,
    GRAD_ONE, 2, 3, GRAD_ONE, 0, 4, 3, GRAD_ONE, 4, 5, 2, GRAD_ONE, 6, SHARE, PAIR_ZERO, 5, 1, 3, 6,
    2, 4, GRAD_ZERO, 7, GRAD_ZERO, 5, 3, 6, 0, 7, 8, 1, 2, GRAD_ZERO, 9, GRAD_ZERO, 8, 10, 4,
    TAPS_ZERO, 9, CONV_ZERO, 10, 7, 5, 2, 3, 6, CONV_ZERO, 2, 8, 0, AWAY_ZERO, 9, 1, 10, NEAR_ZERO,
    4, 3, ROWS, 3, 0, 7, 0, 1, 5, 6, 1, 4, SMALL, 4, 5, SMALL, 8, 6, 5, SMALL, 9, 6, 10, 7, 8,
    SMALL, 7, 9, 7, 10, 8, 8, 9, 10, 9, 10,
)


def backward(
    live_count, squares, grad_branch, block, hidden, second, second_peer,
    first, first_other, first_peer, grad_resid, images, image_peer, w_own, w_peer,
    stats0, stats1, par, small2, pre_embed, emb_weight,
    square_sum, sum1, sum0, images_grad, far_in, block_out, sums, class_rows, mod_out, pre_out,
    sems, sends, recvs, all_sends, all_recvs,
    grads1, grads0, col, turned, full, slope_in, wide_in, source_in, branch_in, hidden_in, grad_hidden,
    far, columns, flat, mod, mod_send, pres, rows_own, rows_in, total, total_in,
    *scratch,
):
    half = lax.axis_index("head")
    place, core, up, deep = position()
    to_x = {"head": 1 - half}
    others = [{"batch": (place + ahead) % 16} for ahead in range(1, 16)]
    near, away = rows(half * 256, 256), rows((1 - half) * 256, 256)
    exchanges = {}
    local = {}

    local["weights"] = fetch_conv(sems.at[pl.ds(6, 2)], full, half, 1, w_own, w_peer)
    local["wide"] = (fetch(sems, 8, hidden, wide_in),)
    local["inputs"] = (
        fetch(sems, 9, second, source_in.at[0]),
        fetch(sems, 10, second_peer, source_in.at[1]),
    )
    meet([to_x] + others)

    def send(slot, source, dest, target):
        exchanges[slot] = remote(source, dest, sends, recvs, slot, target)
        exchanges[slot].start()

    send(0, grad_branch.at[away], branch_in, to_x)

    chains = []
    for low, high in HALVES:
        where = pl.ds(low, high - low)
        chains.append(Sum(squares.at[:, :, :, where], square_sum.at[:, where], scratch[:10], True))
        scratch = scratch[10:]
    for source, dest, parts in ((grads1, sum1, PARTS), (grads0, sum0, PARTS_ZERO)):
        for low, high in parts:
            where = pl.ds(low, high - low)
            chains.append(Sum(source.at[:, where], dest.at[:, where], scratch[:8], False))
            scratch = scratch[8:]

    masks = edge_masks(-1)
    pair = col.at[pl.ds(9 * 256, 9 * 256)]
    picture = source_in.at[0]
    width = emb_weight.shape[2]

    def taps_one(_):
        taps_of(col, masks, grad_branch, 0, 512, 0, -1)
        wait(local["weights"])

    def conv_back(count):
        column = 512 * count
        result = None
        for tap in range(9):
            term = mm(full[tap], col[tap * 512 : (tap + 1) * 512, column : column + 512], TN)
            result = term if result is None else result + term
        slope_in[:, column : column + 512] = result

    def back_one(base):
        def step(group, carry):
            where = rows(base + group * BLOCK, BLOCK)
            unit = unit_of(wide_in[where, :], stats1, where)
            gain = par[where, GAIN + 1 : GAIN + 2]
            unscaled = unit * gain + par[where, BIAS + 1 : BIAS + 2]
            scale = 1.0 + par[where, SCALE : SCALE + 1]
            grad_pre = slope_in[where, :] * silu_slope(unscaled * scale + par[where, SHIFT : SHIFT + 1])
            grad = grad_pre * scale
            low = unit_back(grad * gain, unit, stats1[where, 1:2]).astype(BF)
            grad_hidden[where, :] = low
            columns[where, 2:3] = row_sum(grad_pre * unscaled)
            columns[where, 3:4] = row_sum(grad_pre)
            columns[where, 4:5] = row_sum(grad * unit)
            columns[where, 5:6] = row_sum(grad)
            columns[where, 6:7] = row_sum(low.astype(F32))
            return carry

        lax.fori_loop(0, 256 // BLOCK, step, 0)

    def away_one(_):
        local["weights"] = fetch_conv(sems.at[pl.ds(6, 2)], full, half, 0, w_own, w_peer)
        columns[...] = jnp.zeros_like(columns)
        columns[:, 7:11] = small2[...]
        wait(local["wide"])
        back_one((1 - half) * 256)
        send(1, grad_hidden.at[away], hidden_in, to_x)

    def near_one(_):
        back_one(half * 256)
        local["wide"] = (fetch(sems, 8, grad_resid, wide_in),)
        flat[...] = columns[...].T[0:16]
        mod[place, half] = flat[2:4, near]
        mod_send[...] = flat[2:4, away]
        send(2, mod_send, mod.at[place, half], to_x)
        pres[place] = pre_embed[...]
        for ahead, target in enumerate(others):
            remote(pres.at[place], pres.at[place], all_sends, all_recvs, ahead, target).start()

    def pair_one(_):
        exchanges[0].wait_recv()
        taps_of(col, masks, grad_branch.at[near], 0, 256, 0, -1)
        taps_of(pair, masks, branch_in, 0, 256, 0, -1)
        wait(local["inputs"])
        turned[:PIX, :] = source_in[0].T
        turned[PIX:, :] = source_in[1].T
        local["inputs"] = (
            fetch(sems, 9, first, source_in.at[0]),
            fetch(sems, 10, first_other, source_in.at[1, near]),
            fetch(sems, 11, first_peer, source_in.at[1, away]),
        )

    def grad_one(count):
        weight_back(grads1, range(*PARTS[count]), col, turned)
        if count == 0:
            send(6, block.at[away], block_out.at[half], to_x)
            local["block"] = fetch(sems, 3, block.at[near], block_out.at[half])

    def share(_):
        remote(mod_send, mod.at[place, 1 - half], sends, recvs, 2, to_x).wait_recv()
        for ahead, target in enumerate(others):
            remote(mod.at[place], mod.at[place], all_sends, all_recvs, 15 + ahead, target).start()

    def pair_zero(_):
        exchanges[1].wait_recv()
        taps_of(col, masks, grad_hidden.at[near], 0, 256, 0, -1)
        taps_of(pair, masks, hidden_in, 0, 256, 0, -1)
        wait(local["inputs"])
        turned[:PIX, :] = source_in[0].T
        turned[PIX:, :] = source_in[1].T
        local["inputs"] = (
            fetch(sems, 9, images.at[half], picture.at[near]),
            fetch(sems, 10, image_peer, picture.at[away]),
        )

    def grad_zero(count):
        weight_back(grads0, range(*PARTS_ZERO[count]), col, turned)

    def taps_zero(_):
        taps_of(col, masks, grad_hidden, 0, 512, 0, -1)
        wait(local["weights"])

    def back_zero(base, dest):
        def step(group, carry):
            here = rows(group * BLOCK, BLOCK)
            where = rows(base + group * BLOCK, BLOCK)
            unit = unit_of(picture[where, :].astype(F32), stats0, where)
            gain = par[where, GAIN : GAIN + 1]
            grad = slope_in[where, :] * silu_slope(unit * gain + par[where, BIAS : BIAS + 1])
            result = wide_in[where, :] + unit_back(grad * gain, unit, stats0[where, 1:2])
            dest[here, :] = result.astype(dest.dtype)
            columns[where, 0:1] = row_sum(grad * unit)
            columns[where, 1:2] = row_sum(grad)
            return carry

        lax.fori_loop(0, 256 // BLOCK, step, 0)

    def away_zero(_):
        wait(local["inputs"])
        wait(local["wide"])
        back_zero((1 - half) * 256, far)
        send(3, far, far_in, to_x)

    def near_zero(_):
        back_zero(half * 256, images_grad)
        flat[...] = columns[...].T[0:16]
        total[0] = flat[:, away]
        send(4, total.at[0], total_in.at[0], to_x)

    def class_part(_):
        for ahead in range(15):
            origin = (place + 15 - ahead) % 16
            remote(pres.at[origin], pres.at[origin], all_sends, all_recvs, ahead, to_x).wait_recv()
            remote(mod.at[origin], mod.at[origin], all_sends, all_recvs, 15 + ahead, to_x).wait_recv()
        result = None
        for which in range(2):
            factor = jnp.concatenate([mod[:, 0, which, :], mod[:, 1, which, :]], 0)
            term = mm(split(factor, 0), emb_weight[which])
            result = term if result is None else result + term
        result = result[0:32] + result[32:64] + result[64:96]
        rows_own[0] = result[0:16]
        rows_own[1] = result[16:32]
        send(5, rows_own, rows_in, to_x)

    def landed(slot, step):
        remote(total.at[0], total_in.at[step], sends, recvs, slot, to_x).wait_recv()

    def small_sums(count):
        if count == 0:
            landed(4, 0)
            total[1] = flat[:, near] + total_in[0]
            send(7, total.at[1], total_in.at[1], {"batch": place + 1 - 2 * core})
        elif count == 1:
            landed(7, 1)
            total[2] = total[1] + total_in[1]
            send(8, total.at[2], total_in.at[2], {"batch": place + 2 * (1 - 2 * up)})
        elif count == 2:
            landed(8, 2)
            total[3] = total[2] + total_in[2]
            for ahead in (1, 2, 3):
                target = {"batch": (deep + ahead) % 4 * 4 + place % 4}
                send(8 + ahead, total.at[3], total_in.at[3 + deep], target)
            total_in[3 + deep] = total[3]
        else:
            for ahead in (1, 2, 3):
                landed(8 + ahead, 3 + (deep + 4 - ahead) % 4)
            sums[...] = (total_in[3] + total_in[4]) + (total_in[5] + total_in[6])
            remote(rows_own, rows_in, sends, recvs, 5, to_x).wait_recv()
            for slot in range(2):
                class_rows[slot] = (rows_own[slot] + rows_in[slot]) * silu_slope(pres[:, slot, :width])
            mod_out[...] = mod[...]
            pre_out[...] = pres[...]

    pieces = {
        TAPS_ONE: taps_one, CONV_ONE: conv_back, AWAY_ONE: away_one, NEAR_ONE: near_one,
        PAIR_ONE: pair_one, GRAD_ONE: grad_one, SHARE: share, PAIR_ZERO: pair_zero,
        GRAD_ZERO: grad_zero, TAPS_ZERO: taps_zero, CONV_ZERO: conv_back, AWAY_ZERO: away_zero,
        NEAR_ZERO: near_zero, ROWS: class_part, SMALL: small_sums,
    }
    counts = dict.fromkeys(pieces, 0)
    for entry in ORDER:
        if entry < 100:
            chains[entry].advance()
        else:
            pieces[entry](counts[entry])
            counts[entry] += 1
    remote(far, far_in, sends, recvs, 3, to_x).wait_recv()
    remote(block.at[away], block_out.at[1 - half], sends, recvs, 6, to_x).wait_recv()
    local["block"].wait()
    for copy in exchanges.values():
        copy.wait_send()
    for ahead, target in enumerate(others):
        remote(pres.at[place], pres.at[place], all_sends, all_recvs, ahead, target).wait_send()
        remote(mod.at[place], mod.at[place], all_sends, all_recvs, 15 + ahead, target).wait_send()


def backward_call(*args):
    arrays, specs = operands(args)
    dma = pltpu.SemaphoreType.DMA
    scratch = [
        dma((12,)), dma((12,)), dma((12,)), dma((30,)), dma((30,)),
        pltpu.VMEM((16, 9, 16, 512), BF),
        pltpu.VMEM((16, 9, 16, 512), BF),
        pltpu.VMEM((9 * 512, PIX), BF),
        pltpu.VMEM((2 * PIX, 512), BF),
        pltpu.VMEM((9, 512, 512), BF),
        pltpu.VMEM((512, PIX), F32),
        pltpu.VMEM((512, PIX), F32),
        pltpu.VMEM((2, 512, PIX), BF),
        pltpu.VMEM((256, PIX), BF),
        pltpu.VMEM((256, PIX), BF),
        pltpu.VMEM((512, PIX), BF),
        pltpu.VMEM((256, PIX), BF),
        pltpu.VMEM((512, 128), F32),
        pltpu.VMEM((16, 512), F32),
        pltpu.VMEM((16, 2, 2, 256), F32),
        pltpu.VMEM((2, 256), F32),
        pltpu.VMEM((16, 2, 1024 + 128), F32),
        pltpu.VMEM((2, 16, 1024), F32),
        pltpu.VMEM((2, 16, 1024), F32),
        pltpu.VMEM((4, 16, 256), F32),
        pltpu.VMEM((7, 16, 256), F32),
    ]
    for low, high in HALVES:
        scratch += sum_scratch((high - low, 16, 512), True)
    for low, high in PARTS + PARTS_ZERO:
        scratch += sum_scratch((high - low, 16, 512), False)
    outs = [
        (out((16, 4, 16, 512), BF), ANYWHERE),
        (out((16, 9, 16, 512), BF), ANYWHERE),
        (out((16, 9, 16, 512), BF), ANYWHERE),
        (out((256, PIX), F32), VMEM),
        (out((256, PIX), BF), ANYWHERE),
        (out((2, 256, PIX), BF), ANYWHERE),
        (out((16, 256), F32), VMEM),
        (out((2, 16, 1024), F32), VMEM),
        (out((16, 2, 2, 256), F32), VMEM),
        (out((16, 2, 1024 + 128), F32), VMEM),
    ]
    return pl.pallas_call(
        backward,
        out_shape=[o for o, _ in outs],
        in_specs=specs,
        out_specs=[spec for _, spec in outs],
        scratch_shapes=scratch,
        cost_estimate=pl.CostEstimate(flops=4 * 10**10, bytes_accessed=200 * 2**20, transcendentals=0),
        compiler_params=pltpu.CompilerParams(
            collective_id=2, has_side_effects=True, vmem_limit_bytes=60 * 2**20
        ),
    )(*arrays)


TRIPLES = ((0, 3), (3, 6), (6, 9))


def finish(
    sum0, sum1, squares, near, far, block_in, mod, pres, rows_in, sums,
    block_out, conv, qkv, proj, images_grad, emb, table, gains, biases, conv_biases, emb_biases, proj_bias,
    ins, outs, low, low_square, wide, square, mine, other, block, grads, emb_out, table_out,
):
    half = lax.axis_index("head")
    width = rows_in.shape[2]
    reads = []
    for layer, source in enumerate((sum0, sum1)):
        for number, (start, stop) in enumerate(TRIPLES):
            taps = pl.ds(start, stop - start)
            reads.append(fetch(ins, layer * 3 + number, source.at[:, taps], low.at[layer, :, taps]))
    reads.append(fetch(ins, 6, squares, low_square))
    reads.append(fetch(ins, 7, near, mine))
    reads.append(fetch(ins, 8, far, other))
    reads.append(fetch(ins, 9, block_in, block))
    writes = []

    def write(source, dest):
        writes.append(fetch(outs, len(writes), source, dest))

    for number, row in enumerate((0, 4, 7)):
        gains[number : number + 1] = sums[row : row + 1]
        biases[number : number + 1] = sums[row + 1 : row + 2]
    conv_biases[0:1] = sums[6:7]
    conv_biases[1:2] = sums[9:10]
    emb_biases[...] = sums[2:4]
    proj_bias[...] = sums[10:11]

    numbers = lax.broadcasted_iota(jnp.int32, (32, table.shape[0]), 1)
    ids = jnp.concatenate([pres[:, slot, width : width + 1] for slot in range(2)], 0).astype(jnp.int32)
    chosen = (numbers == ids).astype(F32).astype(BF)
    class_rows = jnp.concatenate([rows_in[0], rows_in[1]], 0)
    table_out[...] = mm(jnp.concatenate([chosen] * 3, 0), split(class_rows, 0), TN)
    write(table_out, table)
    embed = jnp.concatenate([jax.nn.silu(pres[:, slot, :width]) for slot in range(2)], 0)
    parts = split(embed, 0)
    high, middle = parts[0:32], parts[32:64]
    for which in range(2):
        factor = split(jnp.concatenate([mod[:, slot, which, :] for slot in range(2)], 0), 0)
        left = jnp.concatenate([factor[0:32], factor[0:32], factor[32:64]], 0)
        emb_out[which] = mm(left, jnp.concatenate([high, middle, high], 0), TN)
    write(emb_out, emb)
    for layer in range(2):
        for number, (start, stop) in enumerate(TRIPLES):
            reads[layer * 3 + number].wait()
            for tap in range(start, stop):
                wide[layer, tap] = low[layer, :, tap].reshape(256, 512).astype(F32)
            taps = pl.ds(start, stop - start)
            write(wide.at[layer, taps], conv.at[layer, taps])
    reads[6].wait()
    for which in range(4):
        square[which] = low_square[:, which].reshape(256, 512).astype(F32)
    write(square.at[pl.ds(0, 3)], qkv)
    write(square.at[3], proj)
    reads[9].wait()
    write(block, block_out)
    reads[7].wait()
    reads[8].wait()
    grads[half] = mine[...]
    grads[1 - half] = other[...].astype(F32)
    write(grads, images_grad)
    wait(writes)


def finish_call(sum0, sum1, squares, near, far, block, mod, pres, rows_in, sums, table_shape):
    width = table_shape[1]
    shapes = [
        (2, 9, 256, 512),
        (3, 256, 512),
        (256, 512),
        (2, 256, PIX),
        (2, 256, width),
        table_shape,
        (3, 256),
        (3, 256),
        (2, 256),
        (2, 256),
        (1, 256),
    ]
    dma = pltpu.SemaphoreType.DMA
    return pl.pallas_call(
        finish,
        out_shape=[out(block.shape, BF)] + [out(shape, F32) for shape in shapes],
        in_specs=[ANYWHERE] * 6 + [VMEM] * 4,
        out_specs=[ANYWHERE] * 7 + [VMEM] * 5,
        scratch_shapes=[
            dma((10,)), dma((12,)),
            pltpu.VMEM((2,) + sum0.shape, BF),
            pltpu.VMEM(squares.shape, BF),
            pltpu.VMEM(shapes[0], F32),
            pltpu.VMEM((4, 256, 512), F32),
            pltpu.VMEM((256, PIX), F32),
            pltpu.VMEM((256, PIX), BF),
            pltpu.VMEM(block.shape, BF),
            pltpu.VMEM(shapes[3], F32),
            pltpu.VMEM(shapes[4], F32),
            pltpu.VMEM(shapes[5], F32),
        ],
        compiler_params=pltpu.CompilerParams(vmem_limit_bytes=58 * 2**20),
    )(sum0, sum1, squares, near, far, block, mod, pres, rows_in, sums)


def paired(
    images,
    timesteps,
    classes,
    live_count,
    norm_gain,
    norm_bias,
    conv_weight,
    conv_bias,
    emb_weight,
    emb_bias,
    class_table,
    qkv_weight,
    proj_weight,
    proj_bias,
    cotangent,
):
    (
        par, pre_embed, image_peer, cot_peer, conv_peer, q_peer, p_peer,
        first, first_near, first_other, hidden, stats0, stats1, second, resid, stats2, normed,
    ) = forward_call(
        timesteps, classes, norm_gain, norm_bias, conv_bias, proj_bias[None], emb_bias, emb_weight,
        *map(Far, (class_table, images, cotangent, conv_weight, qkv_weight, proj_weight)),
    )
    square_grads, block, grad_resid, grad_branch, small2, second_peer, first_peer = attention_call(
        Scalars(live_count), normed, Far(resid), stats2, par, Far(cotangent), Far(cot_peer),
        Far(qkv_weight), Far(q_peer), Far(proj_weight), Far(p_peer), Far(second), Far(first_near),
    )
    square_sum, conv_sum1, conv_sum0, near, far, block_out, sums, class_rows, mod, pre_all = backward_call(
        Scalars(live_count), square_grads, grad_branch, *map(Far, (block, hidden, second, second_peer)),
        *map(Far, (first, first_other, first_peer, grad_resid, images, image_peer, conv_weight, conv_peer)),
        stats0, stats1, par, small2, pre_embed, emb_weight,
    )
    (
        block_total, conv_total, qkv_total, proj_total, images_grad, emb_total, table_total,
        gains, biases, conv_biases, emb_biases, proj_biases,
    ) = finish_call(
        conv_sum0, conv_sum1, square_sum, near, far, block_out, mod, pre_all, class_rows, sums, class_table.shape
    )
    return (
        block_total,
        images_grad,
        gains,
        biases,
        conv_total,
        conv_biases,
        emb_total,
        emb_biases,
        table_total,
        qkv_total,
        proj_total,
        proj_biases[0],
    )


def solution(mesh):
    in_specs = (
        P("batch", "head", None),
        P("batch"),
        P("batch"),
        P("batch"),
        P(None, "head"),
        P(None, "head"),
        P(None, None, "head", None),
        P(None, "head"),
        P(None, "head", None),
        P(None, "head"),
        P(),
        P(None, "head", None),
        P("head", None),
        P("head"),
        P("batch", "head", None),
    )
    out_specs = (
        P("batch", "head", None),
        P("batch", "head", None),
        P(None, "head"),
        P(None, "head"),
        P(None, None, "head", None),
        P(None, "head"),
        P(None, "head", None),
        P(None, "head"),
        P(),
        P(None, "head", None),
        P("head", None),
        P("head"),
    )
    body = shards
    if mesh.shape["head"] == 2 and mesh.shape["batch"] == 16:
        body = paired
    return jax.shard_map(body, mesh=mesh, in_specs=in_specs, out_specs=out_specs, check_vma=False)
```

```python
import math

import jax
import jax.numpy as jnp
from jax import lax
from jax.experimental import pallas as pl
from jax.experimental.pallas import tpu as pltpu
from jax.sharding import PartitionSpec as P

C = 512
GROUPS = 32
HEADS = 8
SIDE = 32


EPS = 1e-05
HIGH = lax.Precision.HIGHEST
CONTRACT_FIRST = (((0,), (0,)), ((), ()))
CONTRACT_LAST = (((1,), (1,)), ((), ()))


def silu_slope(values):
    sigma = jax.nn.sigmoid(values)
    return sigma * (1.0 + values * (1.0 - sigma))


def moved(source, grid_side, row_step, col_step):
    grid = source.reshape(source.shape[0], grid_side, grid_side)
    padded = jnp.pad(grid, ((0, 0), (1, 1), (1, 1)))
    window = padded[
        :, 1 + row_step : 1 + row_step + grid_side, 1 + col_step : 1 + col_step + grid_side
    ]
    return window.reshape(source.shape)


def group_unit(source, groups):
    grouped = source.reshape(groups, -1)
    centre = grouped - jnp.mean(grouped, axis=1, keepdims=True)
    inverse = lax.rsqrt(jnp.mean(jnp.square(centre), axis=1, keepdims=True) + EPS)
    return ((centre * inverse).reshape(source.shape), inverse)


def group_back(grad_unit, unit_rows, inverse, groups):
    flat_grad = grad_unit.reshape(groups, -1)
    flat_unit = unit_rows.reshape(groups, -1)
    result = flat_grad - jnp.mean(flat_grad, axis=1, keepdims=True)
    result = (result - flat_unit * jnp.mean(flat_grad * flat_unit, axis=1, keepdims=True)) * inverse
    return result.reshape(grad_unit.shape)


def conv_apply(weight, source, grid_side):
    result = jnp.dot(
        weight[0], moved(source, grid_side, -1, -1), preferred_element_type=jnp.float32
    )
    for tap_index in range(1, 9):
        result = result + jnp.dot(
            weight[tap_index],
            moved(source, grid_side, tap_index // 3 - 1, tap_index % 3 - 1),
            preferred_element_type=jnp.float32,
        )
    return result


def conv_transpose(weight, grads, grid_side):
    result = lax.dot_general(
        weight[0], moved(grads, grid_side, 1, 1), CONTRACT_FIRST, preferred_element_type=jnp.float32
    )
    for tap_index in range(1, 9):
        result = result + lax.dot_general(
            weight[tap_index],
            moved(grads, grid_side, 1 - tap_index // 3, 1 - tap_index % 3),
            CONTRACT_FIRST,
            preferred_element_type=jnp.float32,
        )
    return result


def conv_weight_grads(grads, source, grid_side):
    return jnp.stack(
        [
            lax.dot_general(
                grads,
                moved(source, grid_side, tap_index // 3 - 1, tap_index % 3 - 1),
                CONTRACT_LAST,
                preferred_element_type=jnp.float32,
            )
            for tap_index in range(9)
        ]
    )


def features(timestep, emb_width):
    half_width = emb_width // 2
    freqs = jnp.exp(-math.log(10000.0) * jnp.arange(half_width, dtype=jnp.float32) / half_width)
    angles = timestep.astype(jnp.float32) * freqs
    return jnp.concatenate([jnp.cos(angles), jnp.sin(angles)])


def shards(
    images,
    timesteps,
    classes,
    live_count,
    norm_gain,
    norm_bias,
    conv_weight,
    conv_bias,
    emb_weight,
    emb_bias,
    class_table,
    qkv_weight,
    proj_weight,
    proj_bias,
    cotangent,
):
    slot_count, chan_dev, pixel_count = images.shape
    grid_side = SIDE
    groups = chan_dev // (C // GROUPS)
    head_size = C // HEADS
    heads_dev = chan_dev // head_size
    att_scale = head_size ** (-0.5)
    emb_dense = emb_weight.astype(jnp.float32)
    class_total, emb_width = class_table.shape

    def gather_channels(rows_low):
        return lax.all_gather(rows_low, "head", axis=0, tiled=True)

    def input_grad(which_conv, grad_rows):
        weight_cols = conv_weight[which_conv]
        return lax.psum_scatter(
            conv_transpose(weight_cols, grad_rows, grid_side).astype(jnp.bfloat16),
            "head",
            scatter_dimension=0,
            tiled=True,
        ).astype(jnp.float32)

    def per_slot(slot_index, carry):
        (
            outputs,
            grads_in,
            gain_acc,
            bias_acc,
            convw_acc,
            convb_acc,
            embw_acc,
            embb_acc,
            table_acc,
            qkv_acc,
            projw_acc,
            projb_acc,
        ) = carry
        picture = lax.dynamic_index_in_dim(images, slot_index, 0, keepdims=False).astype(
            jnp.float32
        )
        live_flag = (slot_index < live_count[0]).astype(jnp.float32)
        class_id = classes[slot_index]
        table_row = lax.dynamic_index_in_dim(class_table, class_id, 0, keepdims=False).astype(
            jnp.float32
        )
        pre_embed = features(timesteps[slot_index], emb_width) + table_row
        embed = jax.nn.silu(pre_embed)
        scale = jnp.dot(emb_dense[0], embed, precision=HIGH) + emb_bias[0]
        shift = jnp.dot(emb_dense[1], embed, precision=HIGH) + emb_bias[1]
        unit_zero, inverse_zero = group_unit(picture, groups)
        pre_first = unit_zero * norm_gain[0][:, None] + norm_bias[0][:, None]
        first_full = gather_channels(jax.nn.silu(pre_first).astype(jnp.bfloat16))
        hidden = conv_apply(conv_weight[0], first_full, grid_side) + conv_bias[0][:, None]
        unit_one, inverse_one = group_unit(hidden, groups)
        normed_one = unit_one * norm_gain[1][:, None] + norm_bias[1][:, None]
        pre_second = normed_one * (1.0 + scale[:, None]) + shift[:, None]
        second_full = gather_channels(jax.nn.silu(pre_second).astype(jnp.bfloat16))
        resid = picture + conv_apply(conv_weight[1], second_full, grid_side) + conv_bias[1][:, None]
        unit_two, inverse_two = group_unit(resid, groups)
        normed_full = gather_channels(
            (unit_two * norm_gain[2][:, None] + norm_bias[2][:, None]).astype(jnp.bfloat16)
        )
        query = (
            jnp.dot(qkv_weight[0], normed_full, preferred_element_type=jnp.float32)
            .astype(jnp.bfloat16)
            .reshape(heads_dev, head_size, pixel_count)
        )
        keys = (
            jnp.dot(qkv_weight[1], normed_full, preferred_element_type=jnp.float32)
            .astype(jnp.bfloat16)
            .reshape(heads_dev, head_size, pixel_count)
        )
        values = (
            jnp.dot(qkv_weight[2], normed_full, preferred_element_type=jnp.float32)
            .astype(jnp.bfloat16)
            .reshape(heads_dev, head_size, pixel_count)
        )
        scores = (
            jnp.einsum("hdi,hdj->hij", query, keys, preferred_element_type=jnp.float32) * att_scale
        )
        highest = jnp.max(scores, axis=2, keepdims=True)
        expo = jnp.exp(scores - highest)
        totals = jnp.sum(expo, axis=2, keepdims=True)
        log_total = highest + jnp.log(totals)
        weights = (expo / totals).astype(jnp.bfloat16)
        mixed = (
            jnp.einsum("hdj,hij->hdi", values, weights, preferred_element_type=jnp.float32)
            .astype(jnp.bfloat16)
            .reshape(chan_dev, pixel_count)
        )
        weight_cols = proj_weight
        proj_term = lax.psum_scatter(
            lax.dot_general(
                weight_cols, mixed, CONTRACT_FIRST, preferred_element_type=jnp.float32
            ).astype(jnp.bfloat16),
            "head",
            scatter_dimension=0,
            tiled=True,
        ).astype(jnp.float32)
        result = resid + proj_term + proj_bias[:, None]
        outputs = lax.dynamic_update_index_in_dim(
            outputs, (live_flag * result).astype(jnp.bfloat16), slot_index, 0
        )
        grad_low = lax.dynamic_index_in_dim(cotangent, slot_index, 0, keepdims=False)
        grad_out = live_flag * grad_low.astype(jnp.float32)
        grad_full = lax.all_gather(grad_low, "head", axis=0, tiled=True) * live_flag.astype(
            jnp.bfloat16
        )
        grad_mixed = jnp.dot(proj_weight, grad_full, preferred_element_type=jnp.float32).astype(
            jnp.bfloat16
        )
        projw_acc = projw_acc + lax.dot_general(
            mixed, grad_full, CONTRACT_LAST, preferred_element_type=jnp.float32
        )
        projb_acc = projb_acc + jnp.sum(grad_out, axis=1)
        again = (
            jnp.einsum("hdi,hdj->hij", query, keys, preferred_element_type=jnp.float32) * att_scale
        )
        probs = jnp.exp(again - log_total)
        grad_heads = grad_mixed.reshape(heads_dev, head_size, pixel_count)
        grad_probs = jnp.einsum(
            "hdi,hdj->hij", grad_heads, values, preferred_element_type=jnp.float32
        )
        grad_scores = (
            probs * (grad_probs - jnp.sum(grad_probs * probs, axis=2, keepdims=True))
        ).astype(jnp.bfloat16)
        grad_query = (
            jnp.einsum("hij,hdj->hdi", grad_scores, keys, preferred_element_type=jnp.float32)
            * att_scale
        ).astype(jnp.bfloat16)
        grad_keys = (
            jnp.einsum("hij,hdi->hdj", grad_scores, query, preferred_element_type=jnp.float32)
            * att_scale
        ).astype(jnp.bfloat16)
        grad_values = jnp.einsum(
            "hdi,hij->hdj", grad_heads, weights, preferred_element_type=jnp.float32
        ).astype(jnp.bfloat16)
        stacked = jnp.stack([grad_query, grad_keys, grad_values]).reshape(3, chan_dev, pixel_count)
        weight_cols = qkv_weight
        grad_normed = lax.psum_scatter(
            lax.dot_general(
                weight_cols,
                stacked,
                (((0, 1), (0, 1)), ((), ())),
                preferred_element_type=jnp.float32,
            ).astype(jnp.bfloat16),
            "head",
            scatter_dimension=0,
            tiled=True,
        ).astype(jnp.float32)
        qkv_acc = qkv_acc + lax.dot_general(
            stacked, normed_full, (((2,), (1,)), ((), ())), preferred_element_type=jnp.float32
        )
        grad_resid = grad_out + group_back(
            grad_normed * norm_gain[2][:, None], unit_two, inverse_two, groups
        )
        grad_branch = grad_resid.astype(jnp.bfloat16)
        grad_second = input_grad(1, grad_branch)
        grad_pre = grad_second * silu_slope(pre_second)
        scale_grad = jnp.sum(grad_pre * normed_one, axis=1)
        shift_grad = jnp.sum(grad_pre, axis=1)
        grad_normed_one = grad_pre * (1.0 + scale[:, None])
        grad_hidden = group_back(
            grad_normed_one * norm_gain[1][:, None], unit_one, inverse_one, groups
        ).astype(jnp.bfloat16)
        grad_first = input_grad(0, grad_hidden)
        grad_pre_first = grad_first * silu_slope(pre_first)
        picture_grad = grad_resid + group_back(
            grad_pre_first * norm_gain[0][:, None], unit_zero, inverse_zero, groups
        )
        grads_in = lax.dynamic_update_index_in_dim(grads_in, picture_grad, slot_index, 0)
        gain_acc = gain_acc + jnp.stack(
            [
                jnp.sum(grad_pre_first * unit_zero, axis=1),
                jnp.sum(grad_normed_one * unit_one, axis=1),
                jnp.sum(grad_normed * unit_two, axis=1),
            ]
        )
        bias_acc = bias_acc + jnp.stack(
            [
                jnp.sum(grad_pre_first, axis=1),
                jnp.sum(grad_normed_one, axis=1),
                jnp.sum(grad_normed, axis=1),
            ]
        )
        convw_acc = convw_acc + jnp.stack(
            [
                conv_weight_grads(grad_hidden, first_full, grid_side),
                conv_weight_grads(grad_branch, second_full, grid_side),
            ]
        )
        convb_acc = convb_acc + jnp.stack(
            [
                jnp.sum(grad_hidden.astype(jnp.float32), axis=1),
                jnp.sum(grad_branch.astype(jnp.float32), axis=1),
            ]
        )
        embw_acc = embw_acc + jnp.stack(
            [scale_grad[:, None] * embed[None, :], shift_grad[:, None] * embed[None, :]]
        )
        embb_acc = embb_acc + jnp.stack([scale_grad, shift_grad])
        grad_embed = jnp.dot(scale_grad, emb_dense[0], precision=HIGH) + jnp.dot(
            shift_grad, emb_dense[1], precision=HIGH
        )
        class_row = grad_embed * silu_slope(pre_embed)
        old_row = lax.dynamic_index_in_dim(table_acc, class_id, 0, keepdims=True)
        table_acc = lax.dynamic_update_index_in_dim(
            table_acc, old_row + class_row[None, :], class_id, 0
        )
        return (
            outputs,
            grads_in,
            gain_acc,
            bias_acc,
            convw_acc,
            convb_acc,
            embw_acc,
            embb_acc,
            table_acc,
            qkv_acc,
            projw_acc,
            projb_acc,
        )

    table_start = jnp.zeros(class_table.shape, jnp.float32)
    initial = (
        jnp.zeros(images.shape, jnp.bfloat16),
        jnp.zeros(images.shape, jnp.float32),
        jnp.zeros(norm_gain.shape, jnp.float32),
        jnp.zeros(norm_bias.shape, jnp.float32),
        jnp.zeros(conv_weight.shape, jnp.float32),
        jnp.zeros(conv_bias.shape, jnp.float32),
        jnp.zeros(emb_weight.shape, jnp.float32),
        jnp.zeros(emb_bias.shape, jnp.float32),
        table_start,
        jnp.zeros(qkv_weight.shape, jnp.float32),
        jnp.zeros(proj_weight.shape, jnp.float32),
        jnp.zeros(proj_bias.shape, jnp.float32),
    )
    final = lax.fori_loop(0, slot_count, per_slot, initial)
    (
        outputs,
        grads_in,
        gain_acc,
        bias_acc,
        convw_acc,
        convb_acc,
        embw_acc,
        embb_acc,
        table_acc,
        qkv_acc,
        projw_acc,
        projb_acc,
    ) = final
    table_total = lax.psum(table_acc, ("batch", "head"))
    summed = (
        lax.psum(gain_acc.astype(jnp.bfloat16), "batch").astype(jnp.float32),
        lax.psum(bias_acc.astype(jnp.bfloat16), "batch").astype(jnp.float32),
        lax.psum(convw_acc.astype(jnp.bfloat16), "batch").astype(jnp.float32),
        lax.psum(convb_acc.astype(jnp.bfloat16), "batch").astype(jnp.float32),
        lax.psum(embw_acc.astype(jnp.bfloat16), "batch").astype(jnp.float32),
        lax.psum(embb_acc.astype(jnp.bfloat16), "batch").astype(jnp.float32),
        lax.psum(qkv_acc.astype(jnp.bfloat16), "batch").astype(jnp.float32),
        lax.psum(projw_acc.astype(jnp.bfloat16), "batch").astype(jnp.float32),
        lax.psum(projb_acc.astype(jnp.bfloat16), "batch").astype(jnp.float32),
    )
    return (
        outputs,
        grads_in,
        summed[0],
        summed[1],
        summed[2],
        summed[3],
        summed[4],
        summed[5],
        table_total,
        summed[6],
        summed[7],
        summed[8],
    )


PIX = 1024
BLOCK = 256
BF = jnp.bfloat16
F32 = jnp.float32
NN = (((1,), (0,)), ((), ()))
TN = (((0,), (0,)), ((), ()))
NT = (((1,), (1,)), ((), ()))
VMEM = pl.BlockSpec(memory_space=pltpu.VMEM)
SMEM = pl.BlockSpec(memory_space=pltpu.SMEM)

GAIN, BIAS, CONVB, PROJB, SCALE, SHIFT = 0, 3, 6, 8, 9, 10


def mm(left, right, dims=NN):
    return lax.dot_general(left, right, dims, preferred_element_type=F32)


class Far:
    def __init__(self, array):
        self.array = array


ANYWHERE = pl.BlockSpec(memory_space=pl.ANY)


class Scalars(Far):
    pass


def operands(args):
    arrays = [arg.array if isinstance(arg, Far) else arg for arg in args]
    specs = []
    for arg in args:
        if isinstance(arg, Scalars):
            specs.append(SMEM)
        else:
            specs.append(ANYWHERE if isinstance(arg, Far) else VMEM)
    return arrays, specs


def split(value, axis):
    parts = []
    for _ in range(3):
        part = value.astype(BF)
        parts.append(part)
        value = value - part.astype(F32)
    return jnp.concatenate(parts, axis)


def fetch(sems, slot, source, dest):
    copy = pltpu.make_async_copy(source, dest, sems.at[slot])
    copy.start()
    return copy


def out(shape, dtype):
    return jax.ShapeDtypeStruct(shape, dtype)


def rows(start, count):
    return pl.ds(pl.multiple_of(start, count), count)


def edge_masks(sign):
    pixel = lax.broadcasted_iota(jnp.int32, (1, PIX), 1)
    col, row = pixel % SIDE, pixel // SIDE
    table = {}
    for step in (-1, 1):
        moved_step = sign * step
        table["col", step] = ((col + moved_step >= 0) & (col + moved_step < SIDE)).astype(F32)
        table["row", step] = ((row + moved_step >= 0) & (row + moved_step < SIDE)).astype(F32)
    return table


def put_taps(dest, masks, values, first_row, depth, base, sign):
    count = values.shape[0]
    for col_step in (-1, 0, 1):
        across = values
        if col_step:
            across = pltpu.roll(values, (-sign * col_step) % PIX, 1) * masks["col", col_step]
        for row_step in (-1, 0, 1):
            copy = across
            if row_step:
                copy = pltpu.roll(across, (-sign * row_step * SIDE) % PIX, 1) * masks["row", row_step]
            tap = 3 * (row_step + 1) + col_step + 1
            dest[rows(tap * depth + first_row, count), base : base + PIX] = copy.astype(BF)


def taps_of(dest, masks, source, offset, depth, base, sign):
    for start in range(0, source.shape[0], 128):
        piece = source[start : start + 128, :].astype(F32)
        put_taps(dest, masks, piece, offset + start, depth, base, sign)


def fetch_conv(sems, full, half, which, own, peer):
    return (
        fetch(sems, 0, own.at[which], full.at[:, rows(half * 256, 256), :]),
        fetch(sems, 1, peer.at[which], full.at[:, rows((1 - half) * 256, 256), :]),
    )


def wait(copies):
    for copy in copies:
        copy.wait()


def conv_dots(dest, full, col, dims, finish):
    for column in range(0, PIX, 512):
        total = None
        for tap in range(9):
            term = mm(full[tap], col[tap * 512 : (tap + 1) * 512, column : column + 512], dims)
            total = term if total is None else total + term
        dest[:, column : column + 512] = finish(total, column)


def grouped(block):
    return block.reshape((-1, 16) + block.shape[1:])


def group_mean(block):
    return jnp.sum(block, axis=(1, 2), keepdims=True) * (1.0 / (16 * PIX))


def group_stats(block, stats, where):
    parts = grouped(block)
    centre = group_mean(parts)
    parts = parts - centre
    inverse = lax.rsqrt(group_mean(jnp.square(parts)) + EPS)
    count = block.shape[0]
    for column, value in enumerate((centre, inverse)):
        stats[where, column : column + 1] = jnp.broadcast_to(value, (count // 16, 16, 1)).reshape(count, 1)
    return (parts * inverse).reshape(block.shape)


def unit_of(block, stats, where):
    return (block - stats[where, 0:1]) * stats[where, 1:2]


def unit_back(grad, unit, inverse):
    parts, units = grouped(grad), grouped(unit)
    result = parts - group_mean(parts) - units * group_mean(parts * units)
    return result.reshape(grad.shape) * inverse


def row_sum(block):
    return jnp.sum(block, axis=1, keepdims=True)


def fetch_square(sems, slot, full, half, own, peer):
    count = own.shape[-2]
    near, far = rows(half * count, count), rows((1 - half) * count, count)
    if len(full.shape) == 3:
        near, far = (slice(None), near), (slice(None), far)
    return fetch(sems, slot, own, full.at[near]), fetch(sems, slot + 1, peer, full.at[far])


def attention(
    live_count, normed, resid, stats2, par, cotangent, cot_peer, q_own, q_peer, p_own, p_peer,
    second, first_near, squares_out, block_out, grad_resid, grad_branch, small, second_peer, first_peer,
    sems, sends, recvs, wqkv, wp, query, keys, values, grad_mixed, mixed, grad_q, grad_k, grad_v, grad_out,
    grad_normed, resid_in, squares, block, *pixel_scratch,
):
    half = lax.axis_index("head")
    live = (half < live_count[0]).astype(BF)
    arriving = fetch_square(sems, 0, wqkv, half, q_own, q_peer)
    later = fetch_square(sems, 2, wp, half, p_own, p_peer)
    later += (
        fetch(sems, 4, cotangent.at[half], grad_out.at[rows(half * 256, 256)]),
        fetch(sems, 5, cot_peer, grad_out.at[rows((1 - half) * 256, 256)]),
    )
    last = fetch(sems, 6, resid, resid_in)
    to_x = {"head": 1 - half}
    meet([to_x])
    exchanges = (
        remote(second, second_peer, sends, recvs, 0, to_x),
        remote(first_near, first_peer, sends, recvs, 1, to_x),
    )
    exchanges[0].start()
    wait(arriving)
    for column in range(0, PIX, 512):
        where = slice(column, column + 512)
        query[:, where] = (mm(wqkv[0], normed[:, where]).astype(BF).astype(F32) * 0.125).astype(BF)
        keys[:, where] = mm(wqkv[1], normed[:, where]).astype(BF)
        values[:, where] = mm(wqkv[2], normed[:, where]).astype(BF)
    wait(later)
    grad_out[...] = grad_out[...] * live
    for column in range(0, PIX, 512):
        where = slice(column, column + 512)
        grad_mixed[:, where] = mm(wp[...], grad_out[:, where]).astype(BF)

    def head(number, weights, grad_scores):
        where = rows(number * 64, 64)
        q, k, v, g = query[where, :], keys[where, :], values[where, :], grad_mixed[where, :]
        scores = mm(k.T, q)
        low = jnp.exp(scores - jnp.max(scores, axis=0, keepdims=True)).astype(BF)
        weights[...] = low
        mix = mm(jnp.concatenate([v, jnp.ones((16, PIX), BF)], 0), low)
        inverse = 1.0 / mix[64:65]
        mix = mix[0:64] * inverse
        mixed[where, :] = mix.astype(BF)
        g = (g.astype(F32) * inverse).astype(BF)
        delta = jnp.sum(mix * g.astype(F32), axis=0, keepdims=True)
        inner = low * (mm(v.T, g) - delta).astype(BF)
        grad_scores[...] = inner
        grad_q[where, :] = (mm(k, inner) * 0.125).astype(BF)
        grad_k[where, :] = mm(grad_scores[...], q.T).T.astype(BF)
        grad_v[where, :] = mm(weights[...], g.T).T.astype(BF)

    def heads(index, carry):
        for number in range(4):
            head(index * 4 + number, pixel_scratch[2 * number], pixel_scratch[2 * number + 1])
        return carry

    exchanges[1].start()
    lax.fori_loop(0, HEADS // 4, heads, 0)
    pairs = ((grad_q, normed), (grad_k, normed), (grad_v, normed), (mixed, grad_out))
    for which, (left, right) in enumerate(pairs):
        result = mm(left[...], right[...], NT).astype(BF)
        for part in range(32):
            plane, chunk = part // 16, part % 16
            squares[chunk // 8, plane, chunk % 8, which] = result[part * 16 : (part + 1) * 16]
    outgoing = (fetch(sems, 0, squares, squares_out),)
    for column in range(0, PIX, 512):
        where = slice(column, column + 512)
        grad_normed[:, where] = (
            mm(wqkv[0], grad_q[:, where], TN)
            + mm(wqkv[1], grad_k[:, where], TN)
            + mm(wqkv[2], grad_v[:, where], TN)
        )
    last.wait()
    for column in range(0, PIX, 512):
        where = slice(column, column + 512)
        total = resid_in[:, where] + mm(wp[...], mixed[:, where], TN) + par[:, PROJB : PROJB + 1]
        block[:, where] = (total * live.astype(F32)).astype(BF)
    outgoing += (fetch(sems, 1, block, block_out),)

    def back(group, carry):
        where = rows(group * BLOCK, BLOCK)
        unit = unit_of(resid_in[where, :], stats2, where)
        grad = grad_normed[where, :]
        outer = grad_out[where, :].astype(F32)
        total = outer + unit_back(grad * par[where, GAIN + 2 : GAIN + 3], unit, stats2[where, 1:2])
        low = total.astype(BF)
        grad_resid[where, :] = total
        grad_branch[where, :] = low
        small[where, 0:1] = row_sum(grad * unit)
        small[where, 1:2] = row_sum(grad)
        small[where, 2:3] = row_sum(low.astype(F32))
        small[where, 3:4] = row_sum(outer)
        return carry

    lax.fori_loop(0, 512 // BLOCK, back, 0)
    wait(outgoing)
    wait(exchanges)


def attention_call(*args):
    arrays, specs = operands(args)
    dma = pltpu.SemaphoreType.DMA
    full_bf = out((512, PIX), BF)
    squares = out((2, 2, 8, 4, 16, 512), BF)
    wide_bf = pltpu.VMEM((512, PIX), BF)
    wide_f32 = pltpu.VMEM((512, PIX), F32)
    return pl.pallas_call(
        attention,
        out_shape=[
            squares, full_bf, out((512, PIX), F32), full_bf, out((512, 4), F32), full_bf, out((256, PIX), BF),
        ],
        in_specs=specs,
        out_specs=[ANYWHERE] * 2 + [VMEM] * 3 + [ANYWHERE] * 2,
        scratch_shapes=[
            dma((8,)), dma((2,)), dma((2,)),
            pltpu.VMEM((3, 512, 512), BF),
            pltpu.VMEM((512, 512), BF),
        ]
        + [wide_bf] * 9
        + [wide_f32] * 2
        + [pltpu.VMEM(squares.shape, BF), wide_bf]
        + [pltpu.VMEM((PIX, PIX), BF)] * 8,
        cost_estimate=pl.CostEstimate(flops=3 * 10**10, bytes_accessed=20 * 2**20, transcendentals=0),
        compiler_params=pltpu.CompilerParams(
            collective_id=3, has_side_effects=True, vmem_limit_bytes=58 * 2**20
        ),
    )(*arrays)


def remote(source, dest, sends, recvs, slot, target):
    return pltpu.make_async_remote_copy(
        src_ref=source,
        dst_ref=dest,
        send_sem=sends.at[slot],
        recv_sem=recvs.at[slot],
        device_id=target,
        device_id_type=pl.DeviceIdType.MESH,
    )


def meet(targets):
    barrier = pltpu.get_barrier_semaphore()
    for target in targets:
        pl.semaphore_signal(barrier, inc=1, device_id=target, device_id_type=pl.DeviceIdType.MESH)
    pl.semaphore_wait(barrier, len(targets))


def position():
    place = lax.axis_index("batch")
    return place, place % 2, (place // 2) % 2, place // 4


PIECES = 6
KINDS = 10


def forward(
    timesteps, classes, norm_gain, norm_bias, conv_bias, proj_bias, emb_bias, emb_weight, class_table,
    images, cotangent, conv_weight, qkv_weight, proj_weight,
    par, pre_embed, image_peer, cot_peer, conv_peer, qkv_peer, proj_peer,
    first_out, near_out, other_out, hidden_out, stats0, stats1, second_out, resid, stats2, normed,
    sends, recvs, few_sends, few_recvs, sems, put_sems, columns, par_send, par_recv, lines, table, own, peer, other, spare, col, full, full_one, *kept,
):
    half = lax.axis_index("head")
    place, core, up, deep = position()
    z_low = deep % 2
    to_x = {"head": 1 - half}
    to_y = {"batch": place + 2 * (1 - 2 * up)}
    to_z = {"batch": place + 4 * (1 - 2 * z_low)}
    to_core = {"batch": place + (1 - 2 * core)}
    near, away = rows(half * 256, 256), rows((1 - half) * 256, 256)
    pictures = (
        fetch(sems, 0, images.at[half], own),
        fetch(sems, 1, images.at[1 - half], other),
    )
    table_copy = fetch(sems, 2, class_table, table)
    fulls = (full, full_one)
    first, first_near, first_other, hidden, second = kept
    own_weights = fetch(sems, 3, conv_weight.at[0], full.at[:, near, :])
    own_later = fetch(sems, 4, conv_weight.at[1], full_one.at[:, near, :])
    outgoing = []

    def put(source, dest):
        outgoing.append(fetch(put_sems, len(outgoing), source, dest))

    meet([to_x, to_y, to_z, to_core])

    def block(flip_core=0, flip_y=0, flip_z=0):
        c = 1 - core if flip_core else core
        y = 1 - up if flip_y else up
        z = 1 - z_low if flip_z else z_low
        return (c + 2 * y + 4 * z) * 32

    def views(piece, plane, start, count):
        where = rows(start, count)
        if piece < 4:
            taps = pl.ds(0, 5) if piece % 2 == 0 else pl.ds(5, 4)
            return fulls[piece // 2].at[taps, rows(plane * 256 + start, count), :]
        if piece == 4:
            return qkv_peer.at[:, where, :]
        return proj_peer.at[where, :]

    def source(piece, start, count):
        where = rows(start, count)
        if piece < 4:
            taps = pl.ds(0, 5) if piece % 2 == 0 else pl.ds(5, 4)
            return conv_weight.at[piece // 2, taps, where, :]
        if piece == 4:
            return qkv_weight.at[:, where, :]
        return proj_weight.at[where, :]

    def copy(piece, kind, start, count, target, local=False):
        dest = views(piece, half if local else 1 - half, start, count)
        return remote(
            source(piece, start, count) if local else dest, dest,
            sends.at[piece], recvs.at[piece], kind, target,
        )

    def regions(flip_core):
        return (
            (block(flip_core), 32),
            (block(flip_core, 1), 32),
            (block(flip_core, 0, 1), 32),
            (block(flip_core, 1, 1), 16),
            (block(flip_core, 1, 1) + 16, 16),
        )

    mine, others = regions(0), regions(1)

    def arrived(piece, kind):
        start, count = mine[kind] if kind < 5 else others[kind - 5]
        copy(piece, kind, start, count, to_core).wait_recv()

    def over_x(piece):
        arrived(piece, 0)
        for kind, target in ((1, to_y), (2, to_z), (5, to_core)):
            copy(piece, kind, block(), 32, target).start()

    def over_yz(piece):
        arrived(piece, 2)
        copy(piece, 3, block(0, 0, 1), 16, to_y).start()
        copy(piece, 7, block(0, 0, 1), 32, to_core).start()
        arrived(piece, 1)
        copy(piece, 4, block(0, 1, 0) + 16, 16, to_z).start()
        copy(piece, 6, block(0, 1, 0), 32, to_core).start()

    def diagonal(piece):
        arrived(piece, 3)
        copy(piece, 8, block(0, 1, 1), 16, to_core).start()
        arrived(piece, 4)
        copy(piece, 9, block(0, 1, 1) + 16, 16, to_core).start()

    def complete(piece):
        for kind in range(5, 10):
            arrived(piece, kind)

    def fetch_x(*pieces):
        for piece in pieces:
            copy(piece, 0, block(), 32, to_x, local=True).start()

    fetch_x(0, 1)

    table_copy.wait()
    width = class_table.shape[1]
    numbers = lax.broadcasted_iota(jnp.int32, (1, table.shape[0]), 1)
    freqs = jnp.exp(
        lax.broadcasted_iota(jnp.int32, (1, width // 2), 1).astype(F32) * (-math.log(10000.0) / (width // 2))
    )
    for slot in range(2):
        chosen = (numbers == classes[slot]).astype(BF)
        angles = timesteps[slot].astype(F32) * freqs
        pre_embed[slot : slot + 1, : width // 2] = jnp.cos(angles)
        pre_embed[slot : slot + 1, width // 2 : width] = jnp.sin(angles)
        line = mm(jnp.broadcast_to(chosen, (8, table.shape[0])), table[...])
        pre_embed[slot : slot + 1, :width] += line[0:1]
        pre_embed[slot : slot + 1, width:] = jnp.broadcast_to(classes[slot].astype(F32), (1, 128))
    embed = jax.nn.silu(pre_embed[:, :width])
    own_row = jnp.where(half == 0, embed[0:1], embed[1:2])
    peer_row = jnp.where(half == 0, embed[1:2], embed[0:1])
    lines[...] = jnp.zeros_like(lines)
    lines[0:3] = norm_gain[...]
    lines[3:6] = norm_bias[...]
    lines[6:8] = conv_bias[...]
    lines[8:9] = proj_bias[...]
    lines[9:11] = emb_bias[...]
    turned = lines[...].T
    columns[:, 0:11] = turned[:, 0:11]
    par[near, :] = turned[:, 0:11]
    for which in range(2):
        dense = emb_weight[which].astype(F32)
        par[near, SCALE + which : SCALE + which + 1] += row_sum(dense * own_row)
        columns[:, SCALE + which : SCALE + which + 1] += row_sum(dense * peer_row)
    par_send[...] = columns[...].T[0:16]
    block_copy = remote(par_send, par_recv, few_sends, few_recvs, 1, to_x)
    block_copy.start()

    masks = edge_masks(1)
    wait(pictures)

    def norm_zero(source, dest, base, stats, offset, group):
        here = rows(group * BLOCK, BLOCK)
        where = rows(base + group * BLOCK, BLOCK)
        unit = group_stats(source[here, :].astype(F32), stats, rows(offset + group * BLOCK, BLOCK))
        low = jax.nn.silu(unit * par[where, GAIN : GAIN + 1] + par[where, BIAS : BIAS + 1]).astype(BF)
        dest[rows(offset + group * BLOCK, BLOCK), :] = low
        return low.astype(F32)

    def norm_near(group, carry):
        low = norm_zero(own, first, half * 256, stats0, half * 256, group)
        first_near[rows(group * BLOCK, BLOCK), :] = low.astype(BF)
        put_taps(col, masks, low, half * 256 + group * BLOCK, 512, 0, 1)
        return carry

    def norm_other(group, carry):
        norm_zero(other, first_other, half * 256, spare, 0, group)
        return carry

    def conv_part(full, dest, mine, column, bias, inputs=None):
        where = near if mine else away
        result = None
        for tap in range(9):
            depth = slice(None)
            part = pl.ds(tap * 512, 512)
            if inputs is not None:
                depth = near if inputs else away
                part = rows(tap * 512 + (half if inputs else 1 - half) * 256, 256)
            term = mm(full[tap, where, depth], col[part, column : column + 512])
            result = term if result is None else result + term
        if inputs is None or inputs:
            dest[where, column : column + 512] = result + par[where, bias : bias + 1]
        else:
            dest[where, column : column + 512] += result

    over_x(0)
    fetch_x(2, 3)
    over_x(1)
    lax.fori_loop(0, 256 // BLOCK, norm_near, 0)
    over_x(2)
    picture = remote(images.at[1 - half], image_peer, few_sends, few_recvs, 0, to_x)
    picture.start()
    over_yz(0)
    over_yz(1)
    own_weights.wait()
    conv_part(full, hidden, True, 0, CONVB, True)
    diagonal(0)
    diagonal(1)
    over_yz(2)
    conv_part(full, hidden, True, 512, CONVB, True)
    complete(0)
    complete(1)
    put(full.at[:, away, :], conv_peer.at[0])
    diagonal(2)
    block_copy.wait_recv()
    par[away, :] = par_recv[...].T[:, 0:11]
    conv_part(full, hidden, False, 0, CONVB, True)
    conv_part(full, hidden, False, 512, CONVB, True)
    lax.fori_loop(0, 256 // BLOCK, norm_other, 0)
    put(first_other, other_out)
    picture.wait_recv()
    loaded = fetch(sems, 0, image_peer, peer)
    fetch_x(4, 5)
    loaded.wait()

    def norm_far(group, carry):
        low = norm_zero(peer, first, (1 - half) * 256, stats0, (1 - half) * 256, group)
        put_taps(col, masks, low, (1 - half) * 256 + group * BLOCK, 512, 0, 1)
        return carry

    lax.fori_loop(0, 256 // BLOCK, norm_far, 0)
    over_x(3)
    cot_copy = remote(cotangent.at[1 - half], cot_peer, few_sends, few_recvs, 2, to_x)
    cot_copy.start()
    conv_part(full, hidden, True, 0, CONVB, False)
    conv_part(full, hidden, True, 512, CONVB, False)
    over_yz(3)
    over_x(4)
    over_x(5)
    conv_part(full, hidden, False, 0, CONVB, False)
    diagonal(3)
    conv_part(full, hidden, False, 512, CONVB, False)
    over_yz(4)
    over_yz(5)
    put(hidden, hidden_out)
    put(first, first_out)
    put(first_near, near_out)

    def norm_one(group, carry):
        where = rows(group * BLOCK, BLOCK)
        unit = group_stats(hidden[where, :], stats1, where)
        unscaled = unit * par[where, GAIN + 1 : GAIN + 2] + par[where, BIAS + 1 : BIAS + 2]
        pre = unscaled * (1.0 + par[where, SCALE : SCALE + 1]) + par[where, SHIFT : SHIFT + 1]
        low = jax.nn.silu(pre).astype(BF)
        second[where, :] = low
        put_taps(col, masks, low.astype(F32), group * BLOCK, 512, 0, 1)
        return carry

    lax.fori_loop(0, 512 // BLOCK, norm_one, 0)
    complete(2)
    complete(3)
    put(full_one.at[:, away, :], conv_peer.at[1])
    put(second, second_out)
    diagonal(4)
    diagonal(5)
    own_later.wait()
    conv_part(full_one, resid, True, 0, CONVB + 1)
    conv_part(full_one, resid, True, 512, CONVB + 1)
    conv_part(full_one, resid, False, 0, CONVB + 1)
    conv_part(full_one, resid, False, 512, CONVB + 1)
    for image, base in ((own, half * 256), (peer, (1 - half) * 256)):

        def norm_two(group, carry, image=image, base=base):
            where = rows(base + group * BLOCK, BLOCK)
            total = resid[where, :] + image[rows(group * BLOCK, BLOCK), :].astype(F32)
            resid[where, :] = total
            unit = group_stats(total, stats2, where)
            normed[where, :] = (unit * par[where, GAIN + 2 : GAIN + 3] + par[where, BIAS + 2 : BIAS + 3]).astype(BF)
            return carry

        lax.fori_loop(0, 256 // BLOCK, norm_two, 0)
    complete(4)
    complete(5)
    cot_copy.wait_recv()
    for piece in range(PIECES):
        copy(piece, 0, block(), 32, to_x).wait_send()
        for kind, start, count in (
            (1, block(), 32), (2, block(), 32), (5, block(), 32),
            (3, block(0, 0, 1), 16), (7, block(0, 0, 1), 32),
            (4, block(0, 1, 0) + 16, 16), (6, block(0, 1, 0), 32),
            (8, block(0, 1, 1), 16), (9, block(0, 1, 1) + 16, 16),
        ):
            copy(piece, kind, start, count, to_x).wait_send()
    wait(outgoing)
    picture.wait_send()
    block_copy.wait_send()
    cot_copy.wait_send()


def forward_call(timesteps, classes, *args):
    arrays, specs = operands((Scalars(timesteps), Scalars(classes)) + args)
    images, cotangent, conv_weight, qkv_weight, proj_weight = arrays[-5:]
    width = arrays[-6].shape[1]
    half_bf = out((256, PIX), BF)
    full_bf = out((512, PIX), BF)
    full_f32 = out((512, PIX), F32)
    stats = out((512, 2), F32)
    dma = pltpu.SemaphoreType.DMA
    half_scratch = pltpu.VMEM((256, PIX), BF)
    return pl.pallas_call(
        forward,
        out_shape=[
            out((512, 11), F32),
            out((2, width + 128), F32),
            half_bf,
            half_bf,
            out(conv_weight.shape, BF),
            out(qkv_weight.shape, BF),
            out(proj_weight.shape, BF),
            full_bf, half_bf, half_bf, full_f32, stats, stats, full_bf, full_f32, stats, full_bf,
        ],
        in_specs=specs,
        out_specs=[VMEM] * 2 + [ANYWHERE] * 9 + [VMEM] * 2 + [ANYWHERE] + [VMEM] * 3,
        scratch_shapes=[
            dma((PIECES, KINDS)), dma((PIECES, KINDS)), dma((3,)), dma((3,)), dma((5,)), dma((7,)),
            pltpu.VMEM((256, 128), F32),
            pltpu.VMEM((16, 256), F32),
            pltpu.VMEM((16, 256), F32),
            pltpu.VMEM((16, 256), F32),
            pltpu.VMEM(arrays[-6].shape, BF),
            half_scratch, half_scratch, half_scratch,
            pltpu.VMEM((256, 2), F32),
            pltpu.VMEM((9 * 512, PIX), BF),
            pltpu.VMEM((9, 512, 512), BF),
            pltpu.VMEM((9, 512, 512), BF),
            pltpu.VMEM((512, PIX), BF),
            half_scratch,
            half_scratch,
            pltpu.VMEM((512, PIX), F32),
            pltpu.VMEM((512, PIX), BF),
        ],
        cost_estimate=pl.CostEstimate(flops=2 * 10**10, bytes_accessed=100 * 2**20, transcendentals=0),
        compiler_params=pltpu.CompilerParams(
            collective_id=1, has_side_effects=True, vmem_limit_bytes=58 * 2**20
        ),
    )(*arrays)


SENDS = 12


class Sum:
    def __init__(self, source, total, scratch, planes):
        self.source, self.total, self.planes = source, total, planes
        self.sends, self.recvs, self.core_in, self.first, self.y_in, self.second, self.z_in, self.result = scratch[:8]
        if planes:
            self.middle, self.x_in = scratch[8:10]
        self.half = lax.axis_index("head")
        self.place, self.core, self.up, self.deep = position()
        self.steps = [self.start, self.core_done, self.y_done, self.z_done]
        if planes:
            self.steps.append(self.x_done)
        self.steps += [self.z_back, self.y_back, self.finish]
        self.open = []
        self.count = 0

    def advance(self):
        if self.count < len(self.steps):
            self.steps[self.count]()
            self.count += 1

    def part(self, array, start, count):
        where = pl.ds(start, count)
        return array.at[:, where] if self.planes else array.at[where]

    def to_core(self):
        return {"batch": self.place + 1 - 2 * self.core}

    def to_y(self):
        return {"batch": self.place + 2 * (1 - 2 * self.up)}

    def to_z(self, ahead):
        return {"batch": (self.deep + ahead) % 4 * 4 + self.place % 4}

    def send(self, slot, source, dest, target):
        copy = remote(source, dest, self.sends, self.recvs, slot, target)
        copy.start()
        self.open.append(copy)

    def arrived(self, slot, dest):
        remote(dest, dest, self.sends, self.recvs, slot, self.to_core()).wait_recv()

    def of_core(self, core):
        return self.source.at[core] if self.planes else self.source.at[pl.ds(core * 8, 8)]

    def start(self):
        self.send(0, self.of_core(1 - self.core), self.core_in, self.to_core())

    def add(self, dest, left, *right):
        total = left[...].astype(F32)
        for term in right:
            total = total + term[...].astype(F32)
        dest[...] = total.astype(BF)

    def core_done(self):
        self.arrived(0, self.core_in)
        self.add(self.first, self.of_core(self.core), self.core_in)
        self.send(1, self.part(self.first, (1 - self.up) * 4, 4), self.y_in, self.to_y())

    def y_done(self):
        self.arrived(1, self.y_in)
        self.add(self.second, self.part(self.first, self.up * 4, 4), self.y_in)
        for ahead in (2, 1, 3):
            chunk = self.part(self.second, (self.deep + ahead) % 4, 1)
            self.send(1 + ahead, chunk, self.z_in.at[ahead - 1], self.to_z(ahead))

    def z_done(self):
        for ahead in (1, 2, 3):
            self.arrived(1 + ahead, self.z_in.at[ahead - 1])
        mine = self.part(self.second, self.deep, 1)
        terms = [self.z_in.at[number] for number in range(3)]
        if self.planes:
            self.add(self.middle, mine, *terms)
            self.send(10, self.middle.at[1 - self.half], self.x_in, {"head": 1 - self.half})
        else:
            self.add(self.result, mine, *terms)
            self.give()

    def x_done(self):
        self.arrived(10, self.x_in)
        self.add(self.result, self.middle.at[self.half], self.x_in)
        self.give()

    def chunks(self, start, count):
        return self.total.at[pl.ds(start, count)]

    def chunk(self, deep):
        return self.core * 8 + self.up * 4 + deep

    def give(self):
        mine = self.chunks(self.chunk(self.deep), 1)
        for ahead in (2, 1, 3):
            self.send(4 + ahead, self.result, mine, self.to_z(ahead))
        self.kept = pltpu.make_async_copy(self.result, mine, self.sends.at[11])
        self.kept.start()

    def z_back(self):
        for ahead in (1, 2, 3):
            self.arrived(4 + ahead, self.chunks(self.chunk((self.deep + 4 - ahead) % 4), 1))
        self.kept.wait()
        part = self.chunks(self.chunk(0), 4)
        self.send(8, part, part, self.to_y())

    def y_back(self):
        self.arrived(8, self.chunks(self.core * 8 + (1 - self.up) * 4, 4))
        part = self.chunks(self.core * 8, 8)
        self.send(9, part, part, self.to_core())

    def finish(self):
        self.arrived(9, self.chunks((1 - self.core) * 8, 8))
        for copy in self.open:
            copy.wait_send()


def sum_scratch(tail, planes):
    lead = (2,) if planes else ()
    shapes = [
        pltpu.SemaphoreType.DMA((SENDS,)),
        pltpu.SemaphoreType.DMA((SENDS,)),
        pltpu.VMEM(lead + (8,) + tail, BF),
        pltpu.VMEM(lead + (8,) + tail, BF),
        pltpu.VMEM(lead + (4,) + tail, BF),
        pltpu.VMEM(lead + (4,) + tail, BF),
        pltpu.VMEM((3,) + lead + (1,) + tail, BF),
        pltpu.VMEM((1,) + tail, BF),
    ]
    if planes:
        shapes += [pltpu.VMEM((2, 1) + tail, BF), pltpu.VMEM((1,) + tail, BF)]
    return shapes


def weight_back(grads, chunk_taps, col, turned):
    for tap in chunk_taps:
        result = mm(col[tap * 256 : (tap + 1) * 256, :], turned[:PIX, :])
        result = result + mm(col[(9 + tap) * 256 : (10 + tap) * 256, :], turned[PIX:, :])
        result = result.astype(BF)
        for part in range(16):
            grads[part, tap] = result[part * 16 : (part + 1) * 16]


PARTS = ((0, 3), (3, 6), (6, 8), (8, 9))
PARTS_ZERO = ((0, 3), (3, 6), (6, 8), (8, 9))
HALVES = ((0, 2), (2, 4))

(TAPS_ONE, CONV_ONE, AWAY_ONE, NEAR_ONE, PAIR_ONE, GRAD_ONE, SHARE, PAIR_ZERO,
 GRAD_ZERO, TAPS_ZERO, CONV_ZERO, AWAY_ZERO, NEAR_ZERO, ROWS, SMALL) = range(100, 115)
ORDER = (
    TAPS_ONE, 0, 1, CONV_ONE, 0, 1, CONV_ONE, AWAY_ONE, NEAR_ONE, 0, PAIR_ONE, GRAD_ONE, 1, 2,
    GRAD_ONE, 2, 3, 0, GRAD_ONE, 4, 3, GRAD_ONE, 5, SHARE, 4, PAIR_ZERO, 5, 1, 2, GRAD_ZERO, 6, 3,
    GRAD_ZERO, 6, 7, 4, 2, 0, 5, 1, GRAD_ZERO, 7, 8, GRAD_ZERO, 9, 3, TAPS_ZERO, 8, 6, 9, CONV_ZERO,
    4, 7, CONV_ZERO, 2, 8, 9, 0, 5, AWAY_ZERO, NEAR_ZERO, 1, ROWS, 2, 3, 0, 2, 0, 1, 6, 1, 4, SMALL,
    3, SMALL, 3, 7, 4, SMALL, 4, 8, 9, 5, 5, 6, 5, 7, SMALL, 6, 8, 6, 9, 7, 7, 8, 9, 8, 9,
)


def backward(
    live_count, squares, grad_branch, block, hidden, second, second_peer,
    first, first_other, first_peer, grad_resid, images, image_peer, w_own, w_peer,
    stats0, stats1, par, small2, pre_embed, emb_weight,
    square_sum, sum1, sum0, images_grad, far_in, block_out, sums, class_rows, mod_out, pre_out,
    sems, sends, recvs, all_sends, all_recvs,
    grads1, grads0, col, turned, full, slope_in, wide_in, source_in, branch_in, hidden_in, grad_hidden,
    far, columns, flat, mod, mod_send, pres, rows_own, rows_in, total, total_in,
    *scratch,
):
    half = lax.axis_index("head")
    place, core, up, deep = position()
    to_x = {"head": 1 - half}
    others = [{"batch": (place + ahead) % 16} for ahead in range(1, 16)]
    near, away = rows(half * 256, 256), rows((1 - half) * 256, 256)
    exchanges = {}
    local = {}

    local["weights"] = fetch_conv(sems.at[pl.ds(6, 2)], full, half, 1, w_own, w_peer)
    local["wide"] = (fetch(sems, 8, hidden, wide_in),)
    local["inputs"] = (
        fetch(sems, 9, second, source_in.at[0]),
        fetch(sems, 10, second_peer, source_in.at[1]),
    )
    meet([to_x] + others)

    def send(slot, source, dest, target):
        exchanges[slot] = remote(source, dest, sends, recvs, slot, target)
        exchanges[slot].start()

    send(0, grad_branch.at[away], branch_in, to_x)

    chains = []
    for low, high in HALVES:
        where = pl.ds(low, high - low)
        chains.append(Sum(squares.at[:, :, :, where], square_sum.at[:, where], scratch[:10], True))
        scratch = scratch[10:]
    for source, dest, parts in ((grads1, sum1, PARTS), (grads0, sum0, PARTS_ZERO)):
        for low, high in parts:
            where = pl.ds(low, high - low)
            chains.append(Sum(source.at[:, where], dest.at[:, where], scratch[:8], False))
            scratch = scratch[8:]

    masks = edge_masks(-1)
    pair = col.at[pl.ds(9 * 256, 9 * 256)]
    picture = source_in.at[0]
    width = emb_weight.shape[2]

    def taps_one(_):
        taps_of(col, masks, grad_branch, 0, 512, 0, -1)
        wait(local["weights"])

    def conv_back(count):
        column = 512 * count
        result = None
        for tap in range(9):
            term = mm(full[tap], col[tap * 512 : (tap + 1) * 512, column : column + 512], TN)
            result = term if result is None else result + term
        slope_in[:, column : column + 512] = result

    def back_one(base):
        def step(group, carry):
            where = rows(base + group * BLOCK, BLOCK)
            unit = unit_of(wide_in[where, :], stats1, where)
            gain = par[where, GAIN + 1 : GAIN + 2]
            unscaled = unit * gain + par[where, BIAS + 1 : BIAS + 2]
            scale = 1.0 + par[where, SCALE : SCALE + 1]
            grad_pre = slope_in[where, :] * silu_slope(unscaled * scale + par[where, SHIFT : SHIFT + 1])
            grad = grad_pre * scale
            low = unit_back(grad * gain, unit, stats1[where, 1:2]).astype(BF)
            grad_hidden[where, :] = low
            columns[where, 2:3] = row_sum(grad_pre * unscaled)
            columns[where, 3:4] = row_sum(grad_pre)
            columns[where, 4:5] = row_sum(grad * unit)
            columns[where, 5:6] = row_sum(grad)
            columns[where, 6:7] = row_sum(low.astype(F32))
            return carry

        lax.fori_loop(0, 256 // BLOCK, step, 0)

    def away_one(_):
        local["weights"] = fetch_conv(sems.at[pl.ds(6, 2)], full, half, 0, w_own, w_peer)
        columns[...] = jnp.zeros_like(columns)
        columns[:, 7:11] = small2[...]
        wait(local["wide"])
        back_one((1 - half) * 256)
        send(1, grad_hidden.at[away], hidden_in, to_x)

    def near_one(_):
        back_one(half * 256)
        local["wide"] = (fetch(sems, 8, grad_resid, wide_in),)
        flat[...] = columns[...].T[0:16]
        mod[place, half] = flat[2:4, near]
        mod_send[...] = flat[2:4, away]
        send(2, mod_send, mod.at[place, half], to_x)
        pres[place] = pre_embed[...]
        for ahead, target in enumerate(others):
            remote(pres.at[place], pres.at[place], all_sends, all_recvs, ahead, target).start()

    def pair_one(_):
        exchanges[0].wait_recv()
        taps_of(col, masks, grad_branch.at[near], 0, 256, 0, -1)
        taps_of(pair, masks, branch_in, 0, 256, 0, -1)
        wait(local["inputs"])
        turned[:PIX, :] = source_in[0].T
        turned[PIX:, :] = source_in[1].T
        local["inputs"] = (
            fetch(sems, 9, first, source_in.at[0]),
            fetch(sems, 10, first_other, source_in.at[1, near]),
            fetch(sems, 11, first_peer, source_in.at[1, away]),
        )

    def grad_one(count):
        weight_back(grads1, range(*PARTS[count]), col, turned)
        if count == 0:
            send(6, block.at[away], block_out.at[half], to_x)
            local["block"] = fetch(sems, 3, block.at[near], block_out.at[half])

    def share(_):
        remote(mod_send, mod.at[place, 1 - half], sends, recvs, 2, to_x).wait_recv()
        for ahead, target in enumerate(others):
            remote(mod.at[place], mod.at[place], all_sends, all_recvs, 15 + ahead, target).start()

    def pair_zero(_):
        exchanges[1].wait_recv()
        taps_of(col, masks, grad_hidden.at[near], 0, 256, 0, -1)
        taps_of(pair, masks, hidden_in, 0, 256, 0, -1)
        wait(local["inputs"])
        turned[:PIX, :] = source_in[0].T
        turned[PIX:, :] = source_in[1].T
        local["inputs"] = (
            fetch(sems, 9, images.at[half], picture.at[near]),
            fetch(sems, 10, image_peer, picture.at[away]),
        )

    def grad_zero(count):
        weight_back(grads0, range(*PARTS_ZERO[count]), col, turned)

    def taps_zero(_):
        taps_of(col, masks, grad_hidden, 0, 512, 0, -1)
        wait(local["weights"])

    def back_zero(base, dest):
        def step(group, carry):
            here = rows(group * BLOCK, BLOCK)
            where = rows(base + group * BLOCK, BLOCK)
            unit = unit_of(picture[where, :].astype(F32), stats0, where)
            gain = par[where, GAIN : GAIN + 1]
            grad = slope_in[where, :] * silu_slope(unit * gain + par[where, BIAS : BIAS + 1])
            result = wide_in[where, :] + unit_back(grad * gain, unit, stats0[where, 1:2])
            dest[here, :] = result.astype(dest.dtype)
            columns[where, 0:1] = row_sum(grad * unit)
            columns[where, 1:2] = row_sum(grad)
            return carry

        lax.fori_loop(0, 256 // BLOCK, step, 0)

    def away_zero(_):
        wait(local["inputs"])
        wait(local["wide"])
        back_zero((1 - half) * 256, far)
        send(3, far, far_in, to_x)

    def near_zero(_):
        back_zero(half * 256, images_grad)
        flat[...] = columns[...].T[0:16]
        total[0] = flat[:, away]
        send(4, total.at[0], total_in.at[0], to_x)

    def class_part(_):
        for ahead in range(15):
            origin = (place + 15 - ahead) % 16
            remote(pres.at[origin], pres.at[origin], all_sends, all_recvs, ahead, to_x).wait_recv()
            remote(mod.at[origin], mod.at[origin], all_sends, all_recvs, 15 + ahead, to_x).wait_recv()
        result = None
        for which in range(2):
            factor = jnp.concatenate([mod[:, 0, which, :], mod[:, 1, which, :]], 0)
            term = mm(split(factor, 0), emb_weight[which])
            result = term if result is None else result + term
        result = result[0:32] + result[32:64] + result[64:96]
        rows_own[0] = result[0:16]
        rows_own[1] = result[16:32]
        send(5, rows_own, rows_in, to_x)

    def landed(slot, step):
        remote(total.at[0], total_in.at[step], sends, recvs, slot, to_x).wait_recv()

    def small_sums(count):
        if count == 0:
            landed(4, 0)
            total[1] = flat[:, near] + total_in[0]
            send(7, total.at[1], total_in.at[1], {"batch": place + 1 - 2 * core})
        elif count == 1:
            landed(7, 1)
            total[2] = total[1] + total_in[1]
            send(8, total.at[2], total_in.at[2], {"batch": place + 2 * (1 - 2 * up)})
        elif count == 2:
            landed(8, 2)
            total[3] = total[2] + total_in[2]
            for ahead in (1, 2, 3):
                target = {"batch": (deep + ahead) % 4 * 4 + place % 4}
                send(8 + ahead, total.at[3], total_in.at[3 + deep], target)
            total_in[3 + deep] = total[3]
        else:
            for ahead in (1, 2, 3):
                landed(8 + ahead, 3 + (deep + 4 - ahead) % 4)
            sums[...] = (total_in[3] + total_in[4]) + (total_in[5] + total_in[6])
            remote(rows_own, rows_in, sends, recvs, 5, to_x).wait_recv()
            for slot in range(2):
                class_rows[slot] = (rows_own[slot] + rows_in[slot]) * silu_slope(pres[:, slot, :width])
            mod_out[...] = mod[...]
            pre_out[...] = pres[...]

    pieces = {
        TAPS_ONE: taps_one, CONV_ONE: conv_back, AWAY_ONE: away_one, NEAR_ONE: near_one,
        PAIR_ONE: pair_one, GRAD_ONE: grad_one, SHARE: share, PAIR_ZERO: pair_zero,
        GRAD_ZERO: grad_zero, TAPS_ZERO: taps_zero, CONV_ZERO: conv_back, AWAY_ZERO: away_zero,
        NEAR_ZERO: near_zero, ROWS: class_part, SMALL: small_sums,
    }
    counts = dict.fromkeys(pieces, 0)
    for entry in ORDER:
        if entry < 100:
            chains[entry].advance()
        else:
            pieces[entry](counts[entry])
            counts[entry] += 1
    remote(far, far_in, sends, recvs, 3, to_x).wait_recv()
    remote(block.at[away], block_out.at[1 - half], sends, recvs, 6, to_x).wait_recv()
    local["block"].wait()
    for copy in exchanges.values():
        copy.wait_send()
    for ahead, target in enumerate(others):
        remote(pres.at[place], pres.at[place], all_sends, all_recvs, ahead, target).wait_send()
        remote(mod.at[place], mod.at[place], all_sends, all_recvs, 15 + ahead, target).wait_send()


def backward_call(*args):
    arrays, specs = operands(args)
    dma = pltpu.SemaphoreType.DMA
    scratch = [
        dma((12,)), dma((12,)), dma((12,)), dma((30,)), dma((30,)),
        pltpu.VMEM((16, 9, 16, 512), BF),
        pltpu.VMEM((16, 9, 16, 512), BF),
        pltpu.VMEM((9 * 512, PIX), BF),
        pltpu.VMEM((2 * PIX, 512), BF),
        pltpu.VMEM((9, 512, 512), BF),
        pltpu.VMEM((512, PIX), F32),
        pltpu.VMEM((512, PIX), F32),
        pltpu.VMEM((2, 512, PIX), BF),
        pltpu.VMEM((256, PIX), BF),
        pltpu.VMEM((256, PIX), BF),
        pltpu.VMEM((512, PIX), BF),
        pltpu.VMEM((256, PIX), BF),
        pltpu.VMEM((512, 128), F32),
        pltpu.VMEM((16, 512), F32),
        pltpu.VMEM((16, 2, 2, 256), F32),
        pltpu.VMEM((2, 256), F32),
        pltpu.VMEM((16, 2, 1024 + 128), F32),
        pltpu.VMEM((2, 16, 1024), F32),
        pltpu.VMEM((2, 16, 1024), F32),
        pltpu.VMEM((4, 16, 256), F32),
        pltpu.VMEM((7, 16, 256), F32),
    ]
    for low, high in HALVES:
        scratch += sum_scratch((high - low, 16, 512), True)
    for low, high in PARTS + PARTS_ZERO:
        scratch += sum_scratch((high - low, 16, 512), False)
    outs = [
        (out((16, 4, 16, 512), BF), ANYWHERE),
        (out((16, 9, 16, 512), BF), ANYWHERE),
        (out((16, 9, 16, 512), BF), ANYWHERE),
        (out((256, PIX), F32), VMEM),
        (out((256, PIX), BF), ANYWHERE),
        (out((2, 256, PIX), BF), ANYWHERE),
        (out((16, 256), F32), VMEM),
        (out((2, 16, 1024), F32), VMEM),
        (out((16, 2, 2, 256), F32), VMEM),
        (out((16, 2, 1024 + 128), F32), VMEM),
    ]
    return pl.pallas_call(
        backward,
        out_shape=[o for o, _ in outs],
        in_specs=specs,
        out_specs=[spec for _, spec in outs],
        scratch_shapes=scratch,
        cost_estimate=pl.CostEstimate(flops=4 * 10**10, bytes_accessed=200 * 2**20, transcendentals=0),
        compiler_params=pltpu.CompilerParams(
            collective_id=2, has_side_effects=True, vmem_limit_bytes=60 * 2**20
        ),
    )(*arrays)


TRIPLES = ((0, 3), (3, 6), (6, 9))


def finish(
    sum0, sum1, squares, near, far, block_in, mod, pres, rows_in, sums,
    block_out, conv, qkv, proj, images_grad, emb, table, gains, biases, conv_biases, emb_biases, proj_bias,
    ins, outs, low, low_square, wide, square, mine, other, block, grads, emb_out, table_out,
):
    half = lax.axis_index("head")
    width = rows_in.shape[2]
    reads = []
    for layer, source in enumerate((sum0, sum1)):
        for number, (start, stop) in enumerate(TRIPLES):
            taps = pl.ds(start, stop - start)
            reads.append(fetch(ins, layer * 3 + number, source.at[:, taps], low.at[layer, :, taps]))
    reads.append(fetch(ins, 6, squares, low_square))
    reads.append(fetch(ins, 7, near, mine))
    reads.append(fetch(ins, 8, far, other))
    reads.append(fetch(ins, 9, block_in, block))
    writes = []

    def write(source, dest):
        writes.append(fetch(outs, len(writes), source, dest))

    for number, row in enumerate((0, 4, 7)):
        gains[number : number + 1] = sums[row : row + 1]
        biases[number : number + 1] = sums[row + 1 : row + 2]
    conv_biases[0:1] = sums[6:7]
    conv_biases[1:2] = sums[9:10]
    emb_biases[...] = sums[2:4]
    proj_bias[...] = sums[10:11]

    numbers = lax.broadcasted_iota(jnp.int32, (32, table.shape[0]), 1)
    ids = jnp.concatenate([pres[:, slot, width : width + 1] for slot in range(2)], 0).astype(jnp.int32)
    chosen = (numbers == ids).astype(F32).astype(BF)
    class_rows = jnp.concatenate([rows_in[0], rows_in[1]], 0)
    table_out[...] = mm(jnp.concatenate([chosen] * 3, 0), split(class_rows, 0), TN)
    write(table_out, table)
    embed = jnp.concatenate([jax.nn.silu(pres[:, slot, :width]) for slot in range(2)], 0)
    parts = split(embed, 0)
    high, middle = parts[0:32], parts[32:64]
    for which in range(2):
        factor = split(jnp.concatenate([mod[:, slot, which, :] for slot in range(2)], 0), 0)
        left = jnp.concatenate([factor[0:32], factor[0:32], factor[32:64]], 0)
        emb_out[which] = mm(left, jnp.concatenate([high, middle, high], 0), TN)
    write(emb_out, emb)
    for layer in range(2):
        for number, (start, stop) in enumerate(TRIPLES):
            reads[layer * 3 + number].wait()
            for tap in range(start, stop):
                wide[layer, tap] = low[layer, :, tap].reshape(256, 512).astype(F32)
            taps = pl.ds(start, stop - start)
            write(wide.at[layer, taps], conv.at[layer, taps])
    reads[6].wait()
    for which in range(4):
        square[which] = low_square[:, which].reshape(256, 512).astype(F32)
    write(square.at[pl.ds(0, 3)], qkv)
    write(square.at[3], proj)
    reads[9].wait()
    write(block, block_out)
    reads[7].wait()
    reads[8].wait()
    grads[half] = mine[...]
    grads[1 - half] = other[...].astype(F32)
    write(grads, images_grad)
    wait(writes)


def finish_call(sum0, sum1, squares, near, far, block, mod, pres, rows_in, sums, table_shape):
    width = table_shape[1]
    shapes = [
        (2, 9, 256, 512),
        (3, 256, 512),
        (256, 512),
        (2, 256, PIX),
        (2, 256, width),
        table_shape,
        (3, 256),
        (3, 256),
        (2, 256),
        (2, 256),
        (1, 256),
    ]
    dma = pltpu.SemaphoreType.DMA
    return pl.pallas_call(
        finish,
        out_shape=[out(block.shape, BF)] + [out(shape, F32) for shape in shapes],
        in_specs=[ANYWHERE] * 6 + [VMEM] * 4,
        out_specs=[ANYWHERE] * 7 + [VMEM] * 5,
        scratch_shapes=[
            dma((10,)), dma((12,)),
            pltpu.VMEM((2,) + sum0.shape, BF),
            pltpu.VMEM(squares.shape, BF),
            pltpu.VMEM(shapes[0], F32),
            pltpu.VMEM((4, 256, 512), F32),
            pltpu.VMEM((256, PIX), F32),
            pltpu.VMEM((256, PIX), BF),
            pltpu.VMEM(block.shape, BF),
            pltpu.VMEM(shapes[3], F32),
            pltpu.VMEM(shapes[4], F32),
            pltpu.VMEM(shapes[5], F32),
        ],
        compiler_params=pltpu.CompilerParams(vmem_limit_bytes=58 * 2**20),
    )(sum0, sum1, squares, near, far, block, mod, pres, rows_in, sums)


def paired(
    images,
    timesteps,
    classes,
    live_count,
    norm_gain,
    norm_bias,
    conv_weight,
    conv_bias,
    emb_weight,
    emb_bias,
    class_table,
    qkv_weight,
    proj_weight,
    proj_bias,
    cotangent,
):
    (
        par, pre_embed, image_peer, cot_peer, conv_peer, q_peer, p_peer,
        first, first_near, first_other, hidden, stats0, stats1, second, resid, stats2, normed,
    ) = forward_call(
        timesteps, classes, norm_gain, norm_bias, conv_bias, proj_bias[None], emb_bias, emb_weight,
        *map(Far, (class_table, images, cotangent, conv_weight, qkv_weight, proj_weight)),
    )
    square_grads, block, grad_resid, grad_branch, small2, second_peer, first_peer = attention_call(
        Scalars(live_count), normed, Far(resid), stats2, par, Far(cotangent), Far(cot_peer),
        Far(qkv_weight), Far(q_peer), Far(proj_weight), Far(p_peer), Far(second), Far(first_near),
    )
    square_sum, conv_sum1, conv_sum0, near, far, block_out, sums, class_rows, mod, pre_all = backward_call(
        Scalars(live_count), square_grads, grad_branch, *map(Far, (block, hidden, second, second_peer)),
        *map(Far, (first, first_other, first_peer, grad_resid, images, image_peer, conv_weight, conv_peer)),
        stats0, stats1, par, small2, pre_embed, emb_weight,
    )
    (
        block_total, conv_total, qkv_total, proj_total, images_grad, emb_total, table_total,
        gains, biases, conv_biases, emb_biases, proj_biases,
    ) = finish_call(
        conv_sum0, conv_sum1, square_sum, near, far, block_out, mod, pre_all, class_rows, sums, class_table.shape
    )
    return (
        block_total,
        images_grad,
        gains,
        biases,
        conv_total,
        conv_biases,
        emb_total,
        emb_biases,
        table_total,
        qkv_total,
        proj_total,
        proj_biases[0],
    )


def solution(mesh):
    in_specs = (
        P("batch", "head", None),
        P("batch"),
        P("batch"),
        P("batch"),
        P(None, "head"),
        P(None, "head"),
        P(None, None, "head", None),
        P(None, "head"),
        P(None, "head", None),
        P(None, "head"),
        P(),
        P(None, "head", None),
        P("head", None),
        P("head"),
        P("batch", "head", None),
    )
    out_specs = (
        P("batch", "head", None),
        P("batch", "head", None),
        P(None, "head"),
        P(None, "head"),
        P(None, None, "head", None),
        P(None, "head"),
        P(None, "head", None),
        P(None, "head"),
        P(),
        P(None, "head", None),
        P("head", None),
        P("head"),
    )
    body = shards
    if mesh.shape["head"] == 2 and mesh.shape["batch"] == 16:
        body = paired
    return jax.shard_map(body, mesh=mesh, in_specs=in_specs, out_specs=out_specs, check_vma=False)
```
